32 devices in a mesh: ctx: 16 (over z, x, core), fsdp: 2 (over y).
Axes of the slice: x: 2, y: 2, z: 4, core: 2. Of those that a mesh axis runs over, the one named last changes fastest.
Arguments:
- inputs: bfloat16 [2, 2048, 2048], P('fsdp', 'ctx'), may hold values from -6 to 6
- w_query: bfloat16 [2048, 4096], P('fsdp'), may hold values from -0.125 to 0.125
- w_key: bfloat16 [2048, 512], P('fsdp'), may hold values from -0.125 to 0.125
- w_value: bfloat16 [2048, 512], P('fsdp'), may hold values from -0.125 to 0.125
- w_output: bfloat16 [4096, 2048], P('fsdp'), may hold values from -0.75 to 0.75
- norm_attn: bfloat16 [2048], P('fsdp'), may hold values from 0.5 to 1.5
- gain_query: bfloat16 [128], P('fsdp'), may hold values from 0.796875 to 1.59375
- gain_key: bfloat16 [128], P('fsdp'), may hold values from 0.796875 to 1.59375
- w_router: bfloat16 [2048, 16], P('fsdp'), may hold values from -0.0625 to 0.0625
- norm_moe: bfloat16 [2048], P('fsdp'), may hold values from 0.5 to 1.5
- w_gate: bfloat16 [16, 2048, 768], P('ctx', 'fsdp'), may hold values from -0.125 to 0.125
- w_up: bfloat16 [16, 2048, 768], P('ctx', 'fsdp'), may hold values from -0.125 to 0.125
- w_down: bfloat16 [16, 2048, 768], P('ctx', 'fsdp'), may hold values from -0.875 to 0.875
- lengths: int32 [2, 4], P('fsdp'), may hold values from 204 to 1280, as said below
- routes: int32 [2, 2048, 8], P('fsdp', 'ctx'), may hold values from 0 to 15, all different within a row
- pair_order: int32 [2, 16, 1024], P('fsdp', 'ctx'), may hold values from 0 to 1023, each once within a row
- cotangent: bfloat16 [2, 2048, 2048], P('fsdp', 'ctx'), may hold values from -6 to 6
Outputs:
- outputs: bfloat16 [2, 2048, 2048], P('fsdp', 'ctx')
- input_grad: bfloat16 [2, 2048, 2048], P('fsdp', 'ctx')
- grad_w_query: float32 [2048, 4096], P('fsdp')
- grad_w_key: float32 [2048, 512], P('fsdp')
- grad_w_value: float32 [2048, 512], P('fsdp')
- grad_w_output: float32 [4096, 2048], P('fsdp')
- grad_norm_attn: float32 [2048], P('fsdp')
- grad_gain_query: float32 [128], P('fsdp')
- grad_gain_key: float32 [128], P('fsdp')
- grad_w_router: float32 [2048, 16], P('fsdp')
- grad_norm_moe: float32 [2048], P('fsdp')
- grad_w_gate: float32 [16, 2048, 768], P('ctx', 'fsdp')
- grad_w_up: float32 [16, 2048, 768], P('ctx', 'fsdp')
- grad_w_down: float32 [16, 2048, 768], P('ctx', 'fsdp')
The draws below stay inside these ranges and needn't reach their ends.
Inputs may be any that keep to these rules, and one draw needn't show every extreme that they name: Each sequence holds, in an order drawn from the seed, one document of 1280 tokens, one of 204 tokens and two of 204 tokens or more; a sequence's lengths sum to 2048. `routes`: a token's 8 experts differ. `pair_order`: each device's row holds every number below 1024 once.
All inputs are finite; a program needn't handle non-finite values.
Results may differ from the reference program's by a relative error of at most 0.025.
Values may be sent and summed in bfloat16 or wider, within the bound.
No kernel may reach another device: no remote copies, remote signals or barrier semaphores. Data moves between devices by JAX's collectives and lax.ppermute only.
A program may use at most 256 MiB of HBM per device.

```python
import functools
import math
import jax
import jax.numpy as jnp
from jax import lax

D = 2048
H = 32
KVH = 4
HD = 128
F = 768
TOPK = 8
TOK_DEV = 128
DOCS = 4
SPLITS = 16
SEQ = 2048
DOC_LONG = 1280
DOC_MIN = 204
EXPERTS = 16
CAP = 80
N_CTX = 16
N_FSDP = 2


def shuffle_docs(row_key):
    return jax.random.permutation(row_key, DOCS)


def draw_lengths(key, part):
    key = jax.random.fold_in(key, 17)
    split_key, order_key = jax.random.split(key)
    leftover = SEQ - DOC_LONG - 3 * DOC_MIN
    divider = jax.random.randint(split_key, (N_FSDP,), 0, leftover + 1, dtype=jnp.int32)
    longest = jnp.full((N_FSDP,), DOC_LONG, jnp.int32)
    shortest = jnp.full((N_FSDP,), DOC_MIN, jnp.int32)
    lengths_table = jnp.stack([longest, shortest, shortest + divider, shortest + leftover - divider], axis=1)
    orders = jax.vmap(shuffle_docs)(jax.random.split(order_key, N_FSDP)).astype(jnp.int32)
    return jnp.take_along_axis(lengths_table, orders, axis=1).astype(jnp.int32)


def level_of(stream_key, dims, cuts, least, top_value):
    gain, own = 1.0, jax.random.fold_in(stream_key, 6)
    for position, parts in cuts:
        draws = jnp.exp(jax.random.uniform(jax.random.fold_in(own, position), (parts,), jnp.float32, least / len(cuts), top_value / len(cuts)))
        gain = gain * jnp.repeat(draws, dims[position] // parts).reshape([-1 if axis == position else 1 for axis in range(len(dims))])
    return gain


def choose_distinct(stream_key, rows, count, top, lift):
    ranking = jax.random.permutation(jax.random.fold_in(stream_key, 1), count)
    pull = ranking
    for power in range(3):
        pull = pull * pull // count
    pull = pull * lift // count
    lots = jax.random.randint(jax.random.fold_in(stream_key, 2), (rows, count), 0, 4096) + pull
    holders = jax.random.permutation(jax.random.fold_in(stream_key, 3), rows)[jnp.arange(count) % rows]
    lots = jnp.where(jnp.arange(rows)[:, None] == holders[None, :], 1 << 14, lots)
    merit = lots * count + jnp.arange(count)
    return lax.top_k(merit.astype(jnp.int32), top)[1].astype(jnp.int32)


def gaussian(key, dims, scale, most, cuts=(), held_as=jnp.bfloat16):
    values = jax.random.normal(key, dims, jnp.float32) * scale
    if len(cuts) > 0:
        values = level_of(key, dims, cuts, -0.22, 0.18) * values
    return jnp.clip(values, min=-most, max=most).astype(held_as)


def setup_inputs(seed: int = 0) -> dict:
    splits = jax.random.split(jax.random.key(seed), 18)
    return {
        "inputs": gaussian(splits[0], (N_FSDP, SEQ, D), 1.0, 6.0, ((0, 2), (1, 16))),
        "w_query": gaussian(splits[1], (D, H * HD), D ** -0.5, 0.125, ((0, 2),)),
        "w_key": gaussian(splits[2], (D, KVH * HD), D ** -0.5, 0.125, ((0, 2),)),
        "w_value": gaussian(splits[3], (D, KVH * HD), D ** -0.5, 0.125, ((0, 2),)),
        "w_output": gaussian(splits[4], (H * HD, D), (H * HD // 64) ** -0.5, 0.75, ((0, 2),)),
        "norm_attn": jnp.clip(1.0 + 0.1 * jax.random.normal(splits[5], (D,), jnp.float32), 0.5, 1.5).astype(jnp.bfloat16),
        "gain_query": jnp.clip(jnp.exp(math.log(1.59375) - 0.6931472 * jax.random.uniform(splits[6], (HD,), jnp.float32) ** level_of(splits[6], (HD,), ((0, 2),), -0.2, 0.2)), 0.796875, 1.59375).astype(jnp.bfloat16),
        "gain_key": jnp.clip(jnp.exp(math.log(1.59375) - 0.6931472 * jax.random.uniform(splits[7], (HD,), jnp.float32) ** level_of(splits[7], (HD,), ((0, 2),), -0.2, 0.2)), 0.796875, 1.59375).astype(jnp.bfloat16),
        "w_router": gaussian(splits[8], (D, EXPERTS), (4 * D) ** -0.5, 0.0625, ((0, 2),)),
        "norm_moe": jnp.clip(1.0 + 0.1 * jax.random.normal(splits[9], (D,), jnp.float32), 0.5, 1.5).astype(jnp.bfloat16),
        "w_gate": gaussian(splits[10], (EXPERTS, D, F), D ** -0.5, 0.125, ((0, 16), (1, 2))),
        "w_up": gaussian(splits[11], (EXPERTS, D, F), D ** -0.5, 0.125, ((0, 16), (1, 2))),
        "w_down": gaussian(splits[12], (EXPERTS, D, F), (F // 16) ** -0.5, 0.875, ((0, 16), (1, 2))),
        "lengths": draw_lengths(jax.random.fold_in(splits[17], 71), 0),
        "routes": choose_distinct(splits[14], N_FSDP * SEQ, EXPERTS, TOPK, 4096).reshape((N_FSDP, SEQ, TOPK)),
        "pair_order": jax.vmap(lambda own: jax.random.permutation(own, TOK_DEV * TOPK))(jax.random.split(splits[15], N_FSDP * SPLITS)).reshape((N_FSDP, SPLITS, TOK_DEV * TOPK)).astype(jnp.int32),
        "cotangent": gaussian(splits[16], (N_FSDP, SEQ, D), 1.0, 6.0, ((0, 2), (1, 16))),
    }


EPS = 1e-06
THETA = 1000000.0
HIGH = lax.Precision.HIGHEST

@jax.custom_vjp
def low(v):
    return lax.optimization_barrier(v.astype(jnp.bfloat16)).astype(jnp.float32)

@jax.custom_vjp
def low_back(v):
    return v

def low_keep(v):
    return (low(v), None)

def low_pass(kept, grad):
    return (grad,)

def back_keep(v):
    return (v, None)

def back_low(kept, grad):
    return (low(grad),)
low.defvjp(low_keep, low_pass)
low_back.defvjp(back_keep, back_low)

def rms_scale(values):
    return lax.rsqrt(lax.optimization_barrier(jnp.mean(values * values, axis=-1, keepdims=True)) + EPS)

def rotary_tables(positions, width):
    half = width // 2
    steps = jnp.arange(half, dtype=jnp.int32).astype(jnp.float32)
    inverse = jnp.exp(steps * (-2.0 * jnp.log(THETA) / width))
    angles = positions.astype(jnp.float32)[:, None] * inverse[None, :]
    return (jnp.cos(angles), jnp.sin(angles))

def rotate(values, cosine, sine):
    half = values.shape[-1] // 2
    first = values[..., :half]
    second = values[..., half:]
    return jnp.concatenate([first * cosine - second * sine, second * cosine + first * sine], axis=-1)

def documents(positions, lengths_row):
    ends = jnp.cumsum(lengths_row).astype(jnp.int32)
    return lax.optimization_barrier(jnp.sum((positions[:, None] >= ends[None, :]).astype(jnp.int32), axis=1))

def placements(route_row, order_row, experts):
    ranked = jnp.zeros_like(route_row).at[order_row].set(route_row)
    table = (ranked[:, None] == jnp.arange(experts, dtype=jnp.int32)[None, :]).astype(jnp.int32)
    running = jnp.cumsum(table, axis=0)
    return (lax.optimization_barrier(jnp.sum(running * table, axis=1)) - 1)[order_row]

def attend_sequence(operands):
    queries, keys, values, lengths_row = operands
    length = queries.shape[0]
    group = H // KVH
    positions = jnp.arange(length, dtype=jnp.int32)
    segment = documents(positions, lengths_row)
    keys_wide = jnp.repeat(keys, group, axis=1)
    values_wide = jnp.repeat(values, group, axis=1)
    width = min(512, length)
    scale = HD ** (-0.5)

    def one_block(number):
        start = number * width
        query_block = lax.dynamic_slice_in_dim(queries, start, width, 0)
        query_pos = lax.dynamic_slice_in_dim(positions, start, width, 0)
        query_seg = lax.dynamic_slice_in_dim(segment, start, width, 0)
        scores = low_back(jnp.einsum('qhd,khd->hqk', query_block, keys_wide, precision=HIGH) * scale)
        allowed = (positions[None, :] <= query_pos[:, None]) & (segment[None, :] == query_seg[:, None])
        scores = jnp.where(allowed[None], scores, -1e+30)
        weights = low(jax.nn.softmax(scores, axis=-1))
        return jnp.einsum('hqk,khd->qhd', weights, values_wide, precision=HIGH)
    result = lax.map(jax.checkpoint(one_block), jnp.arange(length // width, dtype=jnp.int32))
    return result.reshape(length, H, HD)

def make_forward(lengths, route_index, kept_share, token_table, pair_slot):

    def forward(inputs, w_query, w_key, w_value, w_output, norm_attn, gain_query, gain_key, w_router, norm_moe, w_gate, w_up, w_down):
        tokens = inputs.shape[0]
        positions = jnp.tile(jnp.arange(SEQ, dtype=jnp.int32), N_FSDP)
        cosine, sine = rotary_tables(positions, HD)
        cosine = cosine[:, None, :]
        sine = sine[:, None, :]
        normed = low(inputs * rms_scale(inputs) * norm_attn)
        query_raw = low_back(jnp.dot(normed, w_query, precision=HIGH)).reshape(tokens, H, HD)
        key_raw = low_back(jnp.dot(normed, w_key, precision=HIGH)).reshape(tokens, KVH, HD)
        value_raw = low_back(jnp.dot(normed, w_value, precision=HIGH))
        queries = low(rotate(query_raw * rms_scale(query_raw) * gain_query, cosine, sine))
        keys = low(rotate(key_raw * rms_scale(key_raw) * gain_key, cosine, sine))
        values = low(value_raw).reshape(tokens, KVH, HD)
        mixed = lax.map(attend_sequence, (queries.reshape(N_FSDP, SEQ, H, HD), keys.reshape(N_FSDP, SEQ, KVH, HD), values.reshape(N_FSDP, SEQ, KVH, HD), lengths))
        attended = low(low_back(mixed.reshape(tokens, H * HD)))
        branch = low_back(jnp.dot(attended, w_output, precision=HIGH))
        middle = inputs + branch
        routed_in = low(middle * rms_scale(middle) * norm_moe)
        logits = jnp.dot(routed_in, w_router, precision=HIGH)
        chosen = jnp.take_along_axis(logits, route_index, axis=1)
        gates = jax.nn.softmax(chosen, axis=-1) * kept_share
        padded = jnp.concatenate([routed_in, jnp.zeros((1, D), jnp.float32)], axis=0)

        def expert_rows(operands):
            gate_weight, up_weight, down_weight, rows = operands
            gathered = low_back(padded[rows])
            gate_part = low_back(jnp.dot(gathered, gate_weight, precision=HIGH))
            up_part = low_back(jnp.dot(gathered, up_weight, precision=HIGH))
            hidden = low(jax.nn.silu(gate_part) * up_part)
            return low(low_back(jnp.dot(hidden, down_weight.T, precision=HIGH)))
        returned = lax.map(jax.checkpoint(expert_rows), (w_gate, w_up, w_down, token_table))
        flat = jnp.concatenate([returned.reshape(-1, D), jnp.zeros((1, D), jnp.float32)], axis=0)
        per_pair = flat[pair_slot].reshape(tokens, TOPK, D)
        return middle + jnp.einsum('tk,tkd->td', gates, per_pair, precision=HIGH)
    return forward

def reference(inputs, w_query, w_key, w_value, w_output, norm_attn, gain_query, gain_key, w_router, norm_moe, w_gate, w_up, w_down, lengths, routes, pair_order, cotangent):
    tokens = N_FSDP * SEQ
    blocks = N_FSDP * N_CTX
    pairs = tokens * TOPK
    route_rows = routes.reshape(blocks, TOK_DEV * TOPK)
    place = jax.vmap(functools.partial(placements, experts=EXPERTS))(route_rows, pair_order.reshape(blocks, TOK_DEV * TOPK))
    kept = place < CAP
    rows = jnp.arange(blocks, dtype=jnp.int32)[:, None] * CAP + place
    slots = route_rows * (blocks * CAP) + rows
    total_slots = EXPERTS * blocks * CAP
    pair_slot = jnp.where(kept, slots, total_slots).reshape(pairs).astype(jnp.int32)
    slot_pair = jnp.full((total_slots,), pairs, jnp.int32).at[pair_slot].set(jnp.arange(pairs, dtype=jnp.int32), mode='drop')
    token_table = (slot_pair // TOPK).reshape(EXPERTS, blocks * CAP)
    kept_share = kept.reshape(tokens, TOPK).astype(jnp.float32)
    forward = make_forward(lengths, routes.reshape(tokens, TOPK), kept_share, token_table, pair_slot)
    result, pullback = jax.vjp(forward, inputs.reshape(tokens, D).astype(jnp.float32), w_query.astype(jnp.float32), w_key.astype(jnp.float32), w_value.astype(jnp.float32), w_output.astype(jnp.float32), norm_attn.astype(jnp.float32), gain_query.astype(jnp.float32), gain_key.astype(jnp.float32), w_router.astype(jnp.float32), norm_moe.astype(jnp.float32), w_gate.astype(jnp.float32), w_up.astype(jnp.float32), w_down.astype(jnp.float32))
    grads = pullback(cotangent.reshape(tokens, D).astype(jnp.float32))
    return (result.astype(jnp.bfloat16).reshape(N_FSDP, SEQ, D), grads[0].astype(jnp.bfloat16).reshape(N_FSDP, SEQ, D), grads[1], grads[2], grads[3], grads[4], grads[5], grads[6], grads[7], grads[8], grads[9], grads[10], grads[11], grads[12])
```

```python
import functools

import jax
import jax.numpy as jnp
from jax import lax
from jax.experimental import pallas as pl
from jax.experimental.pallas import tpu as pltpu
from jax.sharding import PartitionSpec as P

H = 32
KVH = 4
HD = 128
TOPK = 8
EPS = 1e-06
THETA = 1000000.0
HIGH = lax.Precision.HIGHEST
LOG2E = 1.4426950408889634
F32 = jnp.float32
BF16 = jnp.bfloat16
ROWS_T = (((1,), (1,)), ((), ()))
COLS_T = (((0,), (0,)), ((), ()))
VMEM_LIMIT = 48 * 1024 * 1024


def dot(a, b, dims=(((1,), (0,)), ((), ()))):
    return lax.dot_general(a, b, dims, preferred_element_type=F32)


def params(limit=VMEM_LIMIT):
    return pltpu.CompilerParams(vmem_limit_bytes=limit)


def cost(flops, moved, transcendentals=0):
    return pl.CostEstimate(
        flops=int(flops), bytes_accessed=int(moved), transcendentals=int(transcendentals)
    )


def flip(n_ctx, bit):
    return [(i, i ^ bit) for i in range(n_ctx)]


def ring(n_ctx, step):
    return [(i, (i + step) % n_ctx) for i in range(n_ctx)]


def block_order(n_ctx):
    c = lax.axis_index("ctx")
    nz = n_ctx // 4
    z, x, core = c // 4, (c // 2) % 2, c % 2
    table = []
    for dc in range(2):
        for k in range(nz):
            for dx in range(2):
                table.append(lax.rem(z + nz - k, nz) * 4 + (x ^ dx) * 2 + (core ^ dc))
    return jnp.stack(table).astype(jnp.int32)


def gather_ctx(piece, n_ctx):
    nz = n_ctx // 4
    pieces = []
    current = piece
    for k in range(nz):
        following = lax.ppermute(current, "ctx", ring(n_ctx, 4)) if k < nz - 1 else None
        pieces += [current, lax.ppermute(current, "ctx", flip(n_ctx, 2))]
        current = following
    mine = jnp.stack(pieces)
    return mine, lax.ppermute(mine, "ctx", flip(n_ctx, 1))


def scatter_ctx(mine, others, n_ctx):
    nz = n_ctx // 4
    arrived = lax.ppermute(others, "ctx", flip(n_ctx, 1))
    both = (mine.astype(F32) + arrived.astype(F32)).astype(BF16)
    carry = None
    for k in reversed(range(nz)):
        other = lax.ppermute(both[2 * k + 1], "ctx", flip(n_ctx, 2))
        total = both[2 * k].astype(F32) + other.astype(F32)
        if carry is not None:
            total = total + carry.astype(F32)
        if k > 0:
            carry = lax.ppermute(total.astype(BF16), "ctx", ring(n_ctx, -4))
    return total


def gather_fsdp(part):
    n_f = lax.axis_size("fsdp")
    if n_f != 2:
        return lax.all_gather(part, "fsdp", axis=0, tiled=True)
    other = lax.ppermute(part, "fsdp", [(0, 1), (1, 0)])
    first = lax.axis_index("fsdp") == 0
    return jnp.concatenate([jnp.where(first, part, other), jnp.where(first, other, part)], axis=0)


def scatter_fsdp(full):
    n_f = lax.axis_size("fsdp")
    if n_f != 2:
        return lax.psum_scatter(
            full.astype(BF16), "fsdp", scatter_dimension=0, tiled=True
        ).astype(F32)
    rows = full.shape[0] // 2
    first = lax.axis_index("fsdp") == 0
    low, high = full[:rows], full[rows:]
    sent = jnp.where(first, high, low).astype(BF16)
    other = lax.ppermute(sent, "fsdp", [(0, 1), (1, 0)])
    return jnp.where(first, low, high).astype(F32) + other.astype(F32)


def rotary_tables(length):
    half = HD // 2
    steps = jnp.arange(half, dtype=jnp.int32).astype(F32)
    inverse = jnp.exp(steps * (-2.0 * jnp.log(THETA) / HD))
    angles = jnp.arange(length, dtype=jnp.int32).astype(F32)[:, None] * inverse[None, :]
    cosine, sine = jnp.cos(angles), jnp.sin(angles)
    return (
        jnp.concatenate([cosine, cosine], axis=1),
        jnp.concatenate([-sine, sine], axis=1),
    )


def half_turn(v):
    return pltpu.roll(v, HD // 2, 1)


def qkv_kernel(
    hpd, table, xa, xb, w, gain, gq, gk, cosine, sine, normed, raw, query, key, value
):
    r = pl.program_id(0)
    half = pl.num_programs(0) // 2

    def body(x_ref):
        x = x_ref[0].astype(F32)
        r1 = lax.rsqrt(jnp.mean(x * x, axis=-1, keepdims=True) + EPS)
        n = (x * r1 * gain[...]).astype(BF16)
        normed[0] = n
        out = dot(n, w[...])
        raw[0] = out
        cos, sin = cosine[...], sine[...]
        for j in range(3 * hpd):
            v = out[:, j * HD : (j + 1) * HD]
            if j >= 2 * hpd:
                value[j - 2 * hpd] = v.astype(BF16)
                continue
            scale = lax.rsqrt(jnp.mean(v * v, axis=-1, keepdims=True) + EPS)
            v = v * scale * (gq[...] if j < hpd else gk[...])
            v = (v * cos + half_turn(v) * sin).astype(BF16)
            if j < hpd:
                query[j] = v
            else:
                key[j - hpd] = v

    @pl.when(r < half)
    def _():
        body(xa)

    @pl.when(r >= half)
    def _():
        body(xb)


def project(xa, xb, w, gain, gq, gk, cosine, sine, table, hpd):
    half, count, width = xa.shape
    n = 2 * half
    length = n * count
    cols = w.shape[1]
    whole = lambda r, t: (0, 0)
    at = lambda r, t: (t[r], 0)
    head_at = lambda r, t: (0, t[r], 0)
    head = jax.ShapeDtypeStruct((hpd, length, HD), BF16)
    return pl.pallas_call(
        functools.partial(qkv_kernel, hpd),
        grid_spec=pltpu.PrefetchScalarGridSpec(
            num_scalar_prefetch=1,
            grid=(n,),
            in_specs=[
                pl.BlockSpec((1, count, width), lambda r, t: (jnp.minimum(r, half - 1), 0, 0)),
                pl.BlockSpec((1, count, width), lambda r, t: (jnp.maximum(r - half, 0), 0, 0)),
                pl.BlockSpec((width, cols), whole),
                pl.BlockSpec((1, width), whole),
                pl.BlockSpec((1, HD), whole),
                pl.BlockSpec((1, HD), whole),
                pl.BlockSpec((count, HD), at),
                pl.BlockSpec((count, HD), at),
            ],
            out_specs=[
                pl.BlockSpec((1, count, width), lambda r, t: (r, 0, 0)),
                pl.BlockSpec((1, count, cols), lambda r, t: (r, 0, 0)),
                pl.BlockSpec((hpd, count, HD), head_at),
                pl.BlockSpec((hpd, count, HD), head_at),
                pl.BlockSpec((hpd, count, HD), head_at),
            ],
        ),
        out_shape=[
            jax.ShapeDtypeStruct((n, count, width), BF16),
            jax.ShapeDtypeStruct((n, count, cols), F32),
            head,
            head,
            head,
        ],
        compiler_params=params(),
        cost_estimate=cost(2 * length * width * cols, 4 * length * width + 8 * length * cols),
        name="project",
    )(table, xa, xb, w, gain, gq, gk, cosine, sine)


def qkv_back_kernel(hpd, table, dq, dk, dv, raw, cosine, sine, gq, gk, out, gains):
    r = pl.program_id(0)

    @pl.when(r == 0)
    def _():
        gains[...] = jnp.zeros_like(gains)

    cos, sin = cosine[...], sine[...]
    factor = HD**-0.5
    for j in range(2 * hpd):
        grad = (dq[j] if j < hpd else dk[j - hpd]) * factor
        gain = gq[...] if j < hpd else gk[...]
        v = raw[0, :, j * HD : (j + 1) * HD]
        scale = lax.rsqrt(jnp.mean(v * v, axis=-1, keepdims=True) + EPS)
        d = grad * cos - half_turn(grad) * sin
        u = d * gain
        inner = jnp.mean(u * v, axis=-1, keepdims=True)
        out[0, :, j * HD : (j + 1) * HD] = (
            scale * u - v * (scale * scale * scale * inner)
        ).astype(BF16)
        term = jnp.sum(d * v * scale, axis=0, keepdims=True)
        row = 0 if j < hpd else 1
        gains[row : row + 1, :] += term
    for j in range(hpd):
        out[0, :, (2 * hpd + j) * HD : (2 * hpd + j + 1) * HD] = dv[j].astype(BF16)


def qkv_back(dq, dk, dv, raw, cosine, sine, gq, gk, table, hpd):
    n, count, cols = raw.shape
    whole = lambda r, t: (0, 0)
    at = lambda r, t: (t[r], 0)
    head_at = lambda r, t: (0, t[r], 0)
    return pl.pallas_call(
        functools.partial(qkv_back_kernel, hpd),
        grid_spec=pltpu.PrefetchScalarGridSpec(
            num_scalar_prefetch=1,
            grid=(n,),
            in_specs=[
                pl.BlockSpec((hpd, count, HD), head_at),
                pl.BlockSpec((hpd, count, HD), head_at),
                pl.BlockSpec((hpd, count, HD), head_at),
                pl.BlockSpec((1, count, cols), lambda r, t: (r, 0, 0)),
                pl.BlockSpec((count, HD), at),
                pl.BlockSpec((count, HD), at),
                pl.BlockSpec((1, HD), whole),
                pl.BlockSpec((1, HD), whole),
            ],
            out_specs=[
                pl.BlockSpec((1, count, cols), lambda r, t: (r, 0, 0)),
                pl.BlockSpec((8, HD), whole),
            ],
        ),
        out_shape=[
            jax.ShapeDtypeStruct((n, count, cols), BF16),
            jax.ShapeDtypeStruct((8, HD), F32),
        ],
        compiler_params=params(),
        cost_estimate=cost(20 * n * count * cols, 10 * n * count * cols),
        name="qkv_back",
    )(table, dq, dk, dv, raw, cosine, sine, gq, gk)


def first_key(ends, docs, position):
    start = jnp.zeros_like(position)
    for d in range(docs):
        start = jnp.where(position >= ends[d], jnp.maximum(start, ends[d]), start)
    return start


def attend_kernel(docs, bq, bk, ends, query, key, value, mixed, total):
    i = pl.program_id(1)
    q = query[0]
    positions = i * bq + lax.broadcasted_iota(jnp.int32, (bq, 1), 0)
    starts = first_key(ends, docs, positions)
    low = lax.div(first_key(ends, docs, i * bq), bk)
    high = lax.div((i + 1) * bq - 1, bk) + 1

    def step(j, carry):
        acc, sums = carry
        rows = pl.ds(pl.multiple_of(j * bk, bk), bk)
        scores = dot(q, key[0, rows, :], ROWS_T)
        spots = j * bk + lax.broadcasted_iota(jnp.int32, (1, bk), 1)
        seen = (spots <= positions) & (spots >= starts)
        p = jnp.where(seen, jnp.exp2(scores * (LOG2E * HD**-0.5)), 0.0)
        return acc + dot(p.astype(BF16), value[0, rows, :]), sums + jnp.sum(
            p, axis=-1, keepdims=True
        )

    acc, sums = lax.fori_loop(
        low, high, step, (jnp.zeros((bq, HD), F32), jnp.zeros((bq, 1), F32))
    )
    mixed[0] = acc / sums
    total[0] = jnp.broadcast_to(jnp.log2(sums), (bq, HD))


def attend(query, key, value, ends, bq=256, bk=256):
    heads, length, _ = query.shape
    docs = ends.shape[0]
    block = pl.BlockSpec((1, bq, HD), lambda h, i, e: (h, i, 0))
    whole = pl.BlockSpec((1, length, HD), lambda h, i, e: (h, 0, 0))
    out = jax.ShapeDtypeStruct((heads, length, HD), F32)
    return pl.pallas_call(
        functools.partial(attend_kernel, docs, bq, bk),
        grid_spec=pltpu.PrefetchScalarGridSpec(
            num_scalar_prefetch=1,
            grid=(heads, length // bq),
            in_specs=[block, whole, whole],
            out_specs=[block, block],
        ),
        out_shape=[out, out],
        compiler_params=params(),
        cost_estimate=cost(
            heads * length * length * HD * 2, heads * length * HD * 14, heads * length * length // 2
        ),
        name="attend",
    )(ends, query, key, value)


def attend_back_kernel(docs, bq, bk, ends, query, grad, total, delta, key, value, dq, dk, dv):
    i = pl.program_id(1)

    @pl.when(i == 0)
    def _():
        dk[...] = jnp.zeros_like(dk)
        dv[...] = jnp.zeros_like(dv)

    q, g = query[0], grad[0]
    log_total, shift = total[0], delta[0]
    positions = i * bq + lax.broadcasted_iota(jnp.int32, (1, bq), 1)
    starts = first_key(ends, docs, positions)
    low = lax.div(first_key(ends, docs, i * bq), bk)
    high = lax.div((i + 1) * bq - 1, bk) + 1

    def step(j, acc):
        rows = pl.ds(pl.multiple_of(j * bk, bk), bk)
        k, v = key[0, rows, :], value[0, rows, :]
        scores = dot(k, q, ROWS_T)
        spots = j * bk + lax.broadcasted_iota(jnp.int32, (bk, 1), 0)
        seen = (spots <= positions) & (spots >= starts)
        p = jnp.where(seen, jnp.exp2(scores * (LOG2E * HD**-0.5) - log_total), 0.0)
        ds = (p * (dot(v, g, ROWS_T) - shift)).astype(BF16)
        dv[0, rows, :] += dot(p.astype(BF16), g)
        dk[0, rows, :] += dot(ds, q)
        return acc + dot(ds, k, COLS_T)

    dq[0] = lax.fori_loop(low, high, step, jnp.zeros((bq, HD), F32))


def attend_back(query, grad, total, delta, key, value, ends, bq=256, bk=256):
    heads, length, _ = query.shape
    docs = ends.shape[0]
    block = pl.BlockSpec((1, bq, HD), lambda h, i, e: (h, i, 0))
    line = pl.BlockSpec((1, 1, bq), lambda h, i, e: (h, 0, i))
    whole = pl.BlockSpec((1, length, HD), lambda h, i, e: (h, 0, 0))
    out = jax.ShapeDtypeStruct((heads, length, HD), F32)
    return pl.pallas_call(
        functools.partial(attend_back_kernel, docs, bq, bk),
        grid_spec=pltpu.PrefetchScalarGridSpec(
            num_scalar_prefetch=1,
            grid=(heads, length // bq),
            in_specs=[block, block, line, line, whole, whole],
            out_specs=[block, whole, whole],
        ),
        out_shape=[out, out, out],
        compiler_params=params(),
        cost_estimate=cost(
            heads * length * length * HD * 5, heads * length * HD * 20, heads * length * length // 2
        ),
        name="attend_back",
    )(ends, query, grad, total, delta, key, value)


def branch_kernel(hpd, table, mixed, w, out):
    total = None
    for j in range(hpd):
        part = dot(mixed[j].astype(BF16), w[j * HD : (j + 1) * HD, :])
        total = part if total is None else total + part
    out[0] = total.astype(BF16)


def branch_half(mixed, w, table, first, blocks):
    hpd, length, _ = mixed.shape
    count = length // (2 * blocks)
    width = w.shape[1]
    return pl.pallas_call(
        functools.partial(branch_kernel, hpd),
        grid_spec=pltpu.PrefetchScalarGridSpec(
            num_scalar_prefetch=1,
            grid=(blocks,),
            in_specs=[
                pl.BlockSpec((hpd, count, HD), lambda r, t: (0, t[r + first], 0)),
                pl.BlockSpec((hpd * HD, width), lambda r, t: (0, 0)),
            ],
            out_specs=pl.BlockSpec((1, count, width), lambda r, t: (r, 0, 0)),
        ),
        out_shape=jax.ShapeDtypeStruct((blocks, count, width), BF16),
        compiler_params=params(),
        cost_estimate=cost(length * hpd * HD * width, length * width),
        name="branch",
    )(table, mixed, w)


def branch_back_kernel(hpd, table, ga, gb, mixed, w, grad, dw):
    r = pl.program_id(0)
    half = pl.num_programs(0) // 2

    @pl.when(r == 0)
    def _():
        dw[...] = jnp.zeros_like(dw)

    def body(g_ref):
        g = g_ref[0]
        back = dot(g, w[...], ROWS_T)
        for j in range(hpd):
            grad[j] = back[:, j * HD : (j + 1) * HD].astype(BF16)
            dw[j * HD : (j + 1) * HD, :] += dot(mixed[j].astype(BF16), g, COLS_T)

    @pl.when(r < half)
    def _():
        body(ga)

    @pl.when(r >= half)
    def _():
        body(gb)


def branch_back(ga, gb, mixed, w, table):
    half, count, width = ga.shape
    hpd, length, _ = mixed.shape
    head_at = lambda r, t: (0, t[r], 0)
    return pl.pallas_call(
        functools.partial(branch_back_kernel, hpd),
        grid_spec=pltpu.PrefetchScalarGridSpec(
            num_scalar_prefetch=1,
            grid=(2 * half,),
            in_specs=[
                pl.BlockSpec((1, count, width), lambda r, t: (jnp.minimum(r, half - 1), 0, 0)),
                pl.BlockSpec((1, count, width), lambda r, t: (jnp.maximum(r - half, 0), 0, 0)),
                pl.BlockSpec((hpd, count, HD), head_at),
                pl.BlockSpec((hpd * HD, width), lambda r, t: (0, 0)),
            ],
            out_specs=[
                pl.BlockSpec((hpd, count, HD), head_at),
                pl.BlockSpec((hpd * HD, width), lambda r, t: (0, 0)),
            ],
        ),
        out_shape=[
            jax.ShapeDtypeStruct((hpd, length, HD), BF16),
            jax.ShapeDtypeStruct((hpd * HD, width), F32),
        ],
        compiler_params=params(),
        cost_estimate=cost(4 * length * hpd * HD * width, 2 * length * width),
        name="branch_back",
    )(table, ga, gb, mixed, w)


def slots_of(place, capacity):
    spots = lax.broadcasted_iota(jnp.int32, (capacity, place.shape[1]), 0)
    return spots == place


def take_rows_kernel(capacity, table, xa, xb, place, router, rows, logits):
    r = pl.program_id(0)
    half = pl.num_programs(0) // 2

    def body(x_ref):
        x = x_ref[0]
        chosen = slots_of(place[0], capacity).astype(BF16)
        rows[0] = dot(chosen, x).astype(BF16)
        logits[0] = dot(x, router[...])

    @pl.when(r < half)
    def _():
        body(xa)

    @pl.when(r >= half)
    def _():
        body(xb)


def take_rows(xa, xb, place, router, table, capacity):
    half, count, width = xa.shape
    n = 2 * half
    lanes = router.shape[1]
    at = lambda r, t: (t[r], 0, 0)
    return pl.pallas_call(
        functools.partial(take_rows_kernel, capacity),
        grid_spec=pltpu.PrefetchScalarGridSpec(
            num_scalar_prefetch=1,
            grid=(n,),
            in_specs=[
                pl.BlockSpec((1, count, width), lambda r, t: (jnp.minimum(r, half - 1), 0, 0)),
                pl.BlockSpec((1, count, width), lambda r, t: (jnp.maximum(r - half, 0), 0, 0)),
                pl.BlockSpec((1, 1, count), at),
                pl.BlockSpec((width, lanes), lambda r, t: (0, 0)),
            ],
            out_specs=[
                pl.BlockSpec((1, capacity, width), lambda r, t: (r, 0, 0)),
                pl.BlockSpec((1, count, lanes), at),
            ],
        ),
        out_shape=[
            jax.ShapeDtypeStruct((n, capacity, width), BF16),
            jax.ShapeDtypeStruct((n, count, lanes), F32),
        ],
        compiler_params=params(),
        cost_estimate=cost(4 * n * count * width * 128, 6 * n * count * width),
        name="take_rows",
    )(table, xa, xb, place, router)


def take_grads_kernel(capacity, table, grads, place, gates, rows, scaled, gate_rows):
    chosen = slots_of(place[0], capacity)
    picked = dot(chosen.astype(BF16), grads[0])
    rows[0] = picked.astype(BF16)
    gate = jnp.sum(jnp.where(chosen, gates[0], 0.0), axis=1, keepdims=True)
    scaled[0] = (picked * gate).astype(BF16)
    gate_rows[0] = jnp.broadcast_to(gate, gate_rows.shape[1:])


def take_grads(grads, place, gates, table, capacity):
    n, count, width = grads.shape
    at = lambda r, t: (t[r], 0, 0)
    own = lambda r, t: (r, 0, 0)
    return pl.pallas_call(
        functools.partial(take_grads_kernel, capacity),
        grid_spec=pltpu.PrefetchScalarGridSpec(
            num_scalar_prefetch=1,
            grid=(n,),
            in_specs=[
                pl.BlockSpec((1, count, width), at),
                pl.BlockSpec((1, 1, count), at),
                pl.BlockSpec((1, 1, count), at),
            ],
            out_specs=[
                pl.BlockSpec((1, capacity, width), own),
                pl.BlockSpec((1, capacity, width), own),
                pl.BlockSpec((1, capacity, 128), own),
            ],
        ),
        out_shape=[
            jax.ShapeDtypeStruct((n, capacity, width), BF16),
            jax.ShapeDtypeStruct((n, capacity, width), BF16),
            jax.ShapeDtypeStruct((n, capacity, 128), F32),
        ],
        compiler_params=params(),
        cost_estimate=cost(2 * n * count * width * 128, 6 * n * count * width),
        name="take_grads",
    )(table, grads, place, gates)


def give_results_kernel(capacity, table, results, grads, gate_rows, place, out, gate_grads):
    chosen = slots_of(place[0], capacity)
    result = results[0].astype(F32)
    scaled = (result * gate_rows[0][:, :1]).astype(BF16)
    out[0] = dot(chosen.astype(BF16), scaled, COLS_T).astype(BF16)
    inner = jnp.sum(result * grads[0].astype(F32), axis=1, keepdims=True)
    gate_grads[0] = jnp.sum(jnp.where(chosen, inner, 0.0), axis=0, keepdims=True)


def give_results(results, grads, gate_rows, place, table):
    n, capacity, width = results.shape
    count = place.shape[2]
    at = lambda r, t: (t[r], 0, 0)
    own = lambda r, t: (r, 0, 0)
    return pl.pallas_call(
        functools.partial(give_results_kernel, capacity),
        grid_spec=pltpu.PrefetchScalarGridSpec(
            num_scalar_prefetch=1,
            grid=(n,),
            in_specs=[
                pl.BlockSpec((1, capacity, width), own),
                pl.BlockSpec((1, capacity, width), own),
                pl.BlockSpec((1, capacity, 128), own),
                pl.BlockSpec((1, 1, count), at),
            ],
            out_specs=[
                pl.BlockSpec((1, count, width), at),
                pl.BlockSpec((1, 1, count), at),
            ],
        ),
        out_shape=[
            jax.ShapeDtypeStruct((n, count, width), BF16),
            jax.ShapeDtypeStruct((n, 1, count), F32),
        ],
        compiler_params=params(),
        cost_estimate=cost(2 * n * count * width * 128, 6 * n * count * width),
        name="give_results",
    )(table, results, grads, gate_rows, place)


def give_rows_kernel(capacity, table, rows, place, out):
    chosen = slots_of(place[0], capacity).astype(BF16)
    out[0] = dot(chosen, rows[0], COLS_T).astype(BF16)


def give_rows_half(rows, place, table, first, blocks):
    n, capacity, width = rows.shape
    count = place.shape[2]
    return pl.pallas_call(
        functools.partial(give_rows_kernel, capacity),
        grid_spec=pltpu.PrefetchScalarGridSpec(
            num_scalar_prefetch=1,
            grid=(blocks,),
            in_specs=[
                pl.BlockSpec((1, capacity, width), lambda r, t: (r + first, 0, 0)),
                pl.BlockSpec((1, 1, count), lambda r, t: (t[r + first], 0, 0)),
            ],
            out_specs=pl.BlockSpec((1, count, width), lambda r, t: (r, 0, 0)),
        ),
        out_shape=jax.ShapeDtypeStruct((blocks, count, width), BF16),
        compiler_params=params(),
        cost_estimate=cost(2 * blocks * count * width * 128, 4 * blocks * count * width),
        name="give_rows",
    )(table, rows, place)


def input_back_kernel(grads, w, x_ref, out, gain_grad):
    @pl.when(pl.program_id(0) == 0)
    def _():
        gain_grad[...] = jnp.zeros_like(gain_grad)

    back = dot(grads[0], w[...], ROWS_T)
    out[0] = back.astype(BF16)
    x = x_ref[0].astype(F32)
    r1 = lax.rsqrt(jnp.mean(x * x, axis=-1, keepdims=True) + EPS)
    gain_grad[0:1, :] += jnp.sum(back * (x * r1), axis=0, keepdims=True)


def input_back_half(grads, w, x, first):
    blocks, count, width = x.shape
    cols = w.shape[1]
    return pl.pallas_call(
        input_back_kernel,
        grid=(blocks,),
        in_specs=[
            pl.BlockSpec((1, count, cols), lambda r: (r + first, 0, 0)),
            pl.BlockSpec((width, cols), lambda r: (0, 0)),
            pl.BlockSpec((1, count, width), lambda r: (r, 0, 0)),
        ],
        out_specs=[
            pl.BlockSpec((1, count, width), lambda r: (r, 0, 0)),
            pl.BlockSpec((8, width), lambda r: (0, 0)),
        ],
        out_shape=[
            jax.ShapeDtypeStruct((blocks, count, width), BF16),
            jax.ShapeDtypeStruct((8, width), F32),
        ],
        compiler_params=params(),
        cost_estimate=cost(2 * blocks * count * width * cols, 4 * blocks * count * width),
        name="input_back",
    )(grads, w, x)


def local(
    inputs,
    w_query,
    w_key,
    w_value,
    w_output,
    norm_attn,
    gain_query,
    gain_key,
    w_router,
    norm_moe,
    w_gate,
    w_up,
    w_down,
    lengths,
    routes,
    pair_order,
    cotangent,
):
    n_ctx = lax.axis_size("ctx")
    n_f = lax.axis_size("fsdp")
    c = lax.axis_index("ctx")
    f = lax.axis_index("fsdp")
    count, width = inputs.shape[1], inputs.shape[2]
    length = count * n_ctx
    half = n_ctx // 2
    hpd = H // n_ctx
    hpf = H // n_f
    group = H // KVH
    n_exp = w_router.shape[1]
    capacity = 5 * count * TOPK // (4 * n_exp)
    table = block_order(n_ctx)

    heads = [c % hpf + hpf * ((c // hpf) * hpd + j) for j in range(hpd)]
    kv_heads = [h // group for h in heads]
    columns = lambda w, h: lax.dynamic_slice_in_dim(w, h * HD, HD, 1)
    w_part = jnp.concatenate(
        [columns(w_query, h) for h in heads]
        + [columns(w_key, h) for h in kv_heads]
        + [columns(w_value, h) for h in kv_heads],
        axis=1,
    )
    xa, xb = gather_ctx(inputs[0], n_ctx)
    w_qkv = gather_fsdp(w_part)
    vectors = jnp.concatenate([norm_attn, gain_query, gain_key, norm_moe])
    vectors = gather_fsdp(vectors[None])
    sizes = [norm_attn.shape[0], gain_query.shape[0], gain_key.shape[0], norm_moe.shape[0]]
    rows_of, at = [], 0
    for size in sizes:
        rows_of.append(vectors[:, at : at + size].reshape(1, n_f * size).astype(F32))
        at += size
    attn_gain, query_gain, key_gain, moe_gain = rows_of
    w_out = gather_fsdp(lax.dynamic_slice_in_dim(w_output, (c % hpf) * HD, HD, 0))
    w_out = lax.dynamic_slice_in_dim(w_out, (c // hpf) * hpd * HD, hpd * HD, 0)
    router = gather_fsdp(w_router)
    router_wide = jnp.pad(router, ((0, 0), (0, 128 - n_exp)))
    cot_all = lax.all_gather(cotangent[0], "ctx", axis=0)
    gate_w = lax.all_gather(w_gate[0], "fsdp", axis=0, tiled=True)
    up_w = lax.all_gather(w_up[0], "fsdp", axis=0, tiled=True)
    down_w = lax.all_gather(w_down[0], "fsdp", axis=0, tiled=True)

    pair_table = jnp.stack([routes[0].reshape(count * TOPK), pair_order[0, 0]])
    pair_table = lax.all_gather(pair_table, "ctx", axis=0)
    routes_all = pair_table[:, 0].reshape(n_ctx, count, TOPK)
    order_all = pair_table[:, 1].reshape(n_ctx, count, TOPK)
    mine = routes_all == c
    has = jnp.any(mine, axis=-1)
    rank = jnp.where(has, jnp.sum(jnp.where(mine, order_all, 0), axis=-1), count * TOPK)
    place = jnp.sum((rank[:, None, :] < rank[:, :, None]).astype(jnp.int32), axis=-1)
    place = jnp.where(has & (place < capacity), place, -1)[:, None, :]
    chosen_all = jnp.any(
        routes_all[..., None] == jnp.arange(n_exp, dtype=jnp.int32), axis=2
    )

    ends = jnp.cumsum(lengths[0]).astype(jnp.int32)
    cosine, sine = rotary_tables(length)

    normed, raw, query, key, value = project(
        xa, xb, w_qkv, attn_gain, query_gain, key_gain, cosine, sine, table, hpd
    )
    mixed, log_total = attend(query, key, value, ends)
    branch_b = branch_half(mixed, w_out, table, half, half)
    branch_a = branch_half(mixed, w_out, table, 0, half)
    x = inputs[0].astype(F32)
    middle = x + scatter_ctx(branch_a, branch_b, n_ctx)
    moe_scale = lax.rsqrt(jnp.mean(middle * middle, axis=-1, keepdims=True) + EPS)
    routed_in = (middle * moe_scale * moe_gain).astype(BF16)

    ra, rb = gather_ctx(routed_in, n_ctx)
    rows, logits = take_rows(ra, rb, place, router_wide, table, capacity)
    logits = logits[:, :, :n_exp]
    top = jnp.max(jnp.where(chosen_all, logits, -1e30), axis=-1, keepdims=True)
    weights = jnp.where(chosen_all, jnp.exp(logits - top), 0.0)
    gates = weights / jnp.sum(weights, axis=-1, keepdims=True)
    own_gates = jnp.sum(
        jnp.where(jnp.arange(n_exp, dtype=jnp.int32) == c, gates, 0.0), axis=-1
    )[:, None, :]
    grad_rows, pair_grad, gate_rows = take_grads(cot_all, place, own_gates, table, capacity)
    slots = n_ctx * capacity
    rows_flat = rows.reshape(slots, width)
    pair_flat = pair_grad.reshape(slots, width)
    gate_part = dot(rows_flat, gate_w)
    up_part = dot(rows_flat, up_w)
    sigma = jax.nn.sigmoid(gate_part)
    silu_gate = gate_part * sigma
    hidden = (silu_gate * up_part).astype(BF16)
    expert_out = dot(hidden, down_w, ROWS_T).astype(BF16)
    results, gate_grads = give_results(
        expert_out.reshape(n_ctx, capacity, width), grad_rows, gate_rows, place, table
    )
    gate_grads = lax.all_gather(gate_grads.reshape(length), "ctx", axis=0)
    moe = lax.psum_scatter(results, "ctx", scatter_dimension=0, tiled=False)
    outputs = (middle + moe.astype(F32)).astype(BF16)
    hidden_grad = dot(pair_flat, down_w)
    gate_part_grad = (hidden_grad * up_part * sigma * (1.0 + gate_part * (1.0 - sigma))).astype(
        BF16
    )
    up_part_grad = (hidden_grad * silu_gate).astype(BF16)
    row_grad = dot(gate_part_grad, gate_w, ROWS_T) + dot(up_part_grad, up_w, ROWS_T)
    row_grad = row_grad.astype(BF16).reshape(n_ctx, capacity, width)
    back_b = give_rows_half(row_grad, place, table, half, half)
    back_a = give_rows_half(row_grad, place, table, 0, half)
    routed_grad = scatter_ctx(back_a, back_b, n_ctx)
    grad_w_gate = scatter_fsdp(dot(rows_flat, gate_part_grad, COLS_T))
    grad_w_up = scatter_fsdp(dot(rows_flat, up_part_grad, COLS_T))
    grad_w_down = scatter_fsdp(dot(pair_flat, hidden, COLS_T))

    gate_grads = gate_grads.T.reshape(n_ctx, count, n_exp)
    logit_grad = gates * (gate_grads - jnp.sum(gates * gate_grads, axis=-1, keepdims=True))
    own_logit_grad = lax.dynamic_index_in_dim(logit_grad, c, 0, keepdims=False)
    routed_grad = routed_grad + lax.dot_general(
        own_logit_grad, router.astype(F32), ROWS_T, precision=HIGH
    )
    places = (table[:, None] == jnp.arange(n_ctx, dtype=jnp.int32)[None, :]).astype(F32)
    ordered = jnp.einsum("rb,bte->rte", places, logit_grad, precision=HIGH).astype(BF16)
    ordered = ordered.reshape(2, half * count, n_exp)
    grad_router = dot(ra.reshape(half * count, width), ordered[0], COLS_T) + dot(
        rb.reshape(half * count, width), ordered[1], COLS_T
    )
    grad_w_router = scatter_fsdp(grad_router)

    grad_out = cotangent[0].astype(F32)
    moe_scaled = routed_grad * moe_gain
    grad_moe_part = jnp.sum(routed_grad * middle * moe_scale, axis=0)
    middle_grad = (
        grad_out
        + moe_scale * moe_scaled
        - middle
        * (
            moe_scale
            * moe_scale
            * moe_scale
            * jnp.mean(moe_scaled * middle, axis=-1, keepdims=True)
        )
    )

    ga, gb = gather_ctx(middle_grad.astype(BF16), n_ctx)
    mixed_grad, grad_out_w = branch_back(ga, gb, mixed, w_out, table)
    delta = jnp.sum(mixed_grad.astype(F32) * mixed, axis=-1)[:, None, :]
    dq, dk, dv = attend_back(
        query, mixed_grad, log_total[:, :, 0][:, None, :], delta, key, value, ends
    )
    qkv_grad, gain_grads = qkv_back(
        dq, dk, dv, raw, cosine, sine, query_gain, key_gain, table, hpd
    )
    qkv_flat = qkv_grad.reshape(length, 3 * hpd * HD)
    normed_flat = normed.reshape(length, width)
    q_cols = hpd * HD
    grad_q = scatter_fsdp(dot(normed_flat, qkv_flat[:, :q_cols], COLS_T)).astype(BF16)
    grad_kv = scatter_fsdp(dot(normed_flat, qkv_flat[:, q_cols:], COLS_T))
    inner_b, gain_b = input_back_half(qkv_grad, w_qkv, xb, half)
    inner_a, gain_a = input_back_half(qkv_grad, w_qkv, xa, 0)
    normed_grad = scatter_ctx(inner_a, inner_b, n_ctx)

    grad_q = lax.all_gather(grad_q, "ctx", axis=0)
    grad_w_query = (
        grad_q.reshape(n_ctx // hpf, hpf, width // n_f, hpd, HD)
        .transpose(2, 0, 3, 1, 4)
        .reshape(width // n_f, H * HD)
        .astype(F32)
    )
    slots_kv = jnp.arange(KVH, dtype=jnp.int32)
    spread = jnp.stack([slots_kv == h for h in kv_heads]).astype(F32)
    grad_kv = grad_kv.reshape(width // n_f, 2, hpd, 1, HD) * spread[None, None, :, :, None]
    grad_kv = jnp.sum(grad_kv, axis=2).reshape(width // n_f, 2 * KVH * HD)
    grad_kv = lax.psum(grad_kv.astype(BF16), "ctx").astype(F32)
    grad_w_key = grad_kv[:, : KVH * HD]
    grad_w_value = grad_kv[:, KVH * HD :]
    spread_out = jnp.arange(n_f, dtype=jnp.int32)[:, None] == (
        (c // hpf) * hpd + jnp.arange(hpd, dtype=jnp.int32)[None, :]
    )
    if n_f == hpd:
        placed = grad_out_w
    else:
        placed = jnp.einsum(
            "fj,jrd->frd", spread_out.astype(F32), grad_out_w.reshape(hpd, HD, width)
        ).reshape(n_f * HD, width)
    grad_o = scatter_fsdp(placed).astype(BF16)
    grad_o = lax.all_gather(grad_o, "ctx", axis=0).reshape(n_ctx // hpf, hpf * HD, width)
    grad_w_output = lax.dynamic_index_in_dim(grad_o, f // hpd, 0, keepdims=False).astype(F32)

    grad_attn_part = gain_a[0] + gain_b[0]
    tiny = jnp.concatenate([grad_attn_part, grad_moe_part, gain_grads[0], gain_grads[1]])
    tiny = lax.psum(tiny, ("ctx", "fsdp"))
    tiny_outs, at = [], 0
    for size in (width, width, HD, HD):
        tiny_outs.append(
            lax.dynamic_slice_in_dim(tiny, at + f * (size // n_f), size // n_f, 0)
        )
        at += size
    grad_norm_attn, grad_norm_moe, grad_gain_query, grad_gain_key = tiny_outs

    attn_scale = lax.rsqrt(jnp.mean(x * x, axis=-1, keepdims=True) + EPS)
    attn_scaled = normed_grad * attn_gain
    input_grad = (
        middle_grad
        + attn_scale * attn_scaled
        - x
        * (
            attn_scale
            * attn_scale
            * attn_scale
            * jnp.mean(attn_scaled * x, axis=-1, keepdims=True)
        )
    )
    return (
        outputs[None],
        input_grad.astype(BF16)[None],
        grad_w_query,
        grad_w_key,
        grad_w_value,
        grad_w_output,
        grad_norm_attn,
        grad_gain_query,
        grad_gain_key,
        grad_w_router,
        grad_norm_moe,
        grad_w_gate[None],
        grad_w_up[None],
        grad_w_down[None],
    )


def solution(mesh):
    in_specs = (
        P("fsdp", "ctx", None),
        P("fsdp", None),
        P("fsdp", None),
        P("fsdp", None),
        P("fsdp", None),
        P("fsdp"),
        P("fsdp"),
        P("fsdp"),
        P("fsdp", None),
        P("fsdp"),
        P("ctx", "fsdp", None),
        P("ctx", "fsdp", None),
        P("ctx", "fsdp", None),
        P("fsdp", None),
        P("fsdp", "ctx", None),
        P("fsdp", "ctx", None),
        P("fsdp", "ctx", None),
    )
    out_specs = (
        P("fsdp", "ctx", None),
        P("fsdp", "ctx", None),
        P("fsdp", None),
        P("fsdp", None),
        P("fsdp", None),
        P("fsdp", None),
        P("fsdp"),
        P("fsdp"),
        P("fsdp"),
        P("fsdp", None),
        P("fsdp"),
        P("ctx", "fsdp", None),
        P("ctx", "fsdp", None),
        P("ctx", "fsdp", None),
    )
    return jax.shard_map(local, mesh=mesh, in_specs=in_specs, out_specs=out_specs, check_vma=False)
```

```python
import functools

import jax
import jax.numpy as jnp
from jax import lax
from jax.experimental import pallas as pl
from jax.experimental.pallas import tpu as pltpu
from jax.sharding import PartitionSpec as P

H = 32
KVH = 4
HD = 128
TOPK = 8
EPS = 1e-06
THETA = 1000000.0
HIGH = lax.Precision.HIGHEST
LOG2E = 1.4426950408889634
F32 = jnp.float32
BF16 = jnp.bfloat16
ROWS_T = (((1,), (1,)), ((), ()))
COLS_T = (((0,), (0,)), ((), ()))
VMEM_LIMIT = 48 * 1024 * 1024


def dot(a, b, dims=(((1,), (0,)), ((), ()))):
    return lax.dot_general(a, b, dims, preferred_element_type=F32)


def params(limit=VMEM_LIMIT):
    return pltpu.CompilerParams(vmem_limit_bytes=limit)


def cost(microseconds):
    return pl.CostEstimate(
        flops=int(microseconds * 1.15e9), bytes_accessed=0, transcendentals=0
    )


def flip(n_ctx, bit):
    return [(i, i ^ bit) for i in range(n_ctx)]


def ring(n_ctx, step):
    return [(i, (i + step) % n_ctx) for i in range(n_ctx)]


def block_order(n_ctx):
    c = lax.axis_index("ctx")
    nz = n_ctx // 4
    z, x, core = c // 4, (c // 2) % 2, c % 2
    table = []
    for k in range(nz):
        for dc in range(2):
            for dx in range(2):
                table.append(lax.rem(z + nz - k, nz) * 4 + (x ^ dx) * 2 + (core ^ dc))
    return jnp.stack(table).astype(jnp.int32)


def tie(*arrays):
    return lax.optimization_barrier(arrays)


class Side:
    def __init__(self, chain):
        self.chain, self.flying, self.left = chain, None, 0
        self.resume(None)

    def resume(self, landed):
        try:
            self.flying, self.left = self.chain.send(landed)
        except StopIteration:
            self.flying = None

    def finish(self):
        while self.flying is not None:
            self.resume(self.flying)


def land(air, sides, *others):
    due = [side for side in sides if side.flying is not None and side.left <= 1]
    for side in sides:
        side.left -= 1
    keys = list(air)
    arrays = tie(*air.values(), *(side.flying for side in due), *others)
    air.clear()
    for side, array in zip(due, arrays[len(keys) :]):
        side.resume(array)
    return dict(zip(keys, arrays)), arrays[len(keys) + len(due) :]


def pipeline(n_ctx, order, compute, token, sides, piece=None, scatter=False, closing=None):
    nz = n_ctx // 4
    air, have, state = {}, {}, ()

    def send(key, array, pairs):
        air[key] = lax.ppermute(array, "ctx", pairs)

    def bring(k):
        send(("beside", k), have["piece", k], flip(n_ctx, 2))
        if k + 1 < nz:
            send(("piece", k + 1), have["piece", k], ring(n_ctx, 4))

    def step_ends(*others):
        landed, others = land(air, sides, *others)
        have.update(landed)
        return others

    def total_of(own):
        total = own + have["away"].astype(F32)
        return total + have["carry"].astype(F32) if "carry" in have else total

    def give(blocks, token):
        mine, theirs = blocks
        arrived = lax.ppermute(theirs, "ctx", flip(n_ctx, 1))
        own = mine[0].astype(F32) + arrived[0].astype(F32)
        away = (mine[1].astype(F32) + arrived[1].astype(F32)).astype(BF16)
        token, own, away = tie(token, own, away)
        send("away", away, flip(n_ctx, 2))
        return own, token

    if piece is not None:
        have["piece", 0] = piece
        for k in range(order[0] + 1):
            bring(k)
            step_ends()
    blocks = own = None
    for s, k in enumerate(order):
        following = order[s + 1 :][:1]
        quarter = None
        if piece is not None:
            for later in following:
                if ("beside", later) not in have:
                    bring(later)
            mine = jnp.stack([have["piece", k], have["beside", k]])
            quarter = mine, lax.ppermute(mine, "ctx", flip(n_ctx, 1))
        if not scatter:
            state = compute(k, quarter, token, state)
            if following:
                token, *state = step_ends(token, *state)
            continue
        if own is not None:
            send("carry", total_of(own).astype(BF16), ring(n_ctx, 4))
        if blocks is not None:
            own, token = give(blocks, token)
        blocks, state = compute(k, quarter, token, state)
        token, *blocks = step_ends(token, *blocks)
    if not scatter:
        return tuple(state)
    send("carry", total_of(own).astype(BF16), ring(n_ctx, 4))
    own, token = give(blocks, token)
    extra = closing(token) if closing else ()
    own, *extra = step_ends(own, *extra)
    return total_of(own), state, extra


def scatter_order(n_ctx):
    return list(range(1, n_ctx // 4)) + [0]


def sum_all(values, result):
    n_ctx = lax.axis_size("ctx")
    bit = 1
    while bit < n_ctx:
        values = values + (yield lax.ppermute(values, "ctx", flip(n_ctx, bit)), 1)
        bit *= 2
    if lax.axis_size("fsdp") == 2:
        values = values + (yield lax.ppermute(values, "fsdp", SWAP), 1)
    else:
        values = lax.psum(values, "fsdp")
    result.append(values)


SWAP = [(0, 1), (1, 0)]


def swap(part):
    return lax.ppermute(part, "fsdp", SWAP)


def fetch(part, steps=1):
    if lax.axis_size("fsdp") != 2:
        return [lax.all_gather(part, "fsdp", axis=0, tiled=True)]
    return [part, (yield swap(part), steps)]


def fetch_blocks(part, block):
    if lax.axis_size("fsdp") != 2:
        return [lax.all_gather(part, "fsdp", axis=0, tiled=True)]
    other = []
    for at in range(0, part.shape[1], block):
        other.append((yield swap(part[:, at : at + block]), 1))
    return [part, jnp.concatenate(other, axis=1)]


def joined(parts):
    if len(parts) == 1:
        return parts[0]
    mine, other = parts
    first = lax.axis_index("fsdp") == 0
    return jnp.concatenate([jnp.where(first, mine, other), jnp.where(first, other, mine)], axis=0)


def part_offsets(width):
    if lax.axis_size("fsdp") != 2:
        return [jnp.int32(0)]
    f = lax.axis_index("fsdp")
    return [f * (width // 2), (1 - f) * (width // 2)]


def scatter_blocks(lefts, right, block):
    if lax.axis_size("fsdp") != 2:
        full = dot(lefts[0], right, COLS_T).astype(BF16)
        return lax.psum_scatter(full, "fsdp", scatter_dimension=0, tiled=True).astype(F32)
    mine, other = lefts
    done = []
    for at in range(0, right.shape[1], block):
        columns = right[:, at : at + block]
        came = yield swap(dot(other, columns, COLS_T).astype(BF16)), 1
        done.append(dot(mine, columns, COLS_T) + came.astype(F32))
    return done[0] if len(done) == 1 else jnp.concatenate(done, axis=1)


def scatter_rows(full):
    if lax.axis_size("fsdp") != 2:
        return lax.psum_scatter(
            full.astype(BF16), "fsdp", scatter_dimension=0, tiled=True
        ).astype(F32)
    rows = full.shape[0] // 2
    first = lax.axis_index("fsdp") == 0
    low, high = full[:rows], full[rows:]
    came = yield swap(jnp.where(first, high, low).astype(BF16)), 1
    return jnp.where(first, low, high) + came.astype(F32)


def first_pair(shape):
    return pl.BlockSpec((1,) + shape, lambda i, t: (jnp.minimum(i, 1),) + (0,) * len(shape))


def last_pair(shape):
    return pl.BlockSpec((1,) + shape, lambda i, t: (jnp.maximum(i - 2, 0),) + (0,) * len(shape))


def whole(shape):
    return pl.BlockSpec(shape, lambda *_: (0,) * len(shape))


def split_pairs(i, body, first, last):
    @pl.when(i < 2)
    def _():
        body(first)

    @pl.when(i >= 2)
    def _():
        body(last)


def rotary_tables(length):
    half = HD // 2
    steps = jnp.arange(half, dtype=jnp.int32).astype(F32)
    inverse = jnp.exp(steps * (-2.0 * jnp.log(THETA) / HD))
    angles = jnp.arange(length, dtype=jnp.int32).astype(F32)[:, None] * inverse[None, :]
    cosine, sine = jnp.cos(angles), jnp.sin(angles)
    return (
        jnp.concatenate([cosine, cosine], axis=1),
        jnp.concatenate([-sine, sine], axis=1),
    )


def half_turn(v):
    return pltpu.roll(v, HD // 2, 1)


def project_kernel(hpd, n_parts, n_ctx, meta, xa, xb, w, gain, gq, gk, cosine, sine, *refs):
    normed, (raw, query, key, value, whole_rows) = refs[-5 - n_parts : -5], refs[-5:]

    def body(x_ref):
        x = x_ref[0].astype(F32)
        r1 = lax.rsqrt(jnp.mean(x * x, axis=-1, keepdims=True) + EPS)
        n = (x * r1 * gain[...]).astype(BF16)
        whole_rows[...] = n
        for p, part in enumerate(normed):
            width = part.shape[2]
            part[0] = whole_rows[:, pl.ds(pl.multiple_of(meta[n_ctx + 1 + p], 128), width)]
        out = dot(n, w[...])
        raw[0] = out
        cos, sin = cosine[...], sine[...]
        for j in range(3 * hpd):
            v = out[:, j * HD : (j + 1) * HD]
            if j >= 2 * hpd:
                value[j - 2 * hpd] = v.astype(BF16)
                continue
            scale = lax.rsqrt(jnp.mean(v * v, axis=-1, keepdims=True) + EPS)
            v = v * scale * (gq[...] if j < hpd else gk[...])
            v = (v * cos + half_turn(v) * sin).astype(BF16)
            if j < hpd:
                query[j] = v
            else:
                key[j - hpd] = v

    split_pairs(pl.program_id(0), body, xa, xb)


def project(k, quarter, w, gain, gq, gk, cosine, sine, meta, hpd, n_ctx, n_parts, before):
    xa, xb = quarter
    _, count, width = xa.shape
    length = n_ctx * count
    cols = w.shape[1]
    at = lambda i, t: (t[4 * k + i], 0)
    head_at = lambda i, t: (0, t[4 * k + i], 0)
    own = lambda i, t: (4 * k + i, 0, 0)
    head = jax.ShapeDtypeStruct((hpd, length, HD), BF16)
    return pl.pallas_call(
        functools.partial(project_kernel, hpd, n_parts, n_ctx),
        grid_spec=pltpu.PrefetchScalarGridSpec(
            num_scalar_prefetch=1,
            grid=(4,),
            in_specs=[
                first_pair((count, width)),
                last_pair((count, width)),
                whole((width, cols)),
                whole((1, width)),
                whole((1, HD)),
                whole((1, HD)),
                pl.BlockSpec((count, HD), at),
                pl.BlockSpec((count, HD), at),
            ]
            + [pl.BlockSpec(memory_space=pl.ANY)] * len(before),
            out_specs=[
                *[pl.BlockSpec((1, count, width // n_parts), own)] * n_parts,
                pl.BlockSpec((1, count, cols), own),
                pl.BlockSpec((hpd, count, HD), head_at),
                pl.BlockSpec((hpd, count, HD), head_at),
                pl.BlockSpec((hpd, count, HD), head_at),
            ],
            scratch_shapes=[pltpu.VMEM((count, width), BF16)],
        ),
        out_shape=[
            *[jax.ShapeDtypeStruct((n_ctx, count, width // n_parts), BF16)] * n_parts,
            jax.ShapeDtypeStruct((n_ctx, count, cols), F32),
            head,
            head,
            head,
        ],
        input_output_aliases={9 + i: i for i in range(len(before))},
        compiler_params=params(),
        cost_estimate=cost(7.3),
        name="project",
    )(meta, xa, xb, w, gain, gq, gk, cosine, sine, *before)


def first_key(ends, docs, position):
    start = jnp.zeros_like(position)
    for d in range(docs):
        start = jnp.where(position >= ends[d], jnp.maximum(start, ends[d]), start)
    return start


def attend_kernel(docs, bq, bk, ends, query, key, value, mixed, total):
    i = pl.program_id(1)
    q = query[0]
    positions = i * bq + lax.broadcasted_iota(jnp.int32, (bq, 1), 0)
    starts = first_key(ends, docs, positions)
    low = lax.div(first_key(ends, docs, i * bq), bk)
    high = lax.div((i + 1) * bq - 1, bk) + 1

    def step(j, carry):
        acc, sums = carry
        rows = pl.ds(pl.multiple_of(j * bk, bk), bk)
        scores = dot(q, key[0, rows, :], ROWS_T)
        spots = j * bk + lax.broadcasted_iota(jnp.int32, (1, bk), 1)
        seen = (spots <= positions) & (spots >= starts)
        p = jnp.where(seen, jnp.exp2(scores * (LOG2E * HD**-0.5)), 0.0)
        return acc + dot(p.astype(BF16), value[0, rows, :]), sums + jnp.sum(
            p, axis=-1, keepdims=True
        )

    acc, sums = lax.fori_loop(
        low, high, step, (jnp.zeros((bq, HD), F32), jnp.zeros((bq, 1), F32))
    )
    mixed[0] = acc / sums
    total[0] = jnp.broadcast_to(jnp.log2(sums), (bq, HD))


def attend(query, key, value, ends, bq=256, bk=256):
    heads, length, _ = query.shape
    docs = ends.shape[0]
    block = pl.BlockSpec((1, bq, HD), lambda h, i, e: (h, i, 0))
    whole = pl.BlockSpec((1, length, HD), lambda h, i, e: (h, 0, 0))
    out = jax.ShapeDtypeStruct((heads, length, HD), F32)
    return pl.pallas_call(
        functools.partial(attend_kernel, docs, bq, bk),
        grid_spec=pltpu.PrefetchScalarGridSpec(
            num_scalar_prefetch=1,
            grid=(heads, length // bq),
            in_specs=[block, whole, whole],
            out_specs=[block, block],
        ),
        out_shape=[out, out],
        compiler_params=params(),
        cost_estimate=cost(18),
        name="attend",
    )(ends, query, key, value)


def attend_back_kernel(docs, bq, bk, ends, query, grad, total, delta, key, value, dq, dk, dv):
    i = pl.program_id(1)

    @pl.when(i == 0)
    def _():
        dk[...] = jnp.zeros_like(dk)
        dv[...] = jnp.zeros_like(dv)

    q, g = query[0], grad[0]
    log_total, shift = total[0], delta[0]
    positions = i * bq + lax.broadcasted_iota(jnp.int32, (1, bq), 1)
    starts = first_key(ends, docs, positions)
    low = lax.div(first_key(ends, docs, i * bq), bk)
    high = lax.div((i + 1) * bq - 1, bk) + 1

    def step(j, acc):
        rows = pl.ds(pl.multiple_of(j * bk, bk), bk)
        k, v = key[0, rows, :], value[0, rows, :]
        scores = dot(k, q, ROWS_T)
        spots = j * bk + lax.broadcasted_iota(jnp.int32, (bk, 1), 0)
        seen = (spots <= positions) & (spots >= starts)
        p = jnp.where(seen, jnp.exp2(scores * (LOG2E * HD**-0.5) - log_total), 0.0)
        ds = (p * (dot(v, g, ROWS_T) - shift)).astype(BF16)
        dv[0, rows, :] += dot(p.astype(BF16), g)
        dk[0, rows, :] += dot(ds, q)
        return acc + dot(ds, k, COLS_T)

    dq[0] = lax.fori_loop(low, high, step, jnp.zeros((bq, HD), F32))


def attend_back(query, grad, total, delta, key, value, ends, bq=256, bk=256):
    heads, length, _ = query.shape
    docs = ends.shape[0]
    block = pl.BlockSpec((1, bq, HD), lambda h, i, e: (h, i, 0))
    line = pl.BlockSpec((1, 1, bq), lambda h, i, e: (h, 0, i))
    whole = pl.BlockSpec((1, length, HD), lambda h, i, e: (h, 0, 0))
    out = jax.ShapeDtypeStruct((heads, length, HD), F32)
    return pl.pallas_call(
        functools.partial(attend_back_kernel, docs, bq, bk),
        grid_spec=pltpu.PrefetchScalarGridSpec(
            num_scalar_prefetch=1,
            grid=(heads, length // bq),
            in_specs=[block, block, line, line, whole, whole],
            out_specs=[block, whole, whole],
        ),
        out_shape=[out, out, out],
        compiler_params=params(),
        cost_estimate=cost(24),
        name="attend_back",
    )(ends, query, grad, total, delta, key, value)


def branch_kernel(hpd, table, mixed, w, theirs, mine):
    def body(out):
        total = None
        for j in range(hpd):
            part = dot(mixed[j].astype(BF16), w[j * HD : (j + 1) * HD, :])
            total = part if total is None else total + part
        out[0] = total.astype(BF16)

    split_pairs(pl.program_id(0), body, theirs, mine)


def branch(k, mixed, w, table, count):
    hpd = mixed.shape[0]
    width = w.shape[1]
    pair = jax.ShapeDtypeStruct((2, count, width), BF16)
    theirs, mine = pl.pallas_call(
        functools.partial(branch_kernel, hpd),
        grid_spec=pltpu.PrefetchScalarGridSpec(
            num_scalar_prefetch=1,
            grid=(4,),
            in_specs=[
                pl.BlockSpec((hpd, count, HD), lambda i, t: (0, t[4 * k + (i ^ 2)], 0)),
                whole((hpd * HD, width)),
            ],
            out_specs=[first_pair((count, width)), last_pair((count, width))],
        ),
        out_shape=[pair, pair],
        compiler_params=params(),
        cost_estimate=cost(2.4),
        name="branch",
    )(table, mixed, w)
    return mine, theirs


def branch_back_kernel(hpd, table, ga, gb, mixed, w, *refs):
    before = refs[0] if len(refs) == 4 else None
    grad, dw = refs[-2:]
    i = pl.program_id(0)

    @pl.when(i == 0)
    def _():
        dw[...] = jnp.zeros_like(dw) if before is None else before[...]

    def body(g_ref):
        g = g_ref[0]
        back = dot(g, w[...])
        for j in range(hpd):
            grad[j] = back[:, j * HD : (j + 1) * HD].astype(BF16)
            dw[j * HD : (j + 1) * HD, :] += dot(mixed[j].astype(BF16), g, COLS_T)

    split_pairs(i, body, ga, gb)


def branch_back(k, quarter, mixed, w, table, before):
    ga, gb = quarter
    _, count, width = ga.shape
    hpd, length, _ = mixed.shape
    head_at = lambda i, t: (0, t[4 * k + i], 0)
    grad, dw = pl.pallas_call(
        functools.partial(branch_back_kernel, hpd),
        grid_spec=pltpu.PrefetchScalarGridSpec(
            num_scalar_prefetch=1,
            grid=(4,),
            in_specs=[
                first_pair((count, width)),
                last_pair((count, width)),
                pl.BlockSpec((hpd, count, HD), head_at),
                whole((width, hpd * HD)),
            ]
            + ([whole((hpd * HD, width)), pl.BlockSpec(memory_space=pl.ANY)] if before else []),
            out_specs=[pl.BlockSpec((hpd, count, HD), head_at), whole((hpd * HD, width))],
        ),
        out_shape=[
            jax.ShapeDtypeStruct((hpd, length, HD), BF16),
            jax.ShapeDtypeStruct((hpd * HD, width), F32),
        ],
        input_output_aliases={6: 0} if before else {},
        compiler_params=params(),
        cost_estimate=cost(7),
        name="branch_back",
    )(table, ga, gb, mixed, w, *before)
    return dw, grad


def experts_kernel(n_parts, width, capacity, n_exp, meta, xa, xb, cot, router, *refs):
    wg, wu, wd = (refs[n_parts * i : n_parts * (i + 1)] for i in range(3))
    outs = refs[-(5 * n_parts + 5 + 2) :]
    rows, pairs = outs[:n_parts], outs[n_parts : 2 * n_parts]
    hidden, gate_grad, up_grad, mine, theirs = outs[2 * n_parts : 2 * n_parts + 5]
    scratch = outs[2 * n_parts + 5 :]
    chosen_ref, gate_ref = scratch[:2]
    picked, out_sum, row_sum = (
        scratch[2 + n_parts * i : 2 + n_parts * (i + 1)] for i in range(3)
    )
    step = pl.program_id(0)
    part = width // n_parts
    c = meta[0]
    lanes = lax.broadcasted_iota(jnp.int32, (1, 128), 1)

    def columns(p, first=0):
        return pl.ds(pl.multiple_of(first + meta[1 + p], 128), part)

    @pl.when(step == 0)
    def _():
        for i in range(4):
            x_ref = (xa, xb)[i // 2].at[i % 2]
            inner = meta[4 + i]
            span = slice(i * capacity, (i + 1) * capacity)
            info = x_ref[:, width:].astype(F32)
            place = jnp.sum(jnp.where(lanes == c, info, 0.0), axis=1, keepdims=True)
            spots = lax.broadcasted_iota(jnp.int32, (1, capacity), 1).astype(F32)
            chosen = (spots == place).astype(BF16)
            chosen_ref[i] = chosen
            logits = dot(x_ref[:, :width], router[...])
            seen = info > -1.5
            top = jnp.max(jnp.where(seen, logits, -1e30), axis=1, keepdims=True)
            weights = jnp.where(seen, jnp.exp(logits - top), 0.0)
            gates = weights / jnp.sum(weights, axis=1, keepdims=True)
            own = jnp.sum(jnp.where(lanes == c, gates, 0.0), axis=1, keepdims=True)
            gate = lax.dot_general(
                chosen.astype(F32),
                jnp.broadcast_to(own, gates.shape),
                COLS_T,
                precision=HIGH,
                preferred_element_type=F32,
            )
            gate_ref[span, :] = gate
            for p in range(n_parts):
                rows[p][span, :] = dot(chosen, x_ref[:, columns(p)], COLS_T).astype(BF16)
                grads = dot(chosen, cot[0, inner, :, columns(p)], COLS_T)
                picked[p][span, :] = grads.astype(BF16)
                pairs[p][span, :] = (grads * gate[:, :1]).astype(BF16)
        for p in range(n_parts):
            out_sum[p][...] = jnp.zeros_like(out_sum[p])
            row_sum[p][...] = jnp.zeros_like(row_sum[p])

    gate_part = sum(dot(rows[p][...], wg[p][...]) for p in range(n_parts))
    up_part = sum(dot(rows[p][...], wu[p][...]) for p in range(n_parts))
    hidden_grad = sum(dot(pairs[p][...], wd[p][...]) for p in range(n_parts))
    sigma = jax.nn.sigmoid(gate_part)
    silu_gate = gate_part * sigma
    h = (silu_gate * up_part).astype(BF16)
    hidden[...] = h
    gg = (hidden_grad * up_part * sigma * (1.0 + gate_part * (1.0 - sigma))).astype(BF16)
    gate_grad[...] = gg
    ug = (hidden_grad * silu_gate).astype(BF16)
    up_grad[...] = ug
    for p in range(n_parts):
        out_sum[p][...] += dot(h, wd[p][...], ROWS_T)
        row_sum[p][...] += dot(gg, wg[p][...], ROWS_T) + dot(ug, wu[p][...], ROWS_T)

    @pl.when(step == pl.num_programs(0) - 1)
    def _():
        for i in range(4):
            back = (mine, theirs)[i // 2].at[i % 2]
            span = slice(i * capacity, (i + 1) * capacity)
            chosen = chosen_ref[i]
            gate = gate_ref[span, :1]
            inner_sum = jnp.zeros((capacity, 1), F32)
            for p in range(n_parts):
                out = out_sum[p][span, :].astype(BF16).astype(F32)
                inner_sum += jnp.sum(
                    out * picked[p][span, :].astype(F32), axis=1, keepdims=True
                )
                scaled = (out * gate).astype(BF16)
                back[:, columns(p, width + 128)] = dot(chosen, scaled).astype(BF16)
                back[:, columns(p)] = dot(chosen, row_sum[p][span, :].astype(BF16)).astype(BF16)
            high = inner_sum.astype(BF16).astype(F32)
            extra = jnp.where(lanes == c, high, 0.0) + jnp.where(
                lanes == c + n_exp, inner_sum - high, 0.0
            )
            back[:, width : width + 128] = dot(chosen, extra.astype(BF16)).astype(BF16)


def experts(k, quarter, cot_all, router, wg, wu, wd, meta, capacity, n_exp, before):
    xa, xb = quarter
    _, count, wide = xa.shape
    nz, width = cot_all.shape[0], cot_all.shape[-1]
    n_parts = len(wg)
    part = width // n_parts
    hid = wg[0].shape[1]
    block = min(256, hid)
    slots = 4 * capacity
    pair = lambda cols: pl.BlockSpec((2, count, cols), lambda j, m: (0, 0, 0))
    weight = lambda: pl.BlockSpec((part, block), lambda j, m: (0, j))
    at_rows = lambda cols: pl.BlockSpec((slots, cols), lambda j, m: (k, 0))
    at_cols = lambda: pl.BlockSpec((slots, block), lambda j, m: (k, j))
    at_group = lambda: pl.BlockSpec((1, 4, count, width), lambda j, m: (m[3], 0, 0, 0))
    whole_rows = lambda cols: jax.ShapeDtypeStruct((nz * slots, cols), BF16)
    n_out = 2 * n_parts + 3
    outs = pl.pallas_call(
        functools.partial(experts_kernel, n_parts, width, capacity, n_exp),
        grid_spec=pltpu.PrefetchScalarGridSpec(
            num_scalar_prefetch=1,
            grid=(hid // block,),
            in_specs=[pair(wide), pair(wide), at_group(), whole(router.shape)]
            + [weight() for _ in range(3 * n_parts)]
            + [pl.BlockSpec(memory_space=pl.ANY)] * len(before),
            out_specs=[at_rows(part) for _ in range(2 * n_parts)]
            + [at_cols(), at_cols(), at_cols(), pair(wide + width), pair(wide + width)],
            scratch_shapes=[
                pltpu.VMEM((4, count, capacity), BF16),
                pltpu.VMEM((slots, 128), F32),
            ]
            + [pltpu.VMEM((slots, part), BF16)] * n_parts
            + [pltpu.VMEM((slots, part), F32)] * (2 * n_parts),
        ),
        out_shape=[whole_rows(part)] * (2 * n_parts)
        + [whole_rows(hid)] * 3
        + [jax.ShapeDtypeStruct((2, count, wide + width), BF16)] * 2,
        input_output_aliases={5 + 3 * n_parts + i: i for i in range(len(before))},
        compiler_params=params(60 * 1024 * 1024),
        cost_estimate=cost(20.5),
        name="experts",
    )(meta, xa, xb, cot_all, router, *wg, *wu, *wd, *before)
    return (outs[n_out], outs[n_out + 1]), outs[:n_out]


def head_back(grad, v, gain, cos, sin):
    scale = lax.rsqrt(jnp.mean(v * v, axis=-1, keepdims=True) + EPS)
    d = grad * cos - half_turn(grad) * sin
    u = d * gain
    inner = jnp.mean(u * v, axis=-1, keepdims=True)
    back = scale * u - v * (scale * scale * scale * inner)
    return back.astype(BF16), jnp.sum(d * v * scale, axis=0, keepdims=True)


def key_back_kernel(hpd, n_ctx, meta, dk, dv, raw, cosine, sine, gk, out, gains):
    @pl.when(pl.program_id(0) == 0)
    def _():
        gains[...] = jnp.zeros_like(gains)

    n_kv = dk.shape[0]
    for j in range(n_kv):
        at = (hpd + j) * HD
        v = raw[0, :, at : at + HD]
        if n_kv < hpd:
            v = jnp.where(meta[n_ctx] == 0, v, raw[0, :, at + HD : at + 2 * HD])
        back, gain = head_back(dk[j] * HD**-0.5, v, gk[...], cosine[...], sine[...])
        out[0, :, j * HD : (j + 1) * HD] = back
        gains[0:1, :] += gain
        out[0, :, (n_kv + j) * HD : (n_kv + j + 1) * HD] = dv[j].astype(BF16)


def key_back(dk, dv, raw, cosine, sine, gk, meta, hpd):
    n_kv = dk.shape[0]
    n_ctx, count, cols = raw.shape
    at = lambda i, t: (t[i], 0)
    head_at = lambda i, t: (0, t[i], 0)
    own = lambda i, t: (i, 0, 0)
    return pl.pallas_call(
        functools.partial(key_back_kernel, hpd, n_ctx),
        grid_spec=pltpu.PrefetchScalarGridSpec(
            num_scalar_prefetch=1,
            grid=(n_ctx,),
            in_specs=[
                pl.BlockSpec((n_kv, count, HD), head_at),
                pl.BlockSpec((n_kv, count, HD), head_at),
                pl.BlockSpec((1, count, cols), own),
                pl.BlockSpec((count, HD), at),
                pl.BlockSpec((count, HD), at),
                whole((1, HD)),
            ],
            out_specs=[pl.BlockSpec((1, count, 2 * n_kv * HD), own), whole((8, HD))],
        ),
        out_shape=[
            jax.ShapeDtypeStruct((n_ctx, count, 2 * n_kv * HD), BF16),
            jax.ShapeDtypeStruct((8, HD), F32),
        ],
        compiler_params=params(),
        cost_estimate=cost(6),
        name="key_back",
    )(meta, dk, dv, raw, cosine, sine, gk)


def input_back_kernel(hpd, meta, dq, kv, raw, cosine, sine, gq, w, xb, xa, *refs):
    grads, theirs, mine, gains, gain_grad = refs[-5:]
    i = pl.program_id(0)

    @pl.when(i == 0)
    def _():
        gains[...] = jnp.zeros_like(gains)
        gain_grad[...] = jnp.zeros_like(gain_grad)

    for j in range(hpd):
        at = slice(j * HD, (j + 1) * HD)
        back, gain = head_back(
            dq[j] * HD**-0.5, raw[0, :, at], gq[...], cosine[...], sine[...]
        )
        grads[0, :, at] = back
        gains[0:1, :] += gain
    back = dot(grads[0], w[: hpd * HD, :]) + dot(kv[0], w[hpd * HD :, :])

    def body(pair):
        out, x_ref = pair
        out[0] = back.astype(BF16)
        x = x_ref[0].astype(F32)
        r1 = lax.rsqrt(jnp.mean(x * x, axis=-1, keepdims=True) + EPS)
        gain_grad[0:1, :] += jnp.sum(back * (x * r1), axis=0, keepdims=True)

    split_pairs(i, body, (theirs, xb), (mine, xa))


def input_back(k, quarter, dq, kv, raw, cosine, sine, gq, w, meta, before):
    xa, xb = quarter
    _, count, width = xa.shape
    hpd = dq.shape[0]
    n_ctx, _, cols = raw.shape
    q_cols = hpd * HD
    at = lambda i, t: (t[4 * k + (i ^ 2)], 0)
    head_at = lambda i, t: (0, t[4 * k + (i ^ 2)], 0)
    own = lambda i, t: (4 * k + (i ^ 2), 0, 0)
    pair = jax.ShapeDtypeStruct((2, count, width), BF16)
    outs = pl.pallas_call(
        functools.partial(input_back_kernel, hpd),
        grid_spec=pltpu.PrefetchScalarGridSpec(
            num_scalar_prefetch=1,
            grid=(4,),
            in_specs=[
                pl.BlockSpec((hpd, count, HD), head_at),
                pl.BlockSpec((1, count, kv.shape[2]), own),
                pl.BlockSpec((1, count, q_cols), own),
                pl.BlockSpec((count, HD), at),
                pl.BlockSpec((count, HD), at),
                whole((1, HD)),
                whole(w.shape),
                first_pair((count, width)),
                last_pair((count, width)),
            ]
            + [pl.BlockSpec(memory_space=pl.ANY)] * len(before),
            out_specs=[
                pl.BlockSpec((1, count, q_cols), own),
                first_pair((count, width)),
                last_pair((count, width)),
                whole((8, HD)),
                whole((8, width)),
            ],
        ),
        out_shape=[
            jax.ShapeDtypeStruct((n_ctx, count, q_cols), BF16),
            pair,
            pair,
            jax.ShapeDtypeStruct((8, HD), F32),
            jax.ShapeDtypeStruct((8, width), F32),
        ],
        input_output_aliases={10: 0} if before else {},
        compiler_params=params(),
        cost_estimate=cost(7),
        name="input_back",
    )(meta, dq, kv, raw, cosine, sine, gq, w, xb, xa, *before)
    grads, theirs, mine, gains, gain_grad = outs
    return (mine, theirs), grads, gains, gain_grad


def place_kernel(parts, table, a, b, *refs):
    out = refs[-1]
    split_pairs(
        pl.program_id(0) // parts, lambda ref: out.__setitem__(..., ref[0].astype(F32)), a, b
    )


def place_columns(k, quarter, table, n_ctx, before):
    a, b = quarter
    _, rows, cols = a.shape
    parts = cols // HD
    return pl.pallas_call(
        functools.partial(place_kernel, parts),
        grid_spec=pltpu.PrefetchScalarGridSpec(
            num_scalar_prefetch=1,
            grid=(4 * parts,),
            in_specs=[
                pl.BlockSpec(
                    (1, rows, HD), lambda i, t: (jnp.minimum(i // parts, 1), 0, i % parts)
                ),
                pl.BlockSpec(
                    (1, rows, HD), lambda i, t: (jnp.maximum(i // parts - 2, 0), 0, i % parts)
                ),
            ]
            + [pl.BlockSpec(memory_space=pl.ANY)] * len(before),
            out_specs=pl.BlockSpec(
                (rows, HD), lambda i, t: (0, (i % parts) * n_ctx + t[4 * k + i // parts])
            ),
        ),
        out_shape=jax.ShapeDtypeStruct((rows, n_ctx * cols), F32),
        input_output_aliases={3: 0} if before else {},
        compiler_params=params(),
        cost_estimate=cost(4.6),
        name="place_columns",
    )(table, a, b, *before)


def place_heads_kernel(pieces, key, value):
    key[...] = pieces[0, :, :HD].astype(F32)
    value[...] = pieces[0, :, HD:].astype(F32)


def place_heads(pieces):
    n_ctx, rows, _ = pieces.shape
    at = lambda i: ((i // 2) % 2 * 2 + (i // 4) % 2, (i % 2) * 2 + i // 8)
    out = jax.ShapeDtypeStruct((4 * rows, KVH * HD), F32)
    return pl.pallas_call(
        place_heads_kernel,
        grid=(n_ctx,),
        in_specs=[pl.BlockSpec((1, rows, 2 * HD), lambda i: (i, 0, 0))],
        out_specs=[pl.BlockSpec((rows, HD), at)] * 2,
        out_shape=[out, out],
        compiler_params=params(),
        cost_estimate=cost(4),
        name="place_heads",
    )(pieces)


def widen_kernel(narrow, wide):
    wide[...] = narrow[0].astype(F32)


def widen(pieces):
    n, rows, cols = pieces.shape
    return pl.pallas_call(
        widen_kernel,
        grid=(n,),
        in_specs=[pl.BlockSpec((1, rows, cols), lambda i: (i, 0, 0))],
        out_specs=pl.BlockSpec((rows, cols), lambda i: (i, 0)),
        out_shape=jax.ShapeDtypeStruct((n * rows, cols), F32),
        compiler_params=params(),
        cost_estimate=cost(8),
        name="widen",
    )(pieces)


def local(
    inputs,
    w_query,
    w_key,
    w_value,
    w_output,
    norm_attn,
    gain_query,
    gain_key,
    w_router,
    norm_moe,
    w_gate,
    w_up,
    w_down,
    lengths,
    routes,
    pair_order,
    cotangent,
):
    n_ctx = lax.axis_size("ctx")
    n_f = lax.axis_size("fsdp")
    c = lax.axis_index("ctx")
    f = lax.axis_index("fsdp")
    count, width = inputs.shape[1], inputs.shape[2]
    length = count * n_ctx
    nz = n_ctx // 4
    later = scatter_order(n_ctx)
    hpd = H // n_ctx
    hpf = H // n_f
    group = H // KVH
    n_exp = w_router.shape[1]
    capacity = 5 * count * TOPK // (4 * n_exp)
    table = block_order(n_ctx)
    core = c % 2

    heads = [c % hpf + hpf * ((c // hpf) * hpd + j) for j in range(hpd)]
    kv_heads = [h // group for h in heads]
    columns = lambda w, h: lax.dynamic_slice_in_dim(w, h * HD, HD, 1)
    shared = n_f == 2 and hpd == 2
    if shared:
        kv_own = heads[0] // group + core * (KVH // 2)
        w_part = jnp.concatenate(
            [columns(w_query, h) for h in heads]
            + [columns(w_key, kv_own), columns(w_value, kv_own)],
            axis=1,
        )
    else:
        w_part = jnp.concatenate(
            [columns(w_query, h) for h in heads]
            + [columns(w_key, h) for h in kv_heads]
            + [columns(w_value, h) for h in kv_heads],
            axis=1,
        )
    vectors = jnp.concatenate([norm_attn, gain_query, gain_key, norm_moe])
    if n_f == 2:
        vectors = joined([vectors[None], swap(vectors[None])])
        router = joined([w_router, swap(w_router)])
    else:
        vectors = lax.all_gather(vectors, "fsdp", axis=0)
        router = lax.all_gather(w_router, "fsdp", axis=0, tiled=True)
    sizes = [norm_attn.shape[0], gain_query.shape[0], gain_key.shape[0], norm_moe.shape[0]]
    rows_of, at = [], 0
    for size in sizes:
        rows_of.append(vectors[:, at : at + size].reshape(1, n_f * size).astype(F32))
        at += size
    attn_gain, query_gain, key_gain, moe_gain = rows_of
    router_wide = jnp.pad(router, ((0, 0), (0, 128 - n_exp)))
    offsets = part_offsets(width)
    n_parts = len(offsets)
    meta_rows = jnp.concatenate([table, jnp.stack([core] + offsets).astype(jnp.int32)])
    q_cols = hpd * HD
    block = min(256, w_gate.shape[2])
    weights = {}

    def fetch_weights():
        w_qkv = joined((yield from fetch(w_part, 2)))
        weights["back"] = w_qkv.T
        if shared:
            kv_mine = w_qkv[:, q_cols:]
            kv_other = lax.ppermute(kv_mine, "ctx", flip(n_ctx, 1))
            low = jnp.where(core == 0, kv_mine, kv_other)
            high = jnp.where(core == 0, kv_other, kv_mine)
            w_qkv = jnp.concatenate(
                [w_qkv[:, :q_cols], low[:, :HD], high[:, :HD], low[:, HD:], high[:, HD:]], axis=1
            )
        weights["qkv"] = w_qkv
        own_rows = lax.dynamic_slice_in_dim(w_output, (c % hpf) * HD, HD, 0)
        w_out = joined((yield from fetch(own_rows)))
        w_out = lax.dynamic_slice_in_dim(w_out, (c // hpf) * hpd * HD, hpd * HD, 0)
        weights["out"], weights["out_back"] = w_out, w_out.T
        weights["gate"] = yield from fetch_blocks(w_gate[0], block)
        weights["up"] = yield from fetch_blocks(w_up[0], block)
        weights["down"] = yield from fetch_blocks(w_down[0], block)

    sides = [Side(fetch_weights())]

    experts_of = jnp.arange(n_exp, dtype=jnp.int32)
    picks = routes[0][:, :, None] == experts_of
    ranks = jnp.sum(
        jnp.where(picks, pair_order[0, 0].reshape(count, TOPK, 1), 0), axis=1
    )
    chosen = jnp.any(picks, axis=1)
    ranks = jnp.where(chosen, ranks, count * TOPK)
    place = jnp.sum((ranks[None, :, :] < ranks[:, None, :]).astype(jnp.int32), axis=1)
    place = jnp.where(chosen, jnp.where(place < capacity, place, -1), -2)
    place = jnp.pad(place, ((0, 0), (0, 128 - n_exp)), constant_values=-2).astype(BF16)

    ends = jnp.cumsum(lengths[0]).astype(jnp.int32)
    cosine, sine = rotary_tables(length)

    xs = {}

    def through_projection(k, quarter, token, before):
        xs[k] = quarter
        if k == 0:
            return ()
        if k == 1:
            before = projection(0, token, ())
        return projection(k, token, before)

    def projection(k, token, before):
        return project(
            k,
            xs[k],
            weights["qkv"],
            attn_gain,
            query_gain,
            key_gain,
            cosine,
            sine,
            token,
            hpd,
            n_ctx,
            n_parts,
            before,
        )

    straight = list(range(nz))
    *normed, raw, query, key, value = pipeline(
        n_ctx, straight, through_projection, meta_rows, sides, piece=inputs[0]
    )
    _, (query, cot) = land({}, sides, query, cotangent[0])
    gathered = {}

    def gather_cotangents():
        gathered["cot"] = yield lax.all_gather(cot, "ctx", axis=0), 5

    sides.append(Side(gather_cotangents()))
    mixed, log_total = attend(query, key, value, ends)
    _, (mixed,) = land({}, sides, mixed)
    x = inputs[0].astype(F32)
    branch_sum, _, _ = pipeline(
        n_ctx,
        later,
        lambda k, _, token, state: (branch(k, mixed, weights["out"], token, count), state),
        table,
        sides,
        scatter=True,
    )
    middle = x + branch_sum
    moe_scale = lax.rsqrt(jnp.mean(middle * middle, axis=-1, keepdims=True) + EPS)
    routed_in = (middle * moe_scale * moe_gain).astype(BF16)

    pad_offsets = (offsets + [jnp.int32(0)])[:2]

    def through_experts(k, quarter, token, before):
        blocks = token[4 * k : 4 * k + 4]
        meta = jnp.concatenate(
            [jnp.stack([c] + pad_offsets + [blocks[0] // 4]).astype(jnp.int32), blocks % 4]
        )
        return experts(
            k,
            quarter,
            gathered["cot"].reshape(nz, 4, count, width),
            router_wide,
            weights["gate"],
            weights["up"],
            weights["down"],
            meta,
            capacity,
            n_exp,
            before,
        )

    routed_grad, seen, _ = pipeline(
        n_ctx,
        later,
        through_experts,
        table,
        sides,
        piece=jnp.concatenate([routed_in, place], axis=1),
        scatter=True,
    )
    rows, pairs = seen[:n_parts], seen[n_parts : 2 * n_parts]
    hidden, gate_part_grad, up_part_grad = seen[2 * n_parts :]
    outputs = (middle + routed_grad[:, width + 128 :]).astype(BF16)

    gate_grad = routed_grad[:, width : width + n_exp] + routed_grad[
        :, width + n_exp : width + 2 * n_exp
    ]
    routed_grad = routed_grad[:, :width]
    logits = dot(routed_in, router)
    top = jnp.max(jnp.where(chosen, logits, -1e30), axis=-1, keepdims=True)
    shares = jnp.where(chosen, jnp.exp(logits - top), 0.0)
    gates = shares / jnp.sum(shares, axis=-1, keepdims=True)
    logit_grad = gates * (gate_grad - jnp.sum(gates * gate_grad, axis=-1, keepdims=True))
    routed_grad = routed_grad + lax.dot_general(
        logit_grad, router.astype(F32), ROWS_T, precision=HIGH
    )
    router_part = lax.dot_general(
        logit_grad, routed_in.astype(F32), COLS_T, precision=HIGH
    )

    grad_out = cotangent[0].astype(F32)
    moe_scaled = routed_grad * moe_gain
    moe_part = jnp.sum(routed_grad * middle * moe_scale, axis=0, keepdims=True)
    middle_grad = (
        grad_out
        + moe_scale * moe_scaled
        - middle
        * (
            moe_scale
            * moe_scale
            * moe_scale
            * jnp.mean(moe_scaled * middle, axis=-1, keepdims=True)
        )
    )

    grads, early, late = {}, [], []

    def scatter_grads():
        grads["gate"] = yield from scatter_blocks(rows, gate_part_grad, block)
        grads["up"] = yield from scatter_blocks(rows, up_part_grad, block)
        grads["down"] = yield from scatter_blocks(pairs, hidden, block)

    grads_side = Side(scatter_grads())
    sides = [
        grads_side,
        Side(sum_all(jnp.concatenate([router_part, moe_part], axis=0), early)),
    ]
    grad_out_w, mixed_grad = pipeline(
        n_ctx,
        straight,
        lambda k, quarter, token, before: branch_back(
            k, quarter, mixed, weights["out_back"], token, before
        ),
        table,
        sides,
        piece=middle_grad.astype(BF16),
    )
    _, (mixed_grad,) = land({}, sides, mixed_grad)

    def sum_out_grad():
        if n_f == hpd:
            placed = grad_out_w
        else:
            spread_out = jnp.arange(n_f, dtype=jnp.int32)[:, None] == (
                (c // hpf) * hpd + jnp.arange(hpd, dtype=jnp.int32)[None, :]
            )
            placed = jnp.einsum(
                "fj,jrd->frd", spread_out.astype(F32), grad_out_w.reshape(hpd, HD, width)
            ).reshape(n_f * HD, width)
        own = yield from scatter_rows(placed)
        whole_grad = yield lax.all_gather(own.astype(BF16), "ctx", axis=0), 5
        whole_grad = whole_grad.reshape(n_ctx // hpf, hpf, HD, width)
        grads["out"] = widen(lax.dynamic_index_in_dim(whole_grad, f // hpd, 0, keepdims=False))

    sides.append(Side(sum_out_grad()))
    delta = jnp.sum(mixed_grad.astype(F32) * mixed, axis=-1)[:, None, :]
    dq, dk, dv = attend_back(
        query, mixed_grad, log_total[:, :, 0][:, None, :], delta, key, value, ends
    )
    _, (dq, dk, dv) = land({}, sides, dq, dk, dv)
    if shared:
        own = lambda d: lax.dynamic_index_in_dim(d, core, 0, keepdims=True)
        away = lambda d: lax.dynamic_index_in_dim(d, 1 - core, 0, keepdims=True)
        sent = jnp.concatenate([away(dk), away(dv)]).astype(BF16)
        got = lax.ppermute(sent, "ctx", flip(n_ctx, 1)).astype(F32)
        dk, dv = own(dk) + got[:1], own(dv) + got[1:]
    kv_grad, key_gains = key_back(dk, dv, raw, cosine, sine, key_gain, meta_rows, hpd)
    normed_flat = [n.reshape(length, -1) for n in normed]

    def sum_key_grads():
        grad_kv = yield from scatter_blocks(
            normed_flat, kv_grad.reshape(length, -1), kv_grad.shape[-1]
        )
        if not shared:
            slots_kv = jnp.arange(KVH, dtype=jnp.int32)
            spread = jnp.stack([slots_kv == h for h in kv_heads]).astype(F32)
            grad_kv = grad_kv.reshape(width // n_f, 2, hpd, 1, HD) * spread[None, None, :, :, None]
            grad_kv = jnp.sum(grad_kv, axis=2).reshape(width // n_f, 2 * KVH * HD)
            grad_kv = lax.psum(grad_kv.astype(BF16), "ctx").astype(F32)
            grads["key"], grads["value"] = grad_kv[:, : KVH * HD], grad_kv[:, KVH * HD :]
            return
        for bit in (2, 4):
            rows_kept = grad_kv.shape[0] // 2
            side = (c // bit) % 2
            kept = lax.dynamic_slice_in_dim(grad_kv, side * rows_kept, rows_kept, 0)
            gone = lax.dynamic_slice_in_dim(grad_kv, (1 - side) * rows_kept, rows_kept, 0)
            got = yield lax.ppermute(gone.astype(BF16), "ctx", flip(n_ctx, bit)), 1
            grad_kv = kept + got.astype(F32)
        pieces = yield lax.all_gather(grad_kv.astype(BF16), "ctx", axis=0), 4
        grads["key"], grads["value"] = place_heads(pieces)

    sides.append(Side(sum_key_grads()))
    gain_parts, attn_parts = [], []

    def through_inputs(k, _, token, before):
        back, q_grad, gains, gain_grad = input_back(
            k,
            xs[k],
            dq,
            kv_grad,
            raw,
            cosine,
            sine,
            query_gain,
            weights["back"],
            token,
            before,
        )
        gain_parts.append(gains)
        attn_parts.append(gain_grad)
        if len(gain_parts) == nz:
            gain_rows = jnp.concatenate([sum(gain_parts)[:1], key_gains[:1]], axis=1)
            rows_last = jnp.concatenate([sum(attn_parts)[:1], gain_rows], axis=1)
            sides.append(Side(sum_all(rows_last.reshape(-1, 128), late)))
        return back, (q_grad,)

    q_grads = []

    def query_weights(token):
        q_flat = q_grads[0].reshape(length, -1)
        if n_f != 2:
            return (
                lax.psum_scatter(
                    dot(normed_flat[0], q_flat, COLS_T).astype(BF16),
                    "fsdp",
                    scatter_dimension=0,
                    tiled=True,
                ),
            )
        mine, other = normed_flat
        came = swap(dot(other, q_flat, COLS_T).astype(BF16))
        return dot(mine, q_flat, COLS_T), came

    def through_inputs_last(k, quarter, token, before):
        back, state = through_inputs(k, quarter, token, before)
        q_grads[:] = state
        return back, state

    normed_grad, _, grad_q = pipeline(
        n_ctx, later, through_inputs_last, meta_rows, sides, scatter=True, closing=query_weights
    )
    grad_q = sum(g.astype(F32) for g in grad_q).astype(BF16)

    if n_ctx == hpf:
        (grad_w_query,) = pipeline(
            n_ctx,
            straight,
            lambda k, quarter, token, before: (place_columns(k, quarter, token, n_ctx, before),),
            table,
            sides,
            piece=grad_q,
        )
    else:
        grad_w_query = (
            lax.all_gather(grad_q, "ctx", axis=0)
            .reshape(n_ctx // hpf, hpf, width // n_f, hpd, HD)
            .transpose(2, 0, 3, 1, 4)
            .reshape(width // n_f, H * HD)
            .astype(F32)
        )
    for side in sides:
        side.finish()
    early, late = early[0], late[0].reshape(-1)
    own_part = lambda v, size: lax.dynamic_slice_in_dim(v, f * (size // n_f), size // n_f, 0)
    grad_w_router = own_part(early[:n_exp].T, width)
    grad_norm_moe = own_part(early[n_exp], width)
    grad_norm_attn = own_part(late[:width], width)
    grad_gain_query = own_part(late[width : width + HD], HD)
    grad_gain_key = own_part(late[width + HD :], HD)

    attn_scale = lax.rsqrt(jnp.mean(x * x, axis=-1, keepdims=True) + EPS)
    attn_scaled = normed_grad * attn_gain
    input_grad = (
        middle_grad
        + attn_scale * attn_scaled
        - x
        * (
            attn_scale
            * attn_scale
            * attn_scale
            * jnp.mean(attn_scaled * x, axis=-1, keepdims=True)
        )
    )
    return (
        outputs[None],
        input_grad.astype(BF16)[None],
        grad_w_query,
        grads["key"],
        grads["value"],
        grads["out"],
        grad_norm_attn,
        grad_gain_query,
        grad_gain_key,
        grad_w_router,
        grad_norm_moe,
        grads["gate"][None],
        grads["up"][None],
        grads["down"][None],
    )


def solution(mesh):
    in_specs = (
        P("fsdp", "ctx", None),
        P("fsdp", None),
        P("fsdp", None),
        P("fsdp", None),
        P("fsdp", None),
        P("fsdp"),
        P("fsdp"),
        P("fsdp"),
        P("fsdp", None),
        P("fsdp"),
        P("ctx", "fsdp", None),
        P("ctx", "fsdp", None),
        P("ctx", "fsdp", None),
        P("fsdp", None),
        P("fsdp", "ctx", None),
        P("fsdp", "ctx", None),
        P("fsdp", "ctx", None),
    )
    out_specs = (
        P("fsdp", "ctx", None),
        P("fsdp", "ctx", None),
        P("fsdp", None),
        P("fsdp", None),
        P("fsdp", None),
        P("fsdp", None),
        P("fsdp"),
        P("fsdp"),
        P("fsdp"),
        P("fsdp", None),
        P("fsdp"),
        P("ctx", "fsdp", None),
        P("ctx", "fsdp", None),
        P("ctx", "fsdp", None),
    )
    return jax.shard_map(local, mesh=mesh, in_specs=in_specs, out_specs=out_specs, check_vma=False)
```

```python
import functools

import jax
import jax.numpy as jnp
from jax import lax
from jax.experimental import pallas as pl
from jax.experimental.pallas import tpu as pltpu
from jax.sharding import PartitionSpec as P

H = 32
KVH = 4
HD = 128
TOPK = 8
EPS = 1e-06
THETA = 1000000.0
HIGH = lax.Precision.HIGHEST
LOG2E = 1.4426950408889634
F32 = jnp.float32
BF16 = jnp.bfloat16
ROWS_T = (((1,), (1,)), ((), ()))
COLS_T = (((0,), (0,)), ((), ()))


def dot(a, b, dims=(((1,), (0,)), ((), ()))):
    return lax.dot_general(a, b, dims, preferred_element_type=F32)


def params(mebibytes):
    return pltpu.CompilerParams(vmem_limit_bytes=mebibytes * 1024 * 1024)


def once(shape, index):
    return pl.BlockSpec(shape, index, pipeline_mode=pl.Buffered(1))


def cost(microseconds):
    return pl.CostEstimate(
        flops=int(microseconds * 1.15e9), bytes_accessed=0, transcendentals=0
    )


def flip(n_ctx, bit):
    return [(i, i ^ bit) for i in range(n_ctx)]


def ring(n_ctx, step):
    return [(i, (i + step) % n_ctx) for i in range(n_ctx)]


def block_order(n_ctx):
    c = lax.axis_index("ctx")
    nz = n_ctx // 4
    z, x, core = c // 4, (c // 2) % 2, c % 2
    table = []
    for k in range(nz):
        for dc in range(2):
            for dx in range(2):
                table.append(lax.rem(z + nz - k, nz) * 4 + (x ^ dx) * 2 + (core ^ dc))
    return jnp.stack(table).astype(jnp.int32)


def tie(*arrays):
    return lax.optimization_barrier(arrays)


class Side:
    def __init__(self, chain):
        self.chain, self.flying, self.left = chain, None, 0
        self.resume(None)

    def resume(self, landed):
        try:
            self.flying, self.left = self.chain.send(landed)
        except StopIteration:
            self.flying = None

    def finish(self):
        while self.flying is not None:
            self.resume(self.flying)


def land(air, sides, *others):
    due = [side for side in sides if side.flying is not None and side.left <= 1]
    for side in sides:
        side.left -= 1
    keys = list(air)
    flying = [array for side in due for array in side.flying]
    arrays = list(tie(*air.values(), *flying, *others))
    air.clear()
    landed = {key: arrays.pop(0) for key in keys}
    for side in due:
        side.resume([arrays.pop(0) for _ in side.flying])
    return landed, arrays


def pipeline(n_ctx, order, compute, token, sides, piece=None, scatter=False, closing=None):
    nz = n_ctx // 4
    air, have, state = {}, {}, ()

    def send(key, array, pairs):
        air[key] = lax.ppermute(array, "ctx", pairs)

    def bring(k):
        send(("beside", k), have["piece", k], flip(n_ctx, 2))
        if k + 1 < nz:
            send(("piece", k + 1), have["piece", k], ring(n_ctx, 4))

    def step_ends(*others):
        landed, others = land(air, sides, *others)
        have.update(landed)
        return others

    def total_of(own):
        parts = [*own, have["away"]] + ([have["carry"]] if "carry" in have else [])
        return sum(part.astype(F32) for part in parts)

    def give(blocks, token):
        mine, theirs = blocks
        arrived = lax.ppermute(theirs, "ctx", flip(n_ctx, 1))
        away = (mine[1].astype(F32) + arrived[1].astype(F32)).astype(BF16)
        token, away = tie(token, away)
        send("away", away, flip(n_ctx, 2))
        return (mine[0], arrived[0]), token

    if piece is not None:
        have["piece", 0] = piece
        for k in range(order[0] + 1):
            bring(k)
            step_ends()
    blocks = own = None
    for s, k in enumerate(order):
        following = order[s + 1 :][:1]
        quarter = None
        if piece is not None:
            for later in following:
                if ("beside", later) not in have:
                    bring(later)
            pair = [have["piece", k], have["beside", k]]
            quarter = pair + [lax.ppermute(array, "ctx", flip(n_ctx, 1)) for array in pair]
        if not scatter:
            state = compute(k, quarter, token, state)
            if following:
                token, *state = step_ends(token, *state)
            continue
        if own is not None:
            send("carry", total_of(own).astype(BF16), ring(n_ctx, 4))
        if blocks is not None:
            own, token = give(blocks, token)
        blocks, state = compute(k, quarter, token, state)
        token, *blocks = step_ends(token, *blocks)
    if not scatter:
        return tuple(state)
    send("carry", total_of(own).astype(BF16), ring(n_ctx, 4))
    own, token = give(blocks, token)
    extra = closing(token) if closing else ()
    extra = step_ends(*extra)
    return total_of(own), state, extra


def gather_quarters(piece, n_ctx):
    nz = n_ctx // 4
    along, beside, others = [piece], [], []
    core = lambda array: lax.ppermute(array, "ctx", flip(n_ctx, 1))
    for step in range(nz + 1):
        going = []
        if step + 1 < nz:
            going.append(lax.ppermute(along[step], "ctx", ring(n_ctx, 4)))
        if step > 0:
            going.append(lax.ppermute(along[step - 1], "ctx", flip(n_ctx, 2)))
        came = list((yield tuple(going), 1))
        if step + 1 < nz:
            along.append(came.pop(0))
        if step > 0:
            beside.append(came.pop(0))
    return [(a, b, core(a), core(b)) for a, b in zip(along, beside)]


def gather_blocks(piece, n_ctx, last):
    nz = n_ctx // 4
    core = lambda array: lax.ppermute(array, "ctx", flip(n_ctx, 1))
    hop = lambda array: lax.ppermute(array, "ctx", ring(n_ctx, 4))
    along = [piece]
    came, following = yield (lax.ppermute(piece, "ctx", flip(n_ctx, 2)), hop(piece)), 1
    beside = [came]
    along.append(following)
    for k in range(1, nz):
        if k > 1:
            along += yield (hop(along[k - 1]),), 1
        beside += yield (hop(beside[k - 1]),), last if k == nz - 1 else 1
    return [(a, b, core(a), core(b)) for a, b in zip(along, beside)]


def scatter_order(n_ctx):
    return list(range(1, n_ctx // 4)) + [0]


def sum_all(values, result):
    n_ctx = lax.axis_size("ctx")
    bit = 1
    while bit < n_ctx:
        (came,) = yield (lax.ppermute(values.astype(BF16), "ctx", flip(n_ctx, bit)),), 1
        values = values + came.astype(F32)
        bit *= 2
    if lax.axis_size("fsdp") == 2:
        (came,) = yield (swap(values.astype(BF16)),), 1
        values = values + came.astype(F32)
    else:
        values = lax.psum(values, "fsdp")
    result.append(values)


SWAP = [(0, 1), (1, 0)]


def swap(part):
    return lax.ppermute(part, "fsdp", SWAP)


def fetch(part, steps=1):
    if lax.axis_size("fsdp") != 2:
        return [lax.all_gather(part, "fsdp", axis=0, tiled=True)]
    (other,) = yield (swap(part),), steps
    return [part, other]


def fetch_thirds(part):
    if lax.axis_size("fsdp") != 2:
        return [lax.all_gather(part, "fsdp", axis=0, tiled=True)]
    step = (part.shape[0] // 3 + 31) // 32 * 32
    other = []
    for at in range(0, part.shape[0], step):
        rows = part[at : at + step]
        if other:
            other[-1], rows = tie(other[-1], rows)
        other += yield (swap(rows),), 1
    return [part, jnp.concatenate(other, axis=0)]


def joined(parts):
    if len(parts) == 1:
        return parts[0]
    mine, other = parts
    first = lax.axis_index("fsdp") == 0
    return jnp.concatenate([jnp.where(first, mine, other), jnp.where(first, other, mine)], axis=0)


def part_offsets(width):
    if lax.axis_size("fsdp") != 2:
        return [jnp.int32(0)]
    f = lax.axis_index("fsdp")
    return [f * (width // 2), (1 - f) * (width // 2)]


def scatter_blocks(lefts, right, block):
    if lax.axis_size("fsdp") != 2:
        full = dot(lefts[0], right, COLS_T).astype(BF16)
        return lax.psum_scatter(full, "fsdp", scatter_dimension=0, tiled=True).astype(F32)
    mine, other = lefts
    columns = [right[:, at : at + block] for at in range(0, right.shape[1], block)]
    product = lambda left, i: dot(left, columns[i], COLS_T)
    done, count = [], len(columns)
    sent = product(other, 0).astype(BF16)
    for i in range(count):
        ahead = [product(other, i + 1).astype(BF16)] if i + 1 < count else []
        fresh = [product(mine, i - 1) + came.astype(F32)] if i > 0 else []
        came, *worked = yield (swap(sent), *ahead, *fresh), 1
        if ahead:
            sent = worked.pop(0)
        done += worked
    done.append(product(mine, count - 1) + came.astype(F32))
    return done[0] if count == 1 else jnp.concatenate(done, axis=1)


def scatter_rows(full):
    if lax.axis_size("fsdp") != 2:
        return lax.psum_scatter(
            full.astype(BF16), "fsdp", scatter_dimension=0, tiled=True
        ).astype(F32)
    rows = full.shape[0] // 2
    first = lax.axis_index("fsdp") == 0
    low, high = full[:rows], full[rows:]
    (came,) = yield (swap(jnp.where(first, high, low).astype(BF16)),), 1
    return jnp.where(first, low, high) + came.astype(F32)


def group_of(k):
    return lambda t: lax.div(t[4 * k], 4)


def span(t, k, i, count):
    return pl.ds(pl.multiple_of(lax.rem(t[4 * k + i], 4) * count, count), count)


IN_HBM = pl.BlockSpec(memory_space=pltpu.HBM)


def whole(shape):
    return once(shape, lambda *_: (0,) * len(shape))


def first_pair(shape):
    return pl.BlockSpec((1,) + shape, lambda i, t: (jnp.minimum(i, 1),) + (0,) * len(shape))


def last_pair(shape):
    return pl.BlockSpec((1,) + shape, lambda i, t: (jnp.maximum(i - 2, 0),) + (0,) * len(shape))


def split_pairs(i, body, first, last):
    @pl.when(i < 2)
    def _():
        body(first)

    @pl.when(i >= 2)
    def _():
        body(last)


def rotary_table(length):
    half = HD // 2
    steps = jnp.arange(half, dtype=jnp.int32).astype(F32)
    inverse = jnp.exp(steps * (-2.0 * jnp.log(THETA) / HD))
    angles = jnp.arange(length, dtype=jnp.int32).astype(F32)[:, None] * inverse[None, :]
    return jnp.concatenate([jnp.cos(angles), jnp.sin(angles)], axis=1)


def turns(table):
    other = pltpu.roll(table, HD // 2, 1)
    first = lax.broadcasted_iota(jnp.int32, (1, HD), 1) < HD // 2
    return jnp.where(first, table, other), jnp.where(first, -other, table)


def half_turn(v):
    return pltpu.roll(v, HD // 2, 1)


def head_norm(v, gain):
    scale = lax.rsqrt(jnp.mean(v * v, axis=-1, keepdims=True) + EPS)
    return v * scale * gain


def project_kernel(k, hpd, n_kv, n_parts, n_ctx, meta, x0, x1, x2, x3, gain, gq, gk, turn, *refs):
    n_outs = n_parts + 5
    w, beside = refs[:n_parts], refs[n_parts : 2 * n_parts] if n_kv < hpd else ()
    outs, refs = refs[-(2 * n_outs + 2) : -(n_outs + 2)], refs[-(n_outs + 2) :]
    here, rows, sems = refs[:n_outs], refs[-2], refs[-1]
    normed, (raw, scales, query, key, value) = here[:n_parts], here[n_parts:]
    count = x0.shape[0]
    group = pl.ds(pl.multiple_of(lax.div(meta[4 * k], 4) * 4 * count, count), 4 * count)
    places = [pl.ds(4 * k, 4)] * (n_parts + 2) + [(slice(None), group)] * 3
    leaving = [
        pltpu.make_async_copy(here[i], outs[i].at[places[i]], sems.at[i]) for i in range(n_outs)
    ]
    for i, piece in enumerate((x0, x1, x2, x3)):
        x = piece[...].astype(F32)
        r1 = lax.rsqrt(jnp.mean(x * x, axis=-1, keepdims=True) + EPS)
        scales[i] = jnp.broadcast_to(r1, scales.shape[1:])
        rows[i * count : (i + 1) * count, :] = (x * r1 * gain[...]).astype(BF16)
        for p, part in enumerate(normed):
            at = pl.ds(pl.multiple_of(meta[n_ctx + 1 + p], 128), part.shape[2])
            part[i] = rows[i * count : (i + 1) * count, at]
    for copy in leaving[:n_parts]:
        copy.start()
    parts = [part[...].reshape(4 * count, part.shape[2]) for part in normed]
    out = sum(dot(n, w_p[...]) for n, w_p in zip(parts, w))
    other = sum(dot(n, w_p[...]) for n, w_p in zip(parts, beside)) if beside else None
    core = meta[n_ctx]
    for i in range(4):
        at = span(meta, k, i, count)
        cos, sin = turns(turn[at, :])
        block = out[i * count : (i + 1) * count, :]
        raw[i] = block[:, : (hpd + n_kv) * HD]

        def turned(v, gain):
            v = head_norm(v, gain[...])
            return (v * cos + half_turn(v) * sin).astype(BF16)

        for j in range(hpd):
            query[j, at, :] = turned(block[:, j * HD : (j + 1) * HD], gq)
        for j in range(n_kv):
            v = block[:, (hpd + j) * HD : (hpd + j + 1) * HD]
            u = block[:, (hpd + n_kv + j) * HD : (hpd + n_kv + j + 1) * HD]
            head = core if beside else j
            key[head, at, :] = turned(v, gk)
            value[head, at, :] = u.astype(BF16)
        if beside:
            block = other[i * count : (i + 1) * count, :]
            key[1 - core, at, :] = turned(block[:, :HD], gk)
            value[1 - core, at, :] = block[:, HD:].astype(BF16)
    for copy in leaving[n_parts:]:
        copy.start()
    for copy in leaving:
        copy.wait()


def project(k, quarter, w, beside, gain, gq, gk, turn, meta, hpd, n_ctx, before):
    count, width = quarter[0].shape
    length = n_ctx * count
    n_parts = len(w)
    n_kv = 1 if beside else hpd
    group = group_of(k)
    turn_at = once((4 * count, HD), lambda i, t: (group(t), 0))
    head = pltpu.HBM((hpd, length, HD), BF16)
    cols = (hpd + n_kv) * HD
    weights = [*w, *beside]
    return pl.pallas_call(
        functools.partial(project_kernel, k, hpd, n_kv, n_parts, n_ctx),
        grid_spec=pltpu.PrefetchScalarGridSpec(
            num_scalar_prefetch=1,
            grid=(1,),
            in_specs=[whole((count, width))] * 4
            + [whole((1, width)), whole((1, HD)), whole((1, HD)), turn_at]
            + [whole(array.shape) for array in weights]
            + [IN_HBM] * len(before),
            out_specs=[IN_HBM] * (n_parts + 5),
            scratch_shapes=[pltpu.VMEM((4, count, width // n_parts), BF16)] * n_parts
            + [pltpu.VMEM((4, count, cols), F32), pltpu.VMEM((4, count, HD), F32)]
            + [pltpu.VMEM((hpd, 4 * count, HD), BF16)] * 3
            + [pltpu.VMEM((4 * count, width), BF16), pltpu.SemaphoreType.DMA((n_parts + 5,))],
        ),
        out_shape=[pltpu.HBM((n_ctx, count, width // n_parts), BF16)] * n_parts
        + [
            pltpu.HBM((n_ctx, count, cols), F32),
            pltpu.HBM((n_ctx, count, HD), F32),
            head,
            head,
            head,
        ],
        input_output_aliases={9 + len(weights) + i: i for i in range(len(before))},
        compiler_params=params(18),
        cost_estimate=cost(6),
        name="project",
    )(meta, *quarter, gain, gq, gk, turn, *weights, *before)


def first_key(ends, docs, position):
    start = jnp.zeros_like(position)
    for d in range(docs):
        start = jnp.where(position >= ends[d], jnp.maximum(start, ends[d]), start)
    return start


def attend_kernel(docs, heads, bq, bk, ends, query, key, value, mixed, total):
    i = pl.program_id(0)
    positions = i * bq + lax.broadcasted_iota(jnp.int32, (bq, 1), 0)
    starts = first_key(ends, docs, positions)
    low = lax.div(first_key(ends, docs, i * bq), bk)
    high = lax.div((i + 1) * bq - 1, bk) + 1

    def step(j, carry):
        rows = pl.ds(pl.multiple_of(j * bk, bk), bk)
        spots = j * bk + lax.broadcasted_iota(jnp.int32, (1, bk), 1)
        seen = (spots <= positions) & (spots >= starts)
        sums = []
        for h, (acc, norm) in enumerate(carry):
            scores = dot(query[h], key[h, rows, :], ROWS_T)
            p = jnp.where(seen, jnp.exp2(scores * (LOG2E * HD**-0.5)), 0.0)
            acc = acc + dot(p.astype(BF16), value[h, rows, :])
            sums.append((acc, norm + jnp.sum(p, axis=-1, keepdims=True)))
        return tuple(sums)

    start = (jnp.zeros((bq, HD), F32), jnp.zeros((bq, 1), F32))
    first_lane = lax.broadcasted_iota(jnp.int32, (1, HD), 1) == 0
    for h, (acc, norm) in enumerate(lax.fori_loop(low, high, step, (start,) * heads)):
        mixed[h] = acc / norm
        column = jnp.where(first_lane, jnp.log2(norm), 0.0)
        total[h] = row_sums(column)


def row_sums(values):
    return lax.dot_general(
        jnp.ones((8, values.shape[1]), F32),
        values,
        ROWS_T,
        precision=HIGH,
        preferred_element_type=F32,
    )


def attend(query, key, value, ends, bq=256, bk=512):
    heads, length, _ = query.shape
    docs = ends.shape[0]
    block = pl.BlockSpec((heads, bq, HD), lambda i, e: (0, i, 0))
    keys = once((heads, length, HD), lambda i, e: (0, 0, 0))
    line = pl.BlockSpec((heads, 8, bq), lambda i, e: (0, 0, i))
    return pl.pallas_call(
        functools.partial(attend_kernel, docs, heads, bq, bk),
        grid_spec=pltpu.PrefetchScalarGridSpec(
            num_scalar_prefetch=1,
            grid=(length // bq,),
            in_specs=[block, keys, keys],
            out_specs=[block, line],
        ),
        out_shape=[
            jax.ShapeDtypeStruct((heads, length, HD), F32),
            jax.ShapeDtypeStruct((heads, 8, length), F32),
        ],
        compiler_params=params(14),
        cost_estimate=cost(12.5),
        name="attend",
    )(ends, query, key, value)


def attend_back_kernel(
    docs, heads, bq, bk, ends, query, grad, total, delta, key, value, dq, dk, dv, *away
):
    i = pl.program_id(0)

    @pl.when(i == 0)
    def _():
        dk[...] = jnp.zeros_like(dk)
        dv[...] = jnp.zeros_like(dv)

    positions = i * bq + lax.broadcasted_iota(jnp.int32, (1, bq), 1)
    starts = first_key(ends, docs, positions)
    low = lax.div(first_key(ends, docs, i * bq), bk)
    high = lax.div((i + 1) * bq - 1, bk) + 1

    def step(j, sums):
        rows = pl.ds(pl.multiple_of(j * bk, bk), bk)
        spots = j * bk + lax.broadcasted_iota(jnp.int32, (bk, 1), 0)
        seen = (spots <= positions) & (spots >= starts)
        out = []
        for h in range(heads):
            q, g, k = query[h], grad[h], key[h, rows, :]
            scores = dot(k, q, ROWS_T)
            p = jnp.exp2(scores * (LOG2E * HD**-0.5) - total[h, 0:1, :])
            p = jnp.where(seen, p, 0.0)
            ds = (p * (dot(value[h, rows, :], g, ROWS_T) - delta[h, 0:1, :])).astype(BF16)
            dv[h, rows, :] += dot(p.astype(BF16), g)
            dk[h, rows, :] += dot(ds, q)
            out.append(sums[h] + dot(ds, k, COLS_T))
        return tuple(out)

    sums = lax.fori_loop(low, high, step, (jnp.zeros((bq, HD), F32),) * heads)
    for h in range(heads):
        dq[h] = sums[h]

    if away:

        @pl.when(i == pl.num_programs(0) - 1)
        def _():
            other = 1 - ends[docs]
            away[0][0] = dk[other].astype(BF16)
            away[0][1] = dv[other].astype(BF16)


def attend_back(query, grad, total, delta, key, value, ends, shared, bq=256, bk=512):
    heads, length, _ = query.shape
    docs = ends.shape[0] - 1
    block = pl.BlockSpec((heads, bq, HD), lambda i, e: (0, i, 0))
    line = pl.BlockSpec((heads, 8, bq), lambda i, e: (0, 0, i))
    keys = once((heads, length, HD), lambda i, e: (0, 0, 0))
    out = jax.ShapeDtypeStruct((heads, length, HD), F32)
    return pl.pallas_call(
        functools.partial(attend_back_kernel, docs, heads, bq, bk),
        grid_spec=pltpu.PrefetchScalarGridSpec(
            num_scalar_prefetch=1,
            grid=(length // bq,),
            in_specs=[block, block, line, line, keys, keys],
            out_specs=[block, keys, keys] + [whole((2, length, HD))] * shared,
        ),
        out_shape=[out, out, out] + [jax.ShapeDtypeStruct((2, length, HD), BF16)] * shared,
        compiler_params=params(24),
        cost_estimate=cost(17),
        name="attend_back",
    )(ends, query, grad, total, delta, key, value)


def branch_kernel(hpd, table, mixed, w, theirs, mine):
    def body(out):
        total = None
        for j in range(hpd):
            part = dot(mixed[j].astype(BF16), w[j * HD : (j + 1) * HD, :])
            total = part if total is None else total + part
        out[0] = total.astype(BF16)

    split_pairs(pl.program_id(0), body, theirs, mine)


def branch(k, mixed, w, table, count):
    hpd = mixed.shape[0]
    width = w.shape[1]
    pair = jax.ShapeDtypeStruct((2, count, width), BF16)
    theirs, mine = pl.pallas_call(
        functools.partial(branch_kernel, hpd),
        grid_spec=pltpu.PrefetchScalarGridSpec(
            num_scalar_prefetch=1,
            grid=(4,),
            in_specs=[
                pl.BlockSpec((hpd, count, HD), lambda i, t: (0, t[4 * k + (i ^ 2)], 0)),
                whole((hpd * HD, width)),
            ],
            out_specs=[first_pair((count, width)), last_pair((count, width))],
        ),
        out_shape=[pair, pair],
        compiler_params=params(10),
        cost_estimate=cost(2.4),
        name="branch",
    )(table, mixed, w)
    return mine, theirs


def branch_back_kernel(k, hpd, meta, g0, g1, g2, g3, mixed, w, *refs):
    grad, delta, dw = refs[-3:]
    pieces = (g0, g1, g2, g3)
    count = g0.shape[0]
    g = jnp.concatenate([piece[...] for piece in pieces], axis=0)
    back = dot(g, w[...], ROWS_T).astype(BF16)
    for j in range(hpd):
        heads = []
        for i in range(4):
            at = span(meta, k, i, count)
            own = back[i * count : (i + 1) * count, j * HD : (j + 1) * HD]
            out = mixed[j, at, :]
            grad[j, at, :] = own
            delta[j, :, at] = row_sums(own.astype(F32) * out)
            heads.append(out.astype(BF16))
        part = dot(jnp.concatenate(heads, axis=0), g, COLS_T)
        rows = slice(j * HD, (j + 1) * HD)
        dw[rows, :] = part if len(refs) == 3 else refs[0][rows, :] + part


def branch_back(k, quarter, mixed, w, table, before):
    count, width = quarter[0].shape
    hpd, length, _ = mixed.shape
    group = group_of(k)
    head_at = once((hpd, 4 * count, HD), lambda i, t: (0, group(t), 0))
    dw_at = whole((hpd * HD, width))
    grad, delta, dw = pl.pallas_call(
        functools.partial(branch_back_kernel, k, hpd),
        grid_spec=pltpu.PrefetchScalarGridSpec(
            num_scalar_prefetch=1,
            grid=(1,),
            in_specs=[whole((count, width))] * 4
            + [head_at, whole((hpd * HD, width))]
            + ([dw_at] + [pl.BlockSpec(memory_space=pl.ANY)] * 2 if before else []),
            out_specs=[
                head_at,
                once((hpd, 8, 4 * count), lambda i, t: (0, 0, group(t))),
                dw_at,
            ],
        ),
        out_shape=[
            jax.ShapeDtypeStruct((hpd, length, HD), BF16),
            jax.ShapeDtypeStruct((hpd, 8, length), F32),
            jax.ShapeDtypeStruct((hpd * HD, width), F32),
        ],
        input_output_aliases={8: 0, 9: 1} if before else {},
        compiler_params=params(20),
        cost_estimate=cost(6),
        name="branch_back",
    )(table, *quarter, mixed, w, *before)
    return dw, grad, delta


def experts_kernel(
    k, n_parts, width, capacity, n_exp, meta, x0, x1, x2, x3, g0, g1, g2, g3, router, *refs
):
    n = n_parts
    w_from = refs[: 3 * n]
    refs = refs[-(2 * n + 5 + 6 * n + 3 + 3) :]
    outs, (mine, theirs) = refs[: 2 * n + 3], refs[2 * n + 3 : 2 * n + 5]
    refs = refs[2 * n + 5 :]
    w_here, refs = refs[: 3 * n], refs[3 * n :]
    rows, pairs, picked, refs = refs[:n], refs[n : 2 * n], refs[2 * n : 3 * n], refs[3 * n :]
    hidden, gate_grad, up_grad, chosen_ref, gate_ref, sems = refs
    slots = 4 * capacity
    part = width // n
    c = meta[0]
    lanes = lax.broadcasted_iota(jnp.int32, (1, 128), 1)
    pieces = (x0, x1, x2, x3)
    arrivals = [
        pltpu.make_async_copy(w_from[i], w_here[i], sems.at[i]) for i in range(3 * n)
    ]
    for copy in arrivals:
        copy.start()
    here = [*rows, *pairs, hidden, gate_grad, up_grad]
    leaving = [
        pltpu.make_async_copy(
            here[i], outs[i].at[pl.ds(k * slots, slots), :], sems.at[3 * n + i]
        )
        for i in range(2 * n + 3)
    ]

    def columns(p, first=0):
        return pl.ds(pl.multiple_of(first + meta[1 + p], 128), part)

    for i, x_ref in enumerate(pieces):
        cot = (g0, g1, g2, g3)[i]
        at = slice(i * capacity, (i + 1) * capacity)
        info = x_ref[:, width:].astype(F32)
        place = jnp.sum(jnp.where(lanes == c, info, 0.0), axis=1, keepdims=True)
        spots = lax.broadcasted_iota(jnp.int32, (1, capacity), 1).astype(F32)
        chosen = (spots == place).astype(BF16)
        chosen_ref[i] = chosen
        logits = dot(x_ref[:, :width], router[...])
        seen = info > -1.5
        top = jnp.max(jnp.where(seen, logits, -1e30), axis=1, keepdims=True)
        shares = jnp.where(seen, jnp.exp(logits - top), 0.0)
        gates = shares / jnp.sum(shares, axis=1, keepdims=True)
        own = jnp.sum(jnp.where(lanes == c, gates, 0.0), axis=1, keepdims=True)
        gate = lax.dot_general(
            chosen.astype(F32),
            jnp.broadcast_to(own, gates.shape),
            COLS_T,
            precision=HIGH,
            preferred_element_type=F32,
        )
        gate_ref[at, :] = gate
        for p in range(n):
            rows[p][at, :] = dot(chosen, x_ref[:, columns(p)], COLS_T).astype(BF16)
            grads = dot(chosen, cot[:, columns(p)], COLS_T)
            picked[p][at, :] = grads.astype(BF16)
            pairs[p][at, :] = (grads * gate[:, :1]).astype(BF16)
    for copy in leaving[: 2 * n]:
        copy.start()
    for copy in arrivals[: 2 * n]:
        copy.wait()
    wg, wu, wd = (w_here[n * i : n * (i + 1)] for i in range(3))
    gate_part = sum(dot(rows[p][...], wg[p][...]) for p in range(n))
    up_part = sum(dot(rows[p][...], wu[p][...]) for p in range(n))
    sigma = jax.nn.sigmoid(gate_part)
    silu_gate = gate_part * sigma
    h = (silu_gate * up_part).astype(BF16)
    hidden[...] = h
    leaving[2 * n].start()
    for copy in arrivals[2 * n :]:
        copy.wait()
    hidden_grad = sum(dot(pairs[p][...], wd[p][...]) for p in range(n))
    gg = (hidden_grad * up_part * sigma * (1.0 + gate_part * (1.0 - sigma))).astype(BF16)
    gate_grad[...] = gg
    leaving[2 * n + 1].start()
    ug = (hidden_grad * silu_gate).astype(BF16)
    up_grad[...] = ug
    leaving[2 * n + 2].start()
    inner_sum = jnp.zeros((slots, 1), F32)
    for p in range(n):
        out = dot(h, wd[p][...], ROWS_T).astype(BF16).astype(F32)
        inner_sum += jnp.sum(out * picked[p][...].astype(F32), axis=1, keepdims=True)
        scaled = (out * gate_ref[:, :1]).astype(BF16)
        row_sum = (dot(gg, wg[p][...], ROWS_T) + dot(ug, wu[p][...], ROWS_T)).astype(BF16)
        for i in range(4):
            back = (mine, theirs)[i // 2].at[i % 2]
            at = slice(i * capacity, (i + 1) * capacity)
            back[:, columns(p)] = dot(chosen_ref[i], row_sum[at, :]).astype(BF16)
            back[:, columns(p, width + 128)] = dot(chosen_ref[i], scaled[at, :]).astype(BF16)
    high = inner_sum.astype(BF16).astype(F32)
    extra = jnp.where(lanes == c, high, 0.0) + jnp.where(
        lanes == c + n_exp, inner_sum - high, 0.0
    )
    extra = extra.astype(BF16)
    for i in range(4):
        back = (mine, theirs)[i // 2].at[i % 2]
        at = slice(i * capacity, (i + 1) * capacity)
        back[:, width : width + 128] = dot(chosen_ref[i], extra[at, :]).astype(BF16)
    for copy in leaving:
        copy.wait()


def experts(k, quarter, cots, router, wg, wu, wd, meta, capacity, n_exp, before):
    count, wide = quarter[0].shape
    nz, width = len(cots), cots[k][0].shape[1]
    n_parts = len(wg)
    part = width // n_parts
    hid = wg[0].shape[1]
    slots = 4 * capacity
    anywhere = pl.BlockSpec(memory_space=pl.ANY)
    pair = once((2, count, wide + width), lambda i, m: (0, 0, 0))
    rows_all = lambda cols: pltpu.HBM((nz * slots, cols), BF16)
    n_out = 2 * n_parts + 3
    outs = pl.pallas_call(
        functools.partial(experts_kernel, k, n_parts, width, capacity, n_exp),
        grid_spec=pltpu.PrefetchScalarGridSpec(
            num_scalar_prefetch=1,
            grid=(1,),
            in_specs=[whole((count, wide))] * 4
            + [whole((count, width))] * 4
            + [whole(router.shape)]
            + [anywhere] * (3 * n_parts)
            + [IN_HBM] * len(before),
            out_specs=[IN_HBM] * n_out + [pair, pair],
            scratch_shapes=[pltpu.VMEM((part, hid), BF16)] * (3 * n_parts)
            + [pltpu.VMEM((slots, part), BF16)] * (3 * n_parts)
            + [pltpu.VMEM((slots, hid), BF16)] * 3
            + [
                pltpu.VMEM((4, count, capacity), BF16),
                pltpu.VMEM((slots, 128), F32),
                pltpu.SemaphoreType.DMA((5 * n_parts + 3,)),
            ],
        ),
        out_shape=[rows_all(part)] * (2 * n_parts)
        + [rows_all(hid)] * 3
        + [jax.ShapeDtypeStruct((2, count, wide + width), BF16)] * 2,
        input_output_aliases={10 + 3 * n_parts + i: i for i in range(len(before))},
        compiler_params=params(42),
        cost_estimate=cost(15),
        name="experts",
    )(meta, *quarter, *cots[k], router, *wg, *wu, *wd, *before)
    return (outs[n_out], outs[n_out + 1]), outs[:n_out]


def head_back(grad, v, gain, cos, sin):
    scale = lax.rsqrt(jnp.mean(v * v, axis=-1, keepdims=True) + EPS)
    d = grad * cos - half_turn(grad) * sin
    u = d * gain
    inner = jnp.mean(u * v, axis=-1, keepdims=True)
    back = scale * u - v * (scale * scale * scale * inner)
    return back.astype(BF16), jnp.sum(d * v * scale, axis=0, keepdims=True)


def key_back_kernel(meta, dk, dv, raw, turn, gk, *refs):
    out, gains = refs[-2:]
    came = refs[:-2]
    z = pl.program_id(0)

    @pl.when(z == 0)
    def _():
        gains[...] = jnp.zeros_like(gains)

    n_kv = dk.shape[0]
    count = raw.shape[1]
    for i in range(4):
        at = pl.ds(pl.multiple_of(lax.rem(meta[4 * z + i], 4) * count, count), count)
        for j in range(n_kv):
            v = raw[i, :, j * HD : (j + 1) * HD]
            key_grad, value_grad = dk[j, at, :], dv[j, at, :]
            if came:
                key_grad = key_grad + came[0][0, at, :].astype(F32)
                value_grad = value_grad + came[0][1, at, :].astype(F32)
            grad = key_grad * HD**-0.5
            back, gain = head_back(grad, v, gk[...], *turns(turn[at, :]))
            out[i, :, j * HD : (j + 1) * HD] = back
            gains[0:1, :] += gain
            out[i, :, (n_kv + j) * HD : (n_kv + j + 1) * HD] = value_grad.astype(BF16)


def key_back(dk, dv, came, raw, turn, gk, meta):
    hpd = dk.shape[0]
    n_kv = 1 if came else hpd
    n_ctx, count, _ = raw.shape
    group = lambda z, t: lax.div(t[4 * z], 4)
    head_at = pl.BlockSpec(
        (n_kv, 4 * count, HD), lambda z, t: (t[n_ctx] if came else 0, group(z, t), 0)
    )
    turn_at = pl.BlockSpec((4 * count, HD), lambda z, t: (group(z, t), 0))
    return pl.pallas_call(
        key_back_kernel,
        grid_spec=pltpu.PrefetchScalarGridSpec(
            num_scalar_prefetch=1,
            grid=(n_ctx // 4,),
            in_specs=[
                head_at,
                head_at,
                pl.BlockSpec((4, count, n_kv * HD), lambda z, t: (z, 0, hpd // n_kv)),
                turn_at,
                whole((1, HD)),
            ]
            + [pl.BlockSpec((2, 4 * count, HD), lambda z, t: (0, group(z, t), 0))] * len(came),
            out_specs=[
                pl.BlockSpec((4, count, 2 * n_kv * HD), lambda z, t: (z, 0, 0)),
                whole((8, HD)),
            ],
        ),
        out_shape=[
            jax.ShapeDtypeStruct((n_ctx, count, 2 * n_kv * HD), BF16),
            jax.ShapeDtypeStruct((8, HD), F32),
        ],
        compiler_params=params(14),
        cost_estimate=cost(5),
        name="key_back",
    )(meta, dk, dv, raw, turn, gk, *came)


def input_back_kernel(k, hpd, meta, dq, kv, raw, scales, turn, gq, w, *refs):
    x, (grads_out, theirs, mine, gains, gain_grad, rows, grads, sem) = refs[:4], refs[-8:]
    copy = pltpu.make_async_copy(grads, grads_out.at[pl.ds(4 * k, 4)], sem)
    count = raw.shape[1]
    q_cols = hpd * HD

    @pl.when(pl.program_id(0) == 0)
    def _():
        gains[...] = jnp.zeros_like(gains)
        for i in range(4):
            at = span(meta, k, i, count)
            for j in range(hpd):
                cols = slice(j * HD, (j + 1) * HD)
                grad = dq[j, at, :] * HD**-0.5
                back, gain = head_back(grad, raw[i, :, cols], gq[...], *turns(turn[at, :]))
                grads[i, :, cols] = back
                gains[0:1, :] += gain
            rows[i * count : (i + 1) * count, :q_cols] = grads[i]
            rows[i * count : (i + 1) * count, q_cols:] = kv[i]
        copy.start()

    @pl.when(pl.program_id(0) == pl.num_programs(0) - 1)
    def _():
        copy.wait()

    back = dot(rows[...], w[...], ROWS_T)
    total = None
    for i in range(4):
        block = back[i * count : (i + 1) * count, :]
        (mine, theirs)[i // 2][i % 2] = block.astype(BF16)
        term = jnp.sum(block * x[i][...].astype(F32) * scales[i, :, :1], axis=0, keepdims=True)
        total = term if total is None else total + term
    gain_grad[...] = jnp.broadcast_to(total, gain_grad.shape)


def input_back(k, quarter, dq, kv, raw, scales, turn, gq, w, meta, before):
    count, width = quarter[0].shape
    hpd = dq.shape[0]
    n_ctx = raw.shape[0]
    q_cols = hpd * HD
    chunk = width // 4
    group = group_of(k)
    turn_at = pl.BlockSpec((4 * count, HD), lambda i, t: (group(t), 0))
    own = lambda cols: pl.BlockSpec((4, count, cols), lambda i, t: (k, 0, 0))
    pair_at = pl.BlockSpec((2, count, chunk), lambda i, t: (0, 0, i))
    pair = jax.ShapeDtypeStruct((2, count, width), BF16)
    outs = pl.pallas_call(
        functools.partial(input_back_kernel, k, hpd),
        grid_spec=pltpu.PrefetchScalarGridSpec(
            num_scalar_prefetch=1,
            grid=(4,),
            in_specs=[
                pl.BlockSpec((hpd, 4 * count, HD), lambda i, t: (0, group(t), 0)),
                own(kv.shape[2]),
                own(q_cols),
                own(HD),
                turn_at,
                whole((1, HD)),
                pl.BlockSpec((chunk, w.shape[1]), lambda i, t: (i, 0)),
            ]
            + [pl.BlockSpec((count, chunk), lambda i, t: (0, i))] * 4
            + [IN_HBM] * len(before),
            out_specs=[
                IN_HBM,
                pair_at,
                pair_at,
                whole((8, HD)),
                pl.BlockSpec((8, chunk), lambda i, t: (0, i)),
            ],
            scratch_shapes=[
                pltpu.VMEM((4 * count, w.shape[1]), BF16),
                pltpu.VMEM((4, count, q_cols), BF16),
                pltpu.SemaphoreType.DMA(()),
            ],
        ),
        out_shape=[
            pltpu.HBM((n_ctx, count, q_cols), BF16),
            pair,
            pair,
            jax.ShapeDtypeStruct((8, HD), F32),
            jax.ShapeDtypeStruct((8, width), F32),
        ],
        input_output_aliases={12: 0} if before else {},
        compiler_params=params(18),
        cost_estimate=cost(6),
        name="input_back",
    )(meta, dq, kv, raw, scales, turn, gq, w, *quarter, *before)
    grads, theirs, mine, gains, gain_grad = outs
    return (mine, theirs), grads, gains, gain_grad


def place_kernel(parts, n_kv, table, *refs):
    columns, keys = refs[:4], refs[4 : 4 + n_kv]
    outs = refs[-3:] if n_kv else refs[-1:]
    for n in range(4):

        @pl.when(pl.program_id(0) // parts == n)
        def _():
            outs[0][...] = columns[n][...].astype(F32)
            if n_kv:
                outs[1][...] = keys[n][:, :HD].astype(F32)
                outs[2][...] = keys[n][:, HD:].astype(F32)


def place_columns(k, quarter, table, n_ctx, rows, before):
    all_rows, cols = quarter[0].shape
    parts = cols // HD
    kv_rows = all_rows - rows

    def piece_at(n):
        return lambda i, t: (0, jnp.clip(i - n * parts, 0, parts - 1))

    def head_at(i, t):
        c = t[4 * k + i // parts]
        rows_part = lax.rem(c // 2, 2) * 2 + lax.rem(c // 4, 2)
        return rows_part, lax.rem(c, 2) * 2 + c // 8

    out_specs = [
        pl.BlockSpec((rows, HD), lambda i, t: (0, (i % parts) * n_ctx + t[4 * k + i // parts]))
    ]
    out_shape = [jax.ShapeDtypeStruct((rows, n_ctx * cols), F32)]
    in_specs = [pl.BlockSpec((rows, HD), piece_at(n)) for n in range(4)]
    pieces = list(quarter)
    if kv_rows:
        in_specs += [once((kv_rows, cols), lambda i, t: (rows // kv_rows, 0))] * 4
        pieces += quarter
        out_specs += [pl.BlockSpec((kv_rows, HD), head_at)] * 2
        out_shape += [jax.ShapeDtypeStruct((rows, KVH * HD), F32)] * 2
    return pl.pallas_call(
        functools.partial(place_kernel, parts, len(pieces) - 4),
        grid_spec=pltpu.PrefetchScalarGridSpec(
            num_scalar_prefetch=1,
            grid=(4 * parts,),
            in_specs=in_specs + [pl.BlockSpec(memory_space=pl.ANY)] * len(before),
            out_specs=out_specs,
        ),
        out_shape=out_shape,
        input_output_aliases={1 + len(pieces) + i: i for i in range(len(before))},
        compiler_params=params(12),
        cost_estimate=cost(4.6),
        name="place_columns",
    )(table, *pieces, *before)


def place_rows_kernel(table, *refs):
    out = refs[-1]
    for n in range(len(refs) - 1):

        @pl.when(pl.program_id(0) == n)
        def _():
            out[...] = refs[n][...].astype(F32)


def place_rows(quarters, table):
    blocks = [block for quarter in quarters for block in quarter]
    rows, cols = blocks[0].shape
    return pl.pallas_call(
        place_rows_kernel,
        grid_spec=pltpu.PrefetchScalarGridSpec(
            num_scalar_prefetch=1,
            grid=(len(blocks),),
            in_specs=[whole((rows, cols))] * len(blocks),
            out_specs=pl.BlockSpec((rows, cols), lambda i, t: (t[i], 0)),
        ),
        out_shape=jax.ShapeDtypeStruct((len(blocks) * rows, cols), F32),
        compiler_params=params(16),
        cost_estimate=cost(8),
        name="place_rows",
    )(table, *blocks)


def local(
    inputs,
    w_query,
    w_key,
    w_value,
    w_output,
    norm_attn,
    gain_query,
    gain_key,
    w_router,
    norm_moe,
    w_gate,
    w_up,
    w_down,
    lengths,
    routes,
    pair_order,
    cotangent,
):
    n_ctx = lax.axis_size("ctx")
    n_f = lax.axis_size("fsdp")
    c = lax.axis_index("ctx")
    f = lax.axis_index("fsdp")
    count, width = inputs.shape[1], inputs.shape[2]
    length = count * n_ctx
    nz = n_ctx // 4
    later = scatter_order(n_ctx)
    hpd = H // n_ctx
    hpf = H // n_f
    group = H // KVH
    n_exp = w_router.shape[1]
    capacity = 5 * count * TOPK // (4 * n_exp)
    table = block_order(n_ctx)
    core = c % 2

    heads = [c % hpf + hpf * ((c // hpf) * hpd + j) for j in range(hpd)]
    kv_heads = [h // group for h in heads]
    columns = lambda w, h: lax.dynamic_slice_in_dim(w, h * HD, HD, 1)
    shared = n_f == 2 and hpd == 2
    if shared:
        kv_own = heads[0] // group + core * (KVH // 2)
        w_part = jnp.concatenate(
            [columns(w_query, h) for h in heads]
            + [columns(w_key, kv_own), columns(w_value, kv_own)],
            axis=1,
        )
    else:
        w_part = jnp.concatenate(
            [columns(w_query, h) for h in heads]
            + [columns(w_key, h) for h in kv_heads]
            + [columns(w_value, h) for h in kv_heads],
            axis=1,
        )
    w_part, norm_first = tie(w_part, norm_attn)
    vectors = jnp.concatenate([norm_first, gain_query, gain_key, norm_moe])
    if n_f == 2:
        vectors = joined([vectors[None], swap(vectors[None])])
        router = joined([w_router, swap(w_router)])
    else:
        vectors = lax.all_gather(vectors, "fsdp", axis=0)
        router = lax.all_gather(w_router, "fsdp", axis=0, tiled=True)
    sizes = [norm_attn.shape[0], gain_query.shape[0], gain_key.shape[0], norm_moe.shape[0]]
    rows_of, at = [], 0
    for size in sizes:
        rows_of.append(vectors[:, at : at + size].reshape(1, n_f * size).astype(F32))
        at += size
    attn_gain, query_gain, key_gain, moe_gain = rows_of
    router_wide = jnp.pad(router, ((0, 0), (0, 128 - n_exp)))
    offsets = part_offsets(width)
    n_parts = len(offsets)
    meta_rows = jnp.concatenate([table, jnp.stack([core] + offsets).astype(jnp.int32)])
    q_cols = hpd * HD
    block = w_gate.shape[2] // 3
    weights = {}

    def fetch_weights():
        parts = yield from fetch(w_part, 2)
        weights["qkv"], weights["beside"] = parts, []
        if shared:
            weights["beside"] = [
                lax.ppermute(part[:, q_cols:], "ctx", flip(n_ctx, 1)) for part in parts
            ]
        weights["back"] = joined(parts)
        own_rows = lax.dynamic_slice_in_dim(w_output, (c % hpf) * HD, HD, 0)
        w_out = joined((yield from fetch(own_rows)))
        weights["out"] = lax.dynamic_slice_in_dim(w_out, (c // hpf) * hpd * HD, hpd * HD, 0)
        weights["gate"] = yield from fetch_thirds(w_gate[0])
        weights["up"] = yield from fetch_thirds(w_up[0])
        weights["down"] = yield from fetch_thirds(w_down[0])

    gathered = {}

    def gather_cotangents():
        (cot,) = yield (cotangent[0],), 3
        gathered["cot"] = yield from gather_quarters(cot, n_ctx)

    sides = [Side(fetch_weights()), Side(gather_cotangents())]

    experts_of = jnp.arange(n_exp, dtype=jnp.int32)
    picks = routes[0][:, :, None] == experts_of
    ranks = jnp.sum(
        jnp.where(picks, pair_order[0, 0].reshape(count, TOPK, 1), 0), axis=1
    )
    chosen = jnp.any(picks, axis=1)
    ranks = jnp.where(chosen, ranks, count * TOPK)
    place = jnp.sum((ranks[None, :, :] < ranks[:, None, :]).astype(jnp.int32), axis=1)
    place = jnp.where(chosen, jnp.where(place < capacity, place, -1), -2)
    place = jnp.pad(place, ((0, 0), (0, 128 - n_exp)), constant_values=-2).astype(BF16)

    ends = jnp.cumsum(lengths[0]).astype(jnp.int32)
    turn = rotary_table(length)

    xs = {}

    def through_projection(k, quarter, token, before):
        xs[k] = quarter
        if k == 0:
            return ()
        if k == 1:
            before = projection(0, token, ())
        return projection(k, token, before)

    def projection(k, token, before):
        return project(
            k,
            xs[k],
            weights["qkv"],
            weights["beside"],
            attn_gain,
            query_gain,
            key_gain,
            turn,
            token,
            hpd,
            n_ctx,
            before,
        )

    straight = list(range(nz))
    *normed, raw, scales, query, key, value = pipeline(
        n_ctx, straight, through_projection, meta_rows, sides, piece=inputs[0]
    )
    _, (query,) = land({}, sides, query)
    mixed, log_total = attend(query, key, value, ends)
    _, (mixed,) = land({}, sides, mixed)
    x = inputs[0].astype(F32)
    branch_sum, _, _ = pipeline(
        n_ctx,
        later,
        lambda k, _, token, state: (branch(k, mixed, weights["out"], token, count), state),
        table,
        sides,
        scatter=True,
    )
    middle = x + branch_sum
    moe_scale = lax.rsqrt(jnp.mean(middle * middle, axis=-1, keepdims=True) + EPS)
    routed_in = (middle * moe_scale * moe_gain).astype(BF16)

    pad_offsets = (offsets + [jnp.int32(0)])[:2]
    head_meta = [jnp.stack([c] + pad_offsets).astype(jnp.int32)]
    expert_meta = jnp.concatenate(head_meta)

    def through_experts(k, quarter, token, before):
        return experts(
            k,
            quarter,
            gathered["cot"],
            router_wide,
            weights["gate"],
            weights["up"],
            weights["down"],
            token,
            capacity,
            n_exp,
            before,
        )

    routed_grad, seen, _ = pipeline(
        n_ctx,
        later,
        through_experts,
        expert_meta,
        sides,
        piece=jnp.concatenate([routed_in, place], axis=1),
        scatter=True,
    )
    rows, pairs = seen[:n_parts], seen[n_parts : 2 * n_parts]
    hidden, gate_part_grad, up_part_grad = seen[2 * n_parts :]
    outputs = (middle + routed_grad[:, width + 128 :]).astype(BF16)

    gate_grad = routed_grad[:, width : width + n_exp] + routed_grad[
        :, width + n_exp : width + 2 * n_exp
    ]
    routed_grad = routed_grad[:, :width]
    logits = dot(routed_in, router)
    top = jnp.max(jnp.where(chosen, logits, -1e30), axis=-1, keepdims=True)
    shares = jnp.where(chosen, jnp.exp(logits - top), 0.0)
    gates = shares / jnp.sum(shares, axis=-1, keepdims=True)
    logit_grad = gates * (gate_grad - jnp.sum(gates * gate_grad, axis=-1, keepdims=True))
    routed_grad = routed_grad + lax.dot_general(
        logit_grad, router.astype(F32), ROWS_T, precision=HIGH
    )
    router_part = lax.dot_general(
        logit_grad, routed_in.astype(F32), COLS_T, precision=HIGH
    )

    grad_out = cotangent[0].astype(F32)
    moe_scaled = routed_grad * moe_gain
    moe_part = jnp.sum(routed_grad * middle * moe_scale, axis=0, keepdims=True)
    middle_grad = (
        grad_out
        + moe_scale * moe_scaled
        - middle
        * (
            moe_scale
            * moe_scale
            * moe_scale
            * jnp.mean(moe_scaled * middle, axis=-1, keepdims=True)
        )
    )

    grads, sums = {}, []

    def scatter_grads():
        grads["gate"] = yield from scatter_blocks(rows, gate_part_grad, block)
        grads["up"] = yield from scatter_blocks(rows, up_part_grad, block)
        grads["down"] = yield from scatter_blocks(pairs, hidden, block)

    sides = [Side(scatter_grads())]
    grad_out_w, mixed_grad, delta = pipeline(
        n_ctx,
        straight,
        lambda k, quarter, token, before: branch_back(
            k, quarter, mixed, weights["out"], token, before
        ),
        table,
        sides,
        piece=middle_grad.astype(BF16),
    )
    def sum_out_grad():
        if n_f == hpd:
            placed = grad_out_w
        else:
            spread_out = jnp.arange(n_f, dtype=jnp.int32)[:, None] == (
                (c // hpf) * hpd + jnp.arange(hpd, dtype=jnp.int32)[None, :]
            )
            placed = jnp.einsum(
                "fj,jrd->frd", spread_out.astype(F32), grad_out_w.reshape(hpd, HD, width)
            ).reshape(n_f * HD, width)
        own = yield from scatter_rows(placed)
        own = own.astype(BF16)
        if n_ctx == hpf:
            grads["out"] = place_rows((yield from gather_blocks(own, n_ctx, 4)), table)
        else:
            whole_grad = lax.all_gather(own, "ctx", axis=0).reshape(-1, hpf * HD, width)
            mine = lax.dynamic_index_in_dim(whole_grad, f // hpd, 0, keepdims=False)
            grads["out"] = mine.astype(F32)

    sides.append(Side(sum_out_grad()))
    ends_and_core = jnp.concatenate([ends, core[None].astype(jnp.int32)])
    dq, dk, dv, *away = attend_back(
        query, mixed_grad, log_total, delta, key, value, ends_and_core, int(shared)
    )
    _, (dq, dk, dv, *away) = land({}, sides, dq, dk, dv, *away)
    came = [lax.ppermute(array, "ctx", flip(n_ctx, 1)) for array in away]
    kv_grad, key_gains = key_back(dk, dv, came, raw, turn, key_gain, meta_rows)
    normed_flat = [n.reshape(length, -1) for n in normed]

    def sum_key_grads():
        grad_kv = yield from scatter_blocks(
            normed_flat, kv_grad.reshape(length, -1), kv_grad.shape[-1]
        )
        if not shared:
            slots_kv = jnp.arange(KVH, dtype=jnp.int32)
            spread = jnp.stack([slots_kv == h for h in kv_heads]).astype(F32)
            grad_kv = grad_kv.reshape(width // n_f, 2, hpd, 1, HD) * spread[None, None, :, :, None]
            grad_kv = jnp.sum(grad_kv, axis=2).reshape(width // n_f, 2 * KVH * HD)
            grad_kv = lax.psum(grad_kv.astype(BF16), "ctx").astype(F32)
            grads["key"], grads["value"] = grad_kv[:, : KVH * HD], grad_kv[:, KVH * HD :]
            return
        for bit in (2, 4):
            rows_kept = grad_kv.shape[0] // 2
            side = (c // bit) % 2
            kept = lax.dynamic_slice_in_dim(grad_kv, side * rows_kept, rows_kept, 0)
            gone = lax.dynamic_slice_in_dim(grad_kv, (1 - side) * rows_kept, rows_kept, 0)
            (got,) = yield (lax.ppermute(gone.astype(BF16), "ctx", flip(n_ctx, bit)),), 1
            grad_kv = kept + got.astype(F32)
        grads["key_piece"] = grad_kv.astype(BF16)

    sides.append(Side(sum_key_grads()))
    gain_parts, attn_parts = [], []

    def through_inputs(k, _, token, before):
        back, q_grad, gains, gain_grad = input_back(
            k,
            xs[k],
            dq,
            kv_grad,
            raw,
            scales,
            turn,
            query_gain,
            weights["back"],
            token,
            before,
        )
        gain_parts.append(gains)
        attn_parts.append(gain_grad)
        if len(gain_parts) == nz:
            gain_rows = jnp.concatenate([sum(gain_parts)[:1], key_gains[:1]], axis=1)
            gain_rows = jnp.pad(gain_rows, ((0, 0), (0, width - 2 * HD)))
            rows_last = [router_part, moe_part, sum(attn_parts)[:1], gain_rows]
            sides.append(Side(sum_all(jnp.concatenate(rows_last, axis=0), sums)))
        return back, (q_grad,)

    q_grads = []

    def query_weights(token):
        q_flat = q_grads[0].reshape(length, -1)
        if n_f != 2:
            return (
                lax.psum_scatter(
                    dot(normed_flat[0], q_flat, COLS_T).astype(BF16),
                    "fsdp",
                    scatter_dimension=0,
                    tiled=True,
                ),
            )
        mine, other = normed_flat
        came = swap(dot(other, q_flat, COLS_T).astype(BF16))
        return dot(mine, q_flat, COLS_T), came

    def through_inputs_last(k, quarter, token, before):
        back, state = through_inputs(k, quarter, token, before)
        q_grads[:] = state
        return back, state

    normed_grad, _, grad_q = pipeline(
        n_ctx, later, through_inputs_last, meta_rows, sides, scatter=True, closing=query_weights
    )
    for side in sides[2:3]:
        side.finish()
    grad_q = sum(g.astype(F32) for g in grad_q).astype(BF16)
    q_rows = grad_q.shape[0]
    if shared:
        grad_q = jnp.concatenate([grad_q, grads["key_piece"]], axis=0)

    if n_ctx == hpf:
        placed = pipeline(
            n_ctx,
            straight,
            lambda k, quarter, token, before: place_columns(
                k, quarter, token, n_ctx, q_rows, before
            ),
            table,
            sides,
            piece=grad_q,
        )
        grad_w_query = placed[0]
        if shared:
            grads["key"], grads["value"] = placed[1:]
    else:
        grad_w_query = (
            lax.all_gather(grad_q, "ctx", axis=0)
            .reshape(n_ctx // hpf, hpf, width // n_f, hpd, HD)
            .transpose(2, 0, 3, 1, 4)
            .reshape(width // n_f, H * HD)
            .astype(F32)
        )
    for side in sides:
        side.finish()
    sums = sums[0]
    own_part = lambda v, size: lax.dynamic_slice_in_dim(v, f * (size // n_f), size // n_f, 0)
    grad_w_router = own_part(sums[:n_exp].T, width)
    grad_norm_moe = own_part(sums[n_exp], width)
    grad_norm_attn = own_part(sums[n_exp + 1], width)
    grad_gain_query = own_part(sums[n_exp + 2, :HD], HD)
    grad_gain_key = own_part(sums[n_exp + 2, HD : 2 * HD], HD)

    attn_scale = lax.rsqrt(jnp.mean(x * x, axis=-1, keepdims=True) + EPS)
    attn_scaled = normed_grad * attn_gain
    input_grad = (
        middle_grad
        + attn_scale * attn_scaled
        - x
        * (
            attn_scale
            * attn_scale
            * attn_scale
            * jnp.mean(attn_scaled * x, axis=-1, keepdims=True)
        )
    )
    return (
        outputs[None],
        input_grad.astype(BF16)[None],
        grad_w_query,
        grads["key"],
        grads["value"],
        grads["out"],
        grad_norm_attn,
        grad_gain_query,
        grad_gain_key,
        grad_w_router,
        grad_norm_moe,
        grads["gate"][None],
        grads["up"][None],
        grads["down"][None],
    )


def solution(mesh):
    in_specs = (
        P("fsdp", "ctx", None),
        P("fsdp", None),
        P("fsdp", None),
        P("fsdp", None),
        P("fsdp", None),
        P("fsdp"),
        P("fsdp"),
        P("fsdp"),
        P("fsdp", None),
        P("fsdp"),
        P("ctx", "fsdp", None),
        P("ctx", "fsdp", None),
        P("ctx", "fsdp", None),
        P("fsdp", None),
        P("fsdp", "ctx", None),
        P("fsdp", "ctx", None),
        P("fsdp", "ctx", None),
    )
    out_specs = (
        P("fsdp", "ctx", None),
        P("fsdp", "ctx", None),
        P("fsdp", None),
        P("fsdp", None),
        P("fsdp", None),
        P("fsdp", None),
        P("fsdp"),
        P("fsdp"),
        P("fsdp"),
        P("fsdp", None),
        P("fsdp"),
        P("ctx", "fsdp", None),
        P("ctx", "fsdp", None),
        P("ctx", "fsdp", None),
    )
    return jax.shard_map(local, mesh=mesh, in_specs=in_specs, out_specs=out_specs, check_vma=False)
```

```python
import functools

import jax
import jax.numpy as jnp
from jax import lax
from jax.experimental import pallas as pl
from jax.experimental.pallas import tpu as pltpu
from jax.sharding import PartitionSpec as P

H = 32
KVH = 4
HD = 128
TOPK = 8
EPS = 1e-06
THETA = 1000000.0
HIGH = lax.Precision.HIGHEST
LOG2E = 1.4426950408889634
F32 = jnp.float32
BF16 = jnp.bfloat16
ROWS_T = (((1,), (1,)), ((), ()))
COLS_T = (((0,), (0,)), ((), ()))


def dot(a, b, dims=(((1,), (0,)), ((), ()))):
    return lax.dot_general(a, b, dims, preferred_element_type=F32)


def params(mebibytes):
    return pltpu.CompilerParams(vmem_limit_bytes=mebibytes * 1024 * 1024)


def once(shape, index):
    return pl.BlockSpec(shape, index, pipeline_mode=pl.Buffered(1))


def cost(microseconds):
    return pl.CostEstimate(
        flops=int(microseconds * 1.15e9), bytes_accessed=0, transcendentals=0
    )


def flip(n_ctx, bit):
    return [(i, i ^ bit) for i in range(n_ctx)]


def ring(n_ctx, step):
    return [(i, (i + step) % n_ctx) for i in range(n_ctx)]


def block_order(n_ctx):
    c = lax.axis_index("ctx")
    nz = n_ctx // 4
    z, x, core = c // 4, (c // 2) % 2, c % 2
    table = []
    for k in range(nz):
        for dc in range(2):
            for dx in range(2):
                table.append(lax.rem(z + nz - k, nz) * 4 + (x ^ dx) * 2 + (core ^ dc))
    return jnp.stack(table).astype(jnp.int32)


def tie(*arrays):
    return lax.optimization_barrier(arrays)


class Side:
    def __init__(self, chain):
        self.chain, self.flying, self.left = chain, None, 0
        self.resume(None)

    def resume(self, landed):
        try:
            self.flying, self.left = self.chain.send(landed)
        except StopIteration:
            self.flying = None

    def finish(self):
        while self.flying is not None:
            self.resume(self.flying)


def land(air, sides, *others):
    due = [side for side in sides if side.flying is not None and side.left <= 1]
    for side in sides:
        side.left -= 1
    keys = list(air)
    flying = [array for side in due for array in side.flying]
    arrays = list(tie(*air.values(), *flying, *others))
    air.clear()
    landed = {key: arrays.pop(0) for key in keys}
    for side in due:
        side.resume([arrays.pop(0) for _ in side.flying])
    return landed, arrays


def pipeline(
    n_ctx, order, compute, token, sides, piece=None, scatter=False, closing=None, along=False
):
    nz = n_ctx // 4
    air, have, state = {}, {}, ()

    def send(key, array, pairs):
        air[key] = lax.ppermute(array, "ctx", pairs)

    def bring(k):
        if along and k + 1 == nz:
            send(("beside", k), have["beside", k - 1], ring(n_ctx, 4))
        else:
            send(("beside", k), have["piece", k], flip(n_ctx, 2))
        if k + 1 < nz:
            send(("piece", k + 1), have["piece", k], ring(n_ctx, 4))

    def step_ends(*others):
        landed, others = land(air, sides, *others)
        have.update(landed)
        return others

    def total_of(own):
        parts = [*own, have["away"]] + ([have["carry"]] if "carry" in have else [])
        return sum(part.astype(F32) for part in parts)

    def give(blocks, token):
        mine, theirs = blocks
        arrived = lax.ppermute(theirs, "ctx", flip(n_ctx, 1))
        away = (mine[1].astype(F32) + arrived[1].astype(F32)).astype(BF16)
        token, away = tie(token, away)
        send("away", away, flip(n_ctx, 2))
        return (mine[0], arrived[0]), token

    if piece is not None:
        have["piece", 0] = piece
        for k in range(order[0] + 1):
            bring(k)
            step_ends()
    blocks = own = None
    for s, k in enumerate(order):
        following = order[s + 1 :][:1]
        quarter = None
        if piece is not None:
            for later in following:
                if ("beside", later) not in have:
                    bring(later)
            pair = [have["piece", k], have["beside", k]]
            quarter = pair + [lax.ppermute(array, "ctx", flip(n_ctx, 1)) for array in pair]
        if not scatter:
            state = compute(k, quarter, token, state)
            if following:
                token, *state = step_ends(token, *state)
            continue
        if own is not None:
            send("carry", total_of(own).astype(BF16), ring(n_ctx, 4))
        if blocks is not None:
            own, token = give(blocks, token)
        blocks, state = compute(k, quarter, token, state)
        token, *blocks = step_ends(token, *blocks)
    if not scatter:
        return tuple(state)
    send("carry", total_of(own).astype(BF16), ring(n_ctx, 4))
    own, token = give(blocks, token)
    extra = closing(token) if closing else ()
    extra = step_ends(*extra)
    return total_of(own), state, extra


def gather_planned(piece, n_ctx, plan):
    arrays = {("along", 0): piece}
    plan = list(plan)
    source = lambda kind, k: ("along", k) if kind == "across" else (kind, k - 1)
    for i, (items, steps) in enumerate(plan):
        going = [
            lax.ppermute(
                arrays[source(*item)], "ctx", flip(n_ctx, 2) if item[0] == "across" else ring(n_ctx, 4)
            )
            for item in items
        ]
        later = {source(*item) for item in plan[i + 1][0]} if i + 1 < len(plan) else set()
        tied = sorted(key for key in later if key in arrays)
        came = list((yield (*going, *(arrays[key] for key in tied)), steps))
        for kind, k in items:
            arrays["along" if kind == "along" else "beside", k] = came.pop(0)
        arrays.update(zip(tied, came))
    core = lambda array: lax.ppermute(array, "ctx", flip(n_ctx, 1))
    pairs = [(arrays["along", k], arrays["beside", k]) for k in range(n_ctx // 4)]
    return [(a, b, core(a), core(b)) for a, b in pairs]


COTANGENT_PLAN = [
    ([("along", 1)], 1),
    ([("along", 2), ("across", 0), ("across", 1)], 1),
    ([("along", 3), ("across", 2)], 1),
    ([("beside", 3)], 2),
]
OUTPUT_GRAD_PLAN = [
    ([("along", 1), ("across", 0)], 1),
    ([("along", 2)], 1),
    ([("along", 3), ("across", 1)], 1),
    ([("beside", 2), ("across", 3)], 1),
]


def scatter_order(n_ctx):
    return list(range(1, n_ctx // 4)) + [0]


def sum_all(values, result):
    n_ctx = lax.axis_size("ctx")
    bit = 1
    while bit < n_ctx:
        (came,) = yield (lax.ppermute(values.astype(BF16), "ctx", flip(n_ctx, bit)),), 1
        values = values + came.astype(F32)
        bit *= 2
    if lax.axis_size("fsdp") == 2:
        (came,) = yield (swap(values.astype(BF16)),), 1
        values = values + came.astype(F32)
    else:
        values = lax.psum(values, "fsdp")
    result.append(values)


SWAP = [(0, 1), (1, 0)]


def swap(part):
    return lax.ppermute(part, "fsdp", SWAP)


def fetch(part, steps=1):
    if lax.axis_size("fsdp") != 2:
        return [lax.all_gather(part, "fsdp", axis=0, tiled=True)]
    (other,) = yield (swap(part),), steps
    return [part, other]


def fetch_thirds(part, after, first=1):
    if lax.axis_size("fsdp") != 2:
        return [lax.all_gather(part, "fsdp", axis=0, tiled=True)], after
    step = (part.shape[0] // 3 + 31) // 32 * 32
    other = []
    for at in range(0, part.shape[0], step):
        after, rows = tie(after, part[at : at + step])
        if other:
            other[-1] = after
        (after,) = yield (swap(rows),), 1 if other else first
        other.append(after)
    return [part, jnp.concatenate(other, axis=0)], after


def joined(parts):
    if len(parts) == 1:
        return parts[0]
    mine, other = parts
    first = lax.axis_index("fsdp") == 0
    return jnp.concatenate([jnp.where(first, mine, other), jnp.where(first, other, mine)], axis=0)


def part_offsets(width):
    if lax.axis_size("fsdp") != 2:
        return [jnp.int32(0)]
    f = lax.axis_index("fsdp")
    return [f * (width // 2), (1 - f) * (width // 2)]


def scatter_products(pairs, block, steps=()):
    if lax.axis_size("fsdp") != 2:
        full = [dot(left[0], right, COLS_T).astype(BF16) for left, right in pairs]
        return [
            lax.psum_scatter(g, "fsdp", scatter_dimension=0, tiled=True).astype(F32) for g in full
        ]
    work = []
    for left, right in pairs:
        step = min(block, right.shape[1])
        work += [(left, right[:, at : at + step]) for at in range(0, right.shape[1], step)]
    product = lambda i, part: dot(work[i][0][part], work[i][1], COLS_T)
    done, sent = [], product(0, 1).astype(BF16)
    for i in range(len(work)):
        ahead = [product(i + 1, 1).astype(BF16)] if i + 1 < len(work) else []
        fresh = [product(i - 1, 0) + came.astype(F32)] if i > 0 else []
        came, *worked = yield (swap(sent), *ahead, *fresh), steps[i] if steps else 1
        if ahead:
            sent = worked.pop(0)
        done += worked
    done.append(product(len(work) - 1, 0) + came.astype(F32))
    sums = []
    for _, right in pairs:
        count = max(1, right.shape[1] // block)
        sums.append(done[0] if count == 1 else jnp.concatenate(done[:count], axis=1))
        done = done[count:]
    return sums


def scatter_rows(full):
    if lax.axis_size("fsdp") != 2:
        return lax.psum_scatter(
            full.astype(BF16), "fsdp", scatter_dimension=0, tiled=True
        ).astype(F32)
    rows = full.shape[0] // 2
    first = lax.axis_index("fsdp") == 0
    low, high = full[:rows], full[rows:]
    (came,) = yield (swap(jnp.where(first, high, low).astype(BF16)),), 1
    return jnp.where(first, low, high) + came.astype(F32)


def group_of(k):
    return lambda t: lax.div(t[4 * k], 4)


def span(t, k, i, count):
    return pl.ds(pl.multiple_of(lax.rem(t[4 * k + i], 4) * count, count), count)


IN_HBM = pl.BlockSpec(memory_space=pltpu.HBM)


def whole(shape):
    return once(shape, lambda *_: (0,) * len(shape))


def first_pair(shape):
    return pl.BlockSpec((1,) + shape, lambda i, t: (jnp.minimum(i, 1),) + (0,) * len(shape))


def last_pair(shape):
    return pl.BlockSpec((1,) + shape, lambda i, t: (jnp.maximum(i - 2, 0),) + (0,) * len(shape))


def split_pairs(i, body, first, last):
    @pl.when(i < 2)
    def _():
        body(first)

    @pl.when(i >= 2)
    def _():
        body(last)


def rotary_table(length):
    half = HD // 2
    steps = jnp.arange(half, dtype=jnp.int32).astype(F32)
    inverse = jnp.exp(steps * (-2.0 * jnp.log(THETA) / HD))
    angles = jnp.arange(length, dtype=jnp.int32).astype(F32)[:, None] * inverse[None, :]
    return jnp.concatenate([jnp.cos(angles), jnp.sin(angles)], axis=1)


def turns(table):
    other = pltpu.roll(table, HD // 2, 1)
    first = lax.broadcasted_iota(jnp.int32, (1, HD), 1) < HD // 2
    return jnp.where(first, table, other), jnp.where(first, -other, table)


def half_turn(v):
    return pltpu.roll(v, HD // 2, 1)


def head_norm(v, gain):
    scale = lax.rsqrt(jnp.mean(v * v, axis=-1, keepdims=True) + EPS)
    return v * scale * gain


def project_kernel(k, hpd, n_kv, n_parts, n_ctx, meta, x0, x1, x2, x3, gain, gq, gk, turn, *refs):
    n_outs = n_parts + 5
    w, beside = refs[:n_parts], refs[n_parts : 2 * n_parts] if n_kv < hpd else ()
    outs, refs = refs[-(2 * n_outs + 2) : -(n_outs + 2)], refs[-(n_outs + 2) :]
    here, rows, sems = refs[:n_outs], refs[-2], refs[-1]
    normed, (raw, scales, query, key, value) = here[:n_parts], here[n_parts:]
    count = x0.shape[0]
    group = pl.ds(pl.multiple_of(lax.div(meta[4 * k], 4) * 4 * count, count), 4 * count)
    places = [pl.ds(4 * k, 4)] * (n_parts + 2) + [(slice(None), group)] * 3
    leaving = [
        pltpu.make_async_copy(here[i], outs[i].at[places[i]], sems.at[i]) for i in range(n_outs)
    ]
    for i, piece in enumerate((x0, x1, x2, x3)):
        x = piece[...].astype(F32)
        r1 = lax.rsqrt(jnp.mean(x * x, axis=-1, keepdims=True) + EPS)
        scales[i] = jnp.broadcast_to(r1, scales.shape[1:])
        rows[i * count : (i + 1) * count, :] = (x * r1 * gain[...]).astype(BF16)
        for p, part in enumerate(normed):
            at = pl.ds(pl.multiple_of(meta[n_ctx + 1 + p], 128), part.shape[2])
            part[i] = rows[i * count : (i + 1) * count, at]
    for copy in leaving[:n_parts]:
        copy.start()
    parts = [part[...].reshape(4 * count, part.shape[2]) for part in normed]
    out = sum(dot(n, w_p[...]) for n, w_p in zip(parts, w))
    other = sum(dot(n, w_p[...]) for n, w_p in zip(parts, beside)) if beside else None
    core = meta[n_ctx]
    for i in range(4):
        at = span(meta, k, i, count)
        cos, sin = turns(turn[at, :])
        block = out[i * count : (i + 1) * count, :]
        raw[i] = block[:, : (hpd + n_kv) * HD]

        def turned(v, gain):
            v = head_norm(v, gain[...])
            return (v * cos + half_turn(v) * sin).astype(BF16)

        for j in range(hpd):
            query[j, at, :] = turned(block[:, j * HD : (j + 1) * HD], gq)
        for j in range(n_kv):
            v = block[:, (hpd + j) * HD : (hpd + j + 1) * HD]
            u = block[:, (hpd + n_kv + j) * HD : (hpd + n_kv + j + 1) * HD]
            head = core if beside else j
            key[head, at, :] = turned(v, gk)
            value[head, at, :] = u.astype(BF16)
        if beside:
            block = other[i * count : (i + 1) * count, :]
            key[1 - core, at, :] = turned(block[:, :HD], gk)
            value[1 - core, at, :] = block[:, HD:].astype(BF16)
    for copy in leaving[n_parts:]:
        copy.start()
    for copy in leaving:
        copy.wait()


def project(k, quarter, w, beside, gain, gq, gk, turn, meta, hpd, n_ctx, before):
    count, width = quarter[0].shape
    length = n_ctx * count
    n_parts = len(w)
    n_kv = 1 if beside else hpd
    group = group_of(k)
    turn_at = once((4 * count, HD), lambda i, t: (group(t), 0))
    head = pltpu.HBM((hpd, length, HD), BF16)
    cols = (hpd + n_kv) * HD
    weights = [*w, *beside]
    return pl.pallas_call(
        functools.partial(project_kernel, k, hpd, n_kv, n_parts, n_ctx),
        grid_spec=pltpu.PrefetchScalarGridSpec(
            num_scalar_prefetch=1,
            grid=(1,),
            in_specs=[whole((count, width))] * 4
            + [whole((1, width)), whole((1, HD)), whole((1, HD)), turn_at]
            + [whole(array.shape) for array in weights]
            + [IN_HBM] * len(before),
            out_specs=[IN_HBM] * (n_parts + 5),
            scratch_shapes=[pltpu.VMEM((4, count, width // n_parts), BF16)] * n_parts
            + [pltpu.VMEM((4, count, cols), F32), pltpu.VMEM((4, count, HD), F32)]
            + [pltpu.VMEM((hpd, 4 * count, HD), BF16)] * 3
            + [pltpu.VMEM((4 * count, width), BF16), pltpu.SemaphoreType.DMA((n_parts + 5,))],
        ),
        out_shape=[pltpu.HBM((n_ctx, count, width // n_parts), BF16)] * n_parts
        + [
            pltpu.HBM((n_ctx, count, cols), F32),
            pltpu.HBM((n_ctx, count, HD), F32),
            head,
            head,
            head,
        ],
        input_output_aliases={9 + len(weights) + i: i for i in range(len(before))},
        compiler_params=params(18),
        cost_estimate=cost(6),
        name="project",
    )(meta, *quarter, gain, gq, gk, turn, *weights, *before)


def first_key(ends, docs, position):
    start = jnp.zeros_like(position)
    for d in range(docs):
        start = jnp.where(position >= ends[d], jnp.maximum(start, ends[d]), start)
    return start


def attend_kernel(docs, heads, bq, bk, ends, query, key, value, mixed, total):
    i = pl.program_id(0)
    positions = i * bq + lax.broadcasted_iota(jnp.int32, (bq, 1), 0)
    starts = first_key(ends, docs, positions)
    low = lax.div(first_key(ends, docs, i * bq), bk)
    high = lax.div((i + 1) * bq - 1, bk) + 1

    def step(j, carry):
        rows = pl.ds(pl.multiple_of(j * bk, bk), bk)
        spots = j * bk + lax.broadcasted_iota(jnp.int32, (1, bk), 1)
        seen = (spots <= positions) & (spots >= starts)
        sums = []
        for h, (acc, norm) in enumerate(carry):
            scores = dot(query[h], key[h, rows, :], ROWS_T)
            p = jnp.where(seen, jnp.exp2(scores * (LOG2E * HD**-0.5)), 0.0)
            acc = acc + dot(p.astype(BF16), value[h, rows, :])
            sums.append((acc, norm + jnp.sum(p, axis=-1, keepdims=True)))
        return tuple(sums)

    start = (jnp.zeros((bq, HD), F32), jnp.zeros((bq, 1), F32))
    first_lane = lax.broadcasted_iota(jnp.int32, (1, HD), 1) == 0
    for h, (acc, norm) in enumerate(lax.fori_loop(low, high, step, (start,) * heads)):
        mixed[h] = acc / norm
        column = jnp.where(first_lane, jnp.log2(norm), 0.0)
        total[h] = row_sums(column)


def row_sums(values):
    return lax.dot_general(
        jnp.ones((8, values.shape[1]), F32),
        values,
        ROWS_T,
        precision=HIGH,
        preferred_element_type=F32,
    )


def attend(query, key, value, ends, bq=256, bk=512):
    heads, length, _ = query.shape
    docs = ends.shape[0]
    block = pl.BlockSpec((heads, bq, HD), lambda i, e: (0, i, 0))
    keys = once((heads, length, HD), lambda i, e: (0, 0, 0))
    line = pl.BlockSpec((heads, 8, bq), lambda i, e: (0, 0, i))
    return pl.pallas_call(
        functools.partial(attend_kernel, docs, heads, bq, bk),
        grid_spec=pltpu.PrefetchScalarGridSpec(
            num_scalar_prefetch=1,
            grid=(length // bq,),
            in_specs=[block, keys, keys],
            out_specs=[block, line],
        ),
        out_shape=[
            jax.ShapeDtypeStruct((heads, length, HD), F32),
            jax.ShapeDtypeStruct((heads, 8, length), F32),
        ],
        compiler_params=params(14),
        cost_estimate=cost(12.5),
        name="attend",
    )(ends, query, key, value)


def attend_back_kernel(
    docs, heads, bq, bk, ends, query, grad, total, delta, key, value, dq, dk, dv, *away
):
    i = pl.program_id(0)

    @pl.when(i == 0)
    def _():
        dk[...] = jnp.zeros_like(dk)
        dv[...] = jnp.zeros_like(dv)

    positions = i * bq + lax.broadcasted_iota(jnp.int32, (1, bq), 1)
    starts = first_key(ends, docs, positions)
    low = lax.div(first_key(ends, docs, i * bq), bk)
    high = lax.div((i + 1) * bq - 1, bk) + 1

    def step(j, sums):
        rows = pl.ds(pl.multiple_of(j * bk, bk), bk)
        spots = j * bk + lax.broadcasted_iota(jnp.int32, (bk, 1), 0)
        seen = (spots <= positions) & (spots >= starts)
        out = []
        for h in range(heads):
            q, g, k = query[h], grad[h], key[h, rows, :]
            scores = dot(k, q, ROWS_T)
            p = jnp.exp2(scores * (LOG2E * HD**-0.5) - total[h, 0:1, :])
            p = jnp.where(seen, p, 0.0)
            ds = (p * (dot(value[h, rows, :], g, ROWS_T) - delta[h, 0:1, :])).astype(BF16)
            dv[h, rows, :] += dot(p.astype(BF16), g)
            dk[h, rows, :] += dot(ds, q)
            out.append(sums[h] + dot(ds, k, COLS_T))
        return tuple(out)

    sums = lax.fori_loop(low, high, step, (jnp.zeros((bq, HD), F32),) * heads)
    for h in range(heads):
        dq[h] = sums[h]

    if away:

        @pl.when(i == pl.num_programs(0) - 1)
        def _():
            other = 1 - ends[docs]
            away[0][0] = dk[other].astype(BF16)
            away[0][1] = dv[other].astype(BF16)


def attend_back(query, grad, total, delta, key, value, ends, shared, bq=256, bk=512):
    heads, length, _ = query.shape
    docs = ends.shape[0] - 1
    block = pl.BlockSpec((heads, bq, HD), lambda i, e: (0, i, 0))
    line = pl.BlockSpec((heads, 8, bq), lambda i, e: (0, 0, i))
    keys = once((heads, length, HD), lambda i, e: (0, 0, 0))
    out = jax.ShapeDtypeStruct((heads, length, HD), F32)
    return pl.pallas_call(
        functools.partial(attend_back_kernel, docs, heads, bq, bk),
        grid_spec=pltpu.PrefetchScalarGridSpec(
            num_scalar_prefetch=1,
            grid=(length // bq,),
            in_specs=[block, block, line, line, keys, keys],
            out_specs=[block, keys, keys] + [whole((2, length, HD))] * shared,
        ),
        out_shape=[out, out, out] + [jax.ShapeDtypeStruct((2, length, HD), BF16)] * shared,
        compiler_params=params(24),
        cost_estimate=cost(17),
        name="attend_back",
    )(ends, query, grad, total, delta, key, value)


def branch_kernel(hpd, table, mixed, w, theirs, mine):
    def body(out):
        total = None
        for j in range(hpd):
            part = dot(mixed[j].astype(BF16), w[j * HD : (j + 1) * HD, :])
            total = part if total is None else total + part
        out[0] = total.astype(BF16)

    split_pairs(pl.program_id(0), body, theirs, mine)


def branch(k, mixed, w, table, count):
    hpd = mixed.shape[0]
    width = w.shape[1]
    pair = jax.ShapeDtypeStruct((2, count, width), BF16)
    theirs, mine = pl.pallas_call(
        functools.partial(branch_kernel, hpd),
        grid_spec=pltpu.PrefetchScalarGridSpec(
            num_scalar_prefetch=1,
            grid=(4,),
            in_specs=[
                pl.BlockSpec((hpd, count, HD), lambda i, t: (0, t[4 * k + (i ^ 2)], 0)),
                whole((hpd * HD, width)),
            ],
            out_specs=[first_pair((count, width)), last_pair((count, width))],
        ),
        out_shape=[pair, pair],
        compiler_params=params(10),
        cost_estimate=cost(2.4),
        name="branch",
    )(table, mixed, w)
    return mine, theirs


def branch_back_kernel(k, hpd, meta, g0, g1, g2, g3, mixed, w, *refs):
    grad, delta, dw = refs[-3:]
    pieces = (g0, g1, g2, g3)
    count = g0.shape[0]
    g = jnp.concatenate([piece[...] for piece in pieces], axis=0)
    back = dot(g, w[...], ROWS_T).astype(BF16)
    for j in range(hpd):
        heads = []
        for i in range(4):
            at = span(meta, k, i, count)
            own = back[i * count : (i + 1) * count, j * HD : (j + 1) * HD]
            out = mixed[j, at, :]
            grad[j, at, :] = own
            delta[j, :, at] = row_sums(own.astype(F32) * out)
            heads.append(out.astype(BF16))
        part = dot(jnp.concatenate(heads, axis=0), g, COLS_T)
        rows = slice(j * HD, (j + 1) * HD)
        dw[rows, :] = part if len(refs) == 3 else refs[0][rows, :] + part


def branch_back(k, quarter, mixed, w, table, before):
    count, width = quarter[0].shape
    hpd, length, _ = mixed.shape
    group = group_of(k)
    head_at = once((hpd, 4 * count, HD), lambda i, t: (0, group(t), 0))
    dw_at = whole((hpd * HD, width))
    grad, delta, dw = pl.pallas_call(
        functools.partial(branch_back_kernel, k, hpd),
        grid_spec=pltpu.PrefetchScalarGridSpec(
            num_scalar_prefetch=1,
            grid=(1,),
            in_specs=[whole((count, width))] * 4
            + [head_at, whole((hpd * HD, width))]
            + ([dw_at] + [pl.BlockSpec(memory_space=pl.ANY)] * 2 if before else []),
            out_specs=[
                head_at,
                once((hpd, 8, 4 * count), lambda i, t: (0, 0, group(t))),
                dw_at,
            ],
        ),
        out_shape=[
            jax.ShapeDtypeStruct((hpd, length, HD), BF16),
            jax.ShapeDtypeStruct((hpd, 8, length), F32),
            jax.ShapeDtypeStruct((hpd * HD, width), F32),
        ],
        input_output_aliases={8: 0, 9: 1} if before else {},
        compiler_params=params(20),
        cost_estimate=cost(6),
        name="branch_back",
    )(table, *quarter, mixed, w, *before)
    return dw, grad, delta


def experts_kernel(
    k, n_parts, width, capacity, n_exp, meta, x0, x1, x2, x3, g0, g1, g2, g3, router, *refs
):
    n = n_parts
    w_from = refs[: 3 * n]
    refs = refs[-(2 * n + 5 + 6 * n + 3 + 3) :]
    outs, (mine, theirs) = refs[: 2 * n + 3], refs[2 * n + 3 : 2 * n + 5]
    refs = refs[2 * n + 5 :]
    w_here, refs = refs[: 3 * n], refs[3 * n :]
    rows, pairs, picked, refs = refs[:n], refs[n : 2 * n], refs[2 * n : 3 * n], refs[3 * n :]
    hidden, gate_grad, up_grad, chosen_ref, gate_ref, sems = refs
    slots = 4 * capacity
    part = width // n
    c = meta[0]
    lanes = lax.broadcasted_iota(jnp.int32, (1, 128), 1)
    pieces = (x0, x1, x2, x3)
    arrivals = [
        pltpu.make_async_copy(w_from[i], w_here[i], sems.at[i]) for i in range(3 * n)
    ]
    for copy in arrivals:
        copy.start()
    here = [*rows, *pairs, hidden, gate_grad, up_grad]
    leaving = [
        pltpu.make_async_copy(
            here[i], outs[i].at[pl.ds(k * slots, slots), :], sems.at[3 * n + i]
        )
        for i in range(2 * n + 3)
    ]

    def columns(p, first=0):
        return pl.ds(pl.multiple_of(first + meta[1 + p], 128), part)

    for i, x_ref in enumerate(pieces):
        cot = (g0, g1, g2, g3)[i]
        at = slice(i * capacity, (i + 1) * capacity)
        info = x_ref[:, width:].astype(F32)
        place = jnp.sum(jnp.where(lanes == c, info, 0.0), axis=1, keepdims=True)
        spots = lax.broadcasted_iota(jnp.int32, (1, capacity), 1).astype(F32)
        chosen = (spots == place).astype(BF16)
        chosen_ref[i] = chosen
        logits = dot(x_ref[:, :width], router[...])
        seen = info > -1.5
        top = jnp.max(jnp.where(seen, logits, -1e30), axis=1, keepdims=True)
        shares = jnp.where(seen, jnp.exp(logits - top), 0.0)
        gates = shares / jnp.sum(shares, axis=1, keepdims=True)
        own = jnp.sum(jnp.where(lanes == c, gates, 0.0), axis=1, keepdims=True)
        gate = lax.dot_general(
            chosen.astype(F32),
            jnp.broadcast_to(own, gates.shape),
            COLS_T,
            precision=HIGH,
            preferred_element_type=F32,
        )
        gate_ref[at, :] = gate
        for p in range(n):
            rows[p][at, :] = dot(chosen, x_ref[:, columns(p)], COLS_T).astype(BF16)
            grads = dot(chosen, cot[:, columns(p)], COLS_T)
            picked[p][at, :] = grads.astype(BF16)
            pairs[p][at, :] = (grads * gate[:, :1]).astype(BF16)
    for copy in leaving[: 2 * n]:
        copy.start()
    for copy in arrivals[: 2 * n]:
        copy.wait()
    wg, wu, wd = (w_here[n * i : n * (i + 1)] for i in range(3))
    gate_part = sum(dot(rows[p][...], wg[p][...]) for p in range(n))
    up_part = sum(dot(rows[p][...], wu[p][...]) for p in range(n))
    sigma = jax.nn.sigmoid(gate_part)
    silu_gate = gate_part * sigma
    h = (silu_gate * up_part).astype(BF16)
    hidden[...] = h
    leaving[2 * n].start()
    for copy in arrivals[2 * n :]:
        copy.wait()
    hidden_grad = sum(dot(pairs[p][...], wd[p][...]) for p in range(n))
    gg = (hidden_grad * up_part * sigma * (1.0 + gate_part * (1.0 - sigma))).astype(BF16)
    gate_grad[...] = gg
    leaving[2 * n + 1].start()
    ug = (hidden_grad * silu_gate).astype(BF16)
    up_grad[...] = ug
    leaving[2 * n + 2].start()
    inner_sum = jnp.zeros((slots, 1), F32)
    for p in range(n):
        out = dot(h, wd[p][...], ROWS_T).astype(BF16).astype(F32)
        inner_sum += jnp.sum(out * picked[p][...].astype(F32), axis=1, keepdims=True)
        scaled = (out * gate_ref[:, :1]).astype(BF16)
        row_sum = (dot(gg, wg[p][...], ROWS_T) + dot(ug, wu[p][...], ROWS_T)).astype(BF16)
        for i in range(4):
            back = (mine, theirs)[i // 2].at[i % 2]
            at = slice(i * capacity, (i + 1) * capacity)
            back[:, columns(p)] = dot(chosen_ref[i], row_sum[at, :]).astype(BF16)
            back[:, columns(p, width + 128)] = dot(chosen_ref[i], scaled[at, :]).astype(BF16)
    high = inner_sum.astype(BF16).astype(F32)
    extra = jnp.where(lanes == c, high, 0.0) + jnp.where(
        lanes == c + n_exp, inner_sum - high, 0.0
    )
    extra = extra.astype(BF16)
    for i in range(4):
        back = (mine, theirs)[i // 2].at[i % 2]
        at = slice(i * capacity, (i + 1) * capacity)
        back[:, width : width + 128] = dot(chosen_ref[i], extra[at, :]).astype(BF16)
    for copy in leaving:
        copy.wait()


def experts(k, quarter, cots, router, wg, wu, wd, meta, capacity, n_exp, before):
    count, wide = quarter[0].shape
    nz, width = len(cots), cots[k][0].shape[1]
    n_parts = len(wg)
    part = width // n_parts
    hid = wg[0].shape[1]
    slots = 4 * capacity
    anywhere = pl.BlockSpec(memory_space=pl.ANY)
    pair = once((2, count, wide + width), lambda i, m: (0, 0, 0))
    rows_all = lambda cols: pltpu.HBM((nz * slots, cols), BF16)
    n_out = 2 * n_parts + 3
    outs = pl.pallas_call(
        functools.partial(experts_kernel, k, n_parts, width, capacity, n_exp),
        grid_spec=pltpu.PrefetchScalarGridSpec(
            num_scalar_prefetch=1,
            grid=(1,),
            in_specs=[whole((count, wide))] * 4
            + [whole((count, width))] * 4
            + [whole(router.shape)]
            + [anywhere] * (3 * n_parts)
            + [IN_HBM] * len(before),
            out_specs=[IN_HBM] * n_out + [pair, pair],
            scratch_shapes=[pltpu.VMEM((part, hid), BF16)] * (3 * n_parts)
            + [pltpu.VMEM((slots, part), BF16)] * (3 * n_parts)
            + [pltpu.VMEM((slots, hid), BF16)] * 3
            + [
                pltpu.VMEM((4, count, capacity), BF16),
                pltpu.VMEM((slots, 128), F32),
                pltpu.SemaphoreType.DMA((5 * n_parts + 3,)),
            ],
        ),
        out_shape=[rows_all(part)] * (2 * n_parts)
        + [rows_all(hid)] * 3
        + [jax.ShapeDtypeStruct((2, count, wide + width), BF16)] * 2,
        input_output_aliases={10 + 3 * n_parts + i: i for i in range(len(before))},
        compiler_params=params(42),
        cost_estimate=cost(15),
        name="experts",
    )(meta, *quarter, *cots[k], router, *wg, *wu, *wd, *before)
    return (outs[n_out], outs[n_out + 1]), outs[:n_out]


def head_back(grad, v, gain, cos, sin):
    scale = lax.rsqrt(jnp.mean(v * v, axis=-1, keepdims=True) + EPS)
    d = grad * cos - half_turn(grad) * sin
    u = d * gain
    inner = jnp.mean(u * v, axis=-1, keepdims=True)
    back = scale * u - v * (scale * scale * scale * inner)
    return back.astype(BF16), jnp.sum(d * v * scale, axis=0, keepdims=True)


def key_back_kernel(meta, dk, dv, raw, turn, gk, *refs):
    out, gains = refs[-2:]
    came = refs[:-2]
    z = pl.program_id(0)

    @pl.when(z == 0)
    def _():
        gains[...] = jnp.zeros_like(gains)

    n_kv = dk.shape[0]
    count = raw.shape[1]
    for i in range(4):
        at = pl.ds(pl.multiple_of(lax.rem(meta[4 * z + i], 4) * count, count), count)
        for j in range(n_kv):
            v = raw[i, :, j * HD : (j + 1) * HD]
            key_grad, value_grad = dk[j, at, :], dv[j, at, :]
            if came:
                key_grad = key_grad + came[0][0, at, :].astype(F32)
                value_grad = value_grad + came[0][1, at, :].astype(F32)
            grad = key_grad * HD**-0.5
            back, gain = head_back(grad, v, gk[...], *turns(turn[at, :]))
            out[i, :, j * HD : (j + 1) * HD] = back
            gains[0:1, :] += gain
            out[i, :, (n_kv + j) * HD : (n_kv + j + 1) * HD] = value_grad.astype(BF16)


def key_back(dk, dv, came, raw, turn, gk, meta):
    hpd = dk.shape[0]
    n_kv = 1 if came else hpd
    n_ctx, count, _ = raw.shape
    group = lambda z, t: lax.div(t[4 * z], 4)
    head_at = pl.BlockSpec(
        (n_kv, 4 * count, HD), lambda z, t: (t[n_ctx] if came else 0, group(z, t), 0)
    )
    turn_at = pl.BlockSpec((4 * count, HD), lambda z, t: (group(z, t), 0))
    return pl.pallas_call(
        key_back_kernel,
        grid_spec=pltpu.PrefetchScalarGridSpec(
            num_scalar_prefetch=1,
            grid=(n_ctx // 4,),
            in_specs=[
                head_at,
                head_at,
                pl.BlockSpec((4, count, n_kv * HD), lambda z, t: (z, 0, hpd // n_kv)),
                turn_at,
                whole((1, HD)),
            ]
            + [pl.BlockSpec((2, 4 * count, HD), lambda z, t: (0, group(z, t), 0))] * len(came),
            out_specs=[
                pl.BlockSpec((4, count, 2 * n_kv * HD), lambda z, t: (z, 0, 0)),
                whole((8, HD)),
            ],
        ),
        out_shape=[
            jax.ShapeDtypeStruct((n_ctx, count, 2 * n_kv * HD), BF16),
            jax.ShapeDtypeStruct((8, HD), F32),
        ],
        compiler_params=params(14),
        cost_estimate=cost(5),
        name="key_back",
    )(meta, dk, dv, raw, turn, gk, *came)


def input_back_kernel(k, hpd, meta, dq, kv, raw, scales, turn, gq, w, *refs):
    x, (grads_out, theirs, mine, gains, gain_grad, rows, grads, sem) = refs[:4], refs[-8:]
    copy = pltpu.make_async_copy(grads, grads_out.at[pl.ds(4 * k, 4)], sem)
    count = raw.shape[1]
    q_cols = hpd * HD

    @pl.when(pl.program_id(0) == 0)
    def _():
        gains[...] = jnp.zeros_like(gains)
        for i in range(4):
            at = span(meta, k, i, count)
            for j in range(hpd):
                cols = slice(j * HD, (j + 1) * HD)
                grad = dq[j, at, :] * HD**-0.5
                back, gain = head_back(grad, raw[i, :, cols], gq[...], *turns(turn[at, :]))
                grads[i, :, cols] = back
                gains[0:1, :] += gain
            rows[i * count : (i + 1) * count, :q_cols] = grads[i]
            rows[i * count : (i + 1) * count, q_cols:] = kv[i]
        copy.start()

    @pl.when(pl.program_id(0) == pl.num_programs(0) - 1)
    def _():
        copy.wait()

    back = dot(rows[...], w[...], ROWS_T)
    total = None
    for i in range(4):
        block = back[i * count : (i + 1) * count, :]
        (mine, theirs)[i // 2][i % 2] = block.astype(BF16)
        term = jnp.sum(block * x[i][...].astype(F32) * scales[i, :, :1], axis=0, keepdims=True)
        total = term if total is None else total + term
    gain_grad[...] = jnp.broadcast_to(total, gain_grad.shape)


def input_back(k, quarter, dq, kv, raw, scales, turn, gq, w, meta, before):
    count, width = quarter[0].shape
    hpd = dq.shape[0]
    n_ctx = raw.shape[0]
    q_cols = hpd * HD
    chunk = width // 4
    group = group_of(k)
    turn_at = pl.BlockSpec((4 * count, HD), lambda i, t: (group(t), 0))
    own = lambda cols: pl.BlockSpec((4, count, cols), lambda i, t: (k, 0, 0))
    pair_at = pl.BlockSpec((2, count, chunk), lambda i, t: (0, 0, i))
    pair = jax.ShapeDtypeStruct((2, count, width), BF16)
    outs = pl.pallas_call(
        functools.partial(input_back_kernel, k, hpd),
        grid_spec=pltpu.PrefetchScalarGridSpec(
            num_scalar_prefetch=1,
            grid=(4,),
            in_specs=[
                pl.BlockSpec((hpd, 4 * count, HD), lambda i, t: (0, group(t), 0)),
                own(kv.shape[2]),
                own(q_cols),
                own(HD),
                turn_at,
                whole((1, HD)),
                pl.BlockSpec((chunk, w.shape[1]), lambda i, t: (i, 0)),
            ]
            + [pl.BlockSpec((count, chunk), lambda i, t: (0, i))] * 4
            + [IN_HBM] * len(before),
            out_specs=[
                IN_HBM,
                pair_at,
                pair_at,
                whole((8, HD)),
                pl.BlockSpec((8, chunk), lambda i, t: (0, i)),
            ],
            scratch_shapes=[
                pltpu.VMEM((4 * count, w.shape[1]), BF16),
                pltpu.VMEM((4, count, q_cols), BF16),
                pltpu.SemaphoreType.DMA(()),
            ],
        ),
        out_shape=[
            pltpu.HBM((n_ctx, count, q_cols), BF16),
            pair,
            pair,
            jax.ShapeDtypeStruct((8, HD), F32),
            jax.ShapeDtypeStruct((8, width), F32),
        ],
        input_output_aliases={12: 0} if before else {},
        compiler_params=params(18),
        cost_estimate=cost(6),
        name="input_back",
    )(meta, dq, kv, raw, scales, turn, gq, w, *quarter, *before)
    grads, theirs, mine, gains, gain_grad = outs
    return (mine, theirs), grads, gains, gain_grad


def place_kernel(parts, n_kv, table, *refs):
    columns, keys = refs[:4], refs[4 : 4 + n_kv]
    outs = refs[-3:] if n_kv else refs[-1:]
    for n in range(4):

        @pl.when(pl.program_id(0) // parts == n)
        def _():
            outs[0][...] = columns[n][...].astype(F32)
            if n_kv:
                outs[1][...] = keys[n][:, :HD].astype(F32)
                outs[2][...] = keys[n][:, HD:].astype(F32)


def place_columns(k, quarter, table, n_ctx, rows, before):
    all_rows, cols = quarter[0].shape
    parts = cols // HD
    kv_rows = all_rows - rows

    def piece_at(n):
        return lambda i, t: (0, jnp.clip(i - n * parts, 0, parts - 1))

    def head_at(i, t):
        c = t[4 * k + i // parts]
        rows_part = lax.rem(c // 4, 2) * 2 + lax.rem(c // 2, 2)
        return rows_part, lax.rem(c, 2) * 2 + c // 8

    out_specs = [
        pl.BlockSpec((rows, HD), lambda i, t: (0, (i % parts) * n_ctx + t[4 * k + i // parts]))
    ]
    out_shape = [jax.ShapeDtypeStruct((rows, n_ctx * cols), F32)]
    in_specs = [pl.BlockSpec((rows, HD), piece_at(n)) for n in range(4)]
    pieces = list(quarter)
    if kv_rows:
        in_specs += [once((kv_rows, cols), lambda i, t: (rows // kv_rows, 0))] * 4
        pieces += quarter
        out_specs += [pl.BlockSpec((kv_rows, HD), head_at)] * 2
        out_shape += [jax.ShapeDtypeStruct((rows, KVH * HD), F32)] * 2
    return pl.pallas_call(
        functools.partial(place_kernel, parts, len(pieces) - 4),
        grid_spec=pltpu.PrefetchScalarGridSpec(
            num_scalar_prefetch=1,
            grid=(4 * parts,),
            in_specs=in_specs + [pl.BlockSpec(memory_space=pl.ANY)] * len(before),
            out_specs=out_specs,
        ),
        out_shape=out_shape,
        input_output_aliases={1 + len(pieces) + i: i for i in range(len(before))},
        compiler_params=params(12),
        cost_estimate=cost(4.6),
        name="place_columns",
    )(table, *pieces, *before)


def place_rows_kernel(table, *refs):
    out = refs[-1]
    for n in range(4):

        @pl.when(pl.program_id(0) == n)
        def _():
            out[...] = refs[n][...].astype(F32)


def place_rows(quarters, table):
    rows, cols = quarters[0][0].shape
    placed = ()
    for k, quarter in enumerate(quarters):
        placed = pl.pallas_call(
            place_rows_kernel,
            grid_spec=pltpu.PrefetchScalarGridSpec(
                num_scalar_prefetch=1,
                grid=(4,),
                in_specs=[whole((rows, cols))] * 4 + [IN_HBM] * len(placed),
                out_specs=[pl.BlockSpec((rows, cols), lambda i, t, k=k: (t[4 * k + i], 0))],
            ),
            out_shape=[pltpu.HBM((4 * len(quarters) * rows, cols), F32)],
            input_output_aliases={5: 0} if placed else {},
            compiler_params=params(10),
            cost_estimate=cost(2.4),
            name="place_rows",
        )(table, *quarter, *placed)
    return placed[0]


def local(
    inputs,
    w_query,
    w_key,
    w_value,
    w_output,
    norm_attn,
    gain_query,
    gain_key,
    w_router,
    norm_moe,
    w_gate,
    w_up,
    w_down,
    lengths,
    routes,
    pair_order,
    cotangent,
):
    n_ctx = lax.axis_size("ctx")
    n_f = lax.axis_size("fsdp")
    c = lax.axis_index("ctx")
    f = lax.axis_index("fsdp")
    count, width = inputs.shape[1], inputs.shape[2]
    length = count * n_ctx
    nz = n_ctx // 4
    later = scatter_order(n_ctx)
    hpd = H // n_ctx
    hpf = H // n_f
    group = H // KVH
    n_exp = w_router.shape[1]
    capacity = 5 * count * TOPK // (4 * n_exp)
    table = block_order(n_ctx)
    core = c % 2

    heads = [c % hpf + hpf * ((c // hpf) * hpd + j) for j in range(hpd)]
    kv_heads = [h // group for h in heads]
    columns = lambda w, h: lax.dynamic_slice_in_dim(w, h * HD, HD, 1)
    shared = n_f == 2 and hpd == 2
    if shared:
        kv_own = heads[0] // group + core * (KVH // 2)
        w_part = jnp.concatenate(
            [columns(w_query, h) for h in heads]
            + [columns(w_key, kv_own), columns(w_value, kv_own)],
            axis=1,
        )
    else:
        w_part = jnp.concatenate(
            [columns(w_query, h) for h in heads]
            + [columns(w_key, h) for h in kv_heads]
            + [columns(w_value, h) for h in kv_heads],
            axis=1,
        )
    w_part, norm_first = tie(w_part, norm_attn)
    vectors = jnp.concatenate([norm_first, gain_query, gain_key, norm_moe])
    if n_f == 2:
        vectors = joined([vectors[None], swap(vectors[None])])
        router = joined([w_router, swap(w_router)])
    else:
        vectors = lax.all_gather(vectors, "fsdp", axis=0)
        router = lax.all_gather(w_router, "fsdp", axis=0, tiled=True)
    sizes = [norm_attn.shape[0], gain_query.shape[0], gain_key.shape[0], norm_moe.shape[0]]
    rows_of, at = [], 0
    for size in sizes:
        rows_of.append(vectors[:, at : at + size].reshape(1, n_f * size).astype(F32))
        at += size
    attn_gain, query_gain, key_gain, moe_gain = rows_of
    router_wide = jnp.pad(router, ((0, 0), (0, 128 - n_exp)))
    offsets = part_offsets(width)
    n_parts = len(offsets)
    meta_rows = jnp.concatenate([table, jnp.stack([core] + offsets).astype(jnp.int32)])
    q_cols = hpd * HD
    block = w_gate.shape[2] // 3
    weights = {}

    def fetch_weights():
        parts = yield from fetch(w_part, 2)
        weights["qkv"], weights["beside"] = parts, []
        if shared:
            weights["beside"] = [
                lax.ppermute(part[:, q_cols:], "ctx", flip(n_ctx, 1)) for part in parts
            ]
        weights["back"] = joined(parts)
        own_rows = lax.dynamic_slice_in_dim(w_output, (c % hpf) * HD, HD, 0)
        rows_parts = yield from fetch(own_rows)
        last = rows_parts[-1]
        w_out = joined(rows_parts)
        weights["out"] = lax.dynamic_slice_in_dim(w_out, (c // hpf) * hpd * HD, hpd * HD, 0)
        weights["gate"], last = yield from fetch_thirds(w_gate[0], last)
        weights["up"], last = yield from fetch_thirds(w_up[0], last, 2)
        weights["down"], last = yield from fetch_thirds(w_down[0], last)

    gathered = {}

    def gather_cotangents():
        (cot,) = yield (cotangent[0],), 3
        gathered["cot"] = yield from gather_planned(cot, n_ctx, COTANGENT_PLAN)

    sides = [Side(fetch_weights()), Side(gather_cotangents())]

    experts_of = jnp.arange(n_exp, dtype=jnp.int32)
    picks = routes[0][:, :, None] == experts_of
    ranks = jnp.sum(
        jnp.where(picks, pair_order[0, 0].reshape(count, TOPK, 1), 0), axis=1
    )
    chosen = jnp.any(picks, axis=1)
    ranks = jnp.where(chosen, ranks, count * TOPK)
    place = jnp.sum((ranks[None, :, :] < ranks[:, None, :]).astype(jnp.int32), axis=1)
    place = jnp.where(chosen, jnp.where(place < capacity, place, -1), -2)
    place = jnp.pad(place, ((0, 0), (0, 128 - n_exp)), constant_values=-2).astype(BF16)

    ends = jnp.cumsum(lengths[0]).astype(jnp.int32)
    turn = rotary_table(length)

    xs = {}

    def through_projection(k, quarter, token, before):
        xs[k] = quarter
        if k == 0:
            return ()
        if k == 1:
            before = projection(0, token, ())
        return projection(k, token, before)

    def projection(k, token, before):
        return project(
            k,
            xs[k],
            weights["qkv"],
            weights["beside"],
            attn_gain,
            query_gain,
            key_gain,
            turn,
            token,
            hpd,
            n_ctx,
            before,
        )

    straight = list(range(nz))
    *normed, raw, scales, query, key, value = pipeline(
        n_ctx, straight, through_projection, meta_rows, sides, piece=inputs[0]
    )
    _, (query,) = land({}, sides, query)
    mixed, log_total = attend(query, key, value, ends)
    _, (mixed,) = land({}, sides, mixed)
    x = inputs[0].astype(F32)
    branch_sum, _, _ = pipeline(
        n_ctx,
        later,
        lambda k, _, token, state: (branch(k, mixed, weights["out"], token, count), state),
        table,
        sides,
        scatter=True,
    )
    middle = x + branch_sum
    moe_scale = lax.rsqrt(jnp.mean(middle * middle, axis=-1, keepdims=True) + EPS)
    routed_in = (middle * moe_scale * moe_gain).astype(BF16)

    pad_offsets = (offsets + [jnp.int32(0)])[:2]
    head_meta = [jnp.stack([c] + pad_offsets).astype(jnp.int32)]
    expert_meta = jnp.concatenate(head_meta)

    def through_experts(k, quarter, token, before):
        return experts(
            k,
            quarter,
            gathered["cot"],
            router_wide,
            weights["gate"],
            weights["up"],
            weights["down"],
            token,
            capacity,
            n_exp,
            before,
        )

    routed_grad, seen, _ = pipeline(
        n_ctx,
        later,
        through_experts,
        expert_meta,
        sides,
        piece=jnp.concatenate([routed_in, place], axis=1),
        scatter=True,
        along=True,
    )
    rows, pairs = seen[:n_parts], seen[n_parts : 2 * n_parts]
    hidden, gate_part_grad, up_part_grad = seen[2 * n_parts :]
    outputs = (middle + routed_grad[:, width + 128 :]).astype(BF16)

    gate_grad = routed_grad[:, width : width + n_exp] + routed_grad[
        :, width + n_exp : width + 2 * n_exp
    ]
    routed_grad = routed_grad[:, :width]
    logits = dot(routed_in, router)
    top = jnp.max(jnp.where(chosen, logits, -1e30), axis=-1, keepdims=True)
    shares = jnp.where(chosen, jnp.exp(logits - top), 0.0)
    gates = shares / jnp.sum(shares, axis=-1, keepdims=True)
    logit_grad = gates * (gate_grad - jnp.sum(gates * gate_grad, axis=-1, keepdims=True))
    routed_grad = routed_grad + lax.dot_general(
        logit_grad, router.astype(F32), ROWS_T, precision=HIGH
    )
    router_part = lax.dot_general(
        logit_grad, routed_in.astype(F32), COLS_T, precision=HIGH
    )

    grad_out = cotangent[0].astype(F32)
    moe_scaled = routed_grad * moe_gain
    moe_part = jnp.sum(routed_grad * middle * moe_scale, axis=0, keepdims=True)
    middle_grad = (
        grad_out
        + moe_scale * moe_scaled
        - middle
        * (
            moe_scale
            * moe_scale
            * moe_scale
            * jnp.mean(moe_scaled * middle, axis=-1, keepdims=True)
        )
    )

    grads, sums = {}, []

    def scatter_grads():
        pairs_of = [(rows, gate_part_grad), (rows, up_part_grad), (pairs, hidden)]
        sums_of = yield from scatter_products(pairs_of, block, (1, 1, 1, 1, 1, 2, 2, 1, 1))
        grads["gate"], grads["up"], grads["down"] = sums_of

    sides = [
        Side(scatter_grads()),
        Side(sum_all(jnp.concatenate([router_part, moe_part], axis=0), sums)),
    ]
    grad_out_w, mixed_grad, delta = pipeline(
        n_ctx,
        straight,
        lambda k, quarter, token, before: branch_back(
            k, quarter, mixed, weights["out"], token, before
        ),
        table,
        sides,
        piece=middle_grad.astype(BF16),
    )
    def sum_out_grad():
        if n_f == hpd:
            placed = grad_out_w
        else:
            spread_out = jnp.arange(n_f, dtype=jnp.int32)[:, None] == (
                (c // hpf) * hpd + jnp.arange(hpd, dtype=jnp.int32)[None, :]
            )
            placed = jnp.einsum(
                "fj,jrd->frd", spread_out.astype(F32), grad_out_w.reshape(hpd, HD, width)
            ).reshape(n_f * HD, width)
        own = yield from scatter_rows(placed)
        own = own.astype(BF16)
        if n_ctx == hpf:
            grads["out"] = place_rows(
                (yield from gather_planned(own, n_ctx, OUTPUT_GRAD_PLAN)), table
            )
        else:
            whole_grad = lax.all_gather(own, "ctx", axis=0).reshape(-1, hpf * HD, width)
            mine = lax.dynamic_index_in_dim(whole_grad, f // hpd, 0, keepdims=False)
            grads["out"] = mine.astype(F32)

    sides.append(Side(sum_out_grad()))
    ends_and_core = jnp.concatenate([ends, core[None].astype(jnp.int32)])
    dq, dk, dv, *away = attend_back(
        query, mixed_grad, log_total, delta, key, value, ends_and_core, int(shared)
    )
    _, (dq, dk, dv, *away) = land({}, sides, dq, dk, dv, *away)
    came = [lax.ppermute(array, "ctx", flip(n_ctx, 1)) for array in away]
    kv_grad, key_gains = key_back(dk, dv, came, raw, turn, key_gain, meta_rows)
    normed_flat = [n.reshape(length, -1) for n in normed]

    def sum_key_grads():
        (grad_kv,) = yield from scatter_products(
            [(normed_flat, kv_grad.reshape(length, -1))], kv_grad.shape[-1]
        )
        if not shared:
            slots_kv = jnp.arange(KVH, dtype=jnp.int32)
            spread = jnp.stack([slots_kv == h for h in kv_heads]).astype(F32)
            grad_kv = grad_kv.reshape(width // n_f, 2, hpd, 1, HD) * spread[None, None, :, :, None]
            grad_kv = jnp.sum(grad_kv, axis=2).reshape(width // n_f, 2 * KVH * HD)
            grad_kv = lax.psum(grad_kv.astype(BF16), "ctx").astype(F32)
            grads["key"], grads["value"] = grad_kv[:, : KVH * HD], grad_kv[:, KVH * HD :]
            return
        for bit in (4, 2):
            rows_kept = grad_kv.shape[0] // 2
            side = (c // bit) % 2
            kept = lax.dynamic_slice_in_dim(grad_kv, side * rows_kept, rows_kept, 0)
            gone = lax.dynamic_slice_in_dim(grad_kv, (1 - side) * rows_kept, rows_kept, 0)
            (got,) = yield (lax.ppermute(gone.astype(BF16), "ctx", flip(n_ctx, bit)),), 1
            grad_kv = kept + got.astype(F32)
        grads["key_piece"] = grad_kv.astype(BF16)

    sides.append(Side(sum_key_grads()))
    gain_parts, attn_parts = [], []

    def through_inputs(k, _, token, before):
        back, q_grad, gains, gain_grad = input_back(
            k,
            xs[k],
            dq,
            kv_grad,
            raw,
            scales,
            turn,
            query_gain,
            weights["back"],
            token,
            before,
        )
        gain_parts.append(gains)
        attn_parts.append(gain_grad)
        if len(gain_parts) == nz:
            gain_rows = jnp.concatenate([sum(gain_parts)[:1], key_gains[:1]], axis=1)
            gain_rows = jnp.pad(gain_rows, ((0, 0), (0, width - 2 * HD)))
            rows_last = [sum(attn_parts)[:1], gain_rows]
            sides.append(Side(sum_all(jnp.concatenate(rows_last, axis=0), sums)))
        return back, (q_grad,)

    q_grads = []

    def query_weights(token):
        q_flat = q_grads[0].reshape(length, -1)
        if n_f != 2:
            return (
                lax.psum_scatter(
                    dot(normed_flat[0], q_flat, COLS_T).astype(BF16),
                    "fsdp",
                    scatter_dimension=0,
                    tiled=True,
                ),
            )
        mine, other = normed_flat
        came = swap(dot(other, q_flat, COLS_T).astype(BF16))
        return dot(mine, q_flat, COLS_T), came

    def through_inputs_last(k, quarter, token, before):
        back, state = through_inputs(k, quarter, token, before)
        q_grads[:] = state
        return back, state

    normed_grad, _, grad_q = pipeline(
        n_ctx, later, through_inputs_last, meta_rows, sides, scatter=True, closing=query_weights
    )
    for side in sides[3:4]:
        side.finish()
    grad_q = sum(g.astype(F32) for g in grad_q).astype(BF16)
    q_rows = grad_q.shape[0]
    if shared:
        grad_q = jnp.concatenate([grad_q, grads["key_piece"]], axis=0)

    if n_ctx == hpf:
        placed = pipeline(
            n_ctx,
            straight,
            lambda k, quarter, token, before: place_columns(
                k, quarter, token, n_ctx, q_rows, before
            ),
            table,
            sides,
            piece=grad_q,
        )
        grad_w_query = placed[0]
        if shared:
            grads["key"], grads["value"] = placed[1:]
    else:
        grad_w_query = (
            lax.all_gather(grad_q, "ctx", axis=0)
            .reshape(n_ctx // hpf, hpf, width // n_f, hpd, HD)
            .transpose(2, 0, 3, 1, 4)
            .reshape(width // n_f, H * HD)
            .astype(F32)
        )
    for side in sides:
        side.finish()
    early, late = sums
    own_part = lambda v, size: lax.dynamic_slice_in_dim(v, f * (size // n_f), size // n_f, 0)
    grad_w_router = own_part(early[:n_exp].T, width)
    grad_norm_moe = own_part(early[n_exp], width)
    grad_norm_attn = own_part(late[0], width)
    grad_gain_query = own_part(late[1, :HD], HD)
    grad_gain_key = own_part(late[1, HD : 2 * HD], HD)

    attn_scale = lax.rsqrt(jnp.mean(x * x, axis=-1, keepdims=True) + EPS)
    attn_scaled = normed_grad * attn_gain
    input_grad = (
        middle_grad
        + attn_scale * attn_scaled
        - x
        * (
            attn_scale
            * attn_scale
            * attn_scale
            * jnp.mean(attn_scaled * x, axis=-1, keepdims=True)
        )
    )
    return (
        outputs[None],
        input_grad.astype(BF16)[None],
        grad_w_query,
        grads["key"],
        grads["value"],
        grads["out"],
        grad_norm_attn,
        grad_gain_query,
        grad_gain_key,
        grad_w_router,
        grad_norm_moe,
        grads["gate"][None],
        grads["up"][None],
        grads["down"][None],
    )


def solution(mesh):
    in_specs = (
        P("fsdp", "ctx", None),
        P("fsdp", None),
        P("fsdp", None),
        P("fsdp", None),
        P("fsdp", None),
        P("fsdp"),
        P("fsdp"),
        P("fsdp"),
        P("fsdp", None),
        P("fsdp"),
        P("ctx", "fsdp", None),
        P("ctx", "fsdp", None),
        P("ctx", "fsdp", None),
        P("fsdp", None),
        P("fsdp", "ctx", None),
        P("fsdp", "ctx", None),
        P("fsdp", "ctx", None),
    )
    out_specs = (
        P("fsdp", "ctx", None),
        P("fsdp", "ctx", None),
        P("fsdp", None),
        P("fsdp", None),
        P("fsdp", None),
        P("fsdp", None),
        P("fsdp"),
        P("fsdp"),
        P("fsdp"),
        P("fsdp", None),
        P("fsdp"),
        P("ctx", "fsdp", None),
        P("ctx", "fsdp", None),
        P("ctx", "fsdp", None),
    )
    return jax.shard_map(local, mesh=mesh, in_specs=in_specs, out_specs=out_specs, check_vma=False)
```

```python
import functools

import jax
import jax.numpy as jnp
from jax import lax
from jax.experimental import pallas as pl
from jax.experimental.pallas import tpu as pltpu
from jax.sharding import PartitionSpec as P

H = 32
KVH = 4
HD = 128
TOPK = 8
EPS = 1e-06
THETA = 1000000.0
HIGH = lax.Precision.HIGHEST
LOG2E = 1.4426950408889634
F32 = jnp.float32
BF16 = jnp.bfloat16
ROWS_T = (((1,), (1,)), ((), ()))
COLS_T = (((0,), (0,)), ((), ()))


def dot(a, b, dims=(((1,), (0,)), ((), ()))):
    return lax.dot_general(a, b, dims, preferred_element_type=F32)


def params(mebibytes):
    return pltpu.CompilerParams(vmem_limit_bytes=mebibytes * 1024 * 1024)


def once(shape, index):
    return pl.BlockSpec(shape, index, pipeline_mode=pl.Buffered(1))


def cost(microseconds):
    return pl.CostEstimate(
        flops=int(microseconds * 1.15e9), bytes_accessed=0, transcendentals=0
    )


def flip(n_ctx, bit):
    return [(i, i ^ bit) for i in range(n_ctx)]


def ring(n_ctx, step):
    return [(i, (i + step) % n_ctx) for i in range(n_ctx)]


def block_order(n_ctx):
    c = lax.axis_index("ctx")
    nz = n_ctx // 4
    z, x, core = c // 4, (c // 2) % 2, c % 2
    table = []
    for k in range(nz):
        for dc in range(2):
            for dx in range(2):
                table.append(lax.rem(z + nz - k, nz) * 4 + (x ^ dx) * 2 + (core ^ dc))
    return jnp.stack(table).astype(jnp.int32)


def tie(*arrays):
    return lax.optimization_barrier(arrays)


class Side:
    def __init__(self, chain):
        self.chain, self.flying, self.left = chain, None, 0
        self.resume(None)

    def resume(self, landed):
        try:
            self.flying, self.left = self.chain.send(landed)
        except StopIteration:
            self.flying = None

    def finish(self):
        while self.flying is not None:
            self.resume(self.flying)


def land(air, sides, *others):
    due = [side for side in sides if side.flying is not None and side.left <= 1]
    for side in sides:
        side.left -= 1
    keys = list(air)
    flying = [array for side in due for array in side.flying]
    arrays = list(tie(*air.values(), *flying, *others))
    air.clear()
    landed = {key: arrays.pop(0) for key in keys}
    for side in due:
        side.resume([arrays.pop(0) for _ in side.flying])
    return landed, arrays


def pipeline(
    n_ctx, order, compute, token, sides, piece=None, scatter=False, closing=None, along=False
):
    nz = n_ctx // 4
    air, have, state = {}, {}, ()

    def send(key, array, pairs):
        air[key] = lax.ppermute(array, "ctx", pairs)

    def bring(k):
        if along and k + 1 == nz:
            send(("beside", k), have["beside", k - 1], ring(n_ctx, 4))
        else:
            send(("beside", k), have["piece", k], flip(n_ctx, 2))
        if k + 1 < nz:
            send(("piece", k + 1), have["piece", k], ring(n_ctx, 4))

    def step_ends(*others):
        landed, others = land(air, sides, *others)
        have.update(landed)
        return others

    def total_of(own):
        parts = [*own, have["away"]] + ([have["carry"]] if "carry" in have else [])
        return sum(part.astype(F32) for part in parts)

    def give(blocks, token):
        mine, theirs = blocks
        arrived = lax.ppermute(theirs, "ctx", flip(n_ctx, 1))
        away = (mine[1].astype(F32) + arrived[1].astype(F32)).astype(BF16)
        token, away = tie(token, away)
        send("away", away, flip(n_ctx, 2))
        return (mine[0], arrived[0]), token

    if piece is not None:
        have["piece", 0] = piece
        for k in range(order[0] + 1):
            bring(k)
            step_ends()
    blocks = own = None
    for s, k in enumerate(order):
        following = order[s + 1 :][:1]
        quarter = None
        if piece is not None:
            for later in following:
                if ("beside", later) not in have:
                    bring(later)
            pair = [have["piece", k], have["beside", k]]
            quarter = pair + [lax.ppermute(array, "ctx", flip(n_ctx, 1)) for array in pair]
        if not scatter:
            state = compute(k, quarter, token, state)
            if following:
                token, *state = step_ends(token, *state)
            continue
        if own is not None:
            send("carry", total_of(own).astype(BF16), ring(n_ctx, 4))
        if blocks is not None:
            own, token = give(blocks, token)
        blocks, state = compute(k, quarter, token, state)
        extra = closing[0]() if closing and not following else ()
        if piece is not None and s < 2:
            token, *blocks = step_ends(token, *blocks)
        else:
            mine, theirs = blocks
            token, mine, *extra = step_ends(token, mine, *extra)
            blocks = mine, theirs
        if extra:
            closing[1](*extra)
    if not scatter:
        return tuple(state)
    send("carry", total_of(own).astype(BF16), ring(n_ctx, 4))
    own, token = give(blocks, token)
    step_ends()
    return total_of(own), state


def gather_planned(piece, n_ctx, plan, arrays):
    arrays["along", 0] = piece
    source = lambda kind, k: ("along", k) if kind == "across" else (kind, k - 1)
    for i, (items, steps) in enumerate(plan):
        going = [
            lax.ppermute(
                arrays[source(*item)], "ctx", flip(n_ctx, 2) if item[0] == "across" else ring(n_ctx, 4)
            )
            for item in items
        ]
        later = {source(*item) for item in plan[i + 1][0]} if i + 1 < len(plan) else set()
        tied = sorted(key for key in later if key in arrays)
        came = list((yield (*going, *(arrays[key] for key in tied)), steps))
        for kind, k in items:
            arrays["along" if kind == "along" else "beside", k] = came.pop(0)
        arrays.update(zip(tied, came))


def planned_quarter(arrays, k, n_ctx):
    pair = [arrays["along", k], arrays["beside", k]]
    return pair + [lax.ppermute(array, "ctx", flip(n_ctx, 1)) for array in pair]


COTANGENT_PLAN = [
    ([("along", 1)], 1),
    ([("along", 2), ("across", 0), ("across", 1)], 1),
    ([("beside", 2)], 2),
    ([("along", 3)], 6),
    ([("beside", 3)], 1),
]
QUERY_GRAD_PLAN = [
    ([("along", 1), ("across", 0)], 1),
    ([("along", 2), ("across", 1)], 1),
    ([("along", 3), ("across", 2)], 1),
    ([("across", 3)], 1),
]
OUTPUT_GRAD_PLAN = [
    ([("along", 1), ("across", 0)], 1),
    ([("along", 2), ("across", 1)], 1),
    ([("along", 3), ("across", 2)], 1),
    ([("across", 3)], 1),
]


def scatter_order(n_ctx):
    return list(range(1, n_ctx // 4)) + [0]


def sum_all(values, result):
    n_ctx = lax.axis_size("ctx")
    bit = 1
    while bit < n_ctx:
        (came,) = yield (lax.ppermute(values.astype(BF16), "ctx", flip(n_ctx, bit)),), 1
        values = values + came.astype(F32)
        bit *= 2
    if lax.axis_size("fsdp") == 2:
        (came,) = yield (swap(values.astype(BF16)),), 1
        values = values + came.astype(F32)
    else:
        values = lax.psum(values, "fsdp")
    result.append(values)


SWAP = [(0, 1), (1, 0)]


def swap(part):
    return lax.ppermute(part, "fsdp", SWAP)


def fetch(part, steps=1):
    if lax.axis_size("fsdp") != 2:
        return [lax.all_gather(part, "fsdp", axis=0, tiled=True)]
    (other,) = yield (swap(part),), steps
    return [part, other]


def fetch_after(part, after, steps):
    if lax.axis_size("fsdp") != 2:
        return [lax.all_gather(part, "fsdp", axis=0, tiled=True)], after
    after, sent = tie(after, part)
    (after,) = yield (swap(sent),), steps
    return [part, after], after


def joined(parts):
    if len(parts) == 1:
        return parts[0]
    mine, other = parts
    first = lax.axis_index("fsdp") == 0
    return jnp.concatenate([jnp.where(first, mine, other), jnp.where(first, other, mine)], axis=0)


def part_offsets(width):
    if lax.axis_size("fsdp") != 2:
        return [jnp.int32(0)]
    f = lax.axis_index("fsdp")
    return [f * (width // 2), (1 - f) * (width // 2)]


def scatter_products(pairs, block, steps=(), pause=()):
    if lax.axis_size("fsdp") != 2:
        full = [dot(left[0], right, COLS_T).astype(BF16) for left, right in pairs]
        return [
            lax.psum_scatter(g, "fsdp", scatter_dimension=0, tiled=True).astype(F32) for g in full
        ]
    work = []
    for left, right in pairs:
        step = min(block, right.shape[1])
        work += [(left, right[:, at : at + step]) for at in range(0, right.shape[1], step)]
    product = lambda i, part: dot(work[i][0][part], work[i][1], COLS_T)
    done, sent = [], product(0, 1).astype(BF16)
    for i in range(len(work)):
        ahead = [product(i + 1, 1).astype(BF16)] if i + 1 < len(work) else []
        fresh = [product(i - 1, 0) + came.astype(F32)] if i > 0 else []
        if i in pause:
            (sent,) = yield (sent,), pause[i]
        came, *worked = yield (swap(sent), *ahead, *fresh), steps[i] if steps else 1
        if ahead:
            sent = worked.pop(0)
        done += worked
    done.append(product(len(work) - 1, 0) + came.astype(F32))
    sums = []
    for _, right in pairs:
        count = max(1, right.shape[1] // block)
        sums.append(done[0] if count == 1 else jnp.concatenate(done[:count], axis=1))
        done = done[count:]
    return sums


def scatter_rows(full):
    if lax.axis_size("fsdp") != 2:
        return lax.psum_scatter(
            full.astype(BF16), "fsdp", scatter_dimension=0, tiled=True
        ).astype(F32)
    rows = full.shape[0] // 2
    first = lax.axis_index("fsdp") == 0
    low, high = full[:rows], full[rows:]
    (came,) = yield (swap(jnp.where(first, high, low).astype(BF16)),), 1
    return jnp.where(first, low, high) + came.astype(F32)


def group_of(k):
    return lambda t: lax.div(t[4 * k], 4)


def span(t, k, i, count):
    return pl.ds(pl.multiple_of(lax.rem(t[4 * k + i], 4) * count, count), count)


IN_HBM = pl.BlockSpec(memory_space=pltpu.HBM)


def whole(shape):
    return once(shape, lambda *_: (0,) * len(shape))


def first_pair(shape):
    return pl.BlockSpec((1,) + shape, lambda i, t: (jnp.minimum(i, 1),) + (0,) * len(shape))


def last_pair(shape):
    return pl.BlockSpec((1,) + shape, lambda i, t: (jnp.maximum(i - 2, 0),) + (0,) * len(shape))


def split_pairs(i, body, first, last):
    @pl.when(i < 2)
    def _():
        body(first)

    @pl.when(i >= 2)
    def _():
        body(last)


def rotary_table(length):
    half = HD // 2
    steps = jnp.arange(half, dtype=jnp.int32).astype(F32)
    inverse = jnp.exp(steps * (-2.0 * jnp.log(THETA) / HD))
    angles = jnp.arange(length, dtype=jnp.int32).astype(F32)[:, None] * inverse[None, :]
    return jnp.concatenate([jnp.cos(angles), jnp.sin(angles)], axis=1)


def turns(table):
    other = pltpu.roll(table, HD // 2, 1)
    first = lax.broadcasted_iota(jnp.int32, (1, HD), 1) < HD // 2
    return jnp.where(first, table, other), jnp.where(first, -other, table)


def half_turn(v):
    return pltpu.roll(v, HD // 2, 1)


def head_norm(v, gain):
    scale = lax.rsqrt(jnp.mean(v * v, axis=-1, keepdims=True) + EPS)
    return v * scale * gain


def project_kernel(k, hpd, n_kv, n_parts, n_ctx, meta, x0, x1, x2, x3, gain, gq, gk, turn, *refs):
    n_outs = n_parts + 5
    w, beside = refs[:n_parts], refs[n_parts : 2 * n_parts] if n_kv < hpd else ()
    outs, refs = refs[-(2 * n_outs + 2) : -(n_outs + 2)], refs[-(n_outs + 2) :]
    here, rows, sems = refs[:n_outs], refs[-2], refs[-1]
    normed, (raw, scales, query, key, value) = here[:n_parts], here[n_parts:]
    count = x0.shape[0]
    group = pl.ds(pl.multiple_of(lax.div(meta[4 * k], 4) * 4 * count, count), 4 * count)
    places = [pl.ds(4 * k, 4)] * (n_parts + 2) + [(slice(None), group)] * 3
    leaving = [
        pltpu.make_async_copy(here[i], outs[i].at[places[i]], sems.at[i]) for i in range(n_outs)
    ]
    for i, piece in enumerate((x0, x1, x2, x3)):
        x = piece[...].astype(F32)
        r1 = lax.rsqrt(jnp.mean(x * x, axis=-1, keepdims=True) + EPS)
        scales[i] = jnp.broadcast_to(r1, scales.shape[1:])
        rows[i * count : (i + 1) * count, :] = (x * r1 * gain[...]).astype(BF16)
        for p, part in enumerate(normed):
            at = pl.ds(pl.multiple_of(meta[n_ctx + 1 + p], 128), part.shape[2])
            part[i] = rows[i * count : (i + 1) * count, at]
    for copy in leaving[:n_parts]:
        copy.start()
    parts = [part[...].reshape(4 * count, part.shape[2]) for part in normed]
    out = sum(dot(n, w_p[...]) for n, w_p in zip(parts, w))
    other = sum(dot(n, w_p[...]) for n, w_p in zip(parts, beside)) if beside else None
    core = meta[n_ctx]
    for i in range(4):
        at = span(meta, k, i, count)
        cos, sin = turns(turn[at, :])
        block = out[i * count : (i + 1) * count, :]
        raw[i] = block[:, : (hpd + n_kv) * HD]

        def turned(v, gain):
            v = head_norm(v, gain[...])
            return (v * cos + half_turn(v) * sin).astype(BF16)

        for j in range(hpd):
            query[j, at, :] = turned(block[:, j * HD : (j + 1) * HD], gq)
        for j in range(n_kv):
            v = block[:, (hpd + j) * HD : (hpd + j + 1) * HD]
            u = block[:, (hpd + n_kv + j) * HD : (hpd + n_kv + j + 1) * HD]
            head = core if beside else j
            key[head, at, :] = turned(v, gk)
            value[head, at, :] = u.astype(BF16)
        if beside:
            block = other[i * count : (i + 1) * count, :]
            key[1 - core, at, :] = turned(block[:, :HD], gk)
            value[1 - core, at, :] = block[:, HD:].astype(BF16)
    for copy in leaving[n_parts:]:
        copy.start()
    for copy in leaving:
        copy.wait()


def project(k, quarter, w, beside, gain, gq, gk, turn, meta, hpd, n_ctx, before):
    count, width = quarter[0].shape
    length = n_ctx * count
    n_parts = len(w)
    n_kv = 1 if beside else hpd
    group = group_of(k)
    turn_at = once((4 * count, HD), lambda i, t: (group(t), 0))
    head = pltpu.HBM((hpd, length, HD), BF16)
    cols = (hpd + n_kv) * HD
    weights = [*w, *beside]
    return pl.pallas_call(
        functools.partial(project_kernel, k, hpd, n_kv, n_parts, n_ctx),
        grid_spec=pltpu.PrefetchScalarGridSpec(
            num_scalar_prefetch=1,
            grid=(1,),
            in_specs=[whole((count, width))] * 4
            + [whole((1, width)), whole((1, HD)), whole((1, HD)), turn_at]
            + [whole(array.shape) for array in weights]
            + [IN_HBM] * len(before),
            out_specs=[IN_HBM] * (n_parts + 5),
            scratch_shapes=[pltpu.VMEM((4, count, width // n_parts), BF16)] * n_parts
            + [pltpu.VMEM((4, count, cols), F32), pltpu.VMEM((4, count, HD), F32)]
            + [pltpu.VMEM((hpd, 4 * count, HD), BF16)] * 3
            + [pltpu.VMEM((4 * count, width), BF16), pltpu.SemaphoreType.DMA((n_parts + 5,))],
        ),
        out_shape=[pltpu.HBM((n_ctx, count, width // n_parts), BF16)] * n_parts
        + [
            pltpu.HBM((n_ctx, count, cols), F32),
            pltpu.HBM((n_ctx, count, HD), F32),
            head,
            head,
            head,
        ],
        input_output_aliases={9 + len(weights) + i: i for i in range(len(before))},
        compiler_params=params(18),
        cost_estimate=cost(6),
        name="project",
    )(meta, *quarter, gain, gq, gk, turn, *weights, *before)


def first_key(ends, docs, position):
    start = jnp.zeros_like(position)
    for d in range(docs):
        start = jnp.where(position >= ends[d], jnp.maximum(start, ends[d]), start)
    return start


def attend_kernel(docs, heads, bq, bk, ends, query, key, value, mixed, total):
    i = pl.program_id(0)
    positions = i * bq + lax.broadcasted_iota(jnp.int32, (bq, 1), 0)
    starts = first_key(ends, docs, positions)
    low = lax.div(first_key(ends, docs, i * bq), bk)
    high = lax.div((i + 1) * bq - 1, bk) + 1

    def step(j, carry):
        rows = pl.ds(pl.multiple_of(j * bk, bk), bk)
        spots = j * bk + lax.broadcasted_iota(jnp.int32, (1, bk), 1)
        seen = (spots <= positions) & (spots >= starts)
        sums = []
        for h, (acc, norm) in enumerate(carry):
            scores = dot(query[h], key[h, rows, :], ROWS_T)
            p = jnp.where(seen, jnp.exp2(scores * (LOG2E * HD**-0.5)), 0.0)
            acc = acc + dot(p.astype(BF16), value[h, rows, :])
            sums.append((acc, norm + jnp.sum(p, axis=-1, keepdims=True)))
        return tuple(sums)

    start = (jnp.zeros((bq, HD), F32), jnp.zeros((bq, 1), F32))
    first_lane = lax.broadcasted_iota(jnp.int32, (1, HD), 1) == 0
    for h, (acc, norm) in enumerate(lax.fori_loop(low, high, step, (start,) * heads)):
        mixed[h] = acc / norm
        column = jnp.where(first_lane, jnp.log2(norm), 0.0)
        total[h] = row_sums(column)


def row_sums(values):
    return lax.dot_general(
        jnp.ones((8, values.shape[1]), F32),
        values,
        ROWS_T,
        precision=HIGH,
        preferred_element_type=F32,
    )


def attend(query, key, value, ends, bq=256, bk=512):
    heads, length, _ = query.shape
    docs = ends.shape[0]
    block = pl.BlockSpec((heads, bq, HD), lambda i, e: (0, i, 0))
    keys = once((heads, length, HD), lambda i, e: (0, 0, 0))
    line = pl.BlockSpec((heads, 8, bq), lambda i, e: (0, 0, i))
    return pl.pallas_call(
        functools.partial(attend_kernel, docs, heads, bq, bk),
        grid_spec=pltpu.PrefetchScalarGridSpec(
            num_scalar_prefetch=1,
            grid=(length // bq,),
            in_specs=[block, keys, keys],
            out_specs=[block, line],
        ),
        out_shape=[
            jax.ShapeDtypeStruct((heads, length, HD), F32),
            jax.ShapeDtypeStruct((heads, 8, length), F32),
        ],
        compiler_params=params(14),
        cost_estimate=cost(12.5),
        name="attend",
    )(ends, query, key, value)


def attend_back_kernel(
    docs, heads, bq, bk, ends, query, grad, total, delta, key, value, dq, dk, dv, *away
):
    i = pl.program_id(0)

    @pl.when(i == 0)
    def _():
        dk[...] = jnp.zeros_like(dk)
        dv[...] = jnp.zeros_like(dv)

    positions = i * bq + lax.broadcasted_iota(jnp.int32, (1, bq), 1)
    starts = first_key(ends, docs, positions)
    low = lax.div(first_key(ends, docs, i * bq), bk)
    high = lax.div((i + 1) * bq - 1, bk) + 1

    def step(j, sums):
        rows = pl.ds(pl.multiple_of(j * bk, bk), bk)
        spots = j * bk + lax.broadcasted_iota(jnp.int32, (bk, 1), 0)
        seen = (spots <= positions) & (spots >= starts)
        out = []
        for h in range(heads):
            q, g, k = query[h], grad[h], key[h, rows, :]
            scores = dot(k, q, ROWS_T)
            p = jnp.exp2(scores * (LOG2E * HD**-0.5) - total[h, 0:1, :])
            p = jnp.where(seen, p, 0.0)
            ds = (p * (dot(value[h, rows, :], g, ROWS_T) - delta[h, 0:1, :])).astype(BF16)
            dv[h, rows, :] += dot(p.astype(BF16), g)
            dk[h, rows, :] += dot(ds, q)
            out.append(sums[h] + dot(ds, k, COLS_T))
        return tuple(out)

    sums = lax.fori_loop(low, high, step, (jnp.zeros((bq, HD), F32),) * heads)
    for h in range(heads):
        dq[h] = sums[h]

    if away:

        @pl.when(i == pl.num_programs(0) - 1)
        def _():
            other = 1 - ends[docs]
            away[0][0] = dk[other].astype(BF16)
            away[0][1] = dv[other].astype(BF16)


def attend_back(query, grad, total, delta, key, value, ends, shared, bq=256, bk=512):
    heads, length, _ = query.shape
    docs = ends.shape[0] - 1
    block = pl.BlockSpec((heads, bq, HD), lambda i, e: (0, i, 0))
    line = pl.BlockSpec((heads, 8, bq), lambda i, e: (0, 0, i))
    keys = once((heads, length, HD), lambda i, e: (0, 0, 0))
    out = jax.ShapeDtypeStruct((heads, length, HD), F32)
    return pl.pallas_call(
        functools.partial(attend_back_kernel, docs, heads, bq, bk),
        grid_spec=pltpu.PrefetchScalarGridSpec(
            num_scalar_prefetch=1,
            grid=(length // bq,),
            in_specs=[block, block, line, line, keys, keys],
            out_specs=[block, keys, keys] + [whole((2, length, HD))] * shared,
        ),
        out_shape=[out, out, out] + [jax.ShapeDtypeStruct((2, length, HD), BF16)] * shared,
        compiler_params=params(24),
        cost_estimate=cost(17),
        name="attend_back",
    )(ends, query, grad, total, delta, key, value)


def branch_kernel(hpd, table, mixed, w, theirs, mine):
    def body(out):
        total = None
        for j in range(hpd):
            part = dot(mixed[j].astype(BF16), w[j * HD : (j + 1) * HD, :])
            total = part if total is None else total + part
        out[0] = total.astype(BF16)

    split_pairs(pl.program_id(0), body, theirs, mine)


def branch(k, mixed, w, table, count):
    hpd = mixed.shape[0]
    width = w.shape[1]
    pair = jax.ShapeDtypeStruct((2, count, width), BF16)
    theirs, mine = pl.pallas_call(
        functools.partial(branch_kernel, hpd),
        grid_spec=pltpu.PrefetchScalarGridSpec(
            num_scalar_prefetch=1,
            grid=(4,),
            in_specs=[
                pl.BlockSpec((hpd, count, HD), lambda i, t: (0, t[4 * k + (i ^ 2)], 0)),
                whole((hpd * HD, width)),
            ],
            out_specs=[first_pair((count, width)), last_pair((count, width))],
        ),
        out_shape=[pair, pair],
        compiler_params=params(10),
        cost_estimate=cost(2.4),
        name="branch",
    )(table, mixed, w)
    return mine, theirs


def branch_back_kernel(k, hpd, meta, g0, g1, g2, g3, mixed, w, *refs):
    grad, delta, dw = refs[-3:]
    pieces = (g0, g1, g2, g3)
    count = g0.shape[0]
    g = jnp.concatenate([piece[...] for piece in pieces], axis=0)
    back = dot(g, w[...], ROWS_T).astype(BF16)
    for j in range(hpd):
        heads = []
        for i in range(4):
            at = span(meta, k, i, count)
            own = back[i * count : (i + 1) * count, j * HD : (j + 1) * HD]
            out = mixed[j, at, :]
            grad[j, at, :] = own
            delta[j, :, at] = row_sums(own.astype(F32) * out)
            heads.append(out.astype(BF16))
        part = dot(jnp.concatenate(heads, axis=0), g, COLS_T)
        rows = slice(j * HD, (j + 1) * HD)
        dw[rows, :] = part if len(refs) == 3 else refs[0][rows, :] + part


def branch_back(k, quarter, mixed, w, table, before):
    count, width = quarter[0].shape
    hpd, length, _ = mixed.shape
    group = group_of(k)
    head_at = once((hpd, 4 * count, HD), lambda i, t: (0, group(t), 0))
    dw_at = whole((hpd * HD, width))
    grad, delta, dw = pl.pallas_call(
        functools.partial(branch_back_kernel, k, hpd),
        grid_spec=pltpu.PrefetchScalarGridSpec(
            num_scalar_prefetch=1,
            grid=(1,),
            in_specs=[whole((count, width))] * 4
            + [head_at, whole((hpd * HD, width))]
            + ([dw_at] + [pl.BlockSpec(memory_space=pl.ANY)] * 2 if before else []),
            out_specs=[
                head_at,
                once((hpd, 8, 4 * count), lambda i, t: (0, 0, group(t))),
                dw_at,
            ],
        ),
        out_shape=[
            jax.ShapeDtypeStruct((hpd, length, HD), BF16),
            jax.ShapeDtypeStruct((hpd, 8, length), F32),
            jax.ShapeDtypeStruct((hpd * HD, width), F32),
        ],
        input_output_aliases={8: 0, 9: 1} if before else {},
        compiler_params=params(20),
        cost_estimate=cost(6),
        name="branch_back",
    )(table, *quarter, mixed, w, *before)
    return dw, grad, delta


def experts_kernel(
    k, n_parts, width, capacity, n_exp, meta, x0, x1, x2, x3, g0, g1, g2, g3, router, *refs
):
    n = n_parts
    w_from = refs[: 3 * n]
    refs = refs[-(2 * n + 5 + 6 * n + 3 + 3) :]
    outs, (mine, theirs) = refs[: 2 * n + 3], refs[2 * n + 3 : 2 * n + 5]
    refs = refs[2 * n + 5 :]
    w_here, refs = refs[: 3 * n], refs[3 * n :]
    rows, pairs, picked, refs = refs[:n], refs[n : 2 * n], refs[2 * n : 3 * n], refs[3 * n :]
    hidden, gate_grad, up_grad, chosen_ref, gate_ref, sems = refs
    slots = 4 * capacity
    part = width // n
    c = meta[0]
    lanes = lax.broadcasted_iota(jnp.int32, (1, 128), 1)
    pieces = (x0, x1, x2, x3)
    arrivals = [
        pltpu.make_async_copy(w_from[i], w_here[i], sems.at[i]) for i in range(3 * n)
    ]
    for copy in arrivals:
        copy.start()
    here = [*rows, *pairs, hidden, gate_grad, up_grad]
    leaving = [
        pltpu.make_async_copy(
            here[i], outs[i].at[pl.ds(k * slots, slots), :], sems.at[3 * n + i]
        )
        for i in range(2 * n + 3)
    ]

    def columns(p, first=0):
        return pl.ds(pl.multiple_of(first + meta[1 + p], 128), part)

    for i, x_ref in enumerate(pieces):
        cot = (g0, g1, g2, g3)[i]
        at = slice(i * capacity, (i + 1) * capacity)
        info = x_ref[:, width:].astype(F32)
        place = jnp.sum(jnp.where(lanes == c, info, 0.0), axis=1, keepdims=True)
        spots = lax.broadcasted_iota(jnp.int32, (1, capacity), 1).astype(F32)
        chosen = (spots == place).astype(BF16)
        chosen_ref[i] = chosen
        logits = dot(x_ref[:, :width], router[...])
        seen = info > -1.5
        top = jnp.max(jnp.where(seen, logits, -1e30), axis=1, keepdims=True)
        shares = jnp.where(seen, jnp.exp(logits - top), 0.0)
        gates = shares / jnp.sum(shares, axis=1, keepdims=True)
        own = jnp.sum(jnp.where(lanes == c, gates, 0.0), axis=1, keepdims=True)
        gate = lax.dot_general(
            chosen.astype(F32),
            jnp.broadcast_to(own, gates.shape),
            COLS_T,
            precision=HIGH,
            preferred_element_type=F32,
        )
        gate_ref[at, :] = gate
        for p in range(n):
            rows[p][at, :] = dot(chosen, x_ref[:, columns(p)], COLS_T).astype(BF16)
            grads = dot(chosen, cot[:, columns(p)], COLS_T)
            picked[p][at, :] = grads.astype(BF16)
            pairs[p][at, :] = (grads * gate[:, :1]).astype(BF16)
    for copy in leaving[: 2 * n]:
        copy.start()
    for copy in arrivals[: 2 * n]:
        copy.wait()
    wg, wu, wd = (w_here[n * i : n * (i + 1)] for i in range(3))
    gate_part = sum(dot(rows[p][...], wg[p][...]) for p in range(n))
    up_part = sum(dot(rows[p][...], wu[p][...]) for p in range(n))
    sigma = jax.nn.sigmoid(gate_part)
    silu_gate = gate_part * sigma
    h = (silu_gate * up_part).astype(BF16)
    hidden[...] = h
    leaving[2 * n].start()
    for copy in arrivals[2 * n :]:
        copy.wait()
    hidden_grad = sum(dot(pairs[p][...], wd[p][...]) for p in range(n))
    gg = (hidden_grad * up_part * sigma * (1.0 + gate_part * (1.0 - sigma))).astype(BF16)
    gate_grad[...] = gg
    leaving[2 * n + 1].start()
    ug = (hidden_grad * silu_gate).astype(BF16)
    up_grad[...] = ug
    leaving[2 * n + 2].start()
    inner_sum = jnp.zeros((slots, 1), F32)
    for p in range(n):
        out = dot(h, wd[p][...], ROWS_T).astype(BF16).astype(F32)
        inner_sum += jnp.sum(out * picked[p][...].astype(F32), axis=1, keepdims=True)
        scaled = (out * gate_ref[:, :1]).astype(BF16)
        row_sum = (dot(gg, wg[p][...], ROWS_T) + dot(ug, wu[p][...], ROWS_T)).astype(BF16)
        for i in range(4):
            back = (mine, theirs)[i // 2].at[i % 2]
            at = slice(i * capacity, (i + 1) * capacity)
            back[:, columns(p)] = dot(chosen_ref[i], row_sum[at, :]).astype(BF16)
            back[:, columns(p, width + 128)] = dot(chosen_ref[i], scaled[at, :]).astype(BF16)
    high = inner_sum.astype(BF16).astype(F32)
    extra = jnp.where(lanes == c, high, 0.0) + jnp.where(
        lanes == c + n_exp, inner_sum - high, 0.0
    )
    extra = extra.astype(BF16)
    for i in range(4):
        back = (mine, theirs)[i // 2].at[i % 2]
        at = slice(i * capacity, (i + 1) * capacity)
        back[:, width : width + 128] = dot(chosen_ref[i], extra[at, :]).astype(BF16)
    for copy in leaving:
        copy.wait()


def experts(k, quarter, cots, router, wg, wu, wd, meta, capacity, n_exp, nz, before):
    count, wide = quarter[0].shape
    width = cots[0].shape[1]
    n_parts = len(wg)
    part = width // n_parts
    hid = wg[0].shape[1]
    slots = 4 * capacity
    anywhere = pl.BlockSpec(memory_space=pl.ANY)
    pair = once((2, count, wide + width), lambda i, m: (0, 0, 0))
    rows_all = lambda cols: pltpu.HBM((nz * slots, cols), BF16)
    n_out = 2 * n_parts + 3
    outs = pl.pallas_call(
        functools.partial(experts_kernel, k, n_parts, width, capacity, n_exp),
        grid_spec=pltpu.PrefetchScalarGridSpec(
            num_scalar_prefetch=1,
            grid=(1,),
            in_specs=[whole((count, wide))] * 4
            + [whole((count, width))] * 4
            + [whole(router.shape)]
            + [anywhere] * (3 * n_parts)
            + [IN_HBM] * len(before),
            out_specs=[IN_HBM] * n_out + [pair, pair],
            scratch_shapes=[pltpu.VMEM((part, hid), BF16)] * (3 * n_parts)
            + [pltpu.VMEM((slots, part), BF16)] * (3 * n_parts)
            + [pltpu.VMEM((slots, hid), BF16)] * 3
            + [
                pltpu.VMEM((4, count, capacity), BF16),
                pltpu.VMEM((slots, 128), F32),
                pltpu.SemaphoreType.DMA((5 * n_parts + 3,)),
            ],
        ),
        out_shape=[rows_all(part)] * (2 * n_parts)
        + [rows_all(hid)] * 3
        + [jax.ShapeDtypeStruct((2, count, wide + width), BF16)] * 2,
        input_output_aliases={10 + 3 * n_parts + i: i for i in range(len(before))},
        compiler_params=params(42),
        cost_estimate=cost(15),
        name="experts",
    )(meta, *quarter, *cots, router, *wg, *wu, *wd, *before)
    return (outs[n_out], outs[n_out + 1]), outs[:n_out]


def head_back(grad, v, gain, cos, sin):
    scale = lax.rsqrt(jnp.mean(v * v, axis=-1, keepdims=True) + EPS)
    d = grad * cos - half_turn(grad) * sin
    u = d * gain
    inner = jnp.mean(u * v, axis=-1, keepdims=True)
    back = scale * u - v * (scale * scale * scale * inner)
    return back.astype(BF16), jnp.sum(d * v * scale, axis=0, keepdims=True)


def key_back_kernel(meta, dk, dv, raw, turn, gk, *refs):
    out, gains = refs[-2:]
    came = refs[:-2]
    z = pl.program_id(0)

    @pl.when(z == 0)
    def _():
        gains[...] = jnp.zeros_like(gains)

    n_kv = dk.shape[0]
    count = raw.shape[1]
    for i in range(4):
        at = pl.ds(pl.multiple_of(lax.rem(meta[4 * z + i], 4) * count, count), count)
        for j in range(n_kv):
            v = raw[i, :, j * HD : (j + 1) * HD]
            key_grad, value_grad = dk[j, at, :], dv[j, at, :]
            if came:
                key_grad = key_grad + came[0][0, at, :].astype(F32)
                value_grad = value_grad + came[0][1, at, :].astype(F32)
            grad = key_grad * HD**-0.5
            back, gain = head_back(grad, v, gk[...], *turns(turn[at, :]))
            out[i, :, j * HD : (j + 1) * HD] = back
            gains[0:1, :] += gain
            out[i, :, (n_kv + j) * HD : (n_kv + j + 1) * HD] = value_grad.astype(BF16)


def key_back(dk, dv, came, raw, turn, gk, meta):
    hpd = dk.shape[0]
    n_kv = 1 if came else hpd
    n_ctx, count, _ = raw.shape
    group = lambda z, t: lax.div(t[4 * z], 4)
    head_at = pl.BlockSpec(
        (n_kv, 4 * count, HD), lambda z, t: (t[n_ctx] if came else 0, group(z, t), 0)
    )
    turn_at = pl.BlockSpec((4 * count, HD), lambda z, t: (group(z, t), 0))
    return pl.pallas_call(
        key_back_kernel,
        grid_spec=pltpu.PrefetchScalarGridSpec(
            num_scalar_prefetch=1,
            grid=(n_ctx // 4,),
            in_specs=[
                head_at,
                head_at,
                pl.BlockSpec((4, count, n_kv * HD), lambda z, t: (z, 0, hpd // n_kv)),
                turn_at,
                whole((1, HD)),
            ]
            + [pl.BlockSpec((2, 4 * count, HD), lambda z, t: (0, group(z, t), 0))] * len(came),
            out_specs=[
                pl.BlockSpec((4, count, 2 * n_kv * HD), lambda z, t: (z, 0, 0)),
                whole((8, HD)),
            ],
        ),
        out_shape=[
            jax.ShapeDtypeStruct((n_ctx, count, 2 * n_kv * HD), BF16),
            jax.ShapeDtypeStruct((8, HD), F32),
        ],
        compiler_params=params(14),
        cost_estimate=cost(5),
        name="key_back",
    )(meta, dk, dv, raw, turn, gk, *came)


def input_back_kernel(k, hpd, meta, dq, kv, raw, scales, turn, gq, w, *refs):
    x, (grads_out, theirs, mine, gains, gain_grad, rows, grads, sem) = refs[:4], refs[-8:]
    copy = pltpu.make_async_copy(grads, grads_out.at[pl.ds(4 * k, 4)], sem)
    count = raw.shape[1]
    q_cols = hpd * HD

    @pl.when(pl.program_id(0) == 0)
    def _():
        gains[...] = jnp.zeros_like(gains)
        for i in range(4):
            at = span(meta, k, i, count)
            for j in range(hpd):
                cols = slice(j * HD, (j + 1) * HD)
                grad = dq[j, at, :] * HD**-0.5
                back, gain = head_back(grad, raw[i, :, cols], gq[...], *turns(turn[at, :]))
                grads[i, :, cols] = back
                gains[0:1, :] += gain
            rows[i * count : (i + 1) * count, :q_cols] = grads[i]
            rows[i * count : (i + 1) * count, q_cols:] = kv[i]
        copy.start()

    @pl.when(pl.program_id(0) == pl.num_programs(0) - 1)
    def _():
        copy.wait()

    back = dot(rows[...], w[...], ROWS_T)
    total = None
    for i in range(4):
        block = back[i * count : (i + 1) * count, :]
        (mine, theirs)[i // 2][i % 2] = block.astype(BF16)
        term = jnp.sum(block * x[i][...].astype(F32) * scales[i, :, :1], axis=0, keepdims=True)
        total = term if total is None else total + term
    gain_grad[...] = jnp.broadcast_to(total, gain_grad.shape)


def input_back(k, quarter, dq, kv, raw, scales, turn, gq, w, meta, before):
    count, width = quarter[0].shape
    hpd = dq.shape[0]
    n_ctx = raw.shape[0]
    q_cols = hpd * HD
    chunk = width // 4
    group = group_of(k)
    turn_at = pl.BlockSpec((4 * count, HD), lambda i, t: (group(t), 0))
    own = lambda cols: pl.BlockSpec((4, count, cols), lambda i, t: (k, 0, 0))
    pair_at = pl.BlockSpec((2, count, chunk), lambda i, t: (0, 0, i))
    pair = jax.ShapeDtypeStruct((2, count, width), BF16)
    outs = pl.pallas_call(
        functools.partial(input_back_kernel, k, hpd),
        grid_spec=pltpu.PrefetchScalarGridSpec(
            num_scalar_prefetch=1,
            grid=(4,),
            in_specs=[
                pl.BlockSpec((hpd, 4 * count, HD), lambda i, t: (0, group(t), 0)),
                own(kv.shape[2]),
                own(q_cols),
                own(HD),
                turn_at,
                whole((1, HD)),
                pl.BlockSpec((chunk, w.shape[1]), lambda i, t: (i, 0)),
            ]
            + [pl.BlockSpec((count, chunk), lambda i, t: (0, i))] * 4
            + [IN_HBM] * len(before),
            out_specs=[
                IN_HBM,
                pair_at,
                pair_at,
                whole((8, HD)),
                pl.BlockSpec((8, chunk), lambda i, t: (0, i)),
            ],
            scratch_shapes=[
                pltpu.VMEM((4 * count, w.shape[1]), BF16),
                pltpu.VMEM((4, count, q_cols), BF16),
                pltpu.SemaphoreType.DMA(()),
            ],
        ),
        out_shape=[
            pltpu.HBM((n_ctx, count, q_cols), BF16),
            pair,
            pair,
            jax.ShapeDtypeStruct((8, HD), F32),
            jax.ShapeDtypeStruct((8, width), F32),
        ],
        input_output_aliases={12: 0} if before else {},
        compiler_params=params(18),
        cost_estimate=cost(6),
        name="input_back",
    )(meta, dq, kv, raw, scales, turn, gq, w, *quarter, *before)
    grads, theirs, mine, gains, gain_grad = outs
    return (mine, theirs), grads, gains, gain_grad


def place_kernel(parts, n_kv, table, *refs):
    columns, keys = refs[:4], refs[4 : 4 + n_kv]
    outs = refs[-3:] if n_kv else refs[-1:]
    for n in range(4):

        @pl.when(pl.program_id(0) // parts == n)
        def _():
            outs[0][...] = columns[n][...].astype(F32)
            if n_kv:
                outs[1][...] = keys[n][:, :HD].astype(F32)
                outs[2][...] = keys[n][:, HD:].astype(F32)


def place_columns(k, quarter, table, n_ctx, rows, before):
    all_rows, cols = quarter[0].shape
    parts = cols // HD
    kv_rows = all_rows - rows

    def piece_at(n):
        return lambda i, t: (0, jnp.clip(i - n * parts, 0, parts - 1))

    def head_at(i, t):
        c = t[4 * k + i // parts]
        rows_part = lax.rem(c // 4, 2) * 2 + lax.rem(c // 2, 2)
        return rows_part, lax.rem(c, 2) * 2 + c // 8

    out_specs = [
        pl.BlockSpec((rows, HD), lambda i, t: (0, (i % parts) * n_ctx + t[4 * k + i // parts]))
    ]
    out_shape = [jax.ShapeDtypeStruct((rows, n_ctx * cols), F32)]
    in_specs = [pl.BlockSpec((rows, HD), piece_at(n)) for n in range(4)]
    pieces = list(quarter)
    if kv_rows:
        in_specs += [once((kv_rows, cols), lambda i, t: (rows // kv_rows, 0))] * 4
        pieces += quarter
        out_specs += [pl.BlockSpec((kv_rows, HD), head_at)] * 2
        out_shape += [jax.ShapeDtypeStruct((rows, KVH * HD), F32)] * 2
    return pl.pallas_call(
        functools.partial(place_kernel, parts, len(pieces) - 4),
        grid_spec=pltpu.PrefetchScalarGridSpec(
            num_scalar_prefetch=1,
            grid=(4 * parts,),
            in_specs=in_specs + [pl.BlockSpec(memory_space=pl.ANY)] * len(before),
            out_specs=out_specs,
        ),
        out_shape=out_shape,
        input_output_aliases={1 + len(pieces) + i: i for i in range(len(before))},
        compiler_params=params(12),
        cost_estimate=cost(4.6),
        name="place_columns",
    )(table, *pieces, *before)


def place_rows_kernel(table, *refs):
    out = refs[-1]
    for n in range(4):

        @pl.when(pl.program_id(0) == n)
        def _():
            out[...] = refs[n][...].astype(F32)


def place_rows(quarters, table):
    rows, cols = quarters[0][0].shape
    placed = ()
    for k, quarter in enumerate(quarters):
        placed = pl.pallas_call(
            place_rows_kernel,
            grid_spec=pltpu.PrefetchScalarGridSpec(
                num_scalar_prefetch=1,
                grid=(4,),
                in_specs=[whole((rows, cols))] * 4 + [IN_HBM] * len(placed),
                out_specs=[pl.BlockSpec((rows, cols), lambda i, t, k=k: (t[4 * k + i], 0))],
            ),
            out_shape=[pltpu.HBM((4 * len(quarters) * rows, cols), F32)],
            input_output_aliases={5: 0} if placed else {},
            compiler_params=params(10),
            cost_estimate=cost(2.4),
            name="place_rows",
        )(table, *quarter, *placed)
    return placed[0]


def local(
    inputs,
    w_query,
    w_key,
    w_value,
    w_output,
    norm_attn,
    gain_query,
    gain_key,
    w_router,
    norm_moe,
    w_gate,
    w_up,
    w_down,
    lengths,
    routes,
    pair_order,
    cotangent,
):
    n_ctx = lax.axis_size("ctx")
    n_f = lax.axis_size("fsdp")
    c = lax.axis_index("ctx")
    f = lax.axis_index("fsdp")
    count, width = inputs.shape[1], inputs.shape[2]
    length = count * n_ctx
    nz = n_ctx // 4
    later = scatter_order(n_ctx)
    hpd = H // n_ctx
    hpf = H // n_f
    group = H // KVH
    n_exp = w_router.shape[1]
    capacity = 5 * count * TOPK // (4 * n_exp)
    table = block_order(n_ctx)
    core = c % 2

    heads = [c % hpf + hpf * ((c // hpf) * hpd + j) for j in range(hpd)]
    kv_heads = [h // group for h in heads]
    columns = lambda w, h: lax.dynamic_slice_in_dim(w, h * HD, HD, 1)
    shared = n_f == 2 and hpd == 2
    if shared:
        kv_own = heads[0] // group + core * (KVH // 2)
        w_part = jnp.concatenate(
            [columns(w_query, h) for h in heads]
            + [columns(w_key, kv_own), columns(w_value, kv_own)],
            axis=1,
        )
    else:
        w_part = jnp.concatenate(
            [columns(w_query, h) for h in heads]
            + [columns(w_key, h) for h in kv_heads]
            + [columns(w_value, h) for h in kv_heads],
            axis=1,
        )
    w_part, norm_first = tie(w_part, norm_attn)
    vectors = jnp.concatenate([norm_first, gain_query, gain_key, norm_moe])
    if n_f == 2:
        vectors = joined([vectors[None], swap(vectors[None])])
        router = joined([w_router, swap(w_router)])
    else:
        vectors = lax.all_gather(vectors, "fsdp", axis=0)
        router = lax.all_gather(w_router, "fsdp", axis=0, tiled=True)
    sizes = [norm_attn.shape[0], gain_query.shape[0], gain_key.shape[0], norm_moe.shape[0]]
    rows_of, at = [], 0
    for size in sizes:
        rows_of.append(vectors[:, at : at + size].reshape(1, n_f * size).astype(F32))
        at += size
    attn_gain, query_gain, key_gain, moe_gain = rows_of
    router_wide = jnp.pad(router, ((0, 0), (0, 128 - n_exp)))
    offsets = part_offsets(width)
    n_parts = len(offsets)
    meta_rows = jnp.concatenate([table, jnp.stack([core] + offsets).astype(jnp.int32)])
    q_cols = hpd * HD
    block = w_gate.shape[2] // 3
    weights = {}

    def fetch_weights():
        parts = yield from fetch(w_part, 2)
        weights["qkv"], weights["beside"] = parts, []
        if shared:
            weights["beside"] = [
                lax.ppermute(part[:, q_cols:], "ctx", flip(n_ctx, 1)) for part in parts
            ]
        weights["back"] = joined(parts)
        own_rows = lax.dynamic_slice_in_dim(w_output, (c % hpf) * HD, HD, 0)
        rows_parts = yield from fetch(own_rows)
        last = rows_parts[-1]
        w_out = joined(rows_parts)
        weights["out"] = lax.dynamic_slice_in_dim(w_out, (c // hpf) * hpd * HD, hpd * HD, 0)
        weights["gate"], last = yield from fetch_after(w_gate[0], last, 2)
        weights["up"], last = yield from fetch_after(w_up[0], last, 4)
        weights["down"], last = yield from fetch_after(w_down[0], last, 3)

    gathered = {}

    def gather_cotangents():
        (cot,) = yield (cotangent[0],), 3
        yield from gather_planned(cot, n_ctx, COTANGENT_PLAN, gathered)

    sides = [Side(fetch_weights()), Side(gather_cotangents())]

    experts_of = jnp.arange(n_exp, dtype=jnp.int32)
    picks = routes[0][:, :, None] == experts_of
    ranks = jnp.sum(
        jnp.where(picks, pair_order[0, 0].reshape(count, TOPK, 1), 0), axis=1
    )
    chosen = jnp.any(picks, axis=1)
    ranks = jnp.where(chosen, ranks, count * TOPK)
    place = jnp.sum((ranks[None, :, :] < ranks[:, None, :]).astype(jnp.int32), axis=1)
    place = jnp.where(chosen, jnp.where(place < capacity, place, -1), -2)
    place = jnp.pad(place, ((0, 0), (0, 128 - n_exp)), constant_values=-2).astype(BF16)

    ends = jnp.cumsum(lengths[0]).astype(jnp.int32)
    turn = rotary_table(length)

    xs = {}

    def through_projection(k, quarter, token, before):
        xs[k] = quarter
        if k == 0:
            return ()
        if k == 1:
            before = projection(0, token, ())
        return projection(k, token, before)

    def projection(k, token, before):
        return project(
            k,
            xs[k],
            weights["qkv"],
            weights["beside"],
            attn_gain,
            query_gain,
            key_gain,
            turn,
            token,
            hpd,
            n_ctx,
            before,
        )

    straight = list(range(nz))
    *normed, raw, scales, query, key, value = pipeline(
        n_ctx, straight, through_projection, meta_rows, sides, piece=inputs[0]
    )
    mixed, log_total = attend(query, key, value, ends)
    _, (mixed,) = land({}, sides, mixed)
    x = inputs[0].astype(F32)
    branch_sum, _ = pipeline(
        n_ctx,
        later,
        lambda k, _, token, state: (branch(k, mixed, weights["out"], token, count), state),
        table,
        sides,
        scatter=True,
    )
    middle = x + branch_sum
    moe_scale = lax.rsqrt(jnp.mean(middle * middle, axis=-1, keepdims=True) + EPS)
    routed_in = (middle * moe_scale * moe_gain).astype(BF16)

    pad_offsets = (offsets + [jnp.int32(0)])[:2]
    head_meta = [jnp.stack([c] + pad_offsets).astype(jnp.int32)]
    expert_meta = jnp.concatenate(head_meta)

    def through_experts(k, quarter, token, before):
        return experts(
            k,
            quarter,
            planned_quarter(gathered, k, n_ctx),
            router_wide,
            weights["gate"],
            weights["up"],
            weights["down"],
            token,
            capacity,
            n_exp,
            nz,
            before,
        )

    routed_grad, seen = pipeline(
        n_ctx,
        later,
        through_experts,
        expert_meta,
        sides,
        piece=jnp.concatenate([routed_in, place], axis=1),
        scatter=True,
        along=True,
    )
    rows, pairs = seen[:n_parts], seen[n_parts : 2 * n_parts]
    hidden, gate_part_grad, up_part_grad = seen[2 * n_parts :]
    outputs = (middle + routed_grad[:, width + 128 :]).astype(BF16)

    gate_grad = routed_grad[:, width : width + n_exp] + routed_grad[
        :, width + n_exp : width + 2 * n_exp
    ]
    routed_grad = routed_grad[:, :width]
    logits = dot(routed_in, router)
    top = jnp.max(jnp.where(chosen, logits, -1e30), axis=-1, keepdims=True)
    shares = jnp.where(chosen, jnp.exp(logits - top), 0.0)
    gates = shares / jnp.sum(shares, axis=-1, keepdims=True)
    logit_grad = gates * (gate_grad - jnp.sum(gates * gate_grad, axis=-1, keepdims=True))
    routed_grad = routed_grad + lax.dot_general(
        logit_grad, router.astype(F32), ROWS_T, precision=HIGH
    )
    router_part = lax.dot_general(
        logit_grad, routed_in.astype(F32), COLS_T, precision=HIGH
    )

    grad_out = cotangent[0].astype(F32)
    moe_scaled = routed_grad * moe_gain
    moe_part = jnp.sum(routed_grad * middle * moe_scale, axis=0, keepdims=True)
    middle_grad = (
        grad_out
        + moe_scale * moe_scaled
        - middle
        * (
            moe_scale
            * moe_scale
            * moe_scale
            * jnp.mean(moe_scaled * middle, axis=-1, keepdims=True)
        )
    )

    grads, sums = {}, []

    def scatter_grads():
        pairs_of = [(rows, gate_part_grad), (rows, up_part_grad), (pairs, hidden)]
        sums_of = yield from scatter_products(
            pairs_of, block, (1, 1, 1, 1, 1, 2, 1, 1, 1), {6: 3}
        )
        grads["gate"], grads["up"], grads["down"] = sums_of

    sides = [
        Side(scatter_grads()),
        Side(sum_all(jnp.concatenate([router_part, moe_part], axis=0), sums)),
    ]
    grad_out_w, mixed_grad, delta = pipeline(
        n_ctx,
        straight,
        lambda k, quarter, token, before: branch_back(
            k, quarter, mixed, weights["out"], token, before
        ),
        table,
        sides,
        piece=middle_grad.astype(BF16),
    )
    def sum_out_grad():
        if n_f == hpd:
            placed = grad_out_w
        else:
            spread_out = jnp.arange(n_f, dtype=jnp.int32)[:, None] == (
                (c // hpf) * hpd + jnp.arange(hpd, dtype=jnp.int32)[None, :]
            )
            placed = jnp.einsum(
                "fj,jrd->frd", spread_out.astype(F32), grad_out_w.reshape(hpd, HD, width)
            ).reshape(n_f * HD, width)
        own = yield from scatter_rows(placed)
        own = own.astype(BF16)
        if n_ctx == hpf:
            arrays = {}
            yield from gather_planned(own, n_ctx, OUTPUT_GRAD_PLAN, arrays)
            quarters = [planned_quarter(arrays, k, n_ctx) for k in range(nz)]
            grads["out"] = place_rows(quarters, table)
        else:
            whole_grad = lax.all_gather(own, "ctx", axis=0).reshape(-1, hpf * HD, width)
            mine = lax.dynamic_index_in_dim(whole_grad, f // hpd, 0, keepdims=False)
            grads["out"] = mine.astype(F32)

    sides.append(Side(sum_out_grad()))
    ends_and_core = jnp.concatenate([ends, core[None].astype(jnp.int32)])
    dq, dk, dv, *away = attend_back(
        query, mixed_grad, log_total, delta, key, value, ends_and_core, int(shared)
    )
    _, (dq, dk, dv, *away) = land({}, sides, dq, dk, dv, *away)
    came = [lax.ppermute(array, "ctx", flip(n_ctx, 1)) for array in away]
    kv_grad, key_gains = key_back(dk, dv, came, raw, turn, key_gain, meta_rows)
    normed_flat = [n.reshape(length, -1) for n in normed]

    def sum_key_grads():
        (grad_kv,) = yield from scatter_products(
            [(normed_flat, kv_grad.reshape(length, -1))], kv_grad.shape[-1]
        )
        if not shared:
            slots_kv = jnp.arange(KVH, dtype=jnp.int32)
            spread = jnp.stack([slots_kv == h for h in kv_heads]).astype(F32)
            grad_kv = grad_kv.reshape(width // n_f, 2, hpd, 1, HD) * spread[None, None, :, :, None]
            grad_kv = jnp.sum(grad_kv, axis=2).reshape(width // n_f, 2 * KVH * HD)
            grad_kv = lax.psum(grad_kv.astype(BF16), "ctx").astype(F32)
            grads["key"], grads["value"] = grad_kv[:, : KVH * HD], grad_kv[:, KVH * HD :]
            return
        for bit in (4, 2):
            rows_kept = grad_kv.shape[0] // 2
            side = (c // bit) % 2
            kept = lax.dynamic_slice_in_dim(grad_kv, side * rows_kept, rows_kept, 0)
            gone = lax.dynamic_slice_in_dim(grad_kv, (1 - side) * rows_kept, rows_kept, 0)
            (got,) = yield (lax.ppermute(gone.astype(BF16), "ctx", flip(n_ctx, bit)),), 1
            grad_kv = kept + got.astype(F32)
        grads["key_piece"] = grad_kv.astype(BF16)

    sides.append(Side(sum_key_grads()))
    gain_parts, attn_parts = [], []

    def through_inputs(k, _, token, before):
        back, q_grad, gains, gain_grad = input_back(
            k,
            xs[k],
            dq,
            kv_grad,
            raw,
            scales,
            turn,
            query_gain,
            weights["back"],
            token,
            before,
        )
        gain_parts.append(gains)
        attn_parts.append(gain_grad)
        if len(gain_parts) == nz:
            gain_rows = jnp.concatenate([sum(gain_parts)[:1], key_gains[:1]], axis=1)
            gain_rows = jnp.pad(gain_rows, ((0, 0), (0, width - 2 * HD)))
            rows_last = [sum(attn_parts)[:1], gain_rows]
            sides.append(Side(sum_all(jnp.concatenate(rows_last, axis=0), sums)))
        return back, (q_grad,)

    q_grads = []

    def through_inputs_last(k, quarter, token, before):
        back, state = through_inputs(k, quarter, token, before)
        q_grads[:] = state
        return back, state

    def query_products():
        q_flat = q_grads[0].reshape(length, -1)
        if n_f != 2:
            full = dot(normed_flat[0], q_flat, COLS_T).astype(BF16)
            return (lax.psum_scatter(full, "fsdp", scatter_dimension=0, tiled=True),)
        mine, other = normed_flat
        came = swap(dot(other, q_flat, COLS_T).astype(BF16))
        return dot(mine, q_flat, COLS_T), came

    def gather_query_grads(*products):
        own = sum(product.astype(F32) for product in products).astype(BF16)
        if n_ctx == hpf:
            sides.append(Side(gather_columns(own)))
            return
        grads["query"] = (
            lax.all_gather(own, "ctx", axis=0)
            .reshape(n_ctx // hpf, hpf, width // n_f, hpd, HD)
            .transpose(2, 0, 3, 1, 4)
            .reshape(width // n_f, H * HD)
            .astype(F32)
        )

    def gather_columns(own):
        q_rows = own.shape[0]
        if shared:
            own = jnp.concatenate([own, grads["key_piece"]], axis=0)
        arrays, placed = {}, ()
        chain = gather_planned(own, n_ctx, QUERY_GRAD_PLAN, arrays)
        going, steps = next(chain)
        for k in range(nz):
            landed = yield (*going, *placed), steps
            placed = landed[len(going) :]
            try:
                going, steps = chain.send(landed[: len(going)])
            except StopIteration:
                going = ()
            quarter = planned_quarter(arrays, k, n_ctx)
            placed = place_columns(k, quarter, table, n_ctx, q_rows, placed)
        grads["query"] = placed[0]
        if shared:
            grads["key"], grads["value"] = placed[1:]

    normed_grad, _ = pipeline(
        n_ctx,
        later,
        through_inputs_last,
        meta_rows,
        sides,
        scatter=True,
        closing=(query_products, gather_query_grads),
    )
    while any(side.flying is not None for side in sides):
        land({}, sides)
    early, late = sums
    own_part = lambda v, size: lax.dynamic_slice_in_dim(v, f * (size // n_f), size // n_f, 0)
    grad_w_router = own_part(early[:n_exp].T, width)
    grad_norm_moe = own_part(early[n_exp], width)
    grad_norm_attn = own_part(late[0], width)
    grad_gain_query = own_part(late[1, :HD], HD)
    grad_gain_key = own_part(late[1, HD : 2 * HD], HD)

    attn_scale = lax.rsqrt(jnp.mean(x * x, axis=-1, keepdims=True) + EPS)
    attn_scaled = normed_grad * attn_gain
    input_grad = (
        middle_grad
        + attn_scale * attn_scaled
        - x
        * (
            attn_scale
            * attn_scale
            * attn_scale
            * jnp.mean(attn_scaled * x, axis=-1, keepdims=True)
        )
    )
    return (
        outputs[None],
        input_grad.astype(BF16)[None],
        grads["query"],
        grads["key"],
        grads["value"],
        grads["out"],
        grad_norm_attn,
        grad_gain_query,
        grad_gain_key,
        grad_w_router,
        grad_norm_moe,
        grads["gate"][None],
        grads["up"][None],
        grads["down"][None],
    )


def solution(mesh):
    in_specs = (
        P("fsdp", "ctx", None),
        P("fsdp", None),
        P("fsdp", None),
        P("fsdp", None),
        P("fsdp", None),
        P("fsdp"),
        P("fsdp"),
        P("fsdp"),
        P("fsdp", None),
        P("fsdp"),
        P("ctx", "fsdp", None),
        P("ctx", "fsdp", None),
        P("ctx", "fsdp", None),
        P("fsdp", None),
        P("fsdp", "ctx", None),
        P("fsdp", "ctx", None),
        P("fsdp", "ctx", None),
    )
    out_specs = (
        P("fsdp", "ctx", None),
        P("fsdp", "ctx", None),
        P("fsdp", None),
        P("fsdp", None),
        P("fsdp", None),
        P("fsdp", None),
        P("fsdp"),
        P("fsdp"),
        P("fsdp"),
        P("fsdp", None),
        P("fsdp"),
        P("ctx", "fsdp", None),
        P("ctx", "fsdp", None),
        P("ctx", "fsdp", None),
    )
    return jax.shard_map(local, mesh=mesh, in_specs=in_specs, out_specs=out_specs, check_vma=False)
```

```python
import functools

import jax
import jax.numpy as jnp
from jax import lax
from jax.experimental import pallas as pl
from jax.experimental.pallas import tpu as pltpu
from jax.sharding import PartitionSpec as P

H = 32
KVH = 4
HD = 128
TOPK = 8
EPS = 1e-06
THETA = 1000000.0
HIGH = lax.Precision.HIGHEST
LOG2E = 1.4426950408889634
F32 = jnp.float32
BF16 = jnp.bfloat16
ROWS_T = (((1,), (1,)), ((), ()))
COLS_T = (((0,), (0,)), ((), ()))


def dot(a, b, dims=(((1,), (0,)), ((), ()))):
    return lax.dot_general(a, b, dims, preferred_element_type=F32)


def params(mebibytes):
    return pltpu.CompilerParams(vmem_limit_bytes=mebibytes * 1024 * 1024)


def once(shape, index):
    return pl.BlockSpec(shape, index, pipeline_mode=pl.Buffered(1))


def cost(microseconds):
    return pl.CostEstimate(
        flops=int(microseconds * 1.15e9), bytes_accessed=0, transcendentals=0
    )


def flip(n_ctx, bit):
    return [(i, i ^ bit) for i in range(n_ctx)]


def ring(n_ctx, step):
    return [(i, (i + step) % n_ctx) for i in range(n_ctx)]


def block_order(n_ctx):
    c = lax.axis_index("ctx")
    nz = n_ctx // 4
    z, x, core = c // 4, (c // 2) % 2, c % 2
    table = []
    for k in range(nz):
        for dc in range(2):
            for dx in range(2):
                table.append(lax.rem(z + nz - k, nz) * 4 + (x ^ dx) * 2 + (core ^ dc))
    return jnp.stack(table).astype(jnp.int32)


def tie(*arrays):
    return lax.optimization_barrier(arrays)


class Side:
    def __init__(self, chain):
        self.chain, self.flying, self.left = chain, None, 0
        self.resume(None)

    def resume(self, landed):
        try:
            self.flying, self.left = self.chain.send(landed)
        except StopIteration:
            self.flying = None

    def finish(self):
        while self.flying is not None:
            self.resume(self.flying)


def land(air, sides, *others):
    due = [side for side in sides if side.flying is not None and side.left <= 1]
    for side in sides:
        side.left -= 1
    keys = list(air)
    flying = [array for side in due for array in side.flying]
    arrays = list(tie(*air.values(), *flying, *others))
    air.clear()
    landed = {key: arrays.pop(0) for key in keys}
    for side in due:
        side.resume([arrays.pop(0) for _ in side.flying])
    return landed, arrays


def pipeline(
    n_ctx, order, compute, token, sides, piece=None, scatter=False, closing=None, along=False
):
    nz = n_ctx // 4
    air, have, state = {}, {}, ()

    def send(key, array, pairs):
        air[key] = lax.ppermute(array, "ctx", pairs)

    def bring(k):
        if along and k + 1 == nz:
            send(("beside", k), have["beside", k - 1], ring(n_ctx, 4))
        else:
            send(("beside", k), have["piece", k], flip(n_ctx, 2))
        if k + 1 < nz:
            send(("piece", k + 1), have["piece", k], ring(n_ctx, 4))

    def step_ends(*others):
        landed, others = land(air, sides, *others)
        have.update(landed)
        return others

    def total_of(own):
        parts = [*own, have["away"]] + ([have["carry"]] if "carry" in have else [])
        return sum(part.astype(F32) for part in parts)

    def give(blocks, token):
        mine, theirs = blocks
        arrived = lax.ppermute(theirs, "ctx", flip(n_ctx, 1))
        away = (mine[1].astype(F32) + arrived[1].astype(F32)).astype(BF16)
        token, away = tie(token, away)
        send("away", away, flip(n_ctx, 2))
        return (mine[0], arrived[0]), token

    if piece is not None:
        have["piece", 0] = piece
        for k in range(order[0] + 1):
            bring(k)
            step_ends()
    blocks = own = None
    for s, k in enumerate(order):
        following = order[s + 1 :][:1]
        quarter = None
        if piece is not None:
            for later in following:
                if ("beside", later) not in have:
                    bring(later)
            pair = [have["piece", k], have["beside", k]]
            quarter = pair + [lax.ppermute(array, "ctx", flip(n_ctx, 1)) for array in pair]
        if not scatter:
            state = compute(k, quarter, token, state)
            if following:
                token, *state = step_ends(token, *state)
            continue
        if own is not None:
            send("carry", total_of(own).astype(BF16), ring(n_ctx, 4))
        if blocks is not None:
            own, token = give(blocks, token)
        blocks, state = compute(k, quarter, token, state)
        extra = closing[0]() if closing and not following else ()
        if piece is not None and s < 2:
            token, *blocks = step_ends(token, *blocks)
        else:
            mine, theirs = blocks
            token, mine, *extra = step_ends(token, mine, *extra)
            blocks = mine, theirs
        if extra:
            closing[1](*extra)
    if not scatter:
        return tuple(state)
    send("carry", total_of(own).astype(BF16), ring(n_ctx, 4))
    own, token = give(blocks, token)
    step_ends()
    return total_of(own), state


def gather_planned(piece, n_ctx, plan, arrays):
    arrays["along", 0] = piece
    source = lambda kind, k: ("along", k) if kind == "across" else (kind, k - 1)
    for i, (items, steps) in enumerate(plan):
        going = [
            lax.ppermute(
                arrays[source(*item)], "ctx", flip(n_ctx, 2) if item[0] == "across" else ring(n_ctx, 4)
            )
            for item in items
        ]
        later = {source(*item) for item in plan[i + 1][0]} if i + 1 < len(plan) else set()
        tied = sorted(key for key in later if key in arrays)
        came = list((yield (*going, *(arrays[key] for key in tied)), steps))
        for kind, k in items:
            arrays["along" if kind == "along" else "beside", k] = came.pop(0)
        arrays.update(zip(tied, came))


def planned_quarter(arrays, k, n_ctx):
    pair = [arrays["along", k], arrays["beside", k]]
    return pair + [lax.ppermute(array, "ctx", flip(n_ctx, 1)) for array in pair]


COTANGENT_PLAN = [
    ([("along", 1)], 1),
    ([("along", 2), ("across", 0), ("across", 1)], 1),
    ([("beside", 2)], 2),
    ([("along", 3)], 6),
    ([("beside", 3)], 1),
]
QUERY_GRAD_PLAN = [
    ([("along", 1), ("across", 0)], 1),
    ([("along", 2), ("across", 1)], 1),
    ([("along", 3), ("across", 2)], 1),
    ([("across", 3)], 1),
]
OUTPUT_GRAD_PLAN = [
    ([("along", 1), ("across", 0)], 1),
    ([("along", 2), ("across", 1)], 1),
    ([("along", 3), ("across", 2)], 1),
    ([("across", 3)], 1),
]


def scatter_order(n_ctx):
    return list(range(1, n_ctx // 4)) + [0]


def sum_all(values, result):
    n_ctx = lax.axis_size("ctx")
    bit = 1
    while bit < n_ctx:
        (came,) = yield (lax.ppermute(values.astype(BF16), "ctx", flip(n_ctx, bit)),), 1
        values = values + came.astype(F32)
        bit *= 2
    if lax.axis_size("fsdp") == 2:
        (came,) = yield (swap(values.astype(BF16)),), 1
        values = values + came.astype(F32)
    else:
        values = lax.psum(values, "fsdp")
    result.append(values)


SWAP = [(0, 1), (1, 0)]


def swap(part):
    return lax.ppermute(part, "fsdp", SWAP)


def fetch(part, steps=1):
    if lax.axis_size("fsdp") != 2:
        return [lax.all_gather(part, "fsdp", axis=0, tiled=True)]
    (other,) = yield (swap(part),), steps
    return [part, other]


def fetch_after(part, after, steps):
    if lax.axis_size("fsdp") != 2:
        return [lax.all_gather(part, "fsdp", axis=0, tiled=True)], after
    after, sent = tie(after, part)
    (after,) = yield (swap(sent),), steps
    return [part, after], after


def joined(parts):
    if len(parts) == 1:
        return parts[0]
    mine, other = parts
    first = lax.axis_index("fsdp") == 0
    return jnp.concatenate([jnp.where(first, mine, other), jnp.where(first, other, mine)], axis=0)


def part_offsets(width):
    if lax.axis_size("fsdp") != 2:
        return [jnp.int32(0)]
    f = lax.axis_index("fsdp")
    return [f * (width // 2), (1 - f) * (width // 2)]


def scatter_products(pairs, block, steps=(), pause=()):
    if lax.axis_size("fsdp") != 2:
        full = [dot(left[0], right, COLS_T).astype(BF16) for left, right in pairs]
        return [
            lax.psum_scatter(g, "fsdp", scatter_dimension=0, tiled=True).astype(F32) for g in full
        ]
    work = []
    for left, right in pairs:
        step = min(block, right.shape[1])
        work += [(left, right[:, at : at + step]) for at in range(0, right.shape[1], step)]
    product = lambda i, part: dot(work[i][0][part], work[i][1], COLS_T)
    done, sent = [], product(0, 1).astype(BF16)
    for i in range(len(work)):
        ahead = [product(i + 1, 1).astype(BF16)] if i + 1 < len(work) else []
        fresh = [product(i - 1, 0) + came.astype(F32)] if i > 0 else []
        if i in pause:
            (sent,) = yield (sent,), pause[i]
        came, *worked = yield (swap(sent), *ahead, *fresh), steps[i] if steps else 1
        if ahead:
            sent = worked.pop(0)
        done += worked
    done.append(product(len(work) - 1, 0) + came.astype(F32))
    sums = []
    for _, right in pairs:
        count = max(1, right.shape[1] // block)
        sums.append(done[0] if count == 1 else jnp.concatenate(done[:count], axis=1))
        done = done[count:]
    return sums


def scatter_rows(full):
    if lax.axis_size("fsdp") != 2:
        return lax.psum_scatter(
            full.astype(BF16), "fsdp", scatter_dimension=0, tiled=True
        ).astype(F32)
    rows = full.shape[0] // 2
    first = lax.axis_index("fsdp") == 0
    low, high = full[:rows], full[rows:]
    (came,) = yield (swap(jnp.where(first, high, low).astype(BF16)),), 1
    return jnp.where(first, low, high) + came.astype(F32)


def group_of(k):
    return lambda t: lax.div(t[4 * k], 4)


def span(t, k, i, count):
    return pl.ds(pl.multiple_of(lax.rem(t[4 * k + i], 4) * count, count), count)


IN_HBM = pl.BlockSpec(memory_space=pltpu.HBM)


def whole(shape):
    return once(shape, lambda *_: (0,) * len(shape))


def first_pair(shape):
    return pl.BlockSpec((1,) + shape, lambda i, t: (jnp.minimum(i, 1),) + (0,) * len(shape))


def last_pair(shape):
    return pl.BlockSpec((1,) + shape, lambda i, t: (jnp.maximum(i - 2, 0),) + (0,) * len(shape))


def split_pairs(i, body, first, last):
    @pl.when(i < 2)
    def _():
        body(first)

    @pl.when(i >= 2)
    def _():
        body(last)


def rotary_table(length):
    half = HD // 2
    steps = jnp.arange(half, dtype=jnp.int32).astype(F32)
    inverse = jnp.exp(steps * (-2.0 * jnp.log(THETA) / HD))
    angles = jnp.arange(length, dtype=jnp.int32).astype(F32)[:, None] * inverse[None, :]
    return jnp.concatenate([jnp.cos(angles), jnp.sin(angles)], axis=1)


def turns(table):
    other = pltpu.roll(table, HD // 2, 1)
    first = lax.broadcasted_iota(jnp.int32, (1, HD), 1) < HD // 2
    return jnp.where(first, table, other), jnp.where(first, -other, table)


def half_turn(v):
    return pltpu.roll(v, HD // 2, 1)


def head_norm(v, gain):
    scale = lax.rsqrt(jnp.mean(v * v, axis=-1, keepdims=True) + EPS)
    return v * scale * gain


def project_kernel(k, hpd, n_kv, n_parts, n_ctx, meta, x0, x1, x2, x3, gain, gq, gk, turn, *refs):
    n_outs = n_parts + 5
    w, beside = refs[:n_parts], refs[n_parts : 2 * n_parts] if n_kv < hpd else ()
    outs, refs = refs[-(2 * n_outs + 2) : -(n_outs + 2)], refs[-(n_outs + 2) :]
    here, rows, sems = refs[:n_outs], refs[-2], refs[-1]
    normed, (raw, scales, query, key, value) = here[:n_parts], here[n_parts:]
    count = x0.shape[0]
    group = pl.ds(pl.multiple_of(lax.div(meta[4 * k], 4) * 4 * count, count), 4 * count)
    places = [pl.ds(4 * k, 4)] * (n_parts + 2) + [(slice(None), group)] * 3
    leaving = [
        pltpu.make_async_copy(here[i], outs[i].at[places[i]], sems.at[i]) for i in range(n_outs)
    ]
    for i, piece in enumerate((x0, x1, x2, x3)):
        x = piece[...].astype(F32)
        r1 = lax.rsqrt(jnp.mean(x * x, axis=-1, keepdims=True) + EPS)
        scales[i] = jnp.broadcast_to(r1, scales.shape[1:])
        rows[i * count : (i + 1) * count, :] = (x * r1 * gain[...]).astype(BF16)
        for p, part in enumerate(normed):
            at = pl.ds(pl.multiple_of(meta[n_ctx + 1 + p], 128), part.shape[2])
            part[i] = rows[i * count : (i + 1) * count, at]
    for copy in leaving[:n_parts]:
        copy.start()
    parts = [part[...].reshape(4 * count, part.shape[2]) for part in normed]
    out = sum(dot(n, w_p[...]) for n, w_p in zip(parts, w))
    other = sum(dot(n, w_p[...]) for n, w_p in zip(parts, beside)) if beside else None
    core = meta[n_ctx]
    for i in range(4):
        at = span(meta, k, i, count)
        cos, sin = turns(turn[at, :])
        block = out[i * count : (i + 1) * count, :]
        raw[i] = block[:, : (hpd + n_kv) * HD]

        def turned(v, gain):
            v = head_norm(v, gain[...])
            return (v * cos + half_turn(v) * sin).astype(BF16)

        for j in range(hpd):
            query[j, at, :] = turned(block[:, j * HD : (j + 1) * HD], gq)
        for j in range(n_kv):
            v = block[:, (hpd + j) * HD : (hpd + j + 1) * HD]
            u = block[:, (hpd + n_kv + j) * HD : (hpd + n_kv + j + 1) * HD]
            head = core if beside else j
            key[head, at, :] = turned(v, gk)
            value[head, at, :] = u.astype(BF16)
        if beside:
            block = other[i * count : (i + 1) * count, :]
            key[1 - core, at, :] = turned(block[:, :HD], gk)
            value[1 - core, at, :] = block[:, HD:].astype(BF16)
    for copy in leaving[n_parts:]:
        copy.start()
    for copy in leaving:
        copy.wait()


def project(k, quarter, w, beside, gain, gq, gk, turn, meta, hpd, n_ctx, before):
    count, width = quarter[0].shape
    length = n_ctx * count
    n_parts = len(w)
    n_kv = 1 if beside else hpd
    group = group_of(k)
    turn_at = once((4 * count, HD), lambda i, t: (group(t), 0))
    head = pltpu.HBM((hpd, length, HD), BF16)
    cols = (hpd + n_kv) * HD
    weights = [*w, *beside]
    return pl.pallas_call(
        functools.partial(project_kernel, k, hpd, n_kv, n_parts, n_ctx),
        grid_spec=pltpu.PrefetchScalarGridSpec(
            num_scalar_prefetch=1,
            grid=(1,),
            in_specs=[whole((count, width))] * 4
            + [whole((1, width)), whole((1, HD)), whole((1, HD)), turn_at]
            + [whole(array.shape) for array in weights]
            + [IN_HBM] * len(before),
            out_specs=[IN_HBM] * (n_parts + 5),
            scratch_shapes=[pltpu.VMEM((4, count, width // n_parts), BF16)] * n_parts
            + [pltpu.VMEM((4, count, cols), F32), pltpu.VMEM((4, count, HD), F32)]
            + [pltpu.VMEM((hpd, 4 * count, HD), BF16)] * 3
            + [pltpu.VMEM((4 * count, width), BF16), pltpu.SemaphoreType.DMA((n_parts + 5,))],
        ),
        out_shape=[pltpu.HBM((n_ctx, count, width // n_parts), BF16)] * n_parts
        + [
            pltpu.HBM((n_ctx, count, cols), F32),
            pltpu.HBM((n_ctx, count, HD), F32),
            head,
            head,
            head,
        ],
        input_output_aliases={9 + len(weights) + i: i for i in range(len(before))},
        compiler_params=params(18),
        cost_estimate=cost(6),
        name="project",
    )(meta, *quarter, gain, gq, gk, turn, *weights, *before)


def first_key(ends, docs, position):
    start = jnp.zeros_like(position)
    for d in range(docs):
        start = jnp.where(position >= ends[d], jnp.maximum(start, ends[d]), start)
    return start


def attend_kernel(docs, heads, bq, bk, ends, query, key, value, mixed, total):
    i = pl.program_id(0)
    positions = i * bq + lax.broadcasted_iota(jnp.int32, (bq, 1), 0)
    starts = first_key(ends, docs, positions)
    low = lax.div(first_key(ends, docs, i * bq), bk)
    high = lax.div((i + 1) * bq - 1, bk) + 1

    def step(j, carry):
        rows = pl.ds(pl.multiple_of(j * bk, bk), bk)
        spots = j * bk + lax.broadcasted_iota(jnp.int32, (1, bk), 1)
        seen = (spots <= positions) & (spots >= starts)
        sums = []
        for h, (acc, norm) in enumerate(carry):
            scores = dot(query[h], key[h, rows, :], ROWS_T)
            p = jnp.where(seen, jnp.exp2(scores * (LOG2E * HD**-0.5)), 0.0)
            acc = acc + dot(p.astype(BF16), value[h, rows, :])
            sums.append((acc, norm + jnp.sum(p, axis=-1, keepdims=True)))
        return tuple(sums)

    start = (jnp.zeros((bq, HD), F32), jnp.zeros((bq, 1), F32))
    first_lane = lax.broadcasted_iota(jnp.int32, (1, HD), 1) == 0
    for h, (acc, norm) in enumerate(lax.fori_loop(low, high, step, (start,) * heads)):
        mixed[h] = acc / norm
        column = jnp.where(first_lane, jnp.log2(norm), 0.0)
        total[h] = row_sums(column)


def row_sums(values):
    return lax.dot_general(
        jnp.ones((8, values.shape[1]), F32),
        values,
        ROWS_T,
        precision=HIGH,
        preferred_element_type=F32,
    )


def attend(query, key, value, ends, bq=256, bk=512):
    heads, length, _ = query.shape
    docs = ends.shape[0]
    block = pl.BlockSpec((heads, bq, HD), lambda i, e: (0, i, 0))
    keys = once((heads, length, HD), lambda i, e: (0, 0, 0))
    line = pl.BlockSpec((heads, 8, bq), lambda i, e: (0, 0, i))
    return pl.pallas_call(
        functools.partial(attend_kernel, docs, heads, bq, bk),
        grid_spec=pltpu.PrefetchScalarGridSpec(
            num_scalar_prefetch=1,
            grid=(length // bq,),
            in_specs=[block, keys, keys],
            out_specs=[block, line],
        ),
        out_shape=[
            jax.ShapeDtypeStruct((heads, length, HD), F32),
            jax.ShapeDtypeStruct((heads, 8, length), F32),
        ],
        compiler_params=params(14),
        cost_estimate=cost(12.5),
        name="attend",
    )(ends, query, key, value)


def attend_back_kernel(
    docs, heads, bq, bk, ends, query, grad, total, delta, key, value, dq, dk, dv, *away
):
    i = pl.program_id(0)

    @pl.when(i == 0)
    def _():
        dk[...] = jnp.zeros_like(dk)
        dv[...] = jnp.zeros_like(dv)

    positions = i * bq + lax.broadcasted_iota(jnp.int32, (1, bq), 1)
    starts = first_key(ends, docs, positions)
    low = lax.div(first_key(ends, docs, i * bq), bk)
    high = lax.div((i + 1) * bq - 1, bk) + 1

    def step(j, sums):
        rows = pl.ds(pl.multiple_of(j * bk, bk), bk)
        spots = j * bk + lax.broadcasted_iota(jnp.int32, (bk, 1), 0)
        seen = (spots <= positions) & (spots >= starts)
        out = []
        for h in range(heads):
            q, g, k = query[h], grad[h], key[h, rows, :]
            scores = dot(k, q, ROWS_T)
            p = jnp.exp2(scores * (LOG2E * HD**-0.5) - total[h, 0:1, :])
            p = jnp.where(seen, p, 0.0)
            ds = (p * (dot(value[h, rows, :], g, ROWS_T) - delta[h, 0:1, :])).astype(BF16)
            dv[h, rows, :] += dot(p.astype(BF16), g)
            dk[h, rows, :] += dot(ds, q)
            out.append(sums[h] + dot(ds, k, COLS_T))
        return tuple(out)

    sums = lax.fori_loop(low, high, step, (jnp.zeros((bq, HD), F32),) * heads)
    for h in range(heads):
        dq[h] = sums[h]

    if away:

        @pl.when(i == pl.num_programs(0) - 1)
        def _():
            other = 1 - ends[docs]
            away[0][0] = dk[other].astype(BF16)
            away[0][1] = dv[other].astype(BF16)


def attend_back(query, grad, total, delta, key, value, ends, shared, bq=256, bk=512):
    heads, length, _ = query.shape
    docs = ends.shape[0] - 1
    block = pl.BlockSpec((heads, bq, HD), lambda i, e: (0, i, 0))
    line = pl.BlockSpec((heads, 8, bq), lambda i, e: (0, 0, i))
    keys = once((heads, length, HD), lambda i, e: (0, 0, 0))
    out = jax.ShapeDtypeStruct((heads, length, HD), F32)
    return pl.pallas_call(
        functools.partial(attend_back_kernel, docs, heads, bq, bk),
        grid_spec=pltpu.PrefetchScalarGridSpec(
            num_scalar_prefetch=1,
            grid=(length // bq,),
            in_specs=[block, block, line, line, keys, keys],
            out_specs=[block, keys, keys] + [whole((2, length, HD))] * shared,
        ),
        out_shape=[out, out, out] + [jax.ShapeDtypeStruct((2, length, HD), BF16)] * shared,
        compiler_params=params(24),
        cost_estimate=cost(17),
        name="attend_back",
    )(ends, query, grad, total, delta, key, value)


def branch_kernel(hpd, table, mixed, w, theirs, mine):
    def body(out):
        total = None
        for j in range(hpd):
            part = dot(mixed[j].astype(BF16), w[j * HD : (j + 1) * HD, :])
            total = part if total is None else total + part
        out[0] = total.astype(BF16)

    split_pairs(pl.program_id(0), body, theirs, mine)


def branch(k, mixed, w, table, count):
    hpd = mixed.shape[0]
    width = w.shape[1]
    pair = jax.ShapeDtypeStruct((2, count, width), BF16)
    theirs, mine = pl.pallas_call(
        functools.partial(branch_kernel, hpd),
        grid_spec=pltpu.PrefetchScalarGridSpec(
            num_scalar_prefetch=1,
            grid=(4,),
            in_specs=[
                pl.BlockSpec((hpd, count, HD), lambda i, t: (0, t[4 * k + (i ^ 2)], 0)),
                whole((hpd * HD, width)),
            ],
            out_specs=[first_pair((count, width)), last_pair((count, width))],
        ),
        out_shape=[pair, pair],
        compiler_params=params(10),
        cost_estimate=cost(2.4),
        name="branch",
    )(table, mixed, w)
    return mine, theirs


def branch_back_kernel(k, hpd, meta, g0, g1, g2, g3, mixed, w, *refs):
    grad, delta, dw = refs[-3:]
    pieces = (g0, g1, g2, g3)
    count = g0.shape[0]
    g = jnp.concatenate([piece[...] for piece in pieces], axis=0)
    back = dot(g, w[...], ROWS_T).astype(BF16)
    for j in range(hpd):
        heads = []
        for i in range(4):
            at = span(meta, k, i, count)
            own = back[i * count : (i + 1) * count, j * HD : (j + 1) * HD]
            out = mixed[j, at, :]
            grad[j, at, :] = own
            delta[j, :, at] = row_sums(own.astype(F32) * out)
            heads.append(out.astype(BF16))
        part = dot(jnp.concatenate(heads, axis=0), g, COLS_T)
        rows = slice(j * HD, (j + 1) * HD)
        dw[rows, :] = part if len(refs) == 3 else refs[0][rows, :] + part


def branch_back(k, quarter, mixed, w, table, before):
    count, width = quarter[0].shape
    hpd, length, _ = mixed.shape
    group = group_of(k)
    head_at = once((hpd, 4 * count, HD), lambda i, t: (0, group(t), 0))
    dw_at = whole((hpd * HD, width))
    grad, delta, dw = pl.pallas_call(
        functools.partial(branch_back_kernel, k, hpd),
        grid_spec=pltpu.PrefetchScalarGridSpec(
            num_scalar_prefetch=1,
            grid=(1,),
            in_specs=[whole((count, width))] * 4
            + [head_at, whole((hpd * HD, width))]
            + ([dw_at] + [pl.BlockSpec(memory_space=pl.ANY)] * 2 if before else []),
            out_specs=[
                head_at,
                once((hpd, 8, 4 * count), lambda i, t: (0, 0, group(t))),
                dw_at,
            ],
        ),
        out_shape=[
            jax.ShapeDtypeStruct((hpd, length, HD), BF16),
            jax.ShapeDtypeStruct((hpd, 8, length), F32),
            jax.ShapeDtypeStruct((hpd * HD, width), F32),
        ],
        input_output_aliases={8: 0, 9: 1} if before else {},
        compiler_params=params(20),
        cost_estimate=cost(6),
        name="branch_back",
    )(table, *quarter, mixed, w, *before)
    return dw, grad, delta


def experts_kernel(
    k, n_parts, width, capacity, n_exp, meta, x0, x1, x2, x3, g0, g1, g2, g3, router, *refs
):
    n = n_parts
    w_from = refs[: 3 * n]
    refs = refs[-(2 * n + 5 + 6 * n + 3 + 3) :]
    outs, (mine, theirs) = refs[: 2 * n + 3], refs[2 * n + 3 : 2 * n + 5]
    refs = refs[2 * n + 5 :]
    w_here, refs = refs[: 3 * n], refs[3 * n :]
    rows, pairs, picked, refs = refs[:n], refs[n : 2 * n], refs[2 * n : 3 * n], refs[3 * n :]
    hidden, gate_grad, up_grad, chosen_ref, gate_ref, sems = refs
    slots = 4 * capacity
    part = width // n
    c = meta[0]
    lanes = lax.broadcasted_iota(jnp.int32, (1, 128), 1)
    pieces = (x0, x1, x2, x3)
    arrivals = [
        pltpu.make_async_copy(w_from[i], w_here[i], sems.at[i]) for i in range(3 * n)
    ]
    for copy in arrivals:
        copy.start()
    here = [*rows, *pairs, hidden, gate_grad, up_grad]
    leaving = [
        pltpu.make_async_copy(
            here[i], outs[i].at[pl.ds(k * slots, slots), :], sems.at[3 * n + i]
        )
        for i in range(2 * n + 3)
    ]

    def columns(p, first=0):
        return pl.ds(pl.multiple_of(first + meta[1 + p], 128), part)

    for i, x_ref in enumerate(pieces):
        cot = (g0, g1, g2, g3)[i]
        at = slice(i * capacity, (i + 1) * capacity)
        info = x_ref[:, width:].astype(F32)
        place = jnp.sum(jnp.where(lanes == c, info, 0.0), axis=1, keepdims=True)
        spots = lax.broadcasted_iota(jnp.int32, (1, capacity), 1).astype(F32)
        chosen = (spots == place).astype(BF16)
        chosen_ref[i] = chosen
        logits = dot(x_ref[:, :width], router[...])
        seen = info > -1.5
        top = jnp.max(jnp.where(seen, logits, -1e30), axis=1, keepdims=True)
        shares = jnp.where(seen, jnp.exp(logits - top), 0.0)
        gates = shares / jnp.sum(shares, axis=1, keepdims=True)
        own = jnp.sum(jnp.where(lanes == c, gates, 0.0), axis=1, keepdims=True)
        gate = lax.dot_general(
            chosen.astype(F32),
            jnp.broadcast_to(own, gates.shape),
            COLS_T,
            precision=HIGH,
            preferred_element_type=F32,
        )
        gate_ref[at, :] = gate
        for p in range(n):
            rows[p][at, :] = dot(chosen, x_ref[:, columns(p)], COLS_T).astype(BF16)
            grads = dot(chosen, cot[:, columns(p)], COLS_T)
            picked[p][at, :] = grads.astype(BF16)
            pairs[p][at, :] = (grads * gate[:, :1]).astype(BF16)
    for copy in leaving[: 2 * n]:
        copy.start()
    for copy in arrivals[: 2 * n]:
        copy.wait()
    wg, wu, wd = (w_here[n * i : n * (i + 1)] for i in range(3))
    gate_part = sum(dot(rows[p][...], wg[p][...]) for p in range(n))
    up_part = sum(dot(rows[p][...], wu[p][...]) for p in range(n))
    sigma = jax.nn.sigmoid(gate_part)
    silu_gate = gate_part * sigma
    h = (silu_gate * up_part).astype(BF16)
    hidden[...] = h
    leaving[2 * n].start()
    for copy in arrivals[2 * n :]:
        copy.wait()
    hidden_grad = sum(dot(pairs[p][...], wd[p][...]) for p in range(n))
    gg = (hidden_grad * up_part * sigma * (1.0 + gate_part * (1.0 - sigma))).astype(BF16)
    gate_grad[...] = gg
    leaving[2 * n + 1].start()
    ug = (hidden_grad * silu_gate).astype(BF16)
    up_grad[...] = ug
    leaving[2 * n + 2].start()
    inner_sum = jnp.zeros((slots, 1), F32)
    for p in range(n):
        out = dot(h, wd[p][...], ROWS_T).astype(BF16).astype(F32)
        inner_sum += jnp.sum(out * picked[p][...].astype(F32), axis=1, keepdims=True)
        scaled = (out * gate_ref[:, :1]).astype(BF16)
        row_sum = (dot(gg, wg[p][...], ROWS_T) + dot(ug, wu[p][...], ROWS_T)).astype(BF16)
        for i in range(4):
            back = (mine, theirs)[i // 2].at[i % 2]
            at = slice(i * capacity, (i + 1) * capacity)
            back[:, columns(p)] = dot(chosen_ref[i], row_sum[at, :]).astype(BF16)
            back[:, columns(p, width + 128)] = dot(chosen_ref[i], scaled[at, :]).astype(BF16)
    high = inner_sum.astype(BF16).astype(F32)
    extra = jnp.where(lanes == c, high, 0.0) + jnp.where(
        lanes == c + n_exp, inner_sum - high, 0.0
    )
    extra = extra.astype(BF16)
    for i in range(4):
        back = (mine, theirs)[i // 2].at[i % 2]
        at = slice(i * capacity, (i + 1) * capacity)
        back[:, width : width + 128] = dot(chosen_ref[i], extra[at, :]).astype(BF16)
    for copy in leaving:
        copy.wait()


def experts(k, quarter, cots, router, wg, wu, wd, meta, capacity, n_exp, nz, before):
    count, wide = quarter[0].shape
    width = cots[0].shape[1]
    n_parts = len(wg)
    part = width // n_parts
    hid = wg[0].shape[1]
    slots = 4 * capacity
    anywhere = pl.BlockSpec(memory_space=pl.ANY)
    pair = once((2, count, wide + width), lambda i, m: (0, 0, 0))
    rows_all = lambda cols: pltpu.HBM((nz * slots, cols), BF16)
    n_out = 2 * n_parts + 3
    outs = pl.pallas_call(
        functools.partial(experts_kernel, k, n_parts, width, capacity, n_exp),
        grid_spec=pltpu.PrefetchScalarGridSpec(
            num_scalar_prefetch=1,
            grid=(1,),
            in_specs=[whole((count, wide))] * 4
            + [whole((count, width))] * 4
            + [whole(router.shape)]
            + [anywhere] * (3 * n_parts)
            + [IN_HBM] * len(before),
            out_specs=[IN_HBM] * n_out + [pair, pair],
            scratch_shapes=[pltpu.VMEM((part, hid), BF16)] * (3 * n_parts)
            + [pltpu.VMEM((slots, part), BF16)] * (3 * n_parts)
            + [pltpu.VMEM((slots, hid), BF16)] * 3
            + [
                pltpu.VMEM((4, count, capacity), BF16),
                pltpu.VMEM((slots, 128), F32),
                pltpu.SemaphoreType.DMA((5 * n_parts + 3,)),
            ],
        ),
        out_shape=[rows_all(part)] * (2 * n_parts)
        + [rows_all(hid)] * 3
        + [jax.ShapeDtypeStruct((2, count, wide + width), BF16)] * 2,
        input_output_aliases={10 + 3 * n_parts + i: i for i in range(len(before))},
        compiler_params=params(34),
        cost_estimate=cost(15),
        name="experts",
    )(meta, *quarter, *cots, router, *wg, *wu, *wd, *before)
    return (outs[n_out], outs[n_out + 1]), outs[:n_out]


def head_back(grad, v, gain, cos, sin):
    scale = lax.rsqrt(jnp.mean(v * v, axis=-1, keepdims=True) + EPS)
    d = grad * cos - half_turn(grad) * sin
    u = d * gain
    inner = jnp.mean(u * v, axis=-1, keepdims=True)
    back = scale * u - v * (scale * scale * scale * inner)
    return back.astype(BF16), jnp.sum(d * v * scale, axis=0, keepdims=True)


def key_back_kernel(meta, dk, dv, raw, turn, gk, *refs):
    out, gains = refs[-2:]
    came = refs[:-2]
    z = pl.program_id(0)

    @pl.when(z == 0)
    def _():
        gains[...] = jnp.zeros_like(gains)

    n_kv = dk.shape[0]
    count = raw.shape[1]
    for i in range(4):
        at = pl.ds(pl.multiple_of(lax.rem(meta[4 * z + i], 4) * count, count), count)
        for j in range(n_kv):
            v = raw[i, :, j * HD : (j + 1) * HD]
            key_grad, value_grad = dk[j, at, :], dv[j, at, :]
            if came:
                key_grad = key_grad + came[0][0, at, :].astype(F32)
                value_grad = value_grad + came[0][1, at, :].astype(F32)
            grad = key_grad * HD**-0.5
            back, gain = head_back(grad, v, gk[...], *turns(turn[at, :]))
            out[i, :, j * HD : (j + 1) * HD] = back
            gains[0:1, :] += gain
            out[i, :, (n_kv + j) * HD : (n_kv + j + 1) * HD] = value_grad.astype(BF16)


def key_back(dk, dv, came, raw, turn, gk, meta):
    hpd = dk.shape[0]
    n_kv = 1 if came else hpd
    n_ctx, count, _ = raw.shape
    group = lambda z, t: lax.div(t[4 * z], 4)
    head_at = pl.BlockSpec(
        (n_kv, 4 * count, HD), lambda z, t: (t[n_ctx] if came else 0, group(z, t), 0)
    )
    turn_at = pl.BlockSpec((4 * count, HD), lambda z, t: (group(z, t), 0))
    return pl.pallas_call(
        key_back_kernel,
        grid_spec=pltpu.PrefetchScalarGridSpec(
            num_scalar_prefetch=1,
            grid=(n_ctx // 4,),
            in_specs=[
                head_at,
                head_at,
                pl.BlockSpec((4, count, n_kv * HD), lambda z, t: (z, 0, hpd // n_kv)),
                turn_at,
                whole((1, HD)),
            ]
            + [pl.BlockSpec((2, 4 * count, HD), lambda z, t: (0, group(z, t), 0))] * len(came),
            out_specs=[
                pl.BlockSpec((4, count, 2 * n_kv * HD), lambda z, t: (z, 0, 0)),
                whole((8, HD)),
            ],
        ),
        out_shape=[
            jax.ShapeDtypeStruct((n_ctx, count, 2 * n_kv * HD), BF16),
            jax.ShapeDtypeStruct((8, HD), F32),
        ],
        compiler_params=params(14),
        cost_estimate=cost(5),
        name="key_back",
    )(meta, dk, dv, raw, turn, gk, *came)


def input_back_kernel(k, hpd, meta, dq, kv, raw, scales, turn, gq, w, *refs):
    x, (grads_out, theirs, mine, gains, gain_grad, rows, grads, sem) = refs[:4], refs[-8:]
    copy = pltpu.make_async_copy(grads, grads_out.at[pl.ds(4 * k, 4)], sem)
    count = raw.shape[1]
    q_cols = hpd * HD

    @pl.when(pl.program_id(0) == 0)
    def _():
        gains[...] = jnp.zeros_like(gains)
        for i in range(4):
            at = span(meta, k, i, count)
            for j in range(hpd):
                cols = slice(j * HD, (j + 1) * HD)
                grad = dq[j, at, :] * HD**-0.5
                back, gain = head_back(grad, raw[i, :, cols], gq[...], *turns(turn[at, :]))
                grads[i, :, cols] = back
                gains[0:1, :] += gain
            rows[i * count : (i + 1) * count, :q_cols] = grads[i]
            rows[i * count : (i + 1) * count, q_cols:] = kv[i]
        copy.start()

    @pl.when(pl.program_id(0) == pl.num_programs(0) - 1)
    def _():
        copy.wait()

    back = dot(rows[...], w[...], ROWS_T)
    total = None
    for i in range(4):
        block = back[i * count : (i + 1) * count, :]
        (mine, theirs)[i // 2][i % 2] = block.astype(BF16)
        term = jnp.sum(block * x[i][...].astype(F32) * scales[i, :, :1], axis=0, keepdims=True)
        total = term if total is None else total + term
    gain_grad[...] = jnp.broadcast_to(total, gain_grad.shape)


def input_back(k, quarter, dq, kv, raw, scales, turn, gq, w, meta, before):
    count, width = quarter[0].shape
    hpd = dq.shape[0]
    n_ctx = raw.shape[0]
    q_cols = hpd * HD
    chunk = width // 4
    group = group_of(k)
    turn_at = pl.BlockSpec((4 * count, HD), lambda i, t: (group(t), 0))
    own = lambda cols: pl.BlockSpec((4, count, cols), lambda i, t: (k, 0, 0))
    pair_at = pl.BlockSpec((2, count, chunk), lambda i, t: (0, 0, i))
    pair = jax.ShapeDtypeStruct((2, count, width), BF16)
    outs = pl.pallas_call(
        functools.partial(input_back_kernel, k, hpd),
        grid_spec=pltpu.PrefetchScalarGridSpec(
            num_scalar_prefetch=1,
            grid=(4,),
            in_specs=[
                pl.BlockSpec((hpd, 4 * count, HD), lambda i, t: (0, group(t), 0)),
                own(kv.shape[2]),
                own(q_cols),
                own(HD),
                turn_at,
                whole((1, HD)),
                pl.BlockSpec((chunk, w.shape[1]), lambda i, t: (i, 0)),
            ]
            + [pl.BlockSpec((count, chunk), lambda i, t: (0, i))] * 4
            + [IN_HBM] * len(before),
            out_specs=[
                IN_HBM,
                pair_at,
                pair_at,
                whole((8, HD)),
                pl.BlockSpec((8, chunk), lambda i, t: (0, i)),
            ],
            scratch_shapes=[
                pltpu.VMEM((4 * count, w.shape[1]), BF16),
                pltpu.VMEM((4, count, q_cols), BF16),
                pltpu.SemaphoreType.DMA(()),
            ],
        ),
        out_shape=[
            pltpu.HBM((n_ctx, count, q_cols), BF16),
            pair,
            pair,
            jax.ShapeDtypeStruct((8, HD), F32),
            jax.ShapeDtypeStruct((8, width), F32),
        ],
        input_output_aliases={12: 0} if before else {},
        compiler_params=params(18),
        cost_estimate=cost(6),
        name="input_back",
    )(meta, dq, kv, raw, scales, turn, gq, w, *quarter, *before)
    grads, theirs, mine, gains, gain_grad = outs
    return (mine, theirs), grads, gains, gain_grad


def place_kernel(parts, n_kv, table, *refs):
    columns, keys = refs[:4], refs[4 : 4 + n_kv]
    outs = refs[-3:] if n_kv else refs[-1:]
    for n in range(4):

        @pl.when(pl.program_id(0) // parts == n)
        def _():
            outs[0][...] = columns[n][...].astype(F32)
            if n_kv:
                outs[1][...] = keys[n][:, :HD].astype(F32)
                outs[2][...] = keys[n][:, HD:].astype(F32)


def place_columns(k, quarter, table, n_ctx, rows, before):
    all_rows, cols = quarter[0].shape
    parts = cols // HD
    kv_rows = all_rows - rows

    def piece_at(n):
        return lambda i, t: (0, jnp.clip(i - n * parts, 0, parts - 1))

    def head_at(i, t):
        c = t[4 * k + i // parts]
        rows_part = lax.rem(c // 4, 2) * 2 + lax.rem(c // 2, 2)
        return rows_part, lax.rem(c, 2) * 2 + c // 8

    out_specs = [
        pl.BlockSpec((rows, HD), lambda i, t: (0, (i % parts) * n_ctx + t[4 * k + i // parts]))
    ]
    out_shape = [jax.ShapeDtypeStruct((rows, n_ctx * cols), F32)]
    in_specs = [pl.BlockSpec((rows, HD), piece_at(n)) for n in range(4)]
    pieces = list(quarter)
    if kv_rows:
        in_specs += [once((kv_rows, cols), lambda i, t: (rows // kv_rows, 0))] * 4
        pieces += quarter
        out_specs += [pl.BlockSpec((kv_rows, HD), head_at)] * 2
        out_shape += [jax.ShapeDtypeStruct((rows, KVH * HD), F32)] * 2
    return pl.pallas_call(
        functools.partial(place_kernel, parts, len(pieces) - 4),
        grid_spec=pltpu.PrefetchScalarGridSpec(
            num_scalar_prefetch=1,
            grid=(4 * parts,),
            in_specs=in_specs + [pl.BlockSpec(memory_space=pl.ANY)] * len(before),
            out_specs=out_specs,
        ),
        out_shape=out_shape,
        input_output_aliases={1 + len(pieces) + i: i for i in range(len(before))},
        compiler_params=params(12),
        cost_estimate=cost(4.6),
        name="place_columns",
    )(table, *pieces, *before)


def place_rows_kernel(table, *refs):
    out = refs[-1]
    for n in range(4):

        @pl.when(pl.program_id(0) == n)
        def _():
            out[...] = refs[n][...].astype(F32)


def place_rows(quarters, table):
    rows, cols = quarters[0][0].shape
    placed = ()
    for k, quarter in enumerate(quarters):
        placed = pl.pallas_call(
            place_rows_kernel,
            grid_spec=pltpu.PrefetchScalarGridSpec(
                num_scalar_prefetch=1,
                grid=(4,),
                in_specs=[whole((rows, cols))] * 4 + [IN_HBM] * len(placed),
                out_specs=[pl.BlockSpec((rows, cols), lambda i, t, k=k: (t[4 * k + i], 0))],
            ),
            out_shape=[pltpu.HBM((4 * len(quarters) * rows, cols), F32)],
            input_output_aliases={5: 0} if placed else {},
            compiler_params=params(10),
            cost_estimate=cost(2.4),
            name="place_rows",
        )(table, *quarter, *placed)
    return placed[0]


def local(
    inputs,
    w_query,
    w_key,
    w_value,
    w_output,
    norm_attn,
    gain_query,
    gain_key,
    w_router,
    norm_moe,
    w_gate,
    w_up,
    w_down,
    lengths,
    routes,
    pair_order,
    cotangent,
):
    n_ctx = lax.axis_size("ctx")
    n_f = lax.axis_size("fsdp")
    c = lax.axis_index("ctx")
    f = lax.axis_index("fsdp")
    count, width = inputs.shape[1], inputs.shape[2]
    length = count * n_ctx
    nz = n_ctx // 4
    later = scatter_order(n_ctx)
    hpd = H // n_ctx
    hpf = H // n_f
    group = H // KVH
    n_exp = w_router.shape[1]
    capacity = 5 * count * TOPK // (4 * n_exp)
    table = block_order(n_ctx)
    core = c % 2

    heads = [c % hpf + hpf * ((c // hpf) * hpd + j) for j in range(hpd)]
    kv_heads = [h // group for h in heads]
    columns = lambda w, h: lax.dynamic_slice_in_dim(w, h * HD, HD, 1)
    shared = n_f == 2 and hpd == 2
    if shared:
        kv_own = heads[0] // group + core * (KVH // 2)
        w_part = jnp.concatenate(
            [columns(w_query, h) for h in heads]
            + [columns(w_key, kv_own), columns(w_value, kv_own)],
            axis=1,
        )
    else:
        w_part = jnp.concatenate(
            [columns(w_query, h) for h in heads]
            + [columns(w_key, h) for h in kv_heads]
            + [columns(w_value, h) for h in kv_heads],
            axis=1,
        )
    w_part, norm_first = tie(w_part, norm_attn)
    vectors = jnp.concatenate([norm_first, gain_query, gain_key, norm_moe])
    if n_f == 2:
        vectors = joined([vectors[None], swap(vectors[None])])
        router = joined([w_router, swap(w_router)])
    else:
        vectors = lax.all_gather(vectors, "fsdp", axis=0)
        router = lax.all_gather(w_router, "fsdp", axis=0, tiled=True)
    sizes = [norm_attn.shape[0], gain_query.shape[0], gain_key.shape[0], norm_moe.shape[0]]
    rows_of, at = [], 0
    for size in sizes:
        rows_of.append(vectors[:, at : at + size].reshape(1, n_f * size).astype(F32))
        at += size
    attn_gain, query_gain, key_gain, moe_gain = rows_of
    router_wide = jnp.pad(router, ((0, 0), (0, 128 - n_exp)))
    offsets = part_offsets(width)
    n_parts = len(offsets)
    meta_rows = jnp.concatenate([table, jnp.stack([core] + offsets).astype(jnp.int32)])
    q_cols = hpd * HD
    block = w_gate.shape[2] // 3
    weights = {}

    def fetch_weights():
        parts = yield from fetch(w_part, 2)
        weights["qkv"], weights["beside"] = parts, []
        if shared:
            weights["beside"] = [
                lax.ppermute(part[:, q_cols:], "ctx", flip(n_ctx, 1)) for part in parts
            ]
        weights["back"] = joined(parts)
        own_rows = lax.dynamic_slice_in_dim(w_output, (c % hpf) * HD, HD, 0)
        rows_parts = yield from fetch(own_rows)
        last = rows_parts[-1]
        w_out = joined(rows_parts)
        weights["out"] = lax.dynamic_slice_in_dim(w_out, (c // hpf) * hpd * HD, hpd * HD, 0)
        weights["gate"], last = yield from fetch_after(w_gate[0], last, 2)
        weights["up"], last = yield from fetch_after(w_up[0], last, 4)
        weights["down"], last = yield from fetch_after(w_down[0], last, 3)

    gathered = {}

    def gather_cotangents():
        (cot,) = yield (cotangent[0],), 3
        yield from gather_planned(cot, n_ctx, COTANGENT_PLAN, gathered)

    sides = [Side(fetch_weights()), Side(gather_cotangents())]

    experts_of = jnp.arange(n_exp, dtype=jnp.int32)
    picks = routes[0][:, :, None] == experts_of
    ranks = jnp.sum(
        jnp.where(picks, pair_order[0, 0].reshape(count, TOPK, 1), 0), axis=1
    )
    chosen = jnp.any(picks, axis=1)
    ranks = jnp.where(chosen, ranks, count * TOPK)
    place = jnp.sum((ranks[None, :, :] < ranks[:, None, :]).astype(jnp.int32), axis=1)
    place = jnp.where(chosen, jnp.where(place < capacity, place, -1), -2)
    place = jnp.pad(place, ((0, 0), (0, 128 - n_exp)), constant_values=-2).astype(BF16)

    ends = jnp.cumsum(lengths[0]).astype(jnp.int32)
    turn = rotary_table(length)

    xs = {}

    def through_projection(k, quarter, token, before):
        xs[k] = quarter
        if k == 0:
            return ()
        if k == 1:
            before = projection(0, token, ())
        return projection(k, token, before)

    def projection(k, token, before):
        return project(
            k,
            xs[k],
            weights["qkv"],
            weights["beside"],
            attn_gain,
            query_gain,
            key_gain,
            turn,
            token,
            hpd,
            n_ctx,
            before,
        )

    straight = list(range(nz))
    *normed, raw, scales, query, key, value = pipeline(
        n_ctx, straight, through_projection, meta_rows, sides, piece=inputs[0]
    )
    mixed, log_total = attend(query, key, value, ends)
    _, (mixed,) = land({}, sides, mixed)
    x = inputs[0].astype(F32)
    branch_sum, _ = pipeline(
        n_ctx,
        later,
        lambda k, _, token, state: (branch(k, mixed, weights["out"], token, count), state),
        table,
        sides,
        scatter=True,
    )
    middle = x + branch_sum
    moe_scale = lax.rsqrt(jnp.mean(middle * middle, axis=-1, keepdims=True) + EPS)
    routed_in = (middle * moe_scale * moe_gain).astype(BF16)

    pad_offsets = (offsets + [jnp.int32(0)])[:2]
    head_meta = [jnp.stack([c] + pad_offsets).astype(jnp.int32)]
    expert_meta = jnp.concatenate(head_meta)

    def through_experts(k, quarter, token, before):
        return experts(
            k,
            quarter,
            planned_quarter(gathered, k, n_ctx),
            router_wide,
            weights["gate"],
            weights["up"],
            weights["down"],
            token,
            capacity,
            n_exp,
            nz,
            before,
        )

    routed_grad, seen = pipeline(
        n_ctx,
        later,
        through_experts,
        expert_meta,
        sides,
        piece=jnp.concatenate([routed_in, place], axis=1),
        scatter=True,
        along=True,
    )
    rows, pairs = seen[:n_parts], seen[n_parts : 2 * n_parts]
    hidden, gate_part_grad, up_part_grad = seen[2 * n_parts :]
    outputs = (middle + routed_grad[:, width + 128 :]).astype(BF16)

    gate_grad = routed_grad[:, width : width + n_exp] + routed_grad[
        :, width + n_exp : width + 2 * n_exp
    ]
    routed_grad = routed_grad[:, :width]
    logits = dot(routed_in, router)
    top = jnp.max(jnp.where(chosen, logits, -1e30), axis=-1, keepdims=True)
    shares = jnp.where(chosen, jnp.exp(logits - top), 0.0)
    gates = shares / jnp.sum(shares, axis=-1, keepdims=True)
    logit_grad = gates * (gate_grad - jnp.sum(gates * gate_grad, axis=-1, keepdims=True))
    routed_grad = routed_grad + lax.dot_general(
        logit_grad, router.astype(F32), ROWS_T, precision=HIGH
    )
    router_part = lax.dot_general(
        logit_grad, routed_in.astype(F32), COLS_T, precision=HIGH
    )

    grad_out = cotangent[0].astype(F32)
    moe_scaled = routed_grad * moe_gain
    moe_part = jnp.sum(routed_grad * middle * moe_scale, axis=0, keepdims=True)
    middle_grad = (
        grad_out
        + moe_scale * moe_scaled
        - middle
        * (
            moe_scale
            * moe_scale
            * moe_scale
            * jnp.mean(moe_scaled * middle, axis=-1, keepdims=True)
        )
    )

    grads, sums = {}, []

    def scatter_grads():
        pairs_of = [(rows, gate_part_grad), (rows, up_part_grad), (pairs, hidden)]
        sums_of = yield from scatter_products(
            pairs_of, block, (1, 1, 1, 1, 1, 2, 1, 1, 1), {6: 3}
        )
        grads["gate"], grads["up"], grads["down"] = sums_of

    sides = [
        Side(scatter_grads()),
        Side(sum_all(jnp.concatenate([router_part, moe_part], axis=0), sums)),
    ]
    grad_out_w, mixed_grad, delta = pipeline(
        n_ctx,
        straight,
        lambda k, quarter, token, before: branch_back(
            k, quarter, mixed, weights["out"], token, before
        ),
        table,
        sides,
        piece=middle_grad.astype(BF16),
    )
    def sum_out_grad():
        if n_f == hpd:
            placed = grad_out_w
        else:
            spread_out = jnp.arange(n_f, dtype=jnp.int32)[:, None] == (
                (c // hpf) * hpd + jnp.arange(hpd, dtype=jnp.int32)[None, :]
            )
            placed = jnp.einsum(
                "fj,jrd->frd", spread_out.astype(F32), grad_out_w.reshape(hpd, HD, width)
            ).reshape(n_f * HD, width)
        own = yield from scatter_rows(placed)
        own = own.astype(BF16)
        if n_ctx == hpf:
            arrays = {}
            yield from gather_planned(own, n_ctx, OUTPUT_GRAD_PLAN, arrays)
            quarters = [planned_quarter(arrays, k, n_ctx) for k in range(nz)]
            grads["out"] = place_rows(quarters, table)
        else:
            whole_grad = lax.all_gather(own, "ctx", axis=0).reshape(-1, hpf * HD, width)
            mine = lax.dynamic_index_in_dim(whole_grad, f // hpd, 0, keepdims=False)
            grads["out"] = mine.astype(F32)

    sides.append(Side(sum_out_grad()))
    ends_and_core = jnp.concatenate([ends, core[None].astype(jnp.int32)])
    dq, dk, dv, *away = attend_back(
        query, mixed_grad, log_total, delta, key, value, ends_and_core, int(shared)
    )
    _, (dq, dk, dv, *away) = land({}, sides, dq, dk, dv, *away)
    came = [lax.ppermute(array, "ctx", flip(n_ctx, 1)) for array in away]
    kv_grad, key_gains = key_back(dk, dv, came, raw, turn, key_gain, meta_rows)
    normed_flat = [n.reshape(length, -1) for n in normed]

    def sum_key_grads():
        (grad_kv,) = yield from scatter_products(
            [(normed_flat, kv_grad.reshape(length, -1))], kv_grad.shape[-1]
        )
        if not shared:
            slots_kv = jnp.arange(KVH, dtype=jnp.int32)
            spread = jnp.stack([slots_kv == h for h in kv_heads]).astype(F32)
            grad_kv = grad_kv.reshape(width // n_f, 2, hpd, 1, HD) * spread[None, None, :, :, None]
            grad_kv = jnp.sum(grad_kv, axis=2).reshape(width // n_f, 2 * KVH * HD)
            grad_kv = lax.psum(grad_kv.astype(BF16), "ctx").astype(F32)
            grads["key"], grads["value"] = grad_kv[:, : KVH * HD], grad_kv[:, KVH * HD :]
            return
        for bit in (4, 2):
            rows_kept = grad_kv.shape[0] // 2
            side = (c // bit) % 2
            kept = lax.dynamic_slice_in_dim(grad_kv, side * rows_kept, rows_kept, 0)
            gone = lax.dynamic_slice_in_dim(grad_kv, (1 - side) * rows_kept, rows_kept, 0)
            (got,) = yield (lax.ppermute(gone.astype(BF16), "ctx", flip(n_ctx, bit)),), 1
            grad_kv = kept + got.astype(F32)
        grads["key_piece"] = grad_kv.astype(BF16)

    sides.append(Side(sum_key_grads()))
    gain_parts, attn_parts = [], []

    def through_inputs(k, _, token, before):
        back, q_grad, gains, gain_grad = input_back(
            k,
            xs[k],
            dq,
            kv_grad,
            raw,
            scales,
            turn,
            query_gain,
            weights["back"],
            token,
            before,
        )
        gain_parts.append(gains)
        attn_parts.append(gain_grad)
        if len(gain_parts) == nz:
            gain_rows = jnp.concatenate([sum(gain_parts)[:1], key_gains[:1]], axis=1)
            gain_rows = jnp.pad(gain_rows, ((0, 0), (0, width - 2 * HD)))
            rows_last = [sum(attn_parts)[:1], gain_rows]
            sides.append(Side(sum_all(jnp.concatenate(rows_last, axis=0), sums)))
        return back, (q_grad,)

    q_grads = []

    def through_inputs_last(k, quarter, token, before):
        back, state = through_inputs(k, quarter, token, before)
        q_grads[:] = state
        return back, state

    def query_products():
        q_flat = q_grads[0].reshape(length, -1)
        if n_f != 2:
            full = dot(normed_flat[0], q_flat, COLS_T).astype(BF16)
            return (lax.psum_scatter(full, "fsdp", scatter_dimension=0, tiled=True),)
        mine, other = normed_flat
        came = swap(dot(other, q_flat, COLS_T).astype(BF16))
        return dot(mine, q_flat, COLS_T), came

    def gather_query_grads(*products):
        own = sum(product.astype(F32) for product in products).astype(BF16)
        if n_ctx == hpf:
            sides.append(Side(gather_columns(own)))
            return
        grads["query"] = (
            lax.all_gather(own, "ctx", axis=0)
            .reshape(n_ctx // hpf, hpf, width // n_f, hpd, HD)
            .transpose(2, 0, 3, 1, 4)
            .reshape(width // n_f, H * HD)
            .astype(F32)
        )

    def gather_columns(own):
        q_rows = own.shape[0]
        if shared:
            own = jnp.concatenate([own, grads["key_piece"]], axis=0)
        arrays, placed = {}, ()
        chain = gather_planned(own, n_ctx, QUERY_GRAD_PLAN, arrays)
        going, steps = next(chain)
        for k in range(nz):
            landed = yield (*going, *placed), steps
            placed = landed[len(going) :]
            try:
                going, steps = chain.send(landed[: len(going)])
            except StopIteration:
                going = ()
            quarter = planned_quarter(arrays, k, n_ctx)
            placed = place_columns(k, quarter, table, n_ctx, q_rows, placed)
        grads["query"] = placed[0]
        if shared:
            grads["key"], grads["value"] = placed[1:]

    normed_grad, _ = pipeline(
        n_ctx,
        later,
        through_inputs_last,
        meta_rows,
        sides,
        scatter=True,
        closing=(query_products, gather_query_grads),
    )
    while any(side.flying is not None for side in sides):
        land({}, sides)
    early, late = sums
    own_part = lambda v, size: lax.dynamic_slice_in_dim(v, f * (size // n_f), size // n_f, 0)
    grad_w_router = own_part(early[:n_exp].T, width)
    grad_norm_moe = own_part(early[n_exp], width)
    grad_norm_attn = own_part(late[0], width)
    grad_gain_query = own_part(late[1, :HD], HD)
    grad_gain_key = own_part(late[1, HD : 2 * HD], HD)

    attn_scale = lax.rsqrt(jnp.mean(x * x, axis=-1, keepdims=True) + EPS)
    attn_scaled = normed_grad * attn_gain
    input_grad = (
        middle_grad
        + attn_scale * attn_scaled
        - x
        * (
            attn_scale
            * attn_scale
            * attn_scale
            * jnp.mean(attn_scaled * x, axis=-1, keepdims=True)
        )
    )
    return (
        outputs[None],
        input_grad.astype(BF16)[None],
        grads["query"],
        grads["key"],
        grads["value"],
        grads["out"],
        grad_norm_attn,
        grad_gain_query,
        grad_gain_key,
        grad_w_router,
        grad_norm_moe,
        grads["gate"][None],
        grads["up"][None],
        grads["down"][None],
    )


def solution(mesh):
    in_specs = (
        P("fsdp", "ctx", None),
        P("fsdp", None),
        P("fsdp", None),
        P("fsdp", None),
        P("fsdp", None),
        P("fsdp"),
        P("fsdp"),
        P("fsdp"),
        P("fsdp", None),
        P("fsdp"),
        P("ctx", "fsdp", None),
        P("ctx", "fsdp", None),
        P("ctx", "fsdp", None),
        P("fsdp", None),
        P("fsdp", "ctx", None),
        P("fsdp", "ctx", None),
        P("fsdp", "ctx", None),
    )
    out_specs = (
        P("fsdp", "ctx", None),
        P("fsdp", "ctx", None),
        P("fsdp", None),
        P("fsdp", None),
        P("fsdp", None),
        P("fsdp", None),
        P("fsdp"),
        P("fsdp"),
        P("fsdp"),
        P("fsdp", None),
        P("fsdp"),
        P("ctx", "fsdp", None),
        P("ctx", "fsdp", None),
        P("ctx", "fsdp", None),
    )
    return jax.shard_map(local, mesh=mesh, in_specs=in_specs, out_specs=out_specs, check_vma=False)
```

```python
import functools

import jax
import jax.numpy as jnp
from jax import lax
from jax.experimental import pallas as pl
from jax.experimental.pallas import tpu as pltpu
from jax.sharding import PartitionSpec as P

H = 32
KVH = 4
HD = 128
TOPK = 8
EPS = 1e-06
THETA = 1000000.0
HIGH = lax.Precision.HIGHEST
LOG2E = 1.4426950408889634
F32 = jnp.float32
BF16 = jnp.bfloat16
ROWS_T = (((1,), (1,)), ((), ()))
COLS_T = (((0,), (0,)), ((), ()))


def dot(a, b, dims=(((1,), (0,)), ((), ()))):
    return lax.dot_general(a, b, dims, preferred_element_type=F32)


def params(mebibytes):
    return pltpu.CompilerParams(vmem_limit_bytes=mebibytes * 1024 * 1024)


def once(shape, index):
    return pl.BlockSpec(shape, index, pipeline_mode=pl.Buffered(1))


def cost(microseconds):
    return pl.CostEstimate(
        flops=int(microseconds * 1.15e9), bytes_accessed=0, transcendentals=0
    )


def flip(n_ctx, bit):
    return [(i, i ^ bit) for i in range(n_ctx)]


def ring(n_ctx, step):
    return [(i, (i + step) % n_ctx) for i in range(n_ctx)]


def block_order(n_ctx):
    c = lax.axis_index("ctx")
    nz = n_ctx // 4
    z, x, core = c // 4, (c // 2) % 2, c % 2
    table = []
    for k in range(nz):
        for dc in range(2):
            for dx in range(2):
                table.append(lax.rem(z + nz - k, nz) * 4 + (x ^ dx) * 2 + (core ^ dc))
    return jnp.stack(table).astype(jnp.int32)


def tie(*arrays):
    return lax.optimization_barrier(arrays)


class Side:
    def __init__(self, chain):
        self.chain, self.flying, self.left = chain, None, 0
        self.resume(None)

    def resume(self, landed):
        try:
            self.flying, self.left = self.chain.send(landed)
        except StopIteration:
            self.flying = None

    def finish(self):
        while self.flying is not None:
            self.resume(self.flying)


def land(air, sides, *others):
    due = [side for side in sides if side.flying is not None and side.left <= 1]
    for side in sides:
        side.left -= 1
    keys = list(air)
    flying = [array for side in due for array in side.flying]
    arrays = list(tie(*air.values(), *flying, *others))
    air.clear()
    landed = {key: arrays.pop(0) for key in keys}
    for side in due:
        side.resume([arrays.pop(0) for _ in side.flying])
    return landed, arrays


def pipeline(
    n_ctx, order, compute, token, sides, piece=None, scatter=False, closing=None, along=False
):
    nz = n_ctx // 4
    air, have, state = {}, {}, ()

    def send(key, array, pairs):
        air[key] = lax.ppermute(array, "ctx", pairs)

    def bring(k):
        if along and k + 1 == nz:
            send(("beside", k), have["beside", k - 1], ring(n_ctx, 4))
        else:
            send(("beside", k), have["piece", k], flip(n_ctx, 2))
        if k + 1 < nz:
            send(("piece", k + 1), have["piece", k], ring(n_ctx, 4))

    def step_ends(*others):
        landed, others = land(air, sides, *others)
        have.update(landed)
        return others

    def total_of(own):
        parts = [*own, have["away"]] + ([have["carry"]] if "carry" in have else [])
        return sum(part.astype(F32) for part in parts)

    def give(blocks, token):
        mine, theirs = blocks
        arrived = lax.ppermute(theirs, "ctx", flip(n_ctx, 1))
        away = (mine[1].astype(F32) + arrived[1].astype(F32)).astype(BF16)
        token, away = tie(token, away)
        send("away", away, flip(n_ctx, 2))
        return (mine[0], arrived[0]), token

    if piece is not None:
        have["piece", 0] = piece
        for k in range(order[0] + 1):
            bring(k)
            step_ends()
    blocks = own = None
    for s, k in enumerate(order):
        following = order[s + 1 :][:1]
        quarter = None
        if piece is not None:
            for later in following:
                if ("beside", later) not in have:
                    bring(later)
            pair = [have["piece", k], have["beside", k]]
            quarter = pair + [lax.ppermute(array, "ctx", flip(n_ctx, 1)) for array in pair]
        if not scatter:
            state = compute(k, quarter, token, state)
            if following:
                token, *state = step_ends(token, *state)
            continue
        if own is not None:
            send("carry", total_of(own).astype(BF16), ring(n_ctx, 4))
        if blocks is not None:
            own, token = give(blocks, token)
        blocks, state = compute(k, quarter, token, state)
        extra = closing[0]() if closing and not following else ()
        if piece is not None and s < 2:
            token, *blocks = step_ends(token, *blocks)
        else:
            mine, theirs = blocks
            token, mine, *extra = step_ends(token, mine, *extra)
            blocks = mine, theirs
        if extra:
            closing[1](*extra)
    if not scatter:
        return tuple(state)
    send("carry", total_of(own).astype(BF16), ring(n_ctx, 4))
    own, token = give(blocks, token)
    step_ends()
    return total_of(own), state


def gather_planned(piece, n_ctx, plan, arrays):
    arrays["along", 0] = piece
    source = lambda kind, k: ("along", k) if kind == "across" else (kind, k - 1)
    for i, (items, steps) in enumerate(plan):
        going = [
            lax.ppermute(
                arrays[source(*item)], "ctx", flip(n_ctx, 2) if item[0] == "across" else ring(n_ctx, 4)
            )
            for item in items
        ]
        later = {source(*item) for item in plan[i + 1][0]} if i + 1 < len(plan) else set()
        tied = sorted(key for key in later if key in arrays)
        came = list((yield (*going, *(arrays[key] for key in tied)), steps))
        for kind, k in items:
            arrays["along" if kind == "along" else "beside", k] = came.pop(0)
        arrays.update(zip(tied, came))


def planned_quarter(arrays, k, n_ctx):
    pair = [arrays["along", k], arrays["beside", k]]
    return pair + [lax.ppermute(array, "ctx", flip(n_ctx, 1)) for array in pair]


COTANGENT_PLAN = [
    ([("along", 1)], 1),
    ([("along", 2), ("across", 0), ("across", 1)], 1),
    ([("beside", 2)], 2),
    ([("along", 3)], 6),
    ([("beside", 3)], 1),
]
QUERY_GRAD_PLAN = [
    ([("along", 1), ("across", 0)], 1),
    ([("along", 2), ("across", 1)], 1),
    ([("along", 3), ("across", 2)], 1),
    ([("across", 3)], 1),
]
OUTPUT_GRAD_PLAN = [
    ([("along", 1), ("across", 0)], 1),
    ([("along", 2), ("across", 1)], 1),
    ([("along", 3), ("across", 2)], 1),
    ([("across", 3)], 1),
]


def scatter_order(n_ctx):
    return list(range(1, n_ctx // 4)) + [0]


def sum_all(values, result):
    n_ctx = lax.axis_size("ctx")
    bit = 1
    while bit < n_ctx:
        (came,) = yield (lax.ppermute(values.astype(BF16), "ctx", flip(n_ctx, bit)),), 1
        values = values + came.astype(F32)
        bit *= 2
    if lax.axis_size("fsdp") == 2:
        (came,) = yield (swap(values.astype(BF16)),), 1
        values = values + came.astype(F32)
    else:
        values = lax.psum(values, "fsdp")
    result.append(values)


SWAP = [(0, 1), (1, 0)]


def swap(part):
    return lax.ppermute(part, "fsdp", SWAP)


def fetch(part, steps=1):
    if lax.axis_size("fsdp") != 2:
        return [lax.all_gather(part, "fsdp", axis=0, tiled=True)]
    (other,) = yield (swap(part),), steps
    return [part, other]


def fetch_after(part, after, steps):
    if lax.axis_size("fsdp") != 2:
        return [lax.all_gather(part, "fsdp", axis=0, tiled=True)], after
    after, sent = tie(after, part)
    (after,) = yield (swap(sent),), steps
    return [part, after], after


def joined(parts):
    if len(parts) == 1:
        return parts[0]
    mine, other = parts
    first = lax.axis_index("fsdp") == 0
    return jnp.concatenate([jnp.where(first, mine, other), jnp.where(first, other, mine)], axis=0)


def part_offsets(width):
    if lax.axis_size("fsdp") != 2:
        return [jnp.int32(0)]
    f = lax.axis_index("fsdp")
    return [f * (width // 2), (1 - f) * (width // 2)]


def scatter_products(pairs, block, steps=(), pause=()):
    if lax.axis_size("fsdp") != 2:
        full = [dot(left[0], right, COLS_T).astype(BF16) for left, right in pairs]
        return [
            lax.psum_scatter(g, "fsdp", scatter_dimension=0, tiled=True).astype(F32) for g in full
        ]
    work = []
    for left, right in pairs:
        step = min(block, right.shape[1])
        work += [(left, right[:, at : at + step]) for at in range(0, right.shape[1], step)]
    product = lambda i, part: dot(work[i][0][part], work[i][1], COLS_T)
    done, sent = [], product(0, 1).astype(BF16)
    for i in range(len(work)):
        ahead = [product(i + 1, 1).astype(BF16)] if i + 1 < len(work) else []
        fresh = [product(i - 1, 0) + came.astype(F32)] if i > 0 else []
        if i in pause:
            (sent,) = yield (sent,), pause[i]
        came, *worked = yield (swap(sent), *ahead, *fresh), steps[i] if steps else 1
        if ahead:
            sent = worked.pop(0)
        done += worked
    done.append(product(len(work) - 1, 0) + came.astype(F32))
    sums = []
    for _, right in pairs:
        count = max(1, right.shape[1] // block)
        sums.append(done[0] if count == 1 else jnp.concatenate(done[:count], axis=1))
        done = done[count:]
    return sums


def scatter_rows(full):
    if lax.axis_size("fsdp") != 2:
        return lax.psum_scatter(
            full.astype(BF16), "fsdp", scatter_dimension=0, tiled=True
        ).astype(F32)
    rows = full.shape[0] // 2
    first = lax.axis_index("fsdp") == 0
    low, high = full[:rows], full[rows:]
    (came,) = yield (swap(jnp.where(first, high, low).astype(BF16)),), 1
    return jnp.where(first, low, high) + came.astype(F32)


def group_of(k):
    return lambda t: lax.div(t[4 * k], 4)


def span(t, k, i, count):
    return pl.ds(pl.multiple_of(lax.rem(t[4 * k + i], 4) * count, count), count)


IN_HBM = pl.BlockSpec(memory_space=pltpu.HBM)


def whole(shape):
    return once(shape, lambda *_: (0,) * len(shape))


def first_pair(shape):
    return pl.BlockSpec((1,) + shape, lambda i, t: (jnp.minimum(i, 1),) + (0,) * len(shape))


def last_pair(shape):
    return pl.BlockSpec((1,) + shape, lambda i, t: (jnp.maximum(i - 2, 0),) + (0,) * len(shape))


def split_pairs(i, body, first, last):
    @pl.when(i < 2)
    def _():
        body(first)

    @pl.when(i >= 2)
    def _():
        body(last)


def rotary_table(length):
    half = HD // 2
    steps = jnp.arange(half, dtype=jnp.int32).astype(F32)
    inverse = jnp.exp(steps * (-2.0 * jnp.log(THETA) / HD))
    angles = jnp.arange(length, dtype=jnp.int32).astype(F32)[:, None] * inverse[None, :]
    return jnp.concatenate([jnp.cos(angles), jnp.sin(angles)], axis=1)


def turns(table):
    other = pltpu.roll(table, HD // 2, 1)
    first = lax.broadcasted_iota(jnp.int32, (1, HD), 1) < HD // 2
    return jnp.where(first, table, other), jnp.where(first, -other, table)


def half_turn(v):
    return pltpu.roll(v, HD // 2, 1)


def head_norm(v, gain):
    scale = lax.rsqrt(jnp.mean(v * v, axis=-1, keepdims=True) + EPS)
    return v * scale * gain


def project_kernel(k, hpd, n_kv, n_parts, n_ctx, meta, x0, x1, x2, x3, gain, gq, gk, turn, *refs):
    n_outs = n_parts + 5
    w, beside = refs[:n_parts], refs[n_parts : 2 * n_parts] if n_kv < hpd else ()
    outs, refs = refs[-(2 * n_outs + 2) : -(n_outs + 2)], refs[-(n_outs + 2) :]
    here, rows, sems = refs[:n_outs], refs[-2], refs[-1]
    normed, (raw, scales, query, key, value) = here[:n_parts], here[n_parts:]
    count = x0.shape[0]
    group = pl.ds(pl.multiple_of(lax.div(meta[4 * k], 4) * 4 * count, count), 4 * count)
    places = [pl.ds(4 * k, 4)] * (n_parts + 2) + [(slice(None), group)] * 3
    leaving = [
        pltpu.make_async_copy(here[i], outs[i].at[places[i]], sems.at[i]) for i in range(n_outs)
    ]
    for i, piece in enumerate((x0, x1, x2, x3)):
        x = piece[...].astype(F32)
        r1 = lax.rsqrt(jnp.mean(x * x, axis=-1, keepdims=True) + EPS)
        scales[i] = jnp.broadcast_to(r1, scales.shape[1:])
        rows[i * count : (i + 1) * count, :] = (x * r1 * gain[...]).astype(BF16)
        for p, part in enumerate(normed):
            at = pl.ds(pl.multiple_of(meta[n_ctx + 1 + p], 128), part.shape[2])
            part[i] = rows[i * count : (i + 1) * count, at]
    for copy in leaving[:n_parts]:
        copy.start()
    parts = [part[...].reshape(4 * count, part.shape[2]) for part in normed]
    out = sum(dot(n, w_p[...]) for n, w_p in zip(parts, w))
    other = sum(dot(n, w_p[...]) for n, w_p in zip(parts, beside)) if beside else None
    core = meta[n_ctx]
    for i in range(4):
        at = span(meta, k, i, count)
        cos, sin = turns(turn[at, :])
        block = out[i * count : (i + 1) * count, :]
        raw[i] = block[:, : (hpd + n_kv) * HD]

        def turned(v, gain):
            v = head_norm(v, gain[...])
            return (v * cos + half_turn(v) * sin).astype(BF16)

        for j in range(hpd):
            query[j, at, :] = turned(block[:, j * HD : (j + 1) * HD], gq)
        for j in range(n_kv):
            v = block[:, (hpd + j) * HD : (hpd + j + 1) * HD]
            u = block[:, (hpd + n_kv + j) * HD : (hpd + n_kv + j + 1) * HD]
            head = core if beside else j
            key[head, at, :] = turned(v, gk)
            value[head, at, :] = u.astype(BF16)
        if beside:
            block = other[i * count : (i + 1) * count, :]
            key[1 - core, at, :] = turned(block[:, :HD], gk)
            value[1 - core, at, :] = block[:, HD:].astype(BF16)
    for copy in leaving[n_parts:]:
        copy.start()
    for copy in leaving:
        copy.wait()


def project(k, quarter, w, beside, gain, gq, gk, turn, meta, hpd, n_ctx, before):
    count, width = quarter[0].shape
    length = n_ctx * count
    n_parts = len(w)
    n_kv = 1 if beside else hpd
    group = group_of(k)
    turn_at = once((4 * count, HD), lambda i, t: (group(t), 0))
    head = pltpu.HBM((hpd, length, HD), BF16)
    cols = (hpd + n_kv) * HD
    weights = [*w, *beside]
    return pl.pallas_call(
        functools.partial(project_kernel, k, hpd, n_kv, n_parts, n_ctx),
        grid_spec=pltpu.PrefetchScalarGridSpec(
            num_scalar_prefetch=1,
            grid=(1,),
            in_specs=[whole((count, width))] * 4
            + [whole((1, width)), whole((1, HD)), whole((1, HD)), turn_at]
            + [whole(array.shape) for array in weights]
            + [IN_HBM] * len(before),
            out_specs=[IN_HBM] * (n_parts + 5),
            scratch_shapes=[pltpu.VMEM((4, count, width // n_parts), BF16)] * n_parts
            + [pltpu.VMEM((4, count, cols), F32), pltpu.VMEM((4, count, HD), F32)]
            + [pltpu.VMEM((hpd, 4 * count, HD), BF16)] * 3
            + [pltpu.VMEM((4 * count, width), BF16), pltpu.SemaphoreType.DMA((n_parts + 5,))],
        ),
        out_shape=[pltpu.HBM((n_ctx, count, width // n_parts), BF16)] * n_parts
        + [
            pltpu.HBM((n_ctx, count, cols), F32),
            pltpu.HBM((n_ctx, count, HD), F32),
            head,
            head,
            head,
        ],
        input_output_aliases={9 + len(weights) + i: i for i in range(len(before))},
        compiler_params=params(18),
        cost_estimate=cost(6),
        name="project",
    )(meta, *quarter, gain, gq, gk, turn, *weights, *before)


def first_key(ends, docs, position):
    start = jnp.zeros_like(position)
    for d in range(docs):
        start = jnp.where(position >= ends[d], jnp.maximum(start, ends[d]), start)
    return start


def attend_kernel(docs, heads, bq, bk, ends, query, key, value, mixed, total):
    i = pl.program_id(0)
    positions = i * bq + lax.broadcasted_iota(jnp.int32, (bq, 1), 0)
    starts = first_key(ends, docs, positions)
    low = lax.div(first_key(ends, docs, i * bq), bk)
    high = lax.div((i + 1) * bq - 1, bk) + 1

    def step(j, carry):
        rows = pl.ds(pl.multiple_of(j * bk, bk), bk)
        spots = j * bk + lax.broadcasted_iota(jnp.int32, (1, bk), 1)
        seen = (spots <= positions) & (spots >= starts)
        sums = []
        for h, (acc, norm) in enumerate(carry):
            scores = dot(query[h], key[h, rows, :], ROWS_T)
            p = jnp.where(seen, jnp.exp2(scores * (LOG2E * HD**-0.5)), 0.0)
            acc = acc + dot(p.astype(BF16), value[h, rows, :])
            sums.append((acc, norm + jnp.sum(p, axis=-1, keepdims=True)))
        return tuple(sums)

    start = (jnp.zeros((bq, HD), F32), jnp.zeros((bq, 1), F32))
    first_lane = lax.broadcasted_iota(jnp.int32, (1, HD), 1) == 0
    for h, (acc, norm) in enumerate(lax.fori_loop(low, high, step, (start,) * heads)):
        mixed[h] = acc / norm
        column = jnp.where(first_lane, jnp.log2(norm), 0.0)
        total[h] = row_sums(column)


def row_sums(values):
    return lax.dot_general(
        jnp.ones((8, values.shape[1]), F32),
        values,
        ROWS_T,
        precision=HIGH,
        preferred_element_type=F32,
    )


def attend(query, key, value, ends, bq=256, bk=512):
    heads, length, _ = query.shape
    docs = ends.shape[0]
    block = pl.BlockSpec((heads, bq, HD), lambda i, e: (0, i, 0))
    keys = once((heads, length, HD), lambda i, e: (0, 0, 0))
    line = pl.BlockSpec((heads, 8, bq), lambda i, e: (0, 0, i))
    return pl.pallas_call(
        functools.partial(attend_kernel, docs, heads, bq, bk),
        grid_spec=pltpu.PrefetchScalarGridSpec(
            num_scalar_prefetch=1,
            grid=(length // bq,),
            in_specs=[block, keys, keys],
            out_specs=[block, line],
        ),
        out_shape=[
            jax.ShapeDtypeStruct((heads, length, HD), F32),
            jax.ShapeDtypeStruct((heads, 8, length), F32),
        ],
        compiler_params=params(14),
        cost_estimate=cost(12.5),
        name="attend",
    )(ends, query, key, value)


def attend_back_kernel(
    docs, heads, bq, bk, ends, query, grad, total, delta, key, value, dq, dk, dv, *away
):
    i = pl.program_id(0)

    @pl.when(i == 0)
    def _():
        dk[...] = jnp.zeros_like(dk)
        dv[...] = jnp.zeros_like(dv)

    positions = i * bq + lax.broadcasted_iota(jnp.int32, (1, bq), 1)
    starts = first_key(ends, docs, positions)
    low = lax.div(first_key(ends, docs, i * bq), bk)
    high = lax.div((i + 1) * bq - 1, bk) + 1

    def step(j, sums):
        rows = pl.ds(pl.multiple_of(j * bk, bk), bk)
        spots = j * bk + lax.broadcasted_iota(jnp.int32, (bk, 1), 0)
        seen = (spots <= positions) & (spots >= starts)
        out = []
        for h in range(heads):
            q, g, k = query[h], grad[h], key[h, rows, :]
            scores = dot(k, q, ROWS_T)
            p = jnp.exp2(scores * (LOG2E * HD**-0.5) - total[h, 0:1, :])
            p = jnp.where(seen, p, 0.0)
            ds = (p * (dot(value[h, rows, :], g, ROWS_T) - delta[h, 0:1, :])).astype(BF16)
            dv[h, rows, :] += dot(p.astype(BF16), g)
            dk[h, rows, :] += dot(ds, q)
            out.append(sums[h] + dot(ds, k, COLS_T))
        return tuple(out)

    sums = lax.fori_loop(low, high, step, (jnp.zeros((bq, HD), F32),) * heads)
    for h in range(heads):
        dq[h] = sums[h]

    if away:

        @pl.when(i == pl.num_programs(0) - 1)
        def _():
            other = 1 - ends[docs]
            away[0][0] = dk[other].astype(BF16)
            away[0][1] = dv[other].astype(BF16)


def attend_back(query, grad, total, delta, key, value, ends, shared, bq=256, bk=512):
    heads, length, _ = query.shape
    docs = ends.shape[0] - 1
    block = pl.BlockSpec((heads, bq, HD), lambda i, e: (0, i, 0))
    line = pl.BlockSpec((heads, 8, bq), lambda i, e: (0, 0, i))
    keys = once((heads, length, HD), lambda i, e: (0, 0, 0))
    out = jax.ShapeDtypeStruct((heads, length, HD), F32)
    return pl.pallas_call(
        functools.partial(attend_back_kernel, docs, heads, bq, bk),
        grid_spec=pltpu.PrefetchScalarGridSpec(
            num_scalar_prefetch=1,
            grid=(length // bq,),
            in_specs=[block, block, line, line, keys, keys],
            out_specs=[block, keys, keys] + [whole((2, length, HD))] * shared,
        ),
        out_shape=[out, out, out] + [jax.ShapeDtypeStruct((2, length, HD), BF16)] * shared,
        compiler_params=params(24),
        cost_estimate=cost(17),
        name="attend_back",
    )(ends, query, grad, total, delta, key, value)


def branch_kernel(hpd, table, mixed, w, theirs, mine):
    def body(out):
        total = None
        for j in range(hpd):
            part = dot(mixed[j].astype(BF16), w[j * HD : (j + 1) * HD, :])
            total = part if total is None else total + part
        out[0] = total.astype(BF16)

    split_pairs(pl.program_id(0), body, theirs, mine)


def branch(k, mixed, w, table, count):
    hpd = mixed.shape[0]
    width = w.shape[1]
    pair = jax.ShapeDtypeStruct((2, count, width), BF16)
    theirs, mine = pl.pallas_call(
        functools.partial(branch_kernel, hpd),
        grid_spec=pltpu.PrefetchScalarGridSpec(
            num_scalar_prefetch=1,
            grid=(4,),
            in_specs=[
                pl.BlockSpec((hpd, count, HD), lambda i, t: (0, t[4 * k + (i ^ 2)], 0)),
                whole((hpd * HD, width)),
            ],
            out_specs=[first_pair((count, width)), last_pair((count, width))],
        ),
        out_shape=[pair, pair],
        compiler_params=params(10),
        cost_estimate=cost(2.4),
        name="branch",
    )(table, mixed, w)
    return mine, theirs


def branch_back_kernel(k, hpd, meta, g0, g1, g2, g3, mixed, w, *refs):
    grad, delta, dw = refs[-3:]
    pieces = (g0, g1, g2, g3)
    count = g0.shape[0]
    g = jnp.concatenate([piece[...] for piece in pieces], axis=0)
    back = dot(g, w[...], ROWS_T).astype(BF16)
    for j in range(hpd):
        heads = []
        for i in range(4):
            at = span(meta, k, i, count)
            own = back[i * count : (i + 1) * count, j * HD : (j + 1) * HD]
            out = mixed[j, at, :]
            grad[j, at, :] = own
            delta[j, :, at] = row_sums(own.astype(F32) * out)
            heads.append(out.astype(BF16))
        part = dot(jnp.concatenate(heads, axis=0), g, COLS_T)
        rows = slice(j * HD, (j + 1) * HD)
        dw[rows, :] = part if len(refs) == 3 else refs[0][rows, :] + part


def branch_back(k, quarter, mixed, w, table, before):
    count, width = quarter[0].shape
    hpd, length, _ = mixed.shape
    group = group_of(k)
    head_at = once((hpd, 4 * count, HD), lambda i, t: (0, group(t), 0))
    dw_at = whole((hpd * HD, width))
    grad, delta, dw = pl.pallas_call(
        functools.partial(branch_back_kernel, k, hpd),
        grid_spec=pltpu.PrefetchScalarGridSpec(
            num_scalar_prefetch=1,
            grid=(1,),
            in_specs=[whole((count, width))] * 4
            + [head_at, whole((hpd * HD, width))]
            + ([dw_at] + [pl.BlockSpec(memory_space=pl.ANY)] * 2 if before else []),
            out_specs=[
                head_at,
                once((hpd, 8, 4 * count), lambda i, t: (0, 0, group(t))),
                dw_at,
            ],
        ),
        out_shape=[
            jax.ShapeDtypeStruct((hpd, length, HD), BF16),
            jax.ShapeDtypeStruct((hpd, 8, length), F32),
            jax.ShapeDtypeStruct((hpd * HD, width), F32),
        ],
        input_output_aliases={8: 0, 9: 1} if before else {},
        compiler_params=params(20),
        cost_estimate=cost(6),
        name="branch_back",
    )(table, *quarter, mixed, w, *before)
    return dw, grad, delta


def experts_kernel(
    k, n_parts, width, capacity, n_exp, meta, x0, x1, x2, x3, g0, g1, g2, g3, router, *refs
):
    n = n_parts
    w_from = refs[: 3 * n]
    refs = refs[-(2 * n + 5 + 6 * n + 3 + 3) :]
    outs, (mine, theirs) = refs[: 2 * n + 3], refs[2 * n + 3 : 2 * n + 5]
    refs = refs[2 * n + 5 :]
    w_here, refs = refs[: 3 * n], refs[3 * n :]
    rows, pairs, picked, refs = refs[:n], refs[n : 2 * n], refs[2 * n : 3 * n], refs[3 * n :]
    hidden, gate_grad, up_grad, chosen_ref, gate_ref, sems = refs
    slots = 4 * capacity
    part = width // n
    c = meta[0]
    lanes = lax.broadcasted_iota(jnp.int32, (1, 128), 1)
    pieces = (x0, x1, x2, x3)
    arrivals = [
        pltpu.make_async_copy(w_from[i], w_here[i], sems.at[i]) for i in range(3 * n)
    ]
    for copy in arrivals:
        copy.start()
    here = [*rows, *pairs, hidden, gate_grad, up_grad]
    leaving = [
        pltpu.make_async_copy(
            here[i], outs[i].at[pl.ds(k * slots, slots), :], sems.at[3 * n + i]
        )
        for i in range(2 * n + 3)
    ]

    def columns(p, first=0):
        return pl.ds(pl.multiple_of(first + meta[1 + p], 128), part)

    for i, x_ref in enumerate(pieces):
        cot = (g0, g1, g2, g3)[i]
        at = slice(i * capacity, (i + 1) * capacity)
        info = x_ref[:, width:].astype(F32)
        place = jnp.sum(jnp.where(lanes == c, info, 0.0), axis=1, keepdims=True)
        spots = lax.broadcasted_iota(jnp.int32, (1, capacity), 1).astype(F32)
        chosen = (spots == place).astype(BF16)
        chosen_ref[i] = chosen
        logits = dot(x_ref[:, :width], router[...])
        seen = info > -1.5
        top = jnp.max(jnp.where(seen, logits, -1e30), axis=1, keepdims=True)
        shares = jnp.where(seen, jnp.exp(logits - top), 0.0)
        gates = shares / jnp.sum(shares, axis=1, keepdims=True)
        own = jnp.sum(jnp.where(lanes == c, gates, 0.0), axis=1, keepdims=True)
        gate = lax.dot_general(
            chosen.astype(F32),
            jnp.broadcast_to(own, gates.shape),
            COLS_T,
            precision=HIGH,
            preferred_element_type=F32,
        )
        gate_ref[at, :] = gate
        for p in range(n):
            rows[p][at, :] = dot(chosen, x_ref[:, columns(p)], COLS_T).astype(BF16)
            grads = dot(chosen, cot[:, columns(p)], COLS_T)
            picked[p][at, :] = grads.astype(BF16)
            pairs[p][at, :] = (grads * gate[:, :1]).astype(BF16)
    for copy in leaving[: 2 * n]:
        copy.start()
    for copy in arrivals[: 2 * n]:
        copy.wait()
    wg, wu, wd = (w_here[n * i : n * (i + 1)] for i in range(3))
    gate_part = sum(dot(rows[p][...], wg[p][...]) for p in range(n))
    up_part = sum(dot(rows[p][...], wu[p][...]) for p in range(n))
    sigma = jax.nn.sigmoid(gate_part)
    silu_gate = gate_part * sigma
    h = (silu_gate * up_part).astype(BF16)
    hidden[...] = h
    leaving[2 * n].start()
    for copy in arrivals[2 * n :]:
        copy.wait()
    hidden_grad = sum(dot(pairs[p][...], wd[p][...]) for p in range(n))
    gg = (hidden_grad * up_part * sigma * (1.0 + gate_part * (1.0 - sigma))).astype(BF16)
    gate_grad[...] = gg
    leaving[2 * n + 1].start()
    ug = (hidden_grad * silu_gate).astype(BF16)
    up_grad[...] = ug
    leaving[2 * n + 2].start()
    inner_sum = jnp.zeros((slots, 1), F32)
    for p in range(n):
        out = dot(h, wd[p][...], ROWS_T).astype(BF16).astype(F32)
        inner_sum += jnp.sum(out * picked[p][...].astype(F32), axis=1, keepdims=True)
        scaled = (out * gate_ref[:, :1]).astype(BF16)
        row_sum = (dot(gg, wg[p][...], ROWS_T) + dot(ug, wu[p][...], ROWS_T)).astype(BF16)
        for i in range(4):
            back = (mine, theirs)[i // 2].at[i % 2]
            at = slice(i * capacity, (i + 1) * capacity)
            back[:, columns(p)] = dot(chosen_ref[i], row_sum[at, :]).astype(BF16)
            back[:, columns(p, width + 128)] = dot(chosen_ref[i], scaled[at, :]).astype(BF16)
    high = inner_sum.astype(BF16).astype(F32)
    extra = jnp.where(lanes == c, high, 0.0) + jnp.where(
        lanes == c + n_exp, inner_sum - high, 0.0
    )
    extra = extra.astype(BF16)
    for i in range(4):
        back = (mine, theirs)[i // 2].at[i % 2]
        at = slice(i * capacity, (i + 1) * capacity)
        back[:, width : width + 128] = dot(chosen_ref[i], extra[at, :]).astype(BF16)
    for copy in leaving:
        copy.wait()


def experts(k, quarter, cots, router, wg, wu, wd, meta, capacity, n_exp, nz, before):
    count, wide = quarter[0].shape
    width = cots[0].shape[1]
    n_parts = len(wg)
    part = width // n_parts
    hid = wg[0].shape[1]
    slots = 4 * capacity
    anywhere = pl.BlockSpec(memory_space=pl.ANY)
    pair = once((2, count, wide + width), lambda i, m: (0, 0, 0))
    rows_all = lambda cols: pltpu.HBM((nz * slots, cols), BF16)
    n_out = 2 * n_parts + 3
    outs = pl.pallas_call(
        functools.partial(experts_kernel, k, n_parts, width, capacity, n_exp),
        grid_spec=pltpu.PrefetchScalarGridSpec(
            num_scalar_prefetch=1,
            grid=(1,),
            in_specs=[whole((count, wide))] * 4
            + [whole((count, width))] * 4
            + [whole(router.shape)]
            + [anywhere] * (3 * n_parts)
            + [IN_HBM] * len(before),
            out_specs=[IN_HBM] * n_out + [pair, pair],
            scratch_shapes=[pltpu.VMEM((part, hid), BF16)] * (3 * n_parts)
            + [pltpu.VMEM((slots, part), BF16)] * (3 * n_parts)
            + [pltpu.VMEM((slots, hid), BF16)] * 3
            + [
                pltpu.VMEM((4, count, capacity), BF16),
                pltpu.VMEM((slots, 128), F32),
                pltpu.SemaphoreType.DMA((5 * n_parts + 3,)),
            ],
        ),
        out_shape=[rows_all(part)] * (2 * n_parts)
        + [rows_all(hid)] * 3
        + [jax.ShapeDtypeStruct((2, count, wide + width), BF16)] * 2,
        input_output_aliases={10 + 3 * n_parts + i: i for i in range(len(before))},
        compiler_params=params(34),
        cost_estimate=cost(15),
        name="experts",
    )(meta, *quarter, *cots, router, *wg, *wu, *wd, *before)
    return (outs[n_out], outs[n_out + 1]), outs[:n_out]


def head_back(grad, v, gain, cos, sin):
    scale = lax.rsqrt(jnp.mean(v * v, axis=-1, keepdims=True) + EPS)
    d = grad * cos - half_turn(grad) * sin
    u = d * gain
    inner = jnp.mean(u * v, axis=-1, keepdims=True)
    back = scale * u - v * (scale * scale * scale * inner)
    return back.astype(BF16), jnp.sum(d * v * scale, axis=0, keepdims=True)


def key_back_kernel(meta, dk, dv, raw, turn, gk, *refs):
    out, gains = refs[-2:]
    came = refs[:-2]
    z = pl.program_id(0)

    @pl.when(z == 0)
    def _():
        gains[...] = jnp.zeros_like(gains)

    n_kv = dk.shape[0]
    count = raw.shape[1]
    for i in range(4):
        at = pl.ds(pl.multiple_of(lax.rem(meta[4 * z + i], 4) * count, count), count)
        for j in range(n_kv):
            v = raw[i, :, j * HD : (j + 1) * HD]
            key_grad, value_grad = dk[j, at, :], dv[j, at, :]
            if came:
                key_grad = key_grad + came[0][0, at, :].astype(F32)
                value_grad = value_grad + came[0][1, at, :].astype(F32)
            grad = key_grad * HD**-0.5
            back, gain = head_back(grad, v, gk[...], *turns(turn[at, :]))
            out[i, :, j * HD : (j + 1) * HD] = back
            gains[0:1, :] += gain
            out[i, :, (n_kv + j) * HD : (n_kv + j + 1) * HD] = value_grad.astype(BF16)


def key_back(dk, dv, came, raw, turn, gk, meta):
    hpd = dk.shape[0]
    n_kv = 1 if came else hpd
    n_ctx, count, _ = raw.shape
    group = lambda z, t: lax.div(t[4 * z], 4)
    head_at = pl.BlockSpec(
        (n_kv, 4 * count, HD), lambda z, t: (t[n_ctx] if came else 0, group(z, t), 0)
    )
    turn_at = pl.BlockSpec((4 * count, HD), lambda z, t: (group(z, t), 0))
    return pl.pallas_call(
        key_back_kernel,
        grid_spec=pltpu.PrefetchScalarGridSpec(
            num_scalar_prefetch=1,
            grid=(n_ctx // 4,),
            in_specs=[
                head_at,
                head_at,
                pl.BlockSpec((4, count, n_kv * HD), lambda z, t: (z, 0, hpd // n_kv)),
                turn_at,
                whole((1, HD)),
            ]
            + [pl.BlockSpec((2, 4 * count, HD), lambda z, t: (0, group(z, t), 0))] * len(came),
            out_specs=[
                pl.BlockSpec((4, count, 2 * n_kv * HD), lambda z, t: (z, 0, 0)),
                whole((8, HD)),
            ],
        ),
        out_shape=[
            jax.ShapeDtypeStruct((n_ctx, count, 2 * n_kv * HD), BF16),
            jax.ShapeDtypeStruct((8, HD), F32),
        ],
        compiler_params=params(14),
        cost_estimate=cost(5),
        name="key_back",
    )(meta, dk, dv, raw, turn, gk, *came)


def input_back_kernel(k, hpd, meta, dq, kv, raw, scales, turn, gq, w, *refs):
    x, (grads_out, theirs, mine, gains, gain_grad, rows, grads, sem) = refs[:4], refs[-8:]
    copy = pltpu.make_async_copy(grads, grads_out.at[pl.ds(4 * k, 4)], sem)
    count = raw.shape[1]
    q_cols = hpd * HD

    @pl.when(pl.program_id(0) == 0)
    def _():
        gains[...] = jnp.zeros_like(gains)
        for i in range(4):
            at = span(meta, k, i, count)
            for j in range(hpd):
                cols = slice(j * HD, (j + 1) * HD)
                grad = dq[j, at, :] * HD**-0.5
                back, gain = head_back(grad, raw[i, :, cols], gq[...], *turns(turn[at, :]))
                grads[i, :, cols] = back
                gains[0:1, :] += gain
            rows[i * count : (i + 1) * count, :q_cols] = grads[i]
            rows[i * count : (i + 1) * count, q_cols:] = kv[i]
        copy.start()

    @pl.when(pl.program_id(0) == pl.num_programs(0) - 1)
    def _():
        copy.wait()

    back = dot(rows[...], w[...], ROWS_T)
    total = None
    for i in range(4):
        block = back[i * count : (i + 1) * count, :]
        (mine, theirs)[i // 2][i % 2] = block.astype(BF16)
        term = jnp.sum(block * x[i][...].astype(F32) * scales[i, :, :1], axis=0, keepdims=True)
        total = term if total is None else total + term
    gain_grad[...] = jnp.broadcast_to(total, gain_grad.shape)


def input_back(k, quarter, dq, kv, raw, scales, turn, gq, w, meta, before):
    count, width = quarter[0].shape
    hpd = dq.shape[0]
    n_ctx = raw.shape[0]
    q_cols = hpd * HD
    chunk = width // 4
    group = group_of(k)
    turn_at = pl.BlockSpec((4 * count, HD), lambda i, t: (group(t), 0))
    own = lambda cols: pl.BlockSpec((4, count, cols), lambda i, t: (k, 0, 0))
    pair_at = pl.BlockSpec((2, count, chunk), lambda i, t: (0, 0, i))
    pair = jax.ShapeDtypeStruct((2, count, width), BF16)
    outs = pl.pallas_call(
        functools.partial(input_back_kernel, k, hpd),
        grid_spec=pltpu.PrefetchScalarGridSpec(
            num_scalar_prefetch=1,
            grid=(4,),
            in_specs=[
                pl.BlockSpec((hpd, 4 * count, HD), lambda i, t: (0, group(t), 0)),
                own(kv.shape[2]),
                own(q_cols),
                own(HD),
                turn_at,
                whole((1, HD)),
                pl.BlockSpec((chunk, w.shape[1]), lambda i, t: (i, 0)),
            ]
            + [pl.BlockSpec((count, chunk), lambda i, t: (0, i))] * 4
            + [IN_HBM] * len(before),
            out_specs=[
                IN_HBM,
                pair_at,
                pair_at,
                whole((8, HD)),
                pl.BlockSpec((8, chunk), lambda i, t: (0, i)),
            ],
            scratch_shapes=[
                pltpu.VMEM((4 * count, w.shape[1]), BF16),
                pltpu.VMEM((4, count, q_cols), BF16),
                pltpu.SemaphoreType.DMA(()),
            ],
        ),
        out_shape=[
            pltpu.HBM((n_ctx, count, q_cols), BF16),
            pair,
            pair,
            jax.ShapeDtypeStruct((8, HD), F32),
            jax.ShapeDtypeStruct((8, width), F32),
        ],
        input_output_aliases={12: 0} if before else {},
        compiler_params=params(18),
        cost_estimate=cost(6),
        name="input_back",
    )(meta, dq, kv, raw, scales, turn, gq, w, *quarter, *before)
    grads, theirs, mine, gains, gain_grad = outs
    return (mine, theirs), grads, gains, gain_grad


def place_kernel(parts, n, n_kv, table, *refs):
    columns, keys = refs[:n], refs[n : n + n_kv]
    outs = refs[-3:] if n_kv else refs[-1:]
    for i in range(n):

        @pl.when(pl.program_id(0) // parts == i)
        def _():
            outs[0][...] = columns[i][...].astype(F32)
            if n_kv:
                outs[1][...] = keys[i][:, :HD].astype(F32)
                outs[2][...] = keys[i][:, HD:].astype(F32)


def place_columns(k, quarter, table, n_ctx, rows, before, first=0, stride=1):
    all_rows, cols = quarter[0].shape
    parts = cols // HD
    kv_rows = all_rows - rows
    pieces = list(quarter[first::stride])
    count = len(pieces)
    block_of = lambda i: 4 * k + first + stride * (i // parts)

    def piece_at(n):
        return lambda i, t: (0, jnp.clip(i - n * parts, 0, parts - 1))

    def head_at(i, t):
        c = t[block_of(i)]
        rows_part = lax.rem(c // 4, 2) * 2 + lax.rem(c // 2, 2)
        return rows_part, lax.rem(c, 2) * 2 + c // 8

    out_specs = [
        pl.BlockSpec((rows, HD), lambda i, t: (0, (i % parts) * n_ctx + t[block_of(i)]))
    ]
    out_shape = [jax.ShapeDtypeStruct((rows, n_ctx * cols), F32)]
    in_specs = [pl.BlockSpec((rows, HD), piece_at(n)) for n in range(count)]
    if kv_rows:
        in_specs += [once((kv_rows, cols), lambda i, t: (rows // kv_rows, 0))] * count
        pieces += pieces
        out_specs += [pl.BlockSpec((kv_rows, HD), head_at)] * 2
        out_shape += [jax.ShapeDtypeStruct((rows, KVH * HD), F32)] * 2
    return pl.pallas_call(
        functools.partial(place_kernel, parts, count, len(pieces) - count),
        grid_spec=pltpu.PrefetchScalarGridSpec(
            num_scalar_prefetch=1,
            grid=(count * parts,),
            in_specs=in_specs + [pl.BlockSpec(memory_space=pl.ANY)] * len(before),
            out_specs=out_specs,
        ),
        out_shape=out_shape,
        input_output_aliases={1 + len(pieces) + i: i for i in range(len(before))},
        compiler_params=params(12),
        cost_estimate=cost(4.6),
        name="place_columns",
    )(table, *pieces, *before)


def place_rows_kernel(table, *refs):
    out = refs[-1]
    for n in range(4):

        @pl.when(pl.program_id(0) == n)
        def _():
            out[...] = refs[n][...].astype(F32)


def place_rows(quarters, table):
    rows, cols = quarters[0][0].shape
    placed = ()
    for k, quarter in enumerate(quarters):
        placed = pl.pallas_call(
            place_rows_kernel,
            grid_spec=pltpu.PrefetchScalarGridSpec(
                num_scalar_prefetch=1,
                grid=(4,),
                in_specs=[whole((rows, cols))] * 4 + [IN_HBM] * len(placed),
                out_specs=[pl.BlockSpec((rows, cols), lambda i, t, k=k: (t[4 * k + i], 0))],
            ),
            out_shape=[pltpu.HBM((4 * len(quarters) * rows, cols), F32)],
            input_output_aliases={5: 0} if placed else {},
            compiler_params=params(10),
            cost_estimate=cost(2.4),
            name="place_rows",
        )(table, *quarter, *placed)
    return placed[0]


def local(
    inputs,
    w_query,
    w_key,
    w_value,
    w_output,
    norm_attn,
    gain_query,
    gain_key,
    w_router,
    norm_moe,
    w_gate,
    w_up,
    w_down,
    lengths,
    routes,
    pair_order,
    cotangent,
):
    n_ctx = lax.axis_size("ctx")
    n_f = lax.axis_size("fsdp")
    c = lax.axis_index("ctx")
    f = lax.axis_index("fsdp")
    count, width = inputs.shape[1], inputs.shape[2]
    length = count * n_ctx
    nz = n_ctx // 4
    later = scatter_order(n_ctx)
    hpd = H // n_ctx
    hpf = H // n_f
    group = H // KVH
    n_exp = w_router.shape[1]
    capacity = 5 * count * TOPK // (4 * n_exp)
    table = block_order(n_ctx)
    core = c % 2

    heads = [c % hpf + hpf * ((c // hpf) * hpd + j) for j in range(hpd)]
    kv_heads = [h // group for h in heads]
    columns = lambda w, h: lax.dynamic_slice_in_dim(w, h * HD, HD, 1)
    shared = n_f == 2 and hpd == 2
    if shared:
        kv_own = heads[0] // group + core * (KVH // 2)
        w_part = jnp.concatenate(
            [columns(w_query, h) for h in heads]
            + [columns(w_key, kv_own), columns(w_value, kv_own)],
            axis=1,
        )
    else:
        w_part = jnp.concatenate(
            [columns(w_query, h) for h in heads]
            + [columns(w_key, h) for h in kv_heads]
            + [columns(w_value, h) for h in kv_heads],
            axis=1,
        )
    w_part, norm_first = tie(w_part, norm_attn)
    vectors = jnp.concatenate([norm_first, gain_query, gain_key, norm_moe])
    if n_f == 2:
        vectors = joined([vectors[None], swap(vectors[None])])
        router = joined([w_router, swap(w_router)])
    else:
        vectors = lax.all_gather(vectors, "fsdp", axis=0)
        router = lax.all_gather(w_router, "fsdp", axis=0, tiled=True)
    sizes = [norm_attn.shape[0], gain_query.shape[0], gain_key.shape[0], norm_moe.shape[0]]
    rows_of, at = [], 0
    for size in sizes:
        rows_of.append(vectors[:, at : at + size].reshape(1, n_f * size).astype(F32))
        at += size
    attn_gain, query_gain, key_gain, moe_gain = rows_of
    router_wide = jnp.pad(router, ((0, 0), (0, 128 - n_exp)))
    offsets = part_offsets(width)
    n_parts = len(offsets)
    meta_rows = jnp.concatenate([table, jnp.stack([core] + offsets).astype(jnp.int32)])
    q_cols = hpd * HD
    block = w_gate.shape[2] // 3
    weights = {}

    def fetch_weights():
        parts = yield from fetch(w_part, 2)
        weights["qkv"], weights["beside"] = parts, []
        if shared:
            weights["beside"] = [
                lax.ppermute(part[:, q_cols:], "ctx", flip(n_ctx, 1)) for part in parts
            ]
        weights["back"] = joined(parts)
        own_rows = lax.dynamic_slice_in_dim(w_output, (c % hpf) * HD, HD, 0)
        rows_parts = yield from fetch(own_rows)
        last = rows_parts[-1]
        w_out = joined(rows_parts)
        weights["out"] = lax.dynamic_slice_in_dim(w_out, (c // hpf) * hpd * HD, hpd * HD, 0)
        weights["gate"], last = yield from fetch_after(w_gate[0], last, 2)
        weights["up"], last = yield from fetch_after(w_up[0], last, 4)
        weights["down"], last = yield from fetch_after(w_down[0], last, 3)

    gathered = {}

    def gather_cotangents():
        (cot,) = yield (cotangent[0],), 3
        yield from gather_planned(cot, n_ctx, COTANGENT_PLAN, gathered)

    sides = [Side(fetch_weights()), Side(gather_cotangents())]

    experts_of = jnp.arange(n_exp, dtype=jnp.int32)
    picks = routes[0][:, :, None] == experts_of
    ranks = jnp.sum(
        jnp.where(picks, pair_order[0, 0].reshape(count, TOPK, 1), 0), axis=1
    )
    chosen = jnp.any(picks, axis=1)
    ranks = jnp.where(chosen, ranks, count * TOPK)
    place = jnp.sum((ranks[None, :, :] < ranks[:, None, :]).astype(jnp.int32), axis=1)
    place = jnp.where(chosen, jnp.where(place < capacity, place, -1), -2)
    place = jnp.pad(place, ((0, 0), (0, 128 - n_exp)), constant_values=-2).astype(BF16)

    ends = jnp.cumsum(lengths[0]).astype(jnp.int32)
    turn = rotary_table(length)

    xs = {}

    def through_projection(k, quarter, token, before):
        xs[k] = quarter
        if k == 0:
            return ()
        if k == 1:
            before = projection(0, token, ())
        return projection(k, token, before)

    def projection(k, token, before):
        return project(
            k,
            xs[k],
            weights["qkv"],
            weights["beside"],
            attn_gain,
            query_gain,
            key_gain,
            turn,
            token,
            hpd,
            n_ctx,
            before,
        )

    straight = list(range(nz))
    *normed, raw, scales, query, key, value = pipeline(
        n_ctx, straight, through_projection, meta_rows, sides, piece=inputs[0]
    )
    mixed, log_total = attend(query, key, value, ends)
    _, (mixed,) = land({}, sides, mixed)
    x = inputs[0].astype(F32)
    branch_sum, _ = pipeline(
        n_ctx,
        later,
        lambda k, _, token, state: (branch(k, mixed, weights["out"], token, count), state),
        table,
        sides,
        scatter=True,
    )
    middle = x + branch_sum
    moe_scale = lax.rsqrt(jnp.mean(middle * middle, axis=-1, keepdims=True) + EPS)
    routed_in = (middle * moe_scale * moe_gain).astype(BF16)

    pad_offsets = (offsets + [jnp.int32(0)])[:2]
    head_meta = [jnp.stack([c] + pad_offsets).astype(jnp.int32)]
    expert_meta = jnp.concatenate(head_meta)

    def through_experts(k, quarter, token, before):
        return experts(
            k,
            quarter,
            planned_quarter(gathered, k, n_ctx),
            router_wide,
            weights["gate"],
            weights["up"],
            weights["down"],
            token,
            capacity,
            n_exp,
            nz,
            before,
        )

    routed_grad, seen = pipeline(
        n_ctx,
        later,
        through_experts,
        expert_meta,
        sides,
        piece=jnp.concatenate([routed_in, place], axis=1),
        scatter=True,
        along=True,
    )
    rows, pairs = seen[:n_parts], seen[n_parts : 2 * n_parts]
    hidden, gate_part_grad, up_part_grad = seen[2 * n_parts :]
    outputs = (middle + routed_grad[:, width + 128 :]).astype(BF16)

    gate_grad = routed_grad[:, width : width + n_exp] + routed_grad[
        :, width + n_exp : width + 2 * n_exp
    ]
    routed_grad = routed_grad[:, :width]
    logits = dot(routed_in, router)
    top = jnp.max(jnp.where(chosen, logits, -1e30), axis=-1, keepdims=True)
    shares = jnp.where(chosen, jnp.exp(logits - top), 0.0)
    gates = shares / jnp.sum(shares, axis=-1, keepdims=True)
    logit_grad = gates * (gate_grad - jnp.sum(gates * gate_grad, axis=-1, keepdims=True))
    routed_grad = routed_grad + lax.dot_general(
        logit_grad, router.astype(F32), ROWS_T, precision=HIGH
    )
    router_part = lax.dot_general(
        logit_grad, routed_in.astype(F32), COLS_T, precision=HIGH
    )

    grad_out = cotangent[0].astype(F32)
    moe_scaled = routed_grad * moe_gain
    moe_part = jnp.sum(routed_grad * middle * moe_scale, axis=0, keepdims=True)
    middle_grad = (
        grad_out
        + moe_scale * moe_scaled
        - middle
        * (
            moe_scale
            * moe_scale
            * moe_scale
            * jnp.mean(moe_scaled * middle, axis=-1, keepdims=True)
        )
    )

    grads, sums = {}, []

    def scatter_grads():
        pairs_of = [(rows, gate_part_grad), (rows, up_part_grad), (pairs, hidden)]
        sums_of = yield from scatter_products(
            pairs_of, block, (1, 1, 1, 1, 1, 2, 1, 1, 1), {6: 3}
        )
        grads["gate"], grads["up"], grads["down"] = sums_of

    sides = [
        Side(scatter_grads()),
        Side(sum_all(jnp.concatenate([router_part, moe_part], axis=0), sums)),
    ]
    grad_out_w, mixed_grad, delta = pipeline(
        n_ctx,
        straight,
        lambda k, quarter, token, before: branch_back(
            k, quarter, mixed, weights["out"], token, before
        ),
        table,
        sides,
        piece=middle_grad.astype(BF16),
    )
    def sum_out_grad():
        if n_f == hpd:
            placed = grad_out_w
        else:
            spread_out = jnp.arange(n_f, dtype=jnp.int32)[:, None] == (
                (c // hpf) * hpd + jnp.arange(hpd, dtype=jnp.int32)[None, :]
            )
            placed = jnp.einsum(
                "fj,jrd->frd", spread_out.astype(F32), grad_out_w.reshape(hpd, HD, width)
            ).reshape(n_f * HD, width)
        own = yield from scatter_rows(placed)
        own = own.astype(BF16)
        if n_ctx == hpf:
            arrays = {}
            yield from gather_planned(own, n_ctx, OUTPUT_GRAD_PLAN, arrays)
            quarters = [planned_quarter(arrays, k, n_ctx) for k in range(nz)]
            grads["out"] = place_rows(quarters, table)
        else:
            whole_grad = lax.all_gather(own, "ctx", axis=0).reshape(-1, hpf * HD, width)
            mine = lax.dynamic_index_in_dim(whole_grad, f // hpd, 0, keepdims=False)
            grads["out"] = mine.astype(F32)

    sides.append(Side(sum_out_grad()))
    ends_and_core = jnp.concatenate([ends, core[None].astype(jnp.int32)])
    dq, dk, dv, *away = attend_back(
        query, mixed_grad, log_total, delta, key, value, ends_and_core, int(shared)
    )
    _, (dq, dk, dv, *away) = land({}, sides, dq, dk, dv, *away)
    came = [lax.ppermute(array, "ctx", flip(n_ctx, 1)) for array in away]
    kv_grad, key_gains = key_back(dk, dv, came, raw, turn, key_gain, meta_rows)
    normed_flat = [n.reshape(length, -1) for n in normed]

    def sum_key_grads():
        (grad_kv,) = yield from scatter_products(
            [(normed_flat, kv_grad.reshape(length, -1))], kv_grad.shape[-1]
        )
        if not shared:
            slots_kv = jnp.arange(KVH, dtype=jnp.int32)
            spread = jnp.stack([slots_kv == h for h in kv_heads]).astype(F32)
            grad_kv = grad_kv.reshape(width // n_f, 2, hpd, 1, HD) * spread[None, None, :, :, None]
            grad_kv = jnp.sum(grad_kv, axis=2).reshape(width // n_f, 2 * KVH * HD)
            grad_kv = lax.psum(grad_kv.astype(BF16), "ctx").astype(F32)
            grads["key"], grads["value"] = grad_kv[:, : KVH * HD], grad_kv[:, KVH * HD :]
            return
        for bit in (4, 2):
            rows_kept = grad_kv.shape[0] // 2
            side = (c // bit) % 2
            kept = lax.dynamic_slice_in_dim(grad_kv, side * rows_kept, rows_kept, 0)
            gone = lax.dynamic_slice_in_dim(grad_kv, (1 - side) * rows_kept, rows_kept, 0)
            (got,) = yield (lax.ppermute(gone.astype(BF16), "ctx", flip(n_ctx, bit)),), 1
            grad_kv = kept + got.astype(F32)
        grads["key_piece"] = grad_kv.astype(BF16)

    sides.append(Side(sum_key_grads()))
    gain_parts, attn_parts = [], []

    def through_inputs(k, _, token, before):
        back, q_grad, gains, gain_grad = input_back(
            k,
            xs[k],
            dq,
            kv_grad,
            raw,
            scales,
            turn,
            query_gain,
            weights["back"],
            token,
            before,
        )
        gain_parts.append(gains)
        attn_parts.append(gain_grad)
        if len(gain_parts) == nz:
            gain_rows = jnp.concatenate([sum(gain_parts)[:1], key_gains[:1]], axis=1)
            gain_rows = jnp.pad(gain_rows, ((0, 0), (0, width - 2 * HD)))
            rows_last = [sum(attn_parts)[:1], gain_rows]
            sides.append(Side(sum_all(jnp.concatenate(rows_last, axis=0), sums)))
        return back, (q_grad,)

    q_grads = []

    def through_inputs_last(k, quarter, token, before):
        back, state = through_inputs(k, quarter, token, before)
        q_grads[:] = state
        return back, state

    def query_products():
        q_flat = q_grads[0].reshape(length, -1)
        if n_f != 2:
            full = dot(normed_flat[0], q_flat, COLS_T).astype(BF16)
            return (lax.psum_scatter(full, "fsdp", scatter_dimension=0, tiled=True),)
        mine, other = normed_flat
        came = swap(dot(other, q_flat, COLS_T).astype(BF16))
        return dot(mine, q_flat, COLS_T), came

    def gather_query_grads(*products):
        own = sum(product.astype(F32) for product in products).astype(BF16)
        if n_ctx == hpf:
            sides.append(Side(gather_columns(own)))
            return
        grads["query"] = (
            lax.all_gather(own, "ctx", axis=0)
            .reshape(n_ctx // hpf, hpf, width // n_f, hpd, HD)
            .transpose(2, 0, 3, 1, 4)
            .reshape(width // n_f, H * HD)
            .astype(F32)
        )

    def gather_columns(own):
        q_rows = own.shape[0]
        if shared:
            own = jnp.concatenate([own, grads["key_piece"]], axis=0)
        arrays, placed = {}, ()
        chain = gather_planned(own, n_ctx, QUERY_GRAD_PLAN, arrays)
        going, steps = next(chain)
        for k in range(nz):
            landed = yield (*going, *placed), steps
            placed = landed[len(going) :]
            try:
                going, steps = chain.send(landed[: len(going)])
            except StopIteration:
                going = ()
            quarter = planned_quarter(arrays, k, n_ctx)
            halves = {"first": 1, "stride": 2} if k == nz - 1 else {}
            placed = place_columns(k, quarter, table, n_ctx, q_rows, placed, **halves)
            if k == nz - 2:
                along = arrays["along", nz - 1]
                pair = [along, None, lax.ppermute(along, "ctx", flip(n_ctx, 1))]
                placed = place_columns(nz - 1, pair, table, n_ctx, q_rows, placed, 0, 2)
        grads["query"] = placed[0]
        if shared:
            grads["key"], grads["value"] = placed[1:]

    normed_grad, _ = pipeline(
        n_ctx,
        later,
        through_inputs_last,
        meta_rows,
        sides,
        scatter=True,
        closing=(query_products, gather_query_grads),
    )
    while any(side.flying is not None for side in sides):
        land({}, sides)
    early, late = sums
    own_part = lambda v, size: lax.dynamic_slice_in_dim(v, f * (size // n_f), size // n_f, 0)
    grad_w_router = own_part(early[:n_exp].T, width)
    grad_norm_moe = own_part(early[n_exp], width)
    grad_norm_attn = own_part(late[0], width)
    grad_gain_query = own_part(late[1, :HD], HD)
    grad_gain_key = own_part(late[1, HD : 2 * HD], HD)

    attn_scale = lax.rsqrt(jnp.mean(x * x, axis=-1, keepdims=True) + EPS)
    attn_scaled = normed_grad * attn_gain
    input_grad = (
        middle_grad
        + attn_scale * attn_scaled
        - x
        * (
            attn_scale
            * attn_scale
            * attn_scale
            * jnp.mean(attn_scaled * x, axis=-1, keepdims=True)
        )
    )
    return (
        outputs[None],
        input_grad.astype(BF16)[None],
        grads["query"],
        grads["key"],
        grads["value"],
        grads["out"],
        grad_norm_attn,
        grad_gain_query,
        grad_gain_key,
        grad_w_router,
        grad_norm_moe,
        grads["gate"][None],
        grads["up"][None],
        grads["down"][None],
    )


def solution(mesh):
    in_specs = (
        P("fsdp", "ctx", None),
        P("fsdp", None),
        P("fsdp", None),
        P("fsdp", None),
        P("fsdp", None),
        P("fsdp"),
        P("fsdp"),
        P("fsdp"),
        P("fsdp", None),
        P("fsdp"),
        P("ctx", "fsdp", None),
        P("ctx", "fsdp", None),
        P("ctx", "fsdp", None),
        P("fsdp", None),
        P("fsdp", "ctx", None),
        P("fsdp", "ctx", None),
        P("fsdp", "ctx", None),
    )
    out_specs = (
        P("fsdp", "ctx", None),
        P("fsdp", "ctx", None),
        P("fsdp", None),
        P("fsdp", None),
        P("fsdp", None),
        P("fsdp", None),
        P("fsdp"),
        P("fsdp"),
        P("fsdp"),
        P("fsdp", None),
        P("fsdp"),
        P("ctx", "fsdp", None),
        P("ctx", "fsdp", None),
        P("ctx", "fsdp", None),
    )
    return jax.shard_map(local, mesh=mesh, in_specs=in_specs, out_specs=out_specs, check_vma=False)
```
